256 devices in a mesh: dp: 2 (over core), expert: 16 (over x, y), tensor: 8 (over z).
Axes of the slice: x: 4, y: 4, z: 8, core: 2. Of those that a mesh axis runs over, the one named last changes fastest.
Arguments:
- tokens: bfloat16 [32768, 1536], P(('dp', 'expert', 'tensor')), may hold values from -6 to 6
- segments: int32 [32, 1024], P(('dp', 'expert')), may hold values from 0 to 18, as said below
- routes: int32 [32768, 8], P(('dp', 'expert', 'tensor')), may hold values from 0 to 31, all different within a row; in each aligned block of 128 rows (0 to 127, 128 to 255, ...) at most 64 rows name the same one
- norm1_gain: float32 [1536], replicated, may hold values from 0.1 to 1.9
- w_query: bfloat16 [1536, 1536], P(None, 'tensor'), may hold values from -0.21875 to 0.21875
- w_key: bfloat16 [1536, 512], P(None, 'tensor'), may hold values from -0.15625 to 0.15625
- w_value: bfloat16 [1536, 512], P(None, 'tensor'), may hold values from -0.15625 to 0.15625
- w_out: bfloat16 [1536, 1536], P('tensor'), may hold values from -0.75 to 0.75
- norm2_gain: float32 [1536], replicated, may hold values from 0.1 to 1.9
- w_router: bfloat16 [1536, 32], replicated, may hold values from -0.078125 to 0.078125
- w_gate: bfloat16 [32, 1536, 512], P('expert', ('dp', 'tensor')), may hold values from -0.15625 to 0.15625
- w_up: bfloat16 [32, 1536, 512], P('expert', ('dp', 'tensor')), may hold values from -0.15625 to 0.15625
- w_down: bfloat16 [32, 512, 1536], P('expert', ('dp', 'tensor')), may hold values from -1 to 1
- cotangent: bfloat16 [32768, 1536], P(('dp', 'expert', 'tensor')), may hold values from -6 to 6
Outputs:
- output: bfloat16 [32768, 1536], P(('dp', 'expert', 'tensor'))
- input_grad: float32 [32768, 1536], P(('dp', 'expert', 'tensor'))
- norm1_gain_grad: float32 [1536], replicated
- w_query_grad: float32 [1536, 1536], P(None, 'tensor')
- w_key_grad: float32 [1536, 512], P(None, 'tensor')
- w_value_grad: float32 [1536, 512], P(None, 'tensor')
- w_out_grad: float32 [1536, 1536], P('tensor')
- norm2_gain_grad: float32 [1536], replicated
- w_router_grad: float32 [1536, 32], replicated
- w_gate_grad: float32 [32, 1536, 512], P('expert', ('dp', 'tensor'))
- w_up_grad: float32 [32, 1536, 512], P('expert', ('dp', 'tensor'))
- w_down_grad: float32 [32, 512, 1536], P('expert', ('dp', 'tensor'))
The draws below stay inside these ranges and needn't reach their ends.
Inputs may be any that keep to these rules, and one draw needn't show every extreme that they name: `segments`: along a sequence the numbers never fall; 0 marks trailing padding and nothing else, and every sequence ends in at least one padding position; documents are numbered 1, 2, ... in order. Every document but the last of a sequence has 60 to 800 positions; the last may be cut shorter by the padding. In every draw some sequence reaches the largest document number. `routes`: each row names 8 different experts. Within the rows of one device no expert is named by more than 64 rows, and in every draw some device names some expert exactly 64 times.
All inputs are finite; a program needn't handle non-finite values.
Results may differ from the reference program's by a relative error of at most 0.023.
Values may be sent and summed in bfloat16 or wider, within the bound.
No kernel may reach another device: no remote copies, remote signals or barrier semaphores. Data moves between devices by JAX's collectives and lax.ppermute only.
A program may use at most 192 MiB of HBM per device.

```python
import math
import jax
import jax.numpy as jnp
import numpy as np
from jax import lax

D = 1536
HEADS = 24
KV_HEADS = 8
HEAD_DIM = 64
FF = 512
TOP = 8
SEQ = 1024
TOK_DEV = 128
SEQS = 32
TOKENS = 32768
EXPERTS = 32
CAP = 64


def draw_segments(key, part):
    key = jax.random.fold_in(key, 7)
    pad_key, length_key, pick_key = jax.random.split(key, 3)
    shortest = min(60, SEQ // 8)
    longest = min(800, SEQ * 25 // 32)
    slots = SEQ // shortest + 1
    picked = jax.random.randint(pick_key, (), 0, SEQS)
    is_picked = jnp.arange(SEQS, dtype=jnp.int32)[:, None] == picked
    lengths = jax.random.randint(length_key, (SEQS, slots), shortest, longest + 1)
    lengths = jnp.where(is_picked, shortest, lengths)
    ends = jnp.cumsum(lengths, axis=1)
    padding = jax.random.randint(pad_key, (SEQS, 1), 1, max(2, shortest))
    padding = jnp.where(is_picked, 1, padding)
    positions = jnp.arange(SEQ, dtype=jnp.int32)[None, :]
    passed = jnp.sum((ends[:, None, :] <= positions[:, :, None]).astype(jnp.int32), axis=2)
    numbers = 1 + passed
    return jnp.where(positions < SEQ - padding, numbers, 0).astype(jnp.int32)


def steps_of(stream_key, extent, cuts, least, high):
    def one(dim, shards_of):
        draws = jax.random.uniform(jax.random.fold_in(jax.random.fold_in(stream_key, 6), dim), (shards_of,), jnp.float32, least / len(cuts), high / len(cuts))
        return jnp.repeat(jnp.exp(draws), extent[dim] // shards_of).reshape((-1,) + (1,) * (len(extent) - dim - 1))

    factor_of = one(*cuts[0])
    for cut in cuts[1:]:
        factor_of = factor_of * one(*cut)
    return factor_of


def shared_out(own_key, own, number, rows, number_of, top, bound, lean):
    sequence = jax.random.permutation(own_key, number_of)
    crowded, ordinary = portions_of(number_of, rows * top, bound, lean, True), portions_of(number_of, rows * top, bound, lean, False)
    places = jnp.arange(number_of)

    def named(sizes, offset_by):
        used = int((sizes > 0).sum())
        fixed = max(1, used // 4)
        moved = fixed + (places - fixed + offset_by * (used - fixed)) % max(1, number_of - fixed)
        return jnp.zeros((number_of,), jnp.int32).at[sequence[jnp.where(places < fixed, places, moved)]].set(jnp.asarray(sizes, jnp.int32))

    sizes = jnp.where(number % 4 == 0, named(crowded, number // 4), named(ordinary, number - number // 4 - 1))
    mixed = jax.random.permutation(jax.random.fold_in(own, 3), number_of)
    source_of, sink = mixed[0:number_of // 2 * 2:2], mixed[1:number_of // 2 * 2:2]
    slack = jnp.minimum(sizes[source_of] - 1, bound - sizes[sink]) // 2
    slack = jnp.where((source_of == sequence[0]) | (sink == sequence[0]) | (sizes[sink] == 0), 0, jnp.maximum(slack, 0))
    moved = jax.random.randint(jax.random.fold_in(own, 4), (number_of // 2,), 0, 1 << 20) % (slack + 1)
    sizes = sizes.at[source_of].add(-moved).at[sink].add(moved)
    members = jnp.searchsorted(jnp.cumsum(sizes), jnp.arange(rows * top), side="right").astype(jnp.int32)
    grid = members.reshape(top, rows).T
    grid = grid[jax.random.permutation(jax.random.fold_in(own, 1), rows)]
    offset_by = jax.random.randint(jax.random.fold_in(own, 2), (rows, 1), 0, top)
    return jnp.take_along_axis(grid, (jnp.arange(top)[None, :] + offset_by) % top, axis=1)


def portions_of(amount, total, limit, skew, full):
    portions = [(1 << 20) // math.isqrt(grade ** skew) + 1 for grade in range(1, amount + 1)]
    largest = limit if full else min(limit, max(-(-total // amount), total * portions[0] // sum(portions)))
    least = 1 if total - largest >= amount - 1 else 0
    holding, rest = [largest] + [least] * (amount - 1), total - largest - least * (amount - 1)
    while rest > 0:
        free = [i for i in range(1, amount) if holding[i] < largest] or [i for i in range(1, amount) if holding[i] < limit]
        pool, remaining = sum([portions[i] for i in free]), rest
        for i in free:
            addition = min(limit - holding[i], max(1, remaining * portions[i] // pool), rest)
            holding[i] = holding[i] + addition
            rest = rest - addition
    return np.array(holding)


def centred(rng, shape, width, limit, pieces=(), held_as=jnp.bfloat16):
    result = width * jax.random.normal(rng, shape, jnp.float32)
    if pieces:
        result = result * steps_of(rng, shape, pieces, -0.22, 0.18)
    return jnp.clip(result, -limit, limit).astype(held_as)


def setup_inputs(seed: int = 0) -> dict:
    keys = jax.random.split(jax.random.key(seed), 15)
    tokens = centred(keys[0], (TOKENS, D), 1.0, 6.0, ((0, 256),))
    segments = draw_segments(jax.random.fold_in(keys[14], 71), 0)
    routes_keys = jax.random.split(jax.random.fold_in(keys[2], 1), TOKENS // TOK_DEV)
    routes_turns = jax.random.permutation(jax.random.fold_in(keys[2], 3), TOKENS // TOK_DEV)
    routes = jax.vmap(lambda own, number: shared_out(jax.random.fold_in(keys[2], 2), own, number, TOK_DEV, EXPERTS, TOP, CAP, 1))(routes_keys, routes_turns).reshape((TOKENS, TOP))
    norm1_gain = jnp.clip(1.0 + 0.18 * jax.random.normal(keys[3], (D,), jnp.float32), 0.1, 1.9)
    w_query = centred(keys[4], (D, HEADS * HEAD_DIM), (D // 2) ** -0.5, 0.21875, ((1, 8),))
    w_key = centred(keys[5], (D, KV_HEADS * HEAD_DIM), D ** -0.5, 0.15625, ((1, 8),))
    w_value = centred(keys[6], (D, KV_HEADS * HEAD_DIM), D ** -0.5, 0.15625, ((1, 8),))
    w_out = centred(keys[7], (HEADS * HEAD_DIM, D), HEAD_DIM ** -0.5, 0.75, ((0, 8),))
    norm2_gain = jnp.clip(1.0 + 0.18 * jax.random.normal(keys[8], (D,), jnp.float32), 0.1, 1.9)
    w_router = centred(keys[9], (D, EXPERTS), (4 * D) ** -0.5, 0.078125)
    w_gate = centred(keys[10], (EXPERTS, D, FF), D ** -0.5, 0.15625, ((0, 16), (1, 16)))
    w_up = centred(keys[11], (EXPERTS, D, FF), D ** -0.5, 0.15625, ((0, 16), (1, 16)))
    w_down = centred(keys[12], (EXPERTS, FF, D), (FF // 16) ** -0.5, 1.0, ((0, 16), (1, 16)))
    cotangent = centred(keys[13], (TOKENS, D), 1.0, 6.0, ((0, 256),))
    return dict(tokens=tokens, segments=segments, routes=routes, norm1_gain=norm1_gain, w_query=w_query, w_key=w_key, w_value=w_value, w_out=w_out, norm2_gain=norm2_gain, w_router=w_router, w_gate=w_gate, w_up=w_up, w_down=w_down, cotangent=cotangent)


epsilon_norm = 1e-06
rope_theta = 10000.0
masked_score = -1e+30
highest = lax.Precision.HIGHEST

@jax.custom_vjp
def low(v):
    return lax.optimization_barrier(v.astype(jnp.bfloat16)).astype(jnp.float32)

@jax.custom_vjp
def low_back(v):
    return v

def low_keep(v):
    return (low(v), None)

def low_pass(kept, grad):
    return (grad,)

def back_keep(v):
    return (v, None)

def back_low(kept, grad):
    return (low(grad),)
low.defvjp(low_keep, low_pass)
low_back.defvjp(back_keep, back_low)

def product(left_side, right_side):
    return jnp.dot(left_side, right_side, precision=highest, preferred_element_type=jnp.float32)

def rms_norm(values, norm_gain):
    return values * lax.rsqrt(lax.optimization_barrier(jnp.mean(values * values, axis=-1, keepdims=True)) + epsilon_norm) * norm_gain

def rope_tables(seq_len, head_width):
    half_dim = head_width // 2
    frequency = rope_theta ** (-2.0 * jnp.arange(half_dim, dtype=jnp.float32) / head_width)
    angles = jnp.arange(seq_len, dtype=jnp.float32)[:, None] * frequency[None, :]
    angles = jnp.concatenate([angles, angles], axis=1)
    return (jnp.cos(angles), jnp.sin(angles))

def rotate_half(values):
    half_dim = values.shape[-1] // 2
    return jnp.concatenate([-values[..., half_dim:], values[..., :half_dim]], axis=-1)

def apply_rope(values, cosine_table, sine_table):
    return values * cosine_table + rotate_half(values) * sine_table

def allowed_mask(query_pos, query_seg, key_pos, key_seg):
    same_doc = query_seg[:, None] == key_seg[None, :]
    causal = key_pos[None, :] <= query_pos[:, None]
    diagonal = key_pos[None, :] == query_pos[:, None]
    return causal & same_doc & ((query_seg[:, None] != 0) | diagonal)

def attend_sequence(normed_seq, seg_row, w_query, w_key, w_value):
    seq_len = normed_seq.shape[0]
    group_size = HEADS // KV_HEADS
    query_raw = product(normed_seq, w_query).reshape(seq_len, KV_HEADS, group_size, HEAD_DIM)
    keys_raw = product(normed_seq, w_key).reshape(seq_len, KV_HEADS, HEAD_DIM)
    values_raw = product(normed_seq, w_value).reshape(seq_len, KV_HEADS, HEAD_DIM)
    cosine_table, sine_table = rope_tables(seq_len, HEAD_DIM)
    query_rot = low(apply_rope(low_back(query_raw), cosine_table[:, None, None, :], sine_table[:, None, None, :]))
    key_rot = low(apply_rope(low_back(keys_raw), cosine_table[:, None, :], sine_table[:, None, :]))
    value_low = low(low_back(values_raw))
    scores = low_back(jnp.einsum('qgrd,kgd->grqk', query_rot, key_rot, precision=highest) * HEAD_DIM ** (-0.5))
    positions = jnp.arange(seq_len, dtype=jnp.int32)
    masked = jnp.where(allowed_mask(positions, seg_row, positions, seg_row), scores, masked_score)
    top_score = lax.optimization_barrier(jnp.max(masked, axis=-1, keepdims=True))
    exp_scores = jnp.exp(masked - top_score)
    attn_probs = low(exp_scores / lax.optimization_barrier(jnp.sum(exp_scores, axis=-1, keepdims=True)))
    context = jnp.einsum('grqk,kgd->qgrd', attn_probs, value_low, precision=highest)
    return context.reshape(seq_len, HEADS * HEAD_DIM)

def layer_block(weights, token_block, seg_block, route_block):
    norm1_gain, w_query, w_key, w_value, w_out, norm2_gain, w_router, w_gate, w_up, w_down = weights
    per_step = token_block.shape[0]
    row_total = per_step * SEQ
    token_rows = token_block.reshape(row_total, D)
    normed_one = low(rms_norm(token_block, norm1_gain))
    attend_one = jax.checkpoint(attend_sequence)

    def attend_pair(seq_in):
        return attend_one(seq_in[0], seq_in[1], w_query, w_key, w_value)
    context = lax.map(attend_pair, (normed_one, seg_block))
    context = low(low_back(context.reshape(row_total, HEADS * HEAD_DIM)))
    attention = low_back(product(context, w_out))
    residual_mid = token_rows + attention
    normed_two = low(rms_norm(residual_mid, norm2_gain))
    logits = low_back(product(normed_two, w_router))
    chosen = jnp.take_along_axis(logits, route_block, axis=1)
    chosen_exp = jnp.exp(chosen - lax.optimization_barrier(jnp.max(chosen, axis=1, keepdims=True)))
    gate_probs = chosen_exp / lax.optimization_barrier(jnp.sum(chosen_exp, axis=1, keepdims=True))
    flat_routes = route_block.reshape(row_total * TOP)
    expert_ids = jnp.arange(EXPERTS, dtype=jnp.int32)
    pair_hot = (flat_routes[:, None] == expert_ids[None, :]).astype(jnp.int32)
    pair_rank = lax.optimization_barrier(jnp.sum(pair_hot * (jnp.cumsum(pair_hot, axis=0) - 1), axis=1)).astype(jnp.int32)
    slot_total = row_total // TOK_DEV * CAP
    slot_pair = jnp.full((EXPERTS, slot_total), row_total * TOP, jnp.int32)
    slot_pair = slot_pair.at[flat_routes, pair_rank].set(jnp.arange(row_total * TOP, dtype=jnp.int32))
    padded = jnp.concatenate([normed_two, jnp.zeros((1, D), jnp.float32)], axis=0)
    expert_in = low_back(padded[slot_pair // TOP])
    gate_pre = low_back(jnp.einsum('esd,edf->esf', expert_in, w_gate, precision=highest))
    up_pre = low_back(jnp.einsum('esd,edf->esf', expert_in, w_up, precision=highest))
    hidden = low(gate_pre * jax.nn.sigmoid(gate_pre) * up_pre)
    expert_out = low_back(low(jnp.einsum('esf,efd->esd', hidden, w_down, precision=highest)))
    pair_out = expert_out[flat_routes, pair_rank].reshape(row_total, TOP, D)
    mixture = lax.optimization_barrier(jnp.sum(gate_probs[:, :, None] * pair_out, axis=1))
    return (residual_mid + mixture).reshape(per_step, SEQ, D)

def reference(tokens, segments, routes, norm1_gain, w_query, w_key, w_value, w_out, norm2_gain, w_router, w_gate, w_up, w_down, cotangent):
    per_step = math.gcd(SEQS, max(1, 4096 // SEQ))
    step_count = SEQS // per_step
    token_steps = tokens.astype(jnp.float32).reshape(step_count, per_step, SEQ, D)
    seg_steps = segments.reshape(step_count, per_step, SEQ)
    route_steps = routes.reshape(step_count, per_step * SEQ, TOP)
    weights = tuple((weight_arg.astype(jnp.float32) for weight_arg in (norm1_gain, w_query, w_key, w_value, w_out, norm2_gain, w_router, w_gate, w_up, w_down)))
    block_fn = jax.checkpoint(layer_block)

    def forward(token_all, weight_all):

        def scan_block(carry_in, block_in):
            return (carry_in, block_fn(weight_all, block_in[0], block_in[1], block_in[2]))
        carry_out, outputs = lax.scan(scan_block, jnp.zeros((), jnp.float32), (token_all, seg_steps, route_steps))
        return outputs
    outputs, pullback = jax.vjp(forward, token_steps, weights)
    token_grad, weight_grads = pullback(cotangent.astype(jnp.float32).reshape(outputs.shape))
    return (outputs.reshape(TOKENS, D).astype(jnp.bfloat16), token_grad.reshape(TOKENS, D), weight_grads[0], weight_grads[1], weight_grads[2], weight_grads[3], weight_grads[4], weight_grads[5], weight_grads[6], weight_grads[7], weight_grads[8], weight_grads[9])
```

```python
import jax
import jax.numpy as jnp
from jax import lax
from jax.sharding import PartitionSpec as P

HEAD_DIM = 64
HALF = HEAD_DIM // 2
TOP = 8
CAP = 64
LANES = 128

epsilon_norm = 1e-06
rope_theta = 10000.0
masked_score = -1e30
block_limit = 512
f32 = jnp.float32
bf16 = jnp.bfloat16


def rms_inverse(values):
    return lax.rsqrt(jnp.mean(values * values, axis=-1, keepdims=True) + epsilon_norm)


def rms_backward(values, inverse, norm_gain, grad_out):
    scaled = grad_out * norm_gain
    grad_in = inverse * scaled - values * (inverse * inverse * inverse) * jnp.mean(
        scaled * values, axis=-1, keepdims=True
    )
    return (grad_in, jnp.sum(grad_out * values * inverse, axis=0))


def rope_tables(seq_len, head_width):
    half_dim = head_width // 2
    frequency = rope_theta ** (-2.0 * jnp.arange(half_dim, dtype=f32) / head_width)
    angles = jnp.arange(seq_len, dtype=f32)[:, None] * frequency[None, :]
    angles = jnp.concatenate([angles, angles], axis=1)
    return (jnp.cos(angles), jnp.sin(angles))


def rotate_half(values):
    return jnp.concatenate([-values[..., HALF:], values[..., :HALF]], axis=-1)


def rotate_back(values):
    return jnp.concatenate([values[..., HALF:], -values[..., :HALF]], axis=-1)


def dot32(left, right):
    return jnp.dot(left, right, preferred_element_type=f32)


def allowed_mask(query_pos, query_seg, key_pos, key_seg):
    same_doc = query_seg[:, None] == key_seg[None, :]
    causal = key_pos[None, :] <= query_pos[:, None]
    diagonal = key_pos[None, :] == query_pos[:, None]
    return causal & same_doc & ((query_seg[:, None] != 0) | diagonal)


def attention_forward(normed_all, joined_weights, key_seg, tables):
    seq_len = normed_all.shape[0]
    kv_width = HEAD_DIM
    query_width = joined_weights.shape[1] - 2 * kv_width
    heads = query_width // HEAD_DIM
    joined = dot32(normed_all, joined_weights)
    cosine, sine = tables
    query = joined[:, :query_width].reshape(seq_len, heads, HEAD_DIM)
    key = joined[:, query_width : query_width + kv_width]
    value_low = joined[:, query_width + kv_width :].astype(bf16)
    query_low = (query * cosine[:, None, :] + rotate_half(query) * sine[:, None, :]).astype(bf16)
    key_low = (key * cosine + rotate_half(key) * sine).astype(bf16)
    pos = jnp.arange(seq_len, dtype=jnp.int32)
    scores = jnp.einsum("qrd,kd->rqk", query_low, key_low, preferred_element_type=f32)
    masked = jnp.where(
        allowed_mask(pos, key_seg, pos, key_seg), scores * HEAD_DIM ** (-0.5), masked_score
    )
    top_score = jnp.max(masked, axis=-1, keepdims=True)
    exp_scores = jnp.exp(masked - top_score)
    exp_total = jnp.sum(exp_scores, axis=-1, keepdims=True)
    probs = (exp_scores / exp_total).astype(bf16)
    context = jnp.einsum("rqk,kd->qrd", probs, value_low, preferred_element_type=f32)
    lse = (top_score + jnp.log(exp_total))[..., 0]
    return context.reshape(seq_len, query_width).astype(bf16), (
        query_low,
        key_low,
        value_low,
        lse,
    )


def attention_backward(saved, context_grad, key_seg, tables):
    query_low, key_low, value_low, lse = saved
    seq_len, heads, _ = query_low.shape
    cosine, sine = tables
    grad = context_grad.reshape(seq_len, heads, HEAD_DIM)
    pos = jnp.arange(seq_len, dtype=jnp.int32)
    scale = HEAD_DIM ** (-0.5)
    scores = jnp.einsum("qrd,kd->rqk", query_low, key_low, preferred_element_type=f32) * scale
    masked = jnp.where(allowed_mask(pos, key_seg, pos, key_seg), scores, masked_score)
    probs = jnp.exp(masked - lse[..., None])
    probs_grad = jnp.einsum("qrd,kd->rqk", grad, value_low, preferred_element_type=f32)
    row_dot = jnp.sum(probs * probs_grad, axis=-1, keepdims=True)
    score_grad = (probs * (probs_grad - row_dot)).astype(bf16)
    query_grad = jnp.einsum("rqk,kd->qrd", score_grad, key_low, preferred_element_type=f32)
    key_grad = jnp.einsum("rqk,qrd->kd", score_grad, query_low, preferred_element_type=f32)
    value_grad = jnp.einsum("rqk,qrd->kd", probs.astype(bf16), grad, preferred_element_type=f32)
    query_grad = query_grad * scale
    key_grad = key_grad * scale
    query_grad = query_grad * cosine[:, None, :] + rotate_back(query_grad * sine[:, None, :])
    key_grad = key_grad * cosine + rotate_back(key_grad * sine)
    return jnp.concatenate(
        [query_grad.reshape(seq_len, heads * HEAD_DIM), key_grad, value_grad], axis=1
    ).astype(bf16)


def split_two(values):
    high = values.astype(bf16)
    return high, (values - high.astype(f32)).astype(bf16)


SIDE = 4
STEPS = (0, 1, -1, 2)


def owner_of(place, me):
    return jnp.asarray([0, 2, 3, 1])[(place - me) % SIDE]


def along(axis, step):
    pairs = []
    for a in range(SIDE):
        for b in range(SIDE):
            to = ((a + step) % SIDE, b) if axis == 0 else (a, (b + step) % SIDE)
            pairs.append((a * SIDE + b, to[0] * SIDE + to[1]))
    return pairs


def move(values, axis, step):
    return lax.ppermute(values, "expert", along(axis, step))


def together(*values):
    return lax.optimization_barrier(values)


def swap_cores(values):
    return lax.ppermute(values, "dp", [(0, 1), (1, 0)])


def line_gather(values, axis):
    return [values] + [move(values, axis, step) for step in STEPS[1:]]


def gather_plane(values):
    half = values.shape[0] // 2
    first = line_gather(jnp.stack(line_gather(values[:half], 1)), 0)
    second = line_gather(jnp.stack(line_gather(values[half:], 0)), 1)
    return first, second


def line_scatter(parts, axis):
    total = parts[0].astype(f32)
    for part, step in zip(parts[1:], STEPS[1:]):
        total = total + move(part, axis, -step).astype(f32)
    return total.astype(bf16)


def scatter_plane(first, second):
    first = line_scatter(first, 0)
    second = line_scatter(second, 1)
    first = line_scatter([first[i] for i in range(SIDE)], 1)
    second = line_scatter([second[i] for i in range(SIDE)], 0)
    return jnp.concatenate([first, second], axis=0)


def local(
    tokens,
    segments,
    routes,
    norm1_gain,
    w_query,
    w_key,
    w_value,
    w_out,
    norm2_gain,
    w_router,
    w_gate,
    w_up,
    w_down,
    cotangent,
):
    tok_rows, width = tokens.shape
    seq_len = segments.shape[1]
    query_width = w_query.shape[1]
    kv_width = w_key.shape[1]
    joined_width = query_width + 2 * kv_width
    local_experts = w_gate.shape[0]
    experts = w_router.shape[1]
    owners = lax.axis_size("expert")
    planes = lax.axis_size("tensor")
    owner = lax.axis_index("expert")
    first_expert = owner * local_experts
    key_seg = segments[0]
    hidden_width = w_gate.shape[2]

    token_f32 = tokens.astype(f32)
    inverse_one = rms_inverse(token_f32)
    normed_low = (token_f32 * inverse_one * norm1_gain).astype(bf16)
    joined_weights = jnp.concatenate([w_query, w_key, w_value], axis=1)
    normed_all = lax.all_gather(normed_low, "tensor", axis=0, tiled=True)
    core = lax.axis_index("dp")

    expert_ids = jnp.arange(experts, dtype=jnp.int32)
    onehot = (routes[:, :, None] == expert_ids[None, None, :]).astype(f32)
    member = jnp.sum(onehot, axis=1)
    lower = (jnp.arange(tok_rows)[:, None] <= jnp.arange(tok_rows)[None, :]).astype(bf16)
    rank = jnp.einsum("te,tu->eu", member.astype(bf16), lower, preferred_element_type=f32)
    rank = jnp.where(member.T > 0, rank - 1.0, -1.0).astype(bf16)
    extra = jnp.pad(rank, ((0, tok_rows - experts), (0, LANES - tok_rows)))
    cot_payload = jnp.concatenate([cotangent, extra], axis=1)

    cot_halves = gather_plane(cot_payload)

    def half_gather(shard):
        count = shard.shape[0] // 2
        half = lax.dynamic_slice_in_dim(shard, core * count, count, 0)
        return lax.all_gather(half, "tensor", axis=0)

    normed_all, cot_halves, w_out = together(normed_all, cot_halves, w_out)
    half_out = half_gather(w_out)
    weights = jnp.concatenate(
        [w_gate, w_up, w_down.reshape(local_experts, -1, hidden_width)], axis=1
    )
    half_out, weights = together(half_out, weights)
    weights_all = lax.all_gather(weights, ("dp", "tensor"), axis=0)
    weights_all, joined_rows = together(weights_all, joined_weights.T)
    half_joined = half_gather(joined_rows)

    tables = rope_tables(seq_len, HEAD_DIM)
    context, saved = attention_forward(normed_all, joined_weights, key_seg, tables)
    context_home = lax.all_to_all(
        context.reshape(planes, tok_rows, query_width), "tensor", split_axis=0, concat_axis=0
    )
    other_out = swap_cores(half_out)

    def both_halves(blocks, mine, other):
        count = blocks.shape[2] // 2
        first = lax.dynamic_slice_in_dim(blocks, core * count, count, 2)
        second = lax.dynamic_slice_in_dim(blocks, (1 - core) * count, count, 2)
        return jnp.einsum("jtq,jqd->td", first, mine, preferred_element_type=f32) + jnp.einsum(
            "jtq,jqd->td", second, other, preferred_element_type=f32
        )

    mid = token_f32 + both_halves(context_home, half_out, other_out)
    inverse_two = rms_inverse(mid)
    normed_two = (mid * inverse_two * norm2_gain).astype(bf16)
    logits = dot32(normed_two, w_router)
    logits = jnp.where(member > 0, logits, masked_score)
    chosen_exp = jnp.where(
        member > 0, jnp.exp(logits - jnp.max(logits, axis=1, keepdims=True)), 0.0
    )
    gates = chosen_exp / jnp.sum(chosen_exp, axis=1, keepdims=True)
    gate_high, gate_low = split_two(gates)
    payload = jnp.concatenate(
        [normed_two, gate_high, gate_low, jnp.zeros((tok_rows, LANES - 2 * experts), bf16)],
        axis=1,
    )
    rows_halves = gather_plane(payload)

    def whole(halves):
        first, second = halves
        first = jnp.stack(first)
        second = jnp.stack(second).transpose(1, 0, 2, 3)
        return jnp.concatenate([first, second], axis=2).reshape(owners, tok_rows, width + LANES)

    cot_all = whole(cot_halves)
    rows_all = whole(rows_halves)
    ranks = lax.dynamic_slice_in_dim(
        cot_all[:, :experts, width : width + tok_rows], first_expert, local_experts, 1
    )
    slots = jnp.arange(CAP, dtype=f32)
    pick = (ranks[:, :, None, :].astype(f32) == slots[:, None]).astype(bf16)
    rows = jnp.einsum("sect,std->secd", pick, rows_all, preferred_element_type=f32).astype(bf16)
    cots = jnp.einsum(
        "sect,std->secd", pick, cot_all[:, :, :width], preferred_element_type=f32
    ).astype(bf16)
    lane = jnp.arange(LANES, dtype=jnp.int32)
    mine = first_expert + jnp.arange(local_experts, dtype=jnp.int32)[:, None]
    mine_mask = ((lane == mine) | (lane == mine + experts)).astype(f32)
    gate_col = jnp.sum(
        rows[..., width:].astype(f32) * mine_mask[:, None, :], axis=-1, keepdims=True
    )
    rows = rows[..., :width]

    group = weights_all.shape[0]
    part_rows = w_gate.shape[1]
    down_rows = w_down.shape[1]
    full_gate = weights_all[:, :, :part_rows].transpose(1, 0, 2, 3).reshape(
        local_experts, group * part_rows, hidden_width
    )
    full_up = weights_all[:, :, part_rows : 2 * part_rows].transpose(1, 0, 2, 3).reshape(
        local_experts, group * part_rows, hidden_width
    )
    full_down = (
        weights_all[:, :, 2 * part_rows :]
        .transpose(1, 0, 2, 3)
        .reshape(local_experts, group * down_rows, width)
    )
    gate_pre = jnp.einsum("secd,edf->secf", rows, full_gate, preferred_element_type=f32)
    up_pre = jnp.einsum("secd,edf->secf", rows, full_up, preferred_element_type=f32)
    gate_sig = jax.nn.sigmoid(gate_pre)
    silu = gate_pre * gate_sig
    hidden = (silu * up_pre).astype(bf16)
    back = jnp.einsum("secd,efd->secf", cots, full_down, preferred_element_type=f32)
    gate_grad = jnp.sum(back * hidden.astype(f32), axis=-1, keepdims=True)
    hidden_grad = gate_col * back
    gate_pre_grad = (hidden_grad * up_pre * (gate_sig + silu * (1.0 - gate_sig))).astype(bf16)
    up_pre_grad = (hidden_grad * silu).astype(bf16)
    row_grads = jnp.einsum("secf,edf->secd", gate_pre_grad, full_gate, preferred_element_type=f32)
    row_grads = row_grads + jnp.einsum(
        "secf,edf->secd", up_pre_grad, full_up, preferred_element_type=f32
    )
    grad_high, grad_low = split_two(gate_grad)
    high_mask = (lane == mine)[:, None, :]
    low_mask = (lane == mine + experts)[:, None, :]
    tail = jnp.where(high_mask, grad_high, jnp.where(low_mask, grad_low, jnp.zeros((), bf16)))
    row_grads = jnp.concatenate([row_grads.astype(bf16), tail], axis=-1)
    back_part = jnp.einsum("sect,secd->std", pick, row_grads, preferred_element_type=f32)
    back_part = back_part.astype(bf16).reshape(SIDE, SIDE, tok_rows, width + LANES)
    half = tok_rows // 2
    back_home = scatter_plane(
        [back_part[i, :, :half] for i in range(SIDE)],
        [back_part[:, i, half:] for i in range(SIDE)],
    )

    expert_out = jnp.einsum("secf,efd->secd", hidden, full_down, preferred_element_type=f32)
    mixture_part = jnp.einsum(
        "sect,secd->std", pick, (gate_col * expert_out).astype(bf16), preferred_element_type=f32
    )
    place = (owner_of(jnp.arange(SIDE), owner // SIDE)[:, None] * SIDE) + owner_of(
        jnp.arange(SIDE), owner % SIDE
    )
    gate_w = jnp.einsum("secd,secf->edf", rows, gate_pre_grad, preferred_element_type=f32)
    up_w = jnp.einsum("secd,secf->edf", rows, up_pre_grad, preferred_element_type=f32)
    scaled_hidden = (gate_col * hidden.astype(f32)).astype(bf16)
    down_w = jnp.einsum("secf,secd->efd", scaled_hidden, cots, preferred_element_type=f32)

    def by_holder(part):
        return part.astype(bf16).reshape(local_experts, group, -1, hidden_width)

    weight_part = jnp.concatenate([by_holder(gate_w), by_holder(up_w), by_holder(down_w)], axis=2)
    weight_part = weight_part.transpose(1, 0, 2, 3)
    kept = lax.dynamic_slice_in_dim(weight_part, core * planes, planes, 0)
    given = lax.dynamic_slice_in_dim(weight_part, (1 - core) * planes, planes, 0)
    kept = (kept.astype(f32) + swap_cores(given).astype(f32)).astype(bf16)
    back_home, mixture_part, kept, half_joined = together(
        back_home, mixture_part.astype(bf16)[place.reshape(-1)], kept, half_joined
    )
    cot_f32 = cotangent.astype(f32)
    grad_tail = back_home[:, width:].astype(f32)
    gate_grad = grad_tail[:, :experts] + grad_tail[:, experts : 2 * experts]
    chosen_grad = gates * (gate_grad - jnp.sum(gates * gate_grad, axis=1, keepdims=True))
    logit_grad = chosen_grad.astype(bf16)
    router_part = jnp.einsum("td,te->de", normed_two, logit_grad, preferred_element_type=f32)
    normed_two_grad = back_home[:, :width].astype(f32) + jnp.einsum(
        "te,de->td", logit_grad, w_router, preferred_element_type=f32
    )
    mid_part, norm2_part = rms_backward(mid, inverse_two, norm2_gain, normed_two_grad)
    mid_grad = cot_f32 + mid_part
    attention_low = mid_grad.astype(bf16)
    def both_back(rows, mine, other):
        first = jnp.einsum("td,jqd->jtq", rows, mine, preferred_element_type=f32)
        second = jnp.einsum("td,jqd->jtq", rows, other, preferred_element_type=f32)
        low = jnp.where(core == 0, first, second)
        high = jnp.where(core == 0, second, first)
        return jnp.concatenate([low, high], axis=2).astype(bf16)

    context_grad = both_back(attention_low, half_out, other_out)
    context_grad = lax.all_to_all(context_grad, "tensor", split_axis=0, concat_axis=0)
    weight_sum = lax.psum_scatter(kept, "tensor", scatter_dimension=0, tiled=True)[0].astype(f32)
    mixture_part, weight_sum = together(mixture_part, weight_sum)
    mixture = lax.psum_scatter(
        mixture_part.reshape(owners * tok_rows, width), "expert", scatter_dimension=0, tiled=True
    )
    output = (mid + mixture.astype(f32)).astype(bf16)
    w_gate_grad = weight_sum[:, :part_rows]
    w_up_grad = weight_sum[:, part_rows : 2 * part_rows]
    w_down_grad = weight_sum[:, 2 * part_rows :].reshape(local_experts, down_rows, width)

    joined_grad = attention_backward(
        saved, context_grad.reshape(seq_len, query_width), key_seg, tables
    )
    joined_grad, weight_sum = together(joined_grad, weight_sum)
    joined_home = lax.all_to_all(
        joined_grad.reshape(planes, tok_rows, joined_width), "tensor", split_axis=0, concat_axis=0
    )
    attention_all = lax.all_gather(attention_low, "tensor", axis=0, tiled=True)
    out_part = jnp.einsum("tq,td->qd", context, attention_all, preferred_element_type=f32)
    joined_part = jnp.einsum("td,tq->dq", normed_all, joined_grad, preferred_element_type=f32)
    normed_one_grad = both_halves(joined_home, half_joined, swap_cores(half_joined))
    input_part, norm1_part = rms_backward(token_f32, inverse_one, norm1_gain, normed_one_grad)
    input_grad = mid_grad + input_part

    sharers = lax.axis_size("dp") * owners
    shared_part = jnp.concatenate([router_part.reshape(-1), norm2_part, norm1_part])
    flat_part = jnp.concatenate(
        [
            part.astype(bf16).reshape(-1, LANES)
            for part in (joined_part, out_part, shared_part)
        ],
        axis=0,
    )
    flat_rows = flat_part.shape[0]
    block = -(-flat_rows // (16 * sharers)) * 16
    flat_part = jnp.pad(flat_part, ((0, sharers * block - flat_rows), (0, 0)))
    arrived = lax.all_to_all(
        flat_part.reshape(sharers, block, LANES), ("dp", "expert"), split_axis=0, concat_axis=0
    )
    total = jnp.sum(arrived.astype(f32), axis=0).astype(bf16)
    flat_sum = lax.all_to_all(
        jnp.broadcast_to(total[None], arrived.shape), ("dp", "expert"), split_axis=0, concat_axis=0
    ).reshape(sharers * block, LANES)
    cut = width * joined_width // LANES
    end = cut + query_width * width // LANES
    joined_sum = flat_sum[:cut].reshape(width, joined_width).astype(f32)
    out_sum = flat_sum[cut:end].reshape(query_width, width).astype(f32)
    shared = flat_sum[end:flat_rows]
    shared = lax.all_to_all(
        jnp.broadcast_to(shared[None], (planes,) + shared.shape),
        "tensor",
        split_axis=0,
        concat_axis=0,
    )
    shared = jnp.sum(shared.astype(f32), axis=0).reshape(-1)
    router_size = width * experts
    return (
        output,
        input_grad,
        shared[router_size + width : router_size + 2 * width],
        joined_sum[:, :query_width],
        joined_sum[:, query_width : query_width + kv_width],
        joined_sum[:, query_width + kv_width :],
        out_sum,
        shared[router_size : router_size + width],
        shared[:router_size].reshape(width, experts),
        w_gate_grad,
        w_up_grad,
        w_down_grad,
    )


def solution(mesh):
    rows = P(("dp", "expert", "tensor"), None)
    columns = P(None, "tensor")
    experts = P("expert", ("dp", "tensor"), None)
    return jax.shard_map(
        local,
        mesh=mesh,
        in_specs=(
            rows,
            P(("dp", "expert"), None),
            rows,
            P(),
            columns,
            columns,
            columns,
            P("tensor", None),
            P(),
            P(),
            experts,
            experts,
            experts,
            rows,
        ),
        out_specs=(
            rows,
            rows,
            P(),
            columns,
            columns,
            columns,
            P("tensor", None),
            P(),
            P(),
            experts,
            experts,
            experts,
        ),
        check_vma=False,
    )
```

```python
import jax
import jax.numpy as jnp
from jax import lax
from jax.experimental import pallas as pl
from jax.experimental.layout import Layout, with_layout_constraint
from jax.experimental.pallas import tpu as pltpu
from jax.sharding import PartitionSpec as P

HEAD_DIM = 64
HALF = HEAD_DIM // 2
TOP = 8
CAP = 64
EXPERTS = 32
LANES = 128

epsilon_norm = 1e-06
rope_theta = 10000.0
masked_score = -1e30
block_limit = 512
f32 = jnp.float32
bf16 = jnp.bfloat16


def rms_inverse(values):
    return lax.rsqrt(jnp.mean(values * values, axis=-1, keepdims=True) + epsilon_norm)


def rms_backward(values, inverse, norm_gain, grad_out):
    scaled = grad_out * norm_gain
    grad_in = inverse * scaled - values * (inverse * inverse * inverse) * jnp.mean(
        scaled * values, axis=-1, keepdims=True
    )
    return (grad_in, jnp.sum(grad_out * values * inverse, axis=0))


def rope_tables(seq_len, head_width):
    half_dim = head_width // 2
    frequency = rope_theta ** (-2.0 * jnp.arange(half_dim, dtype=f32) / head_width)
    angles = jnp.arange(seq_len, dtype=f32)[:, None] * frequency[None, :]
    angles = jnp.concatenate([angles, angles], axis=1)
    return (jnp.cos(angles), jnp.sin(angles))


def rotate_half(values):
    return jnp.concatenate([-values[..., HALF:], values[..., :HALF]], axis=-1)


def rotate_back(values):
    return jnp.concatenate([values[..., HALF:], -values[..., :HALF]], axis=-1)


def dot32(left, right):
    return jnp.dot(left, right, preferred_element_type=f32)


def allowed_mask(query_pos, query_seg, key_pos, key_seg):
    same_doc = query_seg[:, None] == key_seg[None, :]
    causal = key_pos[None, :] <= query_pos[:, None]
    diagonal = key_pos[None, :] == query_pos[:, None]
    return causal & same_doc & ((query_seg[:, None] != 0) | diagonal)


def attention_forward(normed_all, joined_weights, key_seg, tables):
    seq_len = normed_all.shape[0]
    kv_width = HEAD_DIM
    query_width = joined_weights.shape[1] - 2 * kv_width
    heads = query_width // HEAD_DIM
    joined = dot32(normed_all, joined_weights)
    cosine, sine = tables
    query = joined[:, :query_width].reshape(seq_len, heads, HEAD_DIM)
    key = joined[:, query_width : query_width + kv_width]
    value_low = joined[:, query_width + kv_width :].astype(bf16)
    query_low = (query * cosine[:, None, :] + rotate_half(query) * sine[:, None, :]).astype(bf16)
    key_low = (key * cosine + rotate_half(key) * sine).astype(bf16)
    pos = jnp.arange(seq_len, dtype=jnp.int32)
    scores = jnp.einsum("qrd,kd->rqk", query_low, key_low, preferred_element_type=f32)
    masked = jnp.where(
        allowed_mask(pos, key_seg, pos, key_seg), scores * HEAD_DIM ** (-0.5), masked_score
    )
    top_score = jnp.max(masked, axis=-1, keepdims=True)
    exp_scores = jnp.exp(masked - top_score)
    exp_total = jnp.sum(exp_scores, axis=-1, keepdims=True)
    probs = (exp_scores / exp_total).astype(bf16)
    context = jnp.einsum("rqk,kd->qrd", probs, value_low, preferred_element_type=f32)
    lse = (top_score + jnp.log(exp_total))[..., 0]
    return context.reshape(seq_len, query_width).astype(bf16), (
        query_low,
        key_low,
        value_low,
        lse,
    )


def attention_backward(saved, context_grad, key_seg, tables):
    query_low, key_low, value_low, lse = saved
    seq_len, heads, _ = query_low.shape
    cosine, sine = tables
    grad = context_grad.reshape(seq_len, heads, HEAD_DIM)
    pos = jnp.arange(seq_len, dtype=jnp.int32)
    scale = HEAD_DIM ** (-0.5)
    scores = jnp.einsum("qrd,kd->rqk", query_low, key_low, preferred_element_type=f32) * scale
    masked = jnp.where(allowed_mask(pos, key_seg, pos, key_seg), scores, masked_score)
    probs = jnp.exp(masked - lse[..., None])
    probs_grad = jnp.einsum("qrd,kd->rqk", grad, value_low, preferred_element_type=f32)
    row_dot = jnp.sum(probs * probs_grad, axis=-1, keepdims=True)
    score_grad = (probs * (probs_grad - row_dot)).astype(bf16)
    query_grad = jnp.einsum("rqk,kd->qrd", score_grad, key_low, preferred_element_type=f32)
    key_grad = jnp.einsum("rqk,qrd->kd", score_grad, query_low, preferred_element_type=f32)
    value_grad = jnp.einsum("rqk,qrd->kd", probs.astype(bf16), grad, preferred_element_type=f32)
    query_grad = query_grad * scale
    key_grad = key_grad * scale
    query_grad = query_grad * cosine[:, None, :] + rotate_back(query_grad * sine[:, None, :])
    key_grad = key_grad * cosine + rotate_back(key_grad * sine)
    return jnp.concatenate(
        [query_grad.reshape(seq_len, heads * HEAD_DIM), key_grad, value_grad], axis=1
    ).astype(bf16)


def split_two(values):
    high = values.astype(bf16)
    return high, (values - high.astype(f32)).astype(bf16)


SIDE = 4
STEPS = (0, 1, -1, 2)


def by_rows(values):
    return with_layout_constraint(values, Layout(major_to_minor=tuple(range(values.ndim))))


def cross(values, stage, step):
    pairs = []
    plane = SIDE * SIDE
    for core in range(2):
        for x in range(SIDE):
            for y in range(SIDE):
                if core == stage:
                    to = x * SIDE + (y + step) % SIDE
                else:
                    to = (x + step) % SIDE * SIDE + y
                pairs.append((core * plane + x * SIDE + y, core * plane + to))
    return lax.ppermute(values, ("dp", "expert"), pairs)


def gather_plane(values):
    values = by_rows(values)
    line = jnp.stack([values] + [cross(values, 0, step) for step in STEPS[1:]])
    line = by_rows(line)
    return [line] + [cross(line, 1, step) for step in STEPS[1:]]


def scatter_plane(parts):
    arrived = [parts[0]] + [by_rows(cross(part, 1, -step)) for part, step in zip(parts[1:], STEPS[1:])]
    line = [
        by_rows(sum(part[place].astype(f32) for part in arrived).astype(bf16))
        for place in range(SIDE)
    ]
    arrived = [line[0]] + [cross(part, 0, -step) for part, step in zip(line[1:], STEPS[1:])]
    return by_rows(sum(part.astype(f32) for part in arrived))


def together(*values):
    return lax.optimization_barrier(values)


def swap_cores(values):
    return lax.ppermute(values, "dp", [(0, 1), (1, 0)])


def contract(left, right, left_dim, right_dim):
    return lax.dot_general(
        left, right, (((left_dim,), (right_dim,)), ((), ())), preferred_element_type=f32
    )


def expert_kernel(
    first_ref, rows_ref, cots_ref, w_ref, out_ref, x_ref, c_ref, gate_ref, up_ref, hid_ref, *scratch
):
    pick_ref, down_ref, back_ref, gates_ref = scratch
    sources, tokens, _ = rows_ref.shape
    pair = 2 * CAP
    width = x_ref.shape[2]
    inner = w_ref.shape[2]
    experts = EXPERTS
    first = first_ref[0]
    lane = lax.broadcasted_iota(jnp.int32, (pair, LANES), 1)
    expert_of = first + lax.broadcasted_iota(jnp.int32, (pair, LANES), 0) // CAP
    own_high = lane == expert_of
    own_low = lane == expert_of + experts
    row_id = lax.broadcasted_iota(jnp.int32, (experts, tokens), 0)
    slot = lax.broadcasted_iota(jnp.int32, (pair, tokens), 0)
    for source in range(sources):
        table = cots_ref[source, :experts, width:].astype(f32)
        ranks = [
            jnp.sum(jnp.where(row_id == first + e, table, 0.0), axis=0, keepdims=True)
            for e in range(2)
        ]
        rank = jnp.where(slot < CAP, ranks[0], ranks[1])
        pick = (rank == (slot % CAP).astype(f32)).astype(bf16)
        pick_ref[source] = pick
        rows = jnp.dot(pick, rows_ref[source], preferred_element_type=f32)
        cots = jnp.dot(pick, cots_ref[source, :, :width], preferred_element_type=f32)
        gate = jnp.sum(jnp.where(own_high | own_low, rows[:, width:], 0.0), axis=1, keepdims=True)
        place = slice(source * CAP, (source + 1) * CAP)
        for e in range(2):
            part = slice(e * CAP, (e + 1) * CAP)
            x_ref[e, place] = rows[part, :width].astype(bf16)
            c_ref[e, place] = cots[part].astype(bf16)
            gates_ref[e, place] = jnp.broadcast_to(gate[part], (CAP, LANES))

    down_rows = inner // 16
    chunks = width // inner
    for e in range(2):
        for holder in range(16):
            for chunk in range(chunks):
                at = (holder * chunks + chunk) * down_rows
                down_ref[
                    e,
                    holder * down_rows : (holder + 1) * down_rows,
                    chunk * inner : (chunk + 1) * inner,
                ] = w_ref[4 + e, at : at + down_rows, :]

    def one_expert(e, carry):
        x = x_ref[e]
        cot = c_ref[e]
        gate = gates_ref[e][:, :1]
        gate_pre = jnp.dot(x, w_ref[e], preferred_element_type=f32)
        up_pre = jnp.dot(x, w_ref[2 + e], preferred_element_type=f32)
        back = contract(cot, down_ref[e], 1, 1)
        sig = 1.0 / (1.0 + jnp.exp(-gate_pre))
        silu = gate_pre * sig
        hidden = (silu * up_pre).astype(bf16)
        gate_grad = jnp.sum(back * hidden.astype(f32), axis=1, keepdims=True)
        grad = gate * back
        gate_pre_grad = (grad * up_pre * (sig + silu * (1.0 - sig))).astype(bf16)
        up_pre_grad = (grad * silu).astype(bf16)
        gate_ref[e] = gate_pre_grad
        up_ref[e] = up_pre_grad
        hid_ref[e] = (gate * hidden.astype(f32)).astype(bf16)
        row_grad = contract(gate_pre_grad, w_ref[e], 1, 1) + contract(
            up_pre_grad, w_ref[2 + e], 1, 1
        )
        mixed = gate * jnp.dot(hidden, down_ref[e], preferred_element_type=f32)
        high = gate_grad.astype(bf16).astype(f32)
        lane = lax.broadcasted_iota(jnp.int32, (gate_grad.shape[0], LANES), 1)
        tail = jnp.where(lane == first + e, high, 0.0) + jnp.where(
            lane == first + e + experts, gate_grad - high, 0.0
        )
        for source in range(sources):
            place = slice(source * CAP, (source + 1) * CAP)
            to = pl.ds(pl.multiple_of(e * CAP, CAP), CAP)
            back_ref[source, to, :width] = row_grad[place].astype(bf16)
            back_ref[source, to, width : 2 * width] = mixed[place].astype(bf16)
            back_ref[source, to, 2 * width :] = tail[place].astype(bf16)
        return carry

    lax.fori_loop(0, 2, one_expert, 0)
    for source in range(sources):
        out_ref[source] = contract(pick_ref[source], back_ref[source], 0, 0).astype(bf16)


def run_experts(first, rows, cots, weights):
    sources, tokens, padded = rows.shape
    width = padded - LANES
    inner = weights.shape[2]
    slots = sources * CAP
    vmem = pl.BlockSpec(memory_space=pltpu.VMEM)
    acts = jax.ShapeDtypeStruct((2, slots, inner), bf16)
    wide = jax.ShapeDtypeStruct((2, slots, width), bf16)
    return pl.pallas_call(
        expert_kernel,
        out_shape=(
            jax.ShapeDtypeStruct((sources, tokens, 2 * width + LANES), bf16),
            wide,
            wide,
            acts,
            acts,
            acts,
        ),
        in_specs=[pl.BlockSpec(memory_space=pltpu.SMEM), vmem, vmem, vmem],
        out_specs=(vmem,) * 6,
        scratch_shapes=[
            pltpu.VMEM((sources, 2 * CAP, tokens), bf16),
            pltpu.VMEM((2, inner, width), bf16),
            pltpu.VMEM((sources, 2 * CAP, 2 * width + LANES), bf16),
            pltpu.VMEM((2, slots, LANES), f32),
        ],
        compiler_params=pltpu.CompilerParams(vmem_limit_bytes=50 * 1024 * 1024),
        cost_estimate=pl.CostEstimate(
            flops=2 * 2 * 7 * slots * width * inner, bytes_accessed=24 << 20, transcendentals=0
        ),
    )(first, rows, cots, weights)


def weight_grad_kernel(half_ref, *refs):
    groups = SIDE
    x_refs, c_refs, gate_refs, up_refs, hid_refs = (
        refs[i * groups : (i + 1) * groups] for i in range(5)
    )
    out_ref = refs[5 * groups]
    slots, width = x_refs[0].shape[1:]
    inner = gate_refs[0].shape[2]
    half = half_ref[0]
    rows = width // 2
    cols = pl.ds(pl.multiple_of(half * rows, LANES), rows)
    down_cols = pl.ds(pl.multiple_of(half * (inner // 2), LANES), inner // 2)
    down_rows = inner // 16
    chunks = width // inner

    def one_expert(e, carry):
        gate = jnp.zeros((rows, inner), f32)
        up = jnp.zeros((rows, inner), f32)
        down = jnp.zeros((inner // 2, width), f32)
        for i in range(groups):
            x = x_refs[i][e, :, cols]
            gate += contract(x, gate_refs[i][e], 0, 0)
            up += contract(x, up_refs[i][e], 0, 0)
        out_ref[e] = gate.astype(bf16)
        out_ref[2 + e] = up.astype(bf16)
        for i in range(groups):
            down += contract(hid_refs[i][e, :, down_cols], c_refs[i][e], 0, 0)
        for holder in range(8):
            for chunk in range(chunks):
                at = (holder * chunks + chunk) * down_rows
                out_ref[4 + e, at : at + down_rows, :] = down[
                    holder * down_rows : (holder + 1) * down_rows,
                    chunk * inner : (chunk + 1) * inner,
                ].astype(bf16)
        return carry

    lax.fori_loop(0, 2, one_expert, 0)


def run_weight_grads(half, saved):
    x, c, gate, up, hid = zip(*saved)
    slots, width = x[0].shape[1:]
    inner = gate[0].shape[2]
    vmem = pl.BlockSpec(memory_space=pltpu.VMEM)
    operands = (*x, *c, *gate, *up, *hid)
    return pl.pallas_call(
        weight_grad_kernel,
        out_shape=jax.ShapeDtypeStruct((6, width // 2, inner), bf16),
        in_specs=[pl.BlockSpec(memory_space=pltpu.SMEM)] + [vmem] * len(operands),
        out_specs=vmem,
        compiler_params=pltpu.CompilerParams(vmem_limit_bytes=50 * 1024 * 1024),
        cost_estimate=pl.CostEstimate(
            flops=2 * 3 * 4 * slots * width * inner, bytes_accessed=24 << 20, transcendentals=0
        ),
    )(half, *operands)


def local(
    tokens,
    segments,
    routes,
    norm1_gain,
    w_query,
    w_key,
    w_value,
    w_out,
    norm2_gain,
    w_router,
    w_gate,
    w_up,
    w_down,
    cotangent,
):
    tok_rows, width = tokens.shape
    seq_len = segments.shape[1]
    query_width = w_query.shape[1]
    kv_width = w_key.shape[1]
    joined_width = query_width + 2 * kv_width
    local_experts = w_gate.shape[0]
    experts = w_router.shape[1]
    owners = lax.axis_size("expert")
    planes = lax.axis_size("tensor")
    owner = lax.axis_index("expert")
    first_expert = owner * local_experts
    key_seg = segments[0]
    hidden_width = w_gate.shape[2]

    token_f32 = tokens.astype(f32)
    inverse_one = rms_inverse(token_f32)
    normed_low = (token_f32 * inverse_one * norm1_gain).astype(bf16)
    joined_weights = jnp.concatenate([w_query, w_key, w_value], axis=1)
    normed_low = by_rows(normed_low)
    normed_all = lax.all_gather(normed_low, "tensor", axis=0, tiled=True)
    core = lax.axis_index("dp")

    expert_ids = jnp.arange(experts, dtype=jnp.int32)
    onehot = (routes[:, :, None] == expert_ids[None, None, :]).astype(f32)
    member = jnp.sum(onehot, axis=1)
    lower = (jnp.arange(tok_rows)[:, None] <= jnp.arange(tok_rows)[None, :]).astype(bf16)
    rank = jnp.einsum("te,tu->eu", member.astype(bf16), lower, preferred_element_type=f32)
    rank = jnp.where(member.T > 0, rank - 1.0, -1.0).astype(bf16)
    extra = jnp.pad(rank, ((0, tok_rows - experts), (0, LANES - tok_rows)))
    cot_payload = jnp.concatenate([cotangent, extra], axis=1)

    cot_parts = gather_plane(cot_payload)

    def half_gather(shard):
        count = shard.shape[0] // 2
        half = lax.dynamic_slice_in_dim(shard, core * count, count, 0)
        return lax.all_gather(half, "tensor", axis=0)

    normed_all, cot_parts, w_out = together(normed_all, cot_parts, w_out)
    half_out = half_gather(w_out)
    chunks = width // hidden_width
    down_rows = w_down.shape[1]
    part_rows = w_gate.shape[1]
    down_parts = w_down.reshape(local_experts, down_rows, chunks, hidden_width)
    down_parts = down_parts.transpose(0, 2, 1, 3).reshape(local_experts, part_rows, hidden_width)
    weights = jnp.concatenate([w_gate, w_up, down_parts], axis=0)
    half_out, weights = together(half_out, weights)
    weights_all = lax.all_gather(weights, ("dp", "tensor"), axis=1, tiled=True)
    weights_all, joined_rows = together(weights_all, joined_weights.T)
    half_joined = half_gather(joined_rows)

    tables = rope_tables(seq_len, HEAD_DIM)
    context, saved = attention_forward(normed_all, joined_weights, key_seg, tables)
    context_home = lax.all_to_all(
        context.reshape(planes, tok_rows, query_width), "tensor", split_axis=0, concat_axis=0
    )
    other_out = swap_cores(half_out)

    def both_halves(blocks, mine, other):
        count = blocks.shape[2] // 2
        first = lax.dynamic_slice_in_dim(blocks, core * count, count, 2)
        second = lax.dynamic_slice_in_dim(blocks, (1 - core) * count, count, 2)
        return jnp.einsum("jtq,jqd->td", first, mine, preferred_element_type=f32) + jnp.einsum(
            "jtq,jqd->td", second, other, preferred_element_type=f32
        )

    mid = token_f32 + both_halves(context_home, half_out, other_out)
    inverse_two = rms_inverse(mid)
    normed_two = (mid * inverse_two * norm2_gain).astype(bf16)
    logits = dot32(normed_two, w_router)
    logits = jnp.where(member > 0, logits, masked_score)
    chosen_exp = jnp.where(
        member > 0, jnp.exp(logits - jnp.max(logits, axis=1, keepdims=True)), 0.0
    )
    gates = chosen_exp / jnp.sum(chosen_exp, axis=1, keepdims=True)
    gate_high, gate_low = split_two(gates)
    payload = jnp.concatenate(
        [normed_two, gate_high, gate_low, jnp.zeros((tok_rows, LANES - 2 * experts), bf16)],
        axis=1,
    )
    rows_parts = gather_plane(payload)

    first_expert = first_expert.astype(jnp.int32).reshape(1)
    done = [
        run_experts(first_expert, rows, cots, weights_all)
        for rows, cots in zip(rows_parts, cot_parts)
    ]
    back_home = scatter_plane([part[0] for part in done])
    saved_rows = [part[1:] for part in done]
    given = run_weight_grads((1 - core).astype(jnp.int32).reshape(1), saved_rows)
    kept = run_weight_grads(core.astype(jnp.int32).reshape(1), saved_rows)
    kept = (kept.astype(f32) + swap_cores(given).astype(f32)).astype(bf16)
    weight_sum = lax.psum_scatter(kept, "tensor", scatter_dimension=1, tiled=True)
    back_home, kept, half_joined = together(back_home, kept, half_joined)
    output = (mid + back_home[:, width : 2 * width]).astype(bf16)

    cot_f32 = cotangent.astype(f32)
    grad_tail = back_home[:, 2 * width :]
    gate_grad = grad_tail[:, :experts] + grad_tail[:, experts : 2 * experts]
    chosen_grad = gates * (gate_grad - jnp.sum(gates * gate_grad, axis=1, keepdims=True))
    logit_grad = chosen_grad.astype(bf16)
    router_part = jnp.einsum("td,te->de", normed_two, logit_grad, preferred_element_type=f32)
    normed_two_grad = back_home[:, :width] + jnp.einsum(
        "te,de->td", logit_grad, w_router, preferred_element_type=f32
    )
    mid_part, norm2_part = rms_backward(mid, inverse_two, norm2_gain, normed_two_grad)
    mid_grad = cot_f32 + mid_part
    attention_low = by_rows(mid_grad.astype(bf16))
    def both_back(rows, mine, other):
        first = jnp.einsum("td,jqd->jtq", rows, mine, preferred_element_type=f32)
        second = jnp.einsum("td,jqd->jtq", rows, other, preferred_element_type=f32)
        low = jnp.where(core == 0, first, second)
        high = jnp.where(core == 0, second, first)
        return jnp.concatenate([low, high], axis=2).astype(bf16)

    context_grad = both_back(attention_low, half_out, other_out)
    context_grad = lax.all_to_all(context_grad, "tensor", split_axis=0, concat_axis=0)
    joined_grad = attention_backward(
        saved, context_grad.reshape(seq_len, query_width), key_seg, tables
    )
    joined_home = lax.all_to_all(
        joined_grad.reshape(planes, tok_rows, joined_width), "tensor", split_axis=0, concat_axis=0
    )
    attention_all = lax.all_gather(attention_low, "tensor", axis=0, tiled=True)
    out_part = jnp.einsum("tq,td->qd", context, attention_all, preferred_element_type=f32)
    joined_part = jnp.einsum("td,tq->dq", normed_all, joined_grad, preferred_element_type=f32)
    normed_one_grad = both_halves(joined_home, half_joined, swap_cores(half_joined))
    input_part, norm1_part = rms_backward(token_f32, inverse_one, norm1_gain, normed_one_grad)
    input_grad = mid_grad + input_part

    sharers = lax.axis_size("dp") * owners
    shared_part = jnp.concatenate([router_part.reshape(-1), norm2_part, norm1_part])
    flat_part = jnp.concatenate(
        [
            part.astype(bf16).reshape(-1, LANES)
            for part in (joined_part, out_part, shared_part)
        ],
        axis=0,
    )
    flat_rows = flat_part.shape[0]
    block = -(-flat_rows // (16 * sharers)) * 16
    flat_part = jnp.pad(flat_part, ((0, sharers * block - flat_rows), (0, 0)))
    flat_part, weight_sum = together(flat_part, weight_sum)
    arrived = lax.all_to_all(
        flat_part.reshape(sharers, block, LANES), ("dp", "expert"), split_axis=0, concat_axis=0
    )
    total = jnp.sum(arrived.astype(f32), axis=0).astype(bf16)
    flat_sum = lax.all_to_all(
        jnp.broadcast_to(total[None], arrived.shape), ("dp", "expert"), split_axis=0, concat_axis=0
    ).reshape(sharers * block, LANES)
    cut = width * joined_width // LANES
    end = cut + query_width * width // LANES
    joined_sum = flat_sum[:cut].reshape(width, joined_width).astype(f32)
    out_sum = flat_sum[cut:end].reshape(query_width, width).astype(f32)
    shared = flat_sum[end:flat_rows]
    shared = lax.all_to_all(
        jnp.broadcast_to(shared[None], (planes,) + shared.shape),
        "tensor",
        split_axis=0,
        concat_axis=0,
    )
    shared = jnp.sum(shared.astype(f32), axis=0).reshape(-1)
    w_gate_grad = weight_sum[:local_experts].astype(f32)
    w_up_grad = weight_sum[local_experts : 2 * local_experts].astype(f32)
    w_down_grad = weight_sum[2 * local_experts :].reshape(
        local_experts, chunks, down_rows, hidden_width
    )
    w_down_grad = w_down_grad.transpose(0, 2, 1, 3).reshape(local_experts, down_rows, width)
    w_down_grad = w_down_grad.astype(f32)
    router_size = width * experts
    return (
        output,
        input_grad,
        shared[router_size + width : router_size + 2 * width],
        joined_sum[:, :query_width],
        joined_sum[:, query_width : query_width + kv_width],
        joined_sum[:, query_width + kv_width :],
        out_sum,
        shared[router_size : router_size + width],
        shared[:router_size].reshape(width, experts),
        w_gate_grad,
        w_up_grad,
        w_down_grad,
    )


def solution(mesh):
    rows = P(("dp", "expert", "tensor"), None)
    columns = P(None, "tensor")
    experts = P("expert", ("dp", "tensor"), None)
    return jax.shard_map(
        local,
        mesh=mesh,
        in_specs=(
            rows,
            P(("dp", "expert"), None),
            rows,
            P(),
            columns,
            columns,
            columns,
            P("tensor", None),
            P(),
            P(),
            experts,
            experts,
            experts,
            rows,
        ),
        out_specs=(
            rows,
            rows,
            P(),
            columns,
            columns,
            columns,
            P("tensor", None),
            P(),
            P(),
            experts,
            experts,
            experts,
        ),
        check_vma=False,
    )
```

```python
import jax
import jax.numpy as jnp
from jax import lax
from jax.experimental import pallas as pl
from jax.experimental.layout import Layout, with_layout_constraint
from jax.experimental.pallas import tpu as pltpu
from jax.sharding import PartitionSpec as P

HEAD_DIM = 64
HALF = HEAD_DIM // 2
TOP = 8
CAP = 64
EXPERTS = 32
HOLDERS = 16
LANES = 128

epsilon_norm = 1e-06
rope_theta = 10000.0
masked_score = -1e30
block_limit = 512
f32 = jnp.float32
bf16 = jnp.bfloat16


def rms_inverse(values):
    return lax.rsqrt(jnp.mean(values * values, axis=-1, keepdims=True) + epsilon_norm)


def rms_backward(values, inverse, norm_gain, grad_out):
    scaled = grad_out * norm_gain
    grad_in = inverse * scaled - values * (inverse * inverse * inverse) * jnp.mean(
        scaled * values, axis=-1, keepdims=True
    )
    return (grad_in, jnp.sum(grad_out * values * inverse, axis=0))


def rope_tables(seq_len, head_width):
    half_dim = head_width // 2
    frequency = rope_theta ** (-2.0 * jnp.arange(half_dim, dtype=f32) / head_width)
    angles = jnp.arange(seq_len, dtype=f32)[:, None] * frequency[None, :]
    angles = jnp.concatenate([angles, angles], axis=1)
    return (jnp.cos(angles), jnp.sin(angles))


def rotate_half(values):
    return jnp.concatenate([-values[..., HALF:], values[..., :HALF]], axis=-1)


def rotate_back(values):
    return jnp.concatenate([values[..., HALF:], -values[..., :HALF]], axis=-1)


def dot32(left, right):
    return jnp.dot(left, right, preferred_element_type=f32)


def allowed_mask(query_pos, query_seg, key_pos, key_seg):
    same_doc = query_seg[:, None] == key_seg[None, :]
    causal = key_pos[None, :] <= query_pos[:, None]
    diagonal = key_pos[None, :] == query_pos[:, None]
    return causal & same_doc & ((query_seg[:, None] != 0) | diagonal)


def attention_forward(normed_all, joined_weights, key_seg, tables):
    seq_len = normed_all.shape[0]
    kv_width = HEAD_DIM
    query_width = joined_weights.shape[1] - 2 * kv_width
    heads = query_width // HEAD_DIM
    joined = dot32(normed_all, joined_weights)
    cosine, sine = tables
    query = joined[:, :query_width].reshape(seq_len, heads, HEAD_DIM)
    key = joined[:, query_width : query_width + kv_width]
    value_low = joined[:, query_width + kv_width :].astype(bf16)
    query_low = (query * cosine[:, None, :] + rotate_half(query) * sine[:, None, :]).astype(bf16)
    key_low = (key * cosine + rotate_half(key) * sine).astype(bf16)
    pos = jnp.arange(seq_len, dtype=jnp.int32)
    scores = jnp.einsum("qrd,kd->rqk", query_low, key_low, preferred_element_type=f32)
    masked = jnp.where(
        allowed_mask(pos, key_seg, pos, key_seg), scores * HEAD_DIM ** (-0.5), masked_score
    )
    top_score = jnp.max(masked, axis=-1, keepdims=True)
    exp_scores = jnp.exp(masked - top_score)
    exp_total = jnp.sum(exp_scores, axis=-1, keepdims=True)
    probs = (exp_scores / exp_total).astype(bf16)
    context = jnp.einsum("rqk,kd->qrd", probs, value_low, preferred_element_type=f32)
    lse = (top_score + jnp.log(exp_total))[..., 0]
    return context.reshape(seq_len, query_width).astype(bf16), (
        query_low,
        key_low,
        value_low,
        lse,
    )


def attention_backward(saved, context_grad, key_seg, tables):
    query_low, key_low, value_low, lse = saved
    seq_len, heads, _ = query_low.shape
    cosine, sine = tables
    grad = context_grad.reshape(seq_len, heads, HEAD_DIM)
    pos = jnp.arange(seq_len, dtype=jnp.int32)
    scale = HEAD_DIM ** (-0.5)
    scores = jnp.einsum("qrd,kd->rqk", query_low, key_low, preferred_element_type=f32) * scale
    masked = jnp.where(allowed_mask(pos, key_seg, pos, key_seg), scores, masked_score)
    probs = jnp.exp(masked - lse[..., None])
    probs_grad = jnp.einsum("qrd,kd->rqk", grad, value_low, preferred_element_type=f32)
    row_dot = jnp.sum(probs * probs_grad, axis=-1, keepdims=True)
    score_grad = (probs * (probs_grad - row_dot)).astype(bf16)
    query_grad = jnp.einsum("rqk,kd->qrd", score_grad, key_low, preferred_element_type=f32)
    key_grad = jnp.einsum("rqk,qrd->kd", score_grad, query_low, preferred_element_type=f32)
    value_grad = jnp.einsum("rqk,qrd->kd", probs.astype(bf16), grad, preferred_element_type=f32)
    query_grad = query_grad * scale
    key_grad = key_grad * scale
    query_grad = query_grad * cosine[:, None, :] + rotate_back(query_grad * sine[:, None, :])
    key_grad = key_grad * cosine + rotate_back(key_grad * sine)
    return jnp.concatenate(
        [query_grad.reshape(seq_len, heads * HEAD_DIM), key_grad, value_grad], axis=1
    ).astype(bf16)


def split_two(values):
    high = values.astype(bf16)
    return high, (values - high.astype(f32)).astype(bf16)


SIDE = 4
STEPS = (0, 1, -1, 2)


def by_rows(values):
    return with_layout_constraint(values, Layout(major_to_minor=tuple(range(values.ndim))))


def cross(values, stage, step):
    pairs = []
    plane = SIDE * SIDE
    for core in range(2):
        for x in range(SIDE):
            for y in range(SIDE):
                if core == stage:
                    to = x * SIDE + (y + step) % SIDE
                else:
                    to = (x + step) % SIDE * SIDE + y
                pairs.append((core * plane + x * SIDE + y, core * plane + to))
    return lax.ppermute(values, ("dp", "expert"), pairs)


def gather_first(values):
    values = by_rows(values)
    line = jnp.stack([values] + [cross(values, 0, step) for step in STEPS[1:]])
    return by_rows(line)


def gather_second(line):
    return [line] + [cross(line, 1, step) for step in STEPS[1:]]


def scatter_first(parts):
    arrived = [parts[0]] + [
        by_rows(cross(part, 1, -step)) for part, step in zip(parts[1:], STEPS[1:])
    ]
    return [
        by_rows(sum(part[place].astype(f32) for part in arrived).astype(bf16))
        for place in range(SIDE)
    ]


def scatter_second(line):
    arrived = [line[0]] + [cross(part, 0, -step) for part, step in zip(line[1:], STEPS[1:])]
    return by_rows(sum(part.astype(f32) for part in arrived))


def ring_gather(block):
    size = lax.axis_size("tensor")
    me = lax.axis_index("tensor")
    half = block.shape[0] // 2
    held = jnp.zeros((size,) + block.shape, block.dtype)

    def shift(values, step):
        return lax.ppermute(values, "tensor", [(i, (i + step) % size) for i in range(size)])

    def put(held, values, place, row):
        return lax.dynamic_update_slice(held, values[None], ((me + place) % size, row, 0))

    held = put(held, block, 0, 0)
    up = down = block
    for step in range(1, size // 2):
        up, down = shift(up, 1), shift(down, -1)
        held = put(held, up, size - step, 0)
        held = put(held, down, step, 0)
    held = put(held, shift(up[:half], 1), size // 2, 0)
    return put(held, shift(down[half:], -1), size // 2, half)


def ring_scatter(parts):
    size = lax.axis_size("tensor")
    me = lax.axis_index("tensor")
    half = parts.shape[1] // 2

    def shift(values, step):
        return lax.ppermute(values, "tensor", [(i, (i + step) % size) for i in range(size)])

    def part_for(place):
        return lax.dynamic_index_in_dim(parts, (me + place) % size, 0, keepdims=False)

    far = part_for(size // 2)
    up, down = shift(far[:half], 1), shift(far[half:], -1)
    up = jnp.pad(up, ((0, half), (0, 0)))
    down = jnp.pad(down, ((half, 0), (0, 0)))
    for place in range(size // 2 - 1, 0, -1):
        up = (part_for(place).astype(f32) + up.astype(f32)).astype(bf16)
        down = (part_for(-place).astype(f32) + down.astype(f32)).astype(bf16)
        up, down = together(shift(by_rows(up), 1), shift(by_rows(down), -1))
    return part_for(0).astype(f32) + up.astype(f32) + down.astype(f32)


def ring_sum(values):
    size = lax.axis_size("tensor")
    step = 1
    while step < size:
        pairs = [(i, i ^ step) for i in range(size)]
        values = values + lax.ppermute(values, "tensor", pairs)
        step *= 2
    return values


def together(*values):
    return lax.optimization_barrier(values)


def swap_cores(values):
    return lax.ppermute(values, "dp", [(0, 1), (1, 0)])


def contract(left, right, left_dim, right_dim):
    return lax.dot_general(
        left, right, (((left_dim,), (right_dim,)), ((), ())), preferred_element_type=f32
    )


def expert_kernel(
    first_ref, rows_ref, cots_ref, w_ref, back_out, mix_out, x_ref, c_ref, gate_ref, up_ref, hid_ref, *scratch
):
    pick_ref, down_ref, back_ref, mix_ref = scratch
    sources, tokens, _ = rows_ref.shape
    width = x_ref.shape[2]
    inner = w_ref.shape[2]
    e = pl.program_id(0)
    expert = first_ref[0] + e
    lane = lax.broadcasted_iota(jnp.int32, (CAP, LANES), 1)
    row_id = lax.broadcasted_iota(jnp.int32, (EXPERTS, tokens), 0)
    slot = lax.broadcasted_iota(jnp.int32, (CAP, tokens), 0).astype(f32)
    at = pl.ds(pl.multiple_of(e * CAP, CAP), CAP)
    gates = []
    for source in range(sources):
        table = cots_ref[source, :EXPERTS, width:].astype(f32)
        rank = jnp.sum(jnp.where(row_id == expert, table, 0.0), axis=0, keepdims=True)
        pick = (rank == slot).astype(bf16)
        pick_ref[source, at] = pick
        rows = jnp.dot(pick, rows_ref[source], preferred_element_type=f32)
        cots = jnp.dot(pick, cots_ref[source, :, :width], preferred_element_type=f32)
        own = (lane == expert) | (lane == expert + EXPERTS)
        gates.append(jnp.sum(jnp.where(own, rows[:, width:], 0.0), axis=1, keepdims=True))
        x_ref[0, source * CAP : (source + 1) * CAP] = rows[:, :width].astype(bf16)
        c_ref[0, source * CAP : (source + 1) * CAP] = cots.astype(bf16)
    gate = jnp.concatenate(gates, axis=0)

    down_rows = inner // HOLDERS
    chunks = width // inner
    for holder in range(HOLDERS):
        for chunk in range(chunks):
            start = (holder * chunks + chunk) * down_rows
            down_ref[
                holder * down_rows : (holder + 1) * down_rows,
                chunk * inner : (chunk + 1) * inner,
            ] = w_ref[2, start : start + down_rows, :]

    x = x_ref[0]
    gate_pre = jnp.dot(x, w_ref[0], preferred_element_type=f32)
    up_pre = jnp.dot(x, w_ref[1], preferred_element_type=f32)
    back = contract(c_ref[0], down_ref[...], 1, 1)
    sig = 1.0 / (1.0 + jnp.exp(-gate_pre))
    silu = gate_pre * sig
    hidden = (silu * up_pre).astype(bf16)
    gate_grad = jnp.sum(back * hidden.astype(f32), axis=1, keepdims=True)
    grad = gate * back
    gate_pre_grad = (grad * up_pre * (sig + silu * (1.0 - sig))).astype(bf16)
    up_pre_grad = (grad * silu).astype(bf16)
    gate_ref[0] = gate_pre_grad
    up_ref[0] = up_pre_grad
    hid_ref[0] = (gate * hidden.astype(f32)).astype(bf16)
    row_grad = contract(gate_pre_grad, w_ref[0], 1, 1) + contract(up_pre_grad, w_ref[1], 1, 1)
    mixed = gate * jnp.dot(hidden, down_ref[...], preferred_element_type=f32)
    high = gate_grad.astype(bf16).astype(f32)
    lane = lax.broadcasted_iota(jnp.int32, (sources * CAP, LANES), 1)
    tail = jnp.where(lane == expert, high, 0.0)
    tail += jnp.where(lane == expert + EXPERTS, gate_grad - high, 0.0)
    for source in range(sources):
        place = slice(source * CAP, (source + 1) * CAP)
        back_ref[source, at, :width] = row_grad[place].astype(bf16)
        back_ref[source, at, width:] = tail[place].astype(bf16)
        mix_ref[source, at] = mixed[place].astype(bf16)

    @pl.when(e == 1)
    def _():
        for source in range(sources):
            pick = pick_ref[source]
            back_out[source] = contract(pick, back_ref[source], 0, 0).astype(bf16)
            mix_out[source] = contract(pick, mix_ref[source], 0, 0).astype(bf16)


def run_experts(first, rows, cots, weights):
    sources, tokens, padded = rows.shape
    width = padded - LANES
    inner = weights.shape[2]
    slots = sources * CAP

    def whole(columns):
        return pl.BlockSpec((sources, tokens, columns), lambda e: (0, 0, 0))

    def by_expert(*shape):
        return pl.BlockSpec(shape, lambda e: (e, 0, 0))

    acts = jax.ShapeDtypeStruct((2, slots, inner), bf16)
    wide = jax.ShapeDtypeStruct((2, slots, width), bf16)
    return pl.pallas_call(
        expert_kernel,
        grid=(2,),
        out_shape=(
            jax.ShapeDtypeStruct((sources, tokens, padded), bf16),
            jax.ShapeDtypeStruct((sources, tokens, width), bf16),
            wide,
            wide,
            acts,
            acts,
            acts,
        ),
        in_specs=[
            pl.BlockSpec(memory_space=pltpu.SMEM),
            whole(padded),
            whole(padded),
            by_expert(3, width, inner),
        ],
        out_specs=(
            whole(padded),
            whole(width),
            by_expert(1, slots, width),
            by_expert(1, slots, width),
            by_expert(1, slots, inner),
            by_expert(1, slots, inner),
            by_expert(1, slots, inner),
        ),
        scratch_shapes=[
            pltpu.VMEM((sources, 2 * CAP, tokens), bf16),
            pltpu.VMEM((inner, width), bf16),
            pltpu.VMEM((sources, 2 * CAP, padded), bf16),
            pltpu.VMEM((sources, 2 * CAP, width), bf16),
        ],
        compiler_params=pltpu.CompilerParams(vmem_limit_bytes=52 * 1024 * 1024),
        cost_estimate=pl.CostEstimate(
            flops=2 * 2 * 7 * slots * width * inner, bytes_accessed=24 << 20, transcendentals=0
        ),
    )(first, rows, cots, weights)


def weight_grad_kernel(half_ref, *refs):
    groups = SIDE
    x_refs, c_refs, gate_refs, up_refs, hid_refs = (
        refs[i * groups : (i + 1) * groups] for i in range(5)
    )
    outs = refs[5 * groups :]
    slots, width = x_refs[0].shape[1:]
    inner = gate_refs[0].shape[2]
    rows = width // 2
    down_rows = inner // HOLDERS
    chunks = width // inner
    for out_ref, half in zip(outs, (1 - half_ref[0], half_ref[0])):
        cols = pl.ds(pl.multiple_of(half * rows, LANES), rows)
        down_cols = pl.ds(pl.multiple_of(half * (inner // 2), LANES), inner // 2)
        gate = jnp.zeros((rows, inner), f32)
        up = jnp.zeros((rows, inner), f32)
        down = jnp.zeros((inner // 2, width), f32)
        for i in range(groups):
            x = x_refs[i][0, :, cols]
            gate += contract(x, gate_refs[i][0], 0, 0)
            up += contract(x, up_refs[i][0], 0, 0)
        out_ref[0] = gate.astype(bf16)
        out_ref[1] = up.astype(bf16)
        for i in range(groups):
            down += contract(hid_refs[i][0, :, down_cols], c_refs[i][0], 0, 0)
        for holder in range(HOLDERS // 2):
            for chunk in range(chunks):
                at = (holder * chunks + chunk) * down_rows
                out_ref[2, at : at + down_rows, :] = down[
                    holder * down_rows : (holder + 1) * down_rows,
                    chunk * inner : (chunk + 1) * inner,
                ].astype(bf16)


def run_weight_grads(core, saved):
    x, c, gate, up, hid = zip(*saved)
    slots, width = x[0].shape[1:]
    inner = gate[0].shape[2]
    operands = (*x, *c, *gate, *up, *hid)
    out = jax.ShapeDtypeStruct((6, width // 2, inner), bf16)
    out_spec = pl.BlockSpec((3, width // 2, inner), lambda e: (e, 0, 0))
    return pl.pallas_call(
        weight_grad_kernel,
        grid=(2,),
        out_shape=(out, out),
        in_specs=[pl.BlockSpec(memory_space=pltpu.SMEM)]
        + [pl.BlockSpec((1,) + v.shape[1:], lambda e: (e, 0, 0)) for v in operands],
        out_specs=(out_spec, out_spec),
        compiler_params=pltpu.CompilerParams(vmem_limit_bytes=52 * 1024 * 1024),
        cost_estimate=pl.CostEstimate(
            flops=2 * 2 * 3 * 4 * slots * width * inner, bytes_accessed=28 << 20, transcendentals=0
        ),
    )(core, *operands)


def local(
    tokens,
    segments,
    routes,
    norm1_gain,
    w_query,
    w_key,
    w_value,
    w_out,
    norm2_gain,
    w_router,
    w_gate,
    w_up,
    w_down,
    cotangent,
):
    tok_rows, width = tokens.shape
    seq_len = segments.shape[1]
    query_width = w_query.shape[1]
    kv_width = w_key.shape[1]
    joined_width = query_width + 2 * kv_width
    local_experts = w_gate.shape[0]
    experts = w_router.shape[1]
    owners = lax.axis_size("expert")
    planes = lax.axis_size("tensor")
    owner = lax.axis_index("expert")
    first_expert = owner * local_experts
    key_seg = segments[0]
    hidden_width = w_gate.shape[2]

    token_f32 = tokens.astype(f32)
    inverse_one = rms_inverse(token_f32)
    normed_low = (token_f32 * inverse_one * norm1_gain).astype(bf16)
    joined_weights = jnp.concatenate([w_query, w_key, w_value], axis=1)
    normed_low = by_rows(normed_low)
    normed_all = lax.all_gather(normed_low, "tensor", axis=0, tiled=True)
    core = lax.axis_index("dp")

    expert_ids = jnp.arange(experts, dtype=jnp.int32)
    onehot = (routes[:, :, None] == expert_ids[None, None, :]).astype(f32)
    member = jnp.sum(onehot, axis=1)
    lower = (jnp.arange(tok_rows)[:, None] <= jnp.arange(tok_rows)[None, :]).astype(bf16)
    rank = jnp.einsum("te,tu->eu", member.astype(bf16), lower, preferred_element_type=f32)
    rank = jnp.where(member.T > 0, rank - 1.0, -1.0).astype(bf16)
    extra = jnp.pad(rank, ((0, tok_rows - experts), (0, LANES - tok_rows)))
    cot_payload = jnp.concatenate([cotangent, extra], axis=1)

    count = w_out.shape[0] // 2
    half_out = ring_gather(lax.dynamic_slice_in_dim(w_out, core * count, count, 0))
    other_out = swap_cores(half_out)

    chunks = width // hidden_width
    down_rows = w_down.shape[1]
    part_rows = w_gate.shape[1]
    down_parts = w_down.reshape(local_experts, down_rows, chunks, hidden_width)
    down_parts = down_parts.transpose(0, 2, 1, 3).reshape(local_experts, part_rows, hidden_width)
    weights = jnp.stack([w_gate, w_up, down_parts], axis=1)
    weights = weights.reshape(3 * local_experts, part_rows, hidden_width)
    normed_all, half_out, cot_line, weights = together(
        normed_all, half_out, gather_first(cot_payload), weights
    )
    weights_all = lax.all_gather(weights, ("dp", "tensor"), axis=1, tiled=True)
    cot_parts = gather_second(cot_line)

    tables = rope_tables(seq_len, HEAD_DIM)
    context, saved = attention_forward(normed_all, joined_weights, key_seg, tables)
    context_home = lax.all_to_all(
        context.reshape(planes, tok_rows, query_width), "tensor", split_axis=0, concat_axis=0
    )

    def both_halves(blocks, mine, other):
        count = blocks.shape[2] // 2
        first = lax.dynamic_slice_in_dim(blocks, core * count, count, 2)
        second = lax.dynamic_slice_in_dim(blocks, (1 - core) * count, count, 2)
        return jnp.einsum("jtq,jqd->td", first, mine, preferred_element_type=f32) + jnp.einsum(
            "jtq,jqd->td", second, other, preferred_element_type=f32
        )

    mid = token_f32 + both_halves(context_home, half_out, other_out)
    inverse_two = rms_inverse(mid)
    normed_two = (mid * inverse_two * norm2_gain).astype(bf16)
    logits = dot32(normed_two, w_router)
    logits = jnp.where(member > 0, logits, masked_score)
    chosen_exp = jnp.where(
        member > 0, jnp.exp(logits - jnp.max(logits, axis=1, keepdims=True)), 0.0
    )
    gates = chosen_exp / jnp.sum(chosen_exp, axis=1, keepdims=True)
    gate_high, gate_low = split_two(gates)
    payload = jnp.concatenate(
        [normed_two, gate_high, gate_low, jnp.zeros((tok_rows, LANES - 2 * experts), bf16)],
        axis=1,
    )
    payload, *cot_parts = together(payload, *cot_parts)
    rows_parts = gather_second(gather_first(payload))

    first_expert = first_expert.astype(jnp.int32).reshape(1)
    done = [run_experts(first_expert, rows_parts[0], cot_parts[0], weights_all)]
    *travelled, done[0] = together(*rows_parts[1:], done[0])
    rows_parts[1:] = travelled
    for rows, cots in zip(rows_parts[1:], cot_parts[1:]):
        done.append(run_experts(first_expert, rows, cots, weights_all))
    back_line = scatter_first([part[0] for part in done])
    *both, given, kept = together(
        *back_line,
        *[part[1] for part in done],
        *run_weight_grads(core.astype(jnp.int32).reshape(1), [part[2:] for part in done]),
    )
    back_line, mix_parts = both[:SIDE], both[SIDE:]
    kept = (kept.astype(f32) + swap_cores(given).astype(f32)).astype(bf16)
    weight_sum = lax.psum_scatter(kept, "tensor", scatter_dimension=1, tiled=True)
    back_home = scatter_second(back_line)
    back_home, kept = together(back_home, kept)

    cot_f32 = cotangent.astype(f32)
    grad_tail = back_home[:, width:]
    gate_grad = grad_tail[:, :experts] + grad_tail[:, experts : 2 * experts]
    chosen_grad = gates * (gate_grad - jnp.sum(gates * gate_grad, axis=1, keepdims=True))
    logit_grad = chosen_grad.astype(bf16)
    normed_two_grad = back_home[:, :width] + jnp.einsum(
        "te,de->td", logit_grad, w_router, preferred_element_type=f32
    )
    mid_part, norm2_part = rms_backward(mid, inverse_two, norm2_gain, normed_two_grad)
    mid_grad = cot_f32 + mid_part
    attention_low = by_rows(mid_grad.astype(bf16))
    def both_back(rows, mine, other):
        first = jnp.einsum("td,jqd->jtq", rows, mine, preferred_element_type=f32)
        second = jnp.einsum("td,jqd->jtq", rows, other, preferred_element_type=f32)
        low = jnp.where(core == 0, first, second)
        high = jnp.where(core == 0, second, first)
        return jnp.concatenate([low, high], axis=2).astype(bf16)

    context_grad = both_back(attention_low, half_out, other_out)
    context_grad, logit_grad, *mix_parts = together(context_grad, logit_grad, *mix_parts)
    mix_line = scatter_first(mix_parts)
    router_part = contract(normed_two, logit_grad, 0, 0)
    context_grad = lax.all_to_all(context_grad, "tensor", split_axis=0, concat_axis=0)
    joined_grad = attention_backward(
        saved, context_grad.reshape(seq_len, query_width), key_seg, tables
    )
    shared_early = ring_sum(
        jnp.concatenate([router_part.reshape(-1), norm2_part]).astype(bf16).reshape(-1, LANES)
    )
    joined_grad, shared_early, *mix_line = together(joined_grad, shared_early, *mix_line)
    output = (mid + scatter_second(mix_line)).astype(bf16)
    normed_one_grad = ring_scatter(
        contract(joined_grad, joined_weights, 1, 1).astype(bf16).reshape(planes, tok_rows, width)
    )
    attention_all = lax.all_gather(attention_low, "tensor", axis=0, tiled=True)
    out_part = contract(context, attention_all, 0, 0)
    joined_part = contract(normed_all, joined_grad, 0, 0)
    norm1_part = jnp.sum(joined_part * joined_weights.astype(f32), axis=1) / norm1_gain

    sharers = lax.axis_size("dp") * owners
    flat_part = jnp.concatenate(
        [joined_part.astype(bf16).reshape(-1, LANES), out_part.astype(bf16).reshape(-1, LANES), shared_early],
        axis=0,
    )
    flat_rows = flat_part.shape[0]
    block = -(-flat_rows // (16 * sharers)) * 16
    flat_part = jnp.pad(flat_part, ((0, sharers * block - flat_rows), (0, 0)))
    arrived = lax.all_to_all(
        flat_part.reshape(sharers, block, LANES), ("dp", "expert"), split_axis=0, concat_axis=0
    )
    total = jnp.sum(arrived.astype(f32), axis=0).astype(bf16)
    norm1_rows = width // LANES
    norm1_high, norm1_low = split_two(ring_sum(norm1_part).reshape(norm1_rows, LANES))
    norm1_pad = jnp.zeros((-2 * norm1_rows % 16, LANES), bf16)
    total = jnp.concatenate([total, norm1_high, norm1_low, norm1_pad], axis=0)
    spread = lax.all_to_all(
        jnp.broadcast_to(total[None], (sharers,) + total.shape),
        ("dp", "expert"),
        split_axis=0,
        concat_axis=0,
    )
    spread, weight_sum = together(spread, weight_sum)
    flat_sum = spread[:, :block].reshape(sharers * block, LANES)
    norm1_sum = jnp.sum(spread[:, block : block + 2 * norm1_rows].astype(f32), axis=0)
    norm1_sum = norm1_sum[:norm1_rows] + norm1_sum[norm1_rows:]
    cut = width * joined_width // LANES
    end = cut + query_width * width // LANES
    joined_sum = flat_sum[:cut].reshape(width, joined_width).astype(f32)
    out_sum = flat_sum[cut:end].reshape(query_width, width).astype(f32)
    shared = flat_sum[end:flat_rows].astype(f32).reshape(-1)
    weight_sum = weight_sum.reshape(local_experts, 3, part_rows, hidden_width)
    w_gate_grad = weight_sum[:, 0].astype(f32)
    w_up_grad = weight_sum[:, 1].astype(f32)
    w_down_grad = weight_sum[:, 2].reshape(local_experts, chunks, down_rows, hidden_width)
    w_down_grad = w_down_grad.transpose(0, 2, 1, 3).reshape(local_experts, down_rows, width)
    w_down_grad = w_down_grad.astype(f32)
    input_part, _ = rms_backward(token_f32, inverse_one, norm1_gain, normed_one_grad)
    input_grad = mid_grad + input_part
    router_size = width * experts
    return (
        output,
        input_grad,
        norm1_sum.reshape(width),
        joined_sum[:, :query_width],
        joined_sum[:, query_width : query_width + kv_width],
        joined_sum[:, query_width + kv_width :],
        out_sum,
        shared[router_size : router_size + width],
        shared[:router_size].reshape(width, experts),
        w_gate_grad,
        w_up_grad,
        w_down_grad,
    )


def solution(mesh):
    rows = P(("dp", "expert", "tensor"), None)
    columns = P(None, "tensor")
    experts = P("expert", ("dp", "tensor"), None)
    return jax.shard_map(
        local,
        mesh=mesh,
        in_specs=(
            rows,
            P(("dp", "expert"), None),
            rows,
            P(),
            columns,
            columns,
            columns,
            P("tensor", None),
            P(),
            P(),
            experts,
            experts,
            experts,
            rows,
        ),
        out_specs=(
            rows,
            rows,
            P(),
            columns,
            columns,
            columns,
            P("tensor", None),
            P(),
            P(),
            experts,
            experts,
            experts,
        ),
        check_vma=False,
    )
```

```python
import functools

import jax
import jax.numpy as jnp
from jax import lax
from jax.experimental import pallas as pl
from jax.experimental.layout import Layout, with_layout_constraint
from jax.experimental.pallas import tpu as pltpu
from jax.sharding import PartitionSpec as P

HEAD_DIM = 64
HALF = HEAD_DIM // 2
TOP = 8
CAP = 64
EXPERTS = 32
HOLDERS = 16
LANES = 128

epsilon_norm = 1e-06
rope_theta = 10000.0
masked_score = -1e30
QUERY_ROWS = 512
SCALE = HEAD_DIM ** (-0.5)
f32 = jnp.float32
bf16 = jnp.bfloat16


def rms_inverse(values):
    return lax.rsqrt(jnp.mean(values * values, axis=-1, keepdims=True) + epsilon_norm)


def rms_backward(values, inverse, norm_gain, grad_out):
    scaled = grad_out * norm_gain
    grad_in = inverse * scaled - values * (inverse * inverse * inverse) * jnp.mean(
        scaled * values, axis=-1, keepdims=True
    )
    return (grad_in, jnp.sum(grad_out * values * inverse, axis=0))


def dot32(left, right):
    return jnp.dot(left, right, preferred_element_type=f32)


def split_two(values):
    high = values.astype(bf16)
    return high, (values - high.astype(f32)).astype(bf16)


SIDE = 4
STEPS = (0, 1, -1, 2)


def by_rows(values):
    return with_layout_constraint(values, Layout(major_to_minor=tuple(range(values.ndim))))


def cross(values, stage, step):
    pairs = []
    plane = SIDE * SIDE
    for core in range(2):
        for x in range(SIDE):
            for y in range(SIDE):
                if core == stage:
                    to = x * SIDE + (y + step) % SIDE
                else:
                    to = (x + step) % SIDE * SIDE + y
                pairs.append((core * plane + x * SIDE + y, core * plane + to))
    return lax.ppermute(values, ("dp", "expert"), pairs)


def gather_first(values):
    values = by_rows(values)
    line = jnp.stack([values] + [cross(values, 0, step) for step in STEPS[1:]])
    return by_rows(line)


def gather_second(line):
    return [line] + [cross(line, 1, step) for step in STEPS[1:]]


def scatter_first(parts):
    arrived = [parts[0]] + [
        by_rows(cross(part, 1, -step)) for part, step in zip(parts[1:], STEPS[1:])
    ]
    return [
        by_rows(sum(part[place].astype(f32) for part in arrived).astype(bf16))
        for place in range(SIDE)
    ]


def scatter_second(line):
    arrived = [line[0]] + [cross(part, 0, -step) for part, step in zip(line[1:], STEPS[1:])]
    return by_rows(sum(part.astype(f32) for part in arrived))


def ring_gather(block):
    size = lax.axis_size("tensor")
    me = lax.axis_index("tensor")
    half = block.shape[0] // 2
    held = jnp.zeros((size,) + block.shape, block.dtype)

    def shift(values, step):
        return lax.ppermute(values, "tensor", [(i, (i + step) % size) for i in range(size)])

    def put(held, values, place, row):
        return lax.dynamic_update_slice(held, values[None], ((me + place) % size, row, 0))

    held = put(held, block, 0, 0)
    up = down = block
    for step in range(1, size // 2):
        up, down = shift(up, 1), shift(down, -1)
        held = put(held, up, size - step, 0)
        held = put(held, down, step, 0)
    held = put(held, shift(up[:half], 1), size // 2, 0)
    return put(held, shift(down[half:], -1), size // 2, half)


def ring_scatter(parts):
    size = lax.axis_size("tensor")
    me = lax.axis_index("tensor")
    half = parts.shape[1] // 2

    def shift(values, step):
        return lax.ppermute(values, "tensor", [(i, (i + step) % size) for i in range(size)])

    def part_for(place):
        return lax.dynamic_index_in_dim(parts, (me + place) % size, 0, keepdims=False)

    far = part_for(size // 2)
    up, down = shift(far[:half], 1), shift(far[half:], -1)
    up = jnp.pad(up, ((0, half), (0, 0)))
    down = jnp.pad(down, ((half, 0), (0, 0)))
    for place in range(size // 2 - 1, 0, -1):
        up = (part_for(place).astype(f32) + up.astype(f32)).astype(bf16)
        down = (part_for(-place).astype(f32) + down.astype(f32)).astype(bf16)
        up, down = together(shift(by_rows(up), 1), shift(by_rows(down), -1))
    return part_for(0).astype(f32) + up.astype(f32) + down.astype(f32)


def ring_sum(values):
    size = lax.axis_size("tensor")
    step = 1
    while step < size:
        pairs = [(i, i ^ step) for i in range(size)]
        values = values + lax.ppermute(values, "tensor", pairs)
        step *= 2
    return values


def together(*values):
    return lax.optimization_barrier(values)


def swap_cores(values):
    return lax.ppermute(values, "dp", [(0, 1), (1, 0)])


def contract(left, right, left_dim, right_dim):
    return lax.dot_general(
        left, right, (((left_dim,), (right_dim,)), ((), ())), preferred_element_type=f32
    )


def allowed(rows, first, wide, col_ref, row_ref):
    query = first + lax.broadcasted_iota(jnp.int32, (rows, wide), 0)
    key = lax.broadcasted_iota(jnp.int32, (rows, wide), 1)
    return (key <= query) & (col_ref[first : first + rows, :] == row_ref[:, :wide])


def probabilities(query, key, mask):
    scores = jnp.where(mask, contract(query, key, 1, 1), masked_score)
    weights = jnp.exp(scores - jnp.max(scores, axis=1, keepdims=True))
    return weights * (1.0 / jnp.sum(weights, axis=1, keepdims=True))


def turn(values, cosine, low, high):
    size = values.shape[1]
    return (
        values * cosine
        + pltpu.roll(values, size - HALF, 1) * low
        + pltpu.roll(values, HALF, 1) * high
    )


def attention_kernel(
    x_ref, w_ref, col_ref, row_ref, cos_ref, low_ref, high_ref, out_ref, turned_ref, qkv_ref
):
    seq_len = x_ref.shape[0]
    tokens = turned_ref.shape[2]
    heads = out_ref.shape[1] // HEAD_DIM
    last = (heads + 1) * HEAD_DIM
    step = QUERY_ROWS
    for first in range(0, seq_len, step):
        at = slice(first, first + step)
        wide = first + step
        joined = jnp.dot(x_ref[at, :], w_ref[...], preferred_element_type=f32)
        turned_part = turn(joined[:, :last], cos_ref[at, :], low_ref[at, :], high_ref[at, :])
        qkv_ref[at, :last] = turned_part.astype(bf16)
        qkv_ref[at, last:] = joined[:, last:].astype(bf16)
        mask = allowed(step, first, wide, col_ref, row_ref)
        key = qkv_ref[:wide, heads * HEAD_DIM : last]
        value = qkv_ref[:wide, last:]
        for head in range(heads):
            place = slice(head * HEAD_DIM, (head + 1) * HEAD_DIM)
            query = qkv_ref[at, place] * SCALE
            probs = probabilities(query, key, mask).astype(bf16)
            context = jnp.dot(probs, value, preferred_element_type=f32)
            out_ref[at, place] = context.astype(bf16)
            for block in range(step // tokens):
                turned_ref[first // tokens + block, place, :] = context[
                    block * tokens : (block + 1) * tokens
                ].T.astype(bf16)


def attention_back_kernel(
    qkv_ref, grad_ref, col_ref, row_ref, cos_ref, low_ref, high_ref, out_ref, key_sum, value_sum
):
    seq_len = qkv_ref.shape[0]
    heads = grad_ref.shape[1] // HEAD_DIM
    tokens = grad_ref.shape[2]
    last = (heads + 1) * HEAD_DIM
    step = QUERY_ROWS
    for first in reversed(range(0, seq_len, step)):
        at = slice(first, first + step)
        wide = first + step
        mask = allowed(step, first, wide, col_ref, row_ref)
        key = qkv_ref[:wide, heads * HEAD_DIM : last]
        value = qkv_ref[:wide, last:]
        key_grad = jnp.zeros((wide, HEAD_DIM), f32)
        value_grad = jnp.zeros((wide, HEAD_DIM), f32)
        query_grads = []
        for head in range(heads):
            place = slice(head * HEAD_DIM, (head + 1) * HEAD_DIM)
            query = qkv_ref[at, place] * SCALE
            grad = [
                grad_ref[first // tokens + block, place, :].astype(f32).T.astype(bf16)
                for block in range(step // tokens)
            ]
            grad = jnp.concatenate(grad, axis=0)
            probs = probabilities(query, key, mask)
            probs_grad = contract(grad, value, 1, 1)
            row_dot = jnp.sum(probs * probs_grad, axis=1, keepdims=True)
            score_grad = (probs * (probs_grad - row_dot)).astype(bf16)
            query_grads.append(jnp.dot(score_grad, key, preferred_element_type=f32) * SCALE)
            key_grad += contract(score_grad, query, 0, 0)
            value_grad += contract(probs.astype(bf16), grad, 0, 0)
        if wide == seq_len:
            key_sum[...] = key_grad
            value_sum[...] = value_grad
        else:
            key_sum[:wide, :] += key_grad
            value_sum[:wide, :] += value_grad
        both = jnp.concatenate(query_grads + [key_sum[at, :]], axis=1)
        both = turn(both, cos_ref[at, :], -low_ref[at, :], -high_ref[at, :])
        out_ref[at, :last] = both.astype(bf16)
        out_ref[at, last:] = value_sum[at, :].astype(bf16)


def run_attention(normed_all, joined_weights, marks, tables, planes):
    seq_len = normed_all.shape[0]
    joined_width = joined_weights.shape[1]
    query_width = joined_width - 2 * HEAD_DIM
    vmem = pl.BlockSpec(memory_space=pltpu.VMEM)
    return pl.pallas_call(
        attention_kernel,
        out_shape=(
            jax.ShapeDtypeStruct((seq_len, query_width), bf16),
            jax.ShapeDtypeStruct((planes, query_width, seq_len // planes), bf16),
            jax.ShapeDtypeStruct((seq_len, joined_width), bf16),
        ),
        in_specs=[vmem] * 7,
        out_specs=(vmem,) * 3,
        compiler_params=pltpu.CompilerParams(vmem_limit_bytes=48 * 1024 * 1024),
        cost_estimate=pl.CostEstimate(
            flops=4 << 30, bytes_accessed=8 << 20, transcendentals=0
        ),
    )(normed_all, joined_weights, *marks, *tables)


def run_attention_back(qkv, context_grad, marks, tables):
    seq_len, joined_width = qkv.shape
    vmem = pl.BlockSpec(memory_space=pltpu.VMEM)
    return pl.pallas_call(
        attention_back_kernel,
        out_shape=jax.ShapeDtypeStruct((seq_len, joined_width), bf16),
        in_specs=[vmem] * 7,
        out_specs=vmem,
        scratch_shapes=[pltpu.VMEM((seq_len, HEAD_DIM), f32)] * 2,
        compiler_params=pltpu.CompilerParams(vmem_limit_bytes=48 * 1024 * 1024),
        cost_estimate=pl.CostEstimate(
            flops=8 << 30, bytes_accessed=4 << 20, transcendentals=0
        ),
    )(qkv, context_grad, *marks, *tables)


def rope_tables(seq_len, repeats):
    frequency = rope_theta ** (-2.0 * jnp.arange(HALF, dtype=f32) / HEAD_DIM)
    angles = jnp.arange(seq_len, dtype=f32)[:, None] * frequency[None, :]
    sine = jnp.sin(angles)
    nothing = jnp.zeros_like(sine)

    def heads(first, second):
        return jnp.tile(jnp.concatenate([first, second], axis=1), (1, repeats))

    cosine = jnp.cos(angles)
    return heads(cosine, cosine), heads(-sine, nothing), heads(nothing, sine)


def segment_marks(key_seg):
    marks = jnp.where(key_seg == 0, -1 - jnp.arange(key_seg.shape[0], dtype=jnp.int32), key_seg)
    return marks[:, None], marks[None, :]


def expert_kernel(groups, first_ref, *refs):
    rows_refs, cots_refs, (w_ref,), back_outs, mix_outs, rest = (
        refs[:groups],
        refs[groups : 2 * groups],
        refs[2 * groups : 2 * groups + 1],
        refs[2 * groups + 1 : 3 * groups + 1],
        refs[3 * groups + 1 : 4 * groups + 1],
        refs[4 * groups + 1 :],
    )
    x_ref, c_ref, gate_ref, up_ref, hid_ref, pick_ref, down_ref = rest
    sources, tokens, _ = rows_refs[0].shape
    width = x_ref.shape[2]
    inner = w_ref.shape[2]
    e = pl.program_id(0)
    expert = first_ref[0] + e
    lane = lax.broadcasted_iota(jnp.int32, (CAP, LANES), 1)
    row_id = lax.broadcasted_iota(jnp.int32, (EXPERTS, tokens), 0)
    slot = lax.broadcasted_iota(jnp.int32, (CAP, tokens), 0).astype(f32)
    at = pl.ds(pl.multiple_of(e * CAP, CAP), CAP)
    every = [(group, source) for group in range(groups) for source in range(sources)]
    gates = []
    for order, (group, source) in enumerate(every):
        table = cots_refs[group][source, :EXPERTS, width:].astype(f32)
        rank = jnp.sum(jnp.where(row_id == expert, table, 0.0), axis=0, keepdims=True)
        pick = (rank == slot).astype(bf16)
        pick_ref[order, at] = pick
        rows = jnp.dot(pick, rows_refs[group][source], preferred_element_type=f32)
        cots = jnp.dot(pick, cots_refs[group][source, :, :width], preferred_element_type=f32)
        own = (lane == expert) | (lane == expert + EXPERTS)
        gates.append(jnp.sum(jnp.where(own, rows[:, width:], 0.0), axis=1, keepdims=True))
        x_ref[0, order * CAP : (order + 1) * CAP] = rows[:, :width].astype(bf16)
        c_ref[0, order * CAP : (order + 1) * CAP] = cots.astype(bf16)
    gate = jnp.concatenate(gates, axis=0)

    down_rows = inner // HOLDERS
    chunks = width // inner
    for holder in range(HOLDERS):
        for chunk in range(chunks):
            start = (holder * chunks + chunk) * down_rows
            down_ref[
                holder * down_rows : (holder + 1) * down_rows,
                chunk * inner : (chunk + 1) * inner,
            ] = w_ref[2, start : start + down_rows, :]

    x = x_ref[0]
    gate_pre = jnp.dot(x, w_ref[0], preferred_element_type=f32)
    up_pre = jnp.dot(x, w_ref[1], preferred_element_type=f32)
    back = contract(c_ref[0], down_ref[...], 1, 1)
    sig = 1.0 / (1.0 + jnp.exp(-gate_pre))
    silu = gate_pre * sig
    hidden = (silu * up_pre).astype(bf16)
    gate_grad = jnp.sum(back * hidden.astype(f32), axis=1, keepdims=True)
    grad = gate * back
    gate_pre_grad = (grad * up_pre * (sig + silu * (1.0 - sig))).astype(bf16)
    up_pre_grad = (grad * silu).astype(bf16)
    gate_ref[0] = gate_pre_grad
    up_ref[0] = up_pre_grad
    hid_ref[0] = (gate * hidden.astype(f32)).astype(bf16)
    row_grad = contract(gate_pre_grad, w_ref[0], 1, 1) + contract(up_pre_grad, w_ref[1], 1, 1)
    high = gate_grad.astype(bf16).astype(f32)
    lane = lax.broadcasted_iota(jnp.int32, (len(every) * CAP, LANES), 1)
    tail = jnp.where(lane == expert, high, 0.0)
    tail += jnp.where(lane == expert + EXPERTS, gate_grad - high, 0.0)
    for order, (group, source) in enumerate(every):
        place = slice(order * CAP, (order + 1) * CAP)
        back_outs[group][source, at, :width] = row_grad[place].astype(bf16)
        back_outs[group][source, at, width:] = tail[place].astype(bf16)
    mixed = gate * jnp.dot(hidden, down_ref[...], preferred_element_type=f32)
    for order, (group, source) in enumerate(every):
        place = slice(order * CAP, (order + 1) * CAP)
        mix_outs[group][source, at] = mixed[place].astype(bf16)

    @pl.when(e == 1)
    def _():
        for order, (group, source) in enumerate(every):
            pick = pick_ref[order]
            back_outs[group][source] = contract(pick, back_outs[group][source], 0, 0).astype(bf16)
            mix_outs[group][source] = contract(pick, mix_outs[group][source], 0, 0).astype(bf16)


def run_experts(first, rows, cots, weights):
    groups = len(rows)
    sources, tokens, padded = rows[0].shape
    width = padded - LANES
    inner = weights.shape[2]
    slots = groups * sources * CAP

    def once(columns):
        return pl.BlockSpec(
            (sources, tokens, columns), lambda e: (0, 0, 0), pipeline_mode=pl.Buffered(1)
        )

    def by_expert(*shape):
        return pl.BlockSpec(shape, lambda e: (e, 0, 0))

    acts = jax.ShapeDtypeStruct((2, slots, inner), bf16)
    wide = jax.ShapeDtypeStruct((2, slots, width), bf16)
    outs = pl.pallas_call(
        functools.partial(expert_kernel, groups),
        grid=(2,),
        out_shape=(
            *[jax.ShapeDtypeStruct((sources, tokens, padded), bf16)] * groups,
            *[jax.ShapeDtypeStruct((sources, tokens, width), bf16)] * groups,
            wide,
            wide,
            acts,
            acts,
            acts,
        ),
        in_specs=[pl.BlockSpec(memory_space=pltpu.SMEM)]
        + [once(padded)] * (2 * groups)
        + [by_expert(3, width, inner)],
        out_specs=(
            *[once(padded)] * groups,
            *[once(width)] * groups,
            by_expert(1, slots, width),
            by_expert(1, slots, width),
            by_expert(1, slots, inner),
            by_expert(1, slots, inner),
            by_expert(1, slots, inner),
        ),
        scratch_shapes=[
            pltpu.VMEM((groups * sources, 2 * CAP, tokens), bf16),
            pltpu.VMEM((inner, width), bf16),
        ],
        compiler_params=pltpu.CompilerParams(vmem_limit_bytes=56 * 1024 * 1024),
        cost_estimate=pl.CostEstimate(
            flops=2 * 2 * 7 * slots * width * inner, bytes_accessed=24 << 20, transcendentals=0
        ),
    )(first, *rows, *cots, weights)
    return outs[:groups], outs[groups : 2 * groups], outs[2 * groups :]


def weight_grad_kernel(half_ref, *refs):
    groups = (len(refs) - 2) // 5
    x_refs, c_refs, gate_refs, up_refs, hid_refs = (
        refs[i * groups : (i + 1) * groups] for i in range(5)
    )
    outs = refs[5 * groups :]
    width = x_refs[0].shape[2]
    inner = gate_refs[0].shape[2]
    rows = width // 2
    down_rows = inner // HOLDERS
    chunks = width // inner
    for out_ref, half in zip(outs, (1 - half_ref[0], half_ref[0])):
        cols = pl.ds(pl.multiple_of(half * rows, LANES), rows)
        down_cols = pl.ds(pl.multiple_of(half * (inner // 2), LANES), inner // 2)
        gate = jnp.zeros((rows, inner), f32)
        up = jnp.zeros((rows, inner), f32)
        down = jnp.zeros((inner // 2, width), f32)
        for i in range(groups):
            x = x_refs[i][0, :, cols]
            gate += contract(x, gate_refs[i][0], 0, 0)
            up += contract(x, up_refs[i][0], 0, 0)
        out_ref[0] = gate.astype(bf16)
        out_ref[1] = up.astype(bf16)
        for i in range(groups):
            down += contract(hid_refs[i][0, :, down_cols], c_refs[i][0], 0, 0)
        for holder in range(HOLDERS // 2):
            for chunk in range(chunks):
                at = (holder * chunks + chunk) * down_rows
                out_ref[2, at : at + down_rows, :] = down[
                    holder * down_rows : (holder + 1) * down_rows,
                    chunk * inner : (chunk + 1) * inner,
                ].astype(bf16)


def run_weight_grads(core, saved):
    x, c, gate, up, hid = zip(*saved)
    width = x[0].shape[2]
    inner = gate[0].shape[2]
    operands = (*x, *c, *gate, *up, *hid)
    out = jax.ShapeDtypeStruct((6, width // 2, inner), bf16)
    out_spec = pl.BlockSpec((3, width // 2, inner), lambda e: (e, 0, 0))
    return pl.pallas_call(
        weight_grad_kernel,
        grid=(2,),
        out_shape=(out, out),
        in_specs=[pl.BlockSpec(memory_space=pltpu.SMEM)]
        + [pl.BlockSpec((1,) + v.shape[1:], lambda e: (e, 0, 0)) for v in operands],
        out_specs=(out_spec, out_spec),
        compiler_params=pltpu.CompilerParams(vmem_limit_bytes=52 * 1024 * 1024),
        cost_estimate=pl.CostEstimate(
            flops=1 << 28, bytes_accessed=1 << 20, transcendentals=0
        ),
    )(core, *operands)


def local(
    tokens,
    segments,
    routes,
    norm1_gain,
    w_query,
    w_key,
    w_value,
    w_out,
    norm2_gain,
    w_router,
    w_gate,
    w_up,
    w_down,
    cotangent,
):
    tok_rows, width = tokens.shape
    seq_len = segments.shape[1]
    query_width = w_query.shape[1]
    kv_width = w_key.shape[1]
    joined_width = query_width + 2 * kv_width
    local_experts = w_gate.shape[0]
    experts = w_router.shape[1]
    owners = lax.axis_size("expert")
    planes = lax.axis_size("tensor")
    owner = lax.axis_index("expert")
    first_expert = owner * local_experts
    key_seg = segments[0]
    hidden_width = w_gate.shape[2]

    token_f32 = tokens.astype(f32)
    inverse_one = rms_inverse(token_f32)
    normed_low = (token_f32 * inverse_one * norm1_gain).astype(bf16)
    joined_weights = jnp.concatenate([w_query, w_key, w_value], axis=1)
    normed_low = by_rows(normed_low)
    normed_all = lax.all_gather(normed_low, "tensor", axis=0, tiled=True)
    core = lax.axis_index("dp")

    expert_ids = jnp.arange(experts, dtype=jnp.int32)
    onehot = (routes[:, :, None] == expert_ids[None, None, :]).astype(f32)
    member = jnp.sum(onehot, axis=1)
    lower = (jnp.arange(tok_rows)[:, None] <= jnp.arange(tok_rows)[None, :]).astype(bf16)
    rank = jnp.einsum("te,tu->eu", member.astype(bf16), lower, preferred_element_type=f32)
    rank = jnp.where(member.T > 0, rank - 1.0, -1.0).astype(bf16)
    extra = jnp.pad(rank, ((0, tok_rows - experts), (0, LANES - tok_rows)))
    cot_payload = jnp.concatenate([cotangent, extra], axis=1)

    count = w_out.shape[0] // 2
    half_out = ring_gather(lax.dynamic_slice_in_dim(w_out, core * count, count, 0))
    chunks = width // hidden_width
    down_rows = w_down.shape[1]
    part_rows = w_gate.shape[1]
    down_parts = w_down.reshape(local_experts, down_rows, chunks, hidden_width)
    down_parts = down_parts.transpose(0, 2, 1, 3).reshape(local_experts, part_rows, hidden_width)
    weights = jnp.stack([w_gate, w_up, down_parts], axis=1)
    weights = weights.reshape(3 * local_experts, part_rows, hidden_width)
    tables = rope_tables(seq_len, query_width // HEAD_DIM + 1)
    marks = segment_marks(key_seg)
    normed_all, half_out, cot_line, weights, joined_weights, *constants = together(
        normed_all, half_out, gather_first(cot_payload), weights, joined_weights, *tables, *marks
    )
    tables, marks = constants[:3], constants[3:]
    weights_all = lax.all_gather(weights, ("dp", "tensor"), axis=1, tiled=True)
    cot_parts = gather_second(cot_line)

    context, context_blocks, qkv = run_attention(
        normed_all, joined_weights, marks, tables, planes
    )
    context_blocks, cot_parts[1], cot_parts[2] = together(
        context_blocks, cot_parts[1], cot_parts[2]
    )
    context_home = lax.all_to_all(context_blocks, "tensor", split_axis=0, concat_axis=0)
    other_out = swap_cores(half_out)
    w_out_all = jnp.concatenate(
        [jnp.where(core == 0, half_out, other_out), jnp.where(core == 0, other_out, half_out)],
        axis=1,
    ).reshape(planes * query_width, width)
    context_home, w_out_all = together(context_home, w_out_all)
    context_home = context_home.reshape(planes * query_width, tok_rows)
    mid = token_f32 + contract(context_home, w_out_all, 0, 0)
    inverse_two = rms_inverse(mid)
    normed_two = (mid * inverse_two * norm2_gain).astype(bf16)
    logits = dot32(normed_two, w_router)
    logits = jnp.where(member > 0, logits, masked_score)
    chosen_exp = jnp.where(
        member > 0, jnp.exp(logits - jnp.max(logits, axis=1, keepdims=True)), 0.0
    )
    gates = chosen_exp / jnp.sum(chosen_exp, axis=1, keepdims=True)
    gate_high, gate_low = split_two(gates)
    payload = jnp.concatenate(
        [normed_two, gate_high, gate_low, jnp.zeros((tok_rows, LANES - 2 * experts), bf16)],
        axis=1,
    )
    payload, *cot_parts = together(payload, *cot_parts)
    line = gather_first(payload)
    before, behind = (cross(line, 1, step) for step in STEPS[1:3])

    first_expert = first_expert.astype(jnp.int32).reshape(1)
    def compute(rows, cots):
        return run_experts(first_expert, rows, cots, weights_all)

    own = compute([line], cot_parts[:1])
    line, before, behind, *own_saved = together(line, before, behind, *own[2])
    far = cross(line, 1, STEPS[3])
    near = compute([before, behind], cot_parts[1:3])
    far, *near_saved = together(far, *near[2])
    last = compute([far], cot_parts[3:])
    done = [(*own[:2], own_saved), (*near[:2], near_saved), last]
    back_line = scatter_first([part for some in done for part in some[0]])
    *both, given, kept = together(
        *back_line,
        *[part for some in done for part in some[1]],
        *run_weight_grads(core.astype(jnp.int32).reshape(1), [some[2] for some in done]),
    )
    back_line, mix_parts = both[:SIDE], both[SIDE:]
    kept = (kept.astype(f32) + swap_cores(given).astype(f32)).astype(bf16)
    weight_sum = lax.psum_scatter(kept, "tensor", scatter_dimension=1, tiled=True)
    back_home = scatter_second(back_line)
    back_home, kept = together(back_home, kept)

    cot_f32 = cotangent.astype(f32)
    grad_tail = back_home[:, width:]
    gate_grad = grad_tail[:, :experts] + grad_tail[:, experts : 2 * experts]
    chosen_grad = gates * (gate_grad - jnp.sum(gates * gate_grad, axis=1, keepdims=True))
    logit_grad = chosen_grad.astype(bf16)
    normed_two_grad = back_home[:, :width] + jnp.einsum(
        "te,de->td", logit_grad, w_router, preferred_element_type=f32
    )
    mid_part, norm2_part = rms_backward(mid, inverse_two, norm2_gain, normed_two_grad)
    mid_grad = cot_f32 + mid_part
    attention_low = by_rows(mid_grad.astype(bf16))
    context_grad = by_rows(contract(w_out_all, attention_low, 1, 1).astype(bf16))
    context_grad, logit_grad, *mix_parts = together(context_grad, logit_grad, *mix_parts)
    mix_line = scatter_first(mix_parts)
    router_part = contract(normed_two, logit_grad, 0, 0)
    context_grad = lax.all_to_all(
        context_grad.reshape(planes, query_width, tok_rows), "tensor", split_axis=0, concat_axis=0
    )
    joined_grad = run_attention_back(qkv, context_grad, marks, tables)
    normed_one_grad = ring_scatter(
        contract(joined_grad, joined_weights, 1, 1).astype(bf16).reshape(planes, tok_rows, width)
    )
    attention_all = lax.all_gather(attention_low, "tensor", axis=0, tiled=True)
    joined_part = contract(normed_all, joined_grad, 0, 0)
    out_part = contract(attention_all, context, 0, 0)
    norm1_part = jnp.sum(joined_part * joined_weights.astype(f32), axis=1) / norm1_gain

    sharers = lax.axis_size("dp") * owners
    sides = jnp.concatenate([joined_part.astype(bf16), out_part.astype(bf16)], axis=1)
    columns = sides.shape[1]
    block = width // sharers
    shared = jnp.concatenate([router_part.T, norm2_part[None], norm1_part[None]]).astype(bf16)
    shared_size = shared.size
    extra = -(-shared_size // (columns * sharers))
    shared = jnp.pad(shared.reshape(-1), (0, extra * columns * sharers - shared_size))
    blocks = jnp.concatenate(
        [sides.reshape(sharers, block, columns), shared.reshape(sharers, extra, columns)], axis=1
    )
    blocks, *mix_line = together(blocks, *mix_line)
    output = (mid + scatter_second(mix_line)).astype(bf16)
    arrived = lax.all_to_all(blocks, ("dp", "expert"), split_axis=0, concat_axis=0)
    total = jnp.sum(arrived.astype(f32), axis=0).astype(bf16)
    spread = lax.all_to_all(
        jnp.broadcast_to(total[None], arrived.shape), ("dp", "expert"), split_axis=0, concat_axis=0
    )
    spread, weight_sum = together(spread, weight_sum)
    sides = spread[:, :block].reshape(width, columns).astype(f32)
    shared = ring_sum(spread[:, block:].reshape(-1, LANES)).astype(f32).reshape(-1)
    shared = shared[:shared_size].reshape(experts + 2, width)
    joined_sum = sides[:, :joined_width]
    out_sum = sides[:, joined_width:].T
    weight_sum = weight_sum.reshape(local_experts, 3, part_rows, hidden_width)
    w_gate_grad = weight_sum[:, 0].astype(f32)
    w_up_grad = weight_sum[:, 1].astype(f32)
    w_down_grad = weight_sum[:, 2].reshape(local_experts, chunks, down_rows, hidden_width)
    w_down_grad = w_down_grad.transpose(0, 2, 1, 3).reshape(local_experts, down_rows, width)
    w_down_grad = w_down_grad.astype(f32)
    input_part, _ = rms_backward(token_f32, inverse_one, norm1_gain, normed_one_grad)
    input_grad = mid_grad + input_part
    return (
        output,
        input_grad,
        shared[experts + 1],
        joined_sum[:, :query_width],
        joined_sum[:, query_width : query_width + kv_width],
        joined_sum[:, query_width + kv_width :],
        out_sum,
        shared[experts],
        shared[:experts].T,
        w_gate_grad,
        w_up_grad,
        w_down_grad,
    )


def solution(mesh):
    rows = P(("dp", "expert", "tensor"), None)
    columns = P(None, "tensor")
    experts = P("expert", ("dp", "tensor"), None)
    return jax.shard_map(
        local,
        mesh=mesh,
        in_specs=(
            rows,
            P(("dp", "expert"), None),
            rows,
            P(),
            columns,
            columns,
            columns,
            P("tensor", None),
            P(),
            P(),
            experts,
            experts,
            experts,
            rows,
        ),
        out_specs=(
            rows,
            rows,
            P(),
            columns,
            columns,
            columns,
            P("tensor", None),
            P(),
            P(),
            experts,
            experts,
            experts,
        ),
        check_vma=False,
    )
```

```python
import functools

import jax
import jax.numpy as jnp
import numpy as np
from jax import lax
from jax.experimental import pallas as pl
from jax.experimental.layout import Layout, with_layout_constraint
from jax.experimental.pallas import tpu as pltpu
from jax.sharding import PartitionSpec as P

HEAD_DIM = 64
HALF = HEAD_DIM // 2
TOP = 8
CAP = 64
EXPERTS = 32
HOLDERS = 16
LANES = 128

epsilon_norm = 1e-06
rope_theta = 10000.0
masked_score = -1e30
QUERY_ROWS = 512
SCALE = HEAD_DIM ** (-0.5)
f32 = jnp.float32
bf16 = jnp.bfloat16


def rms_inverse(values):
    return lax.rsqrt(jnp.mean(values * values, axis=-1, keepdims=True) + epsilon_norm)


def rms_backward(values, inverse, norm_gain, grad_out):
    scaled = grad_out * norm_gain
    grad_in = inverse * scaled - values * (inverse * inverse * inverse) * jnp.mean(
        scaled * values, axis=-1, keepdims=True
    )
    return (grad_in, jnp.sum(grad_out * values * inverse, axis=0))


def dot32(left, right):
    return jnp.dot(left, right, preferred_element_type=f32)


def split_two(values):
    high = values.astype(bf16)
    return high, (values - high.astype(f32)).astype(bf16)


SIDE = 4
STEPS = (0, 1, -1, 2)


def by_rows(values):
    return with_layout_constraint(values, Layout(major_to_minor=tuple(range(values.ndim))))


def cross(values, stage, step):
    pairs = []
    plane = SIDE * SIDE
    for core in range(2):
        for x in range(SIDE):
            for y in range(SIDE):
                if core == stage:
                    to = x * SIDE + (y + step) % SIDE
                else:
                    to = (x + step) % SIDE * SIDE + y
                pairs.append((core * plane + x * SIDE + y, core * plane + to))
    return lax.ppermute(values, ("dp", "expert"), pairs)


def gather_first(values):
    values = by_rows(values)
    line = jnp.stack([values] + [cross(values, 0, step) for step in STEPS[1:]])
    return by_rows(line)


def gather_second(line):
    return [line] + [cross(line, 1, step) for step in STEPS[1:]]


def scatter_first(parts):
    arrived = [parts[0]] + [
        by_rows(cross(part, 1, -step)) for part, step in zip(parts[1:], STEPS[1:])
    ]
    return [
        by_rows(sum(part[place].astype(f32) for part in arrived).astype(bf16))
        for place in range(SIDE)
    ]


def scatter_second(line, *beside):
    arrived = [cross(part, 0, -step) for part, step in zip(line[1:], STEPS[1:])]
    arrived[0], *beside = together(arrived[0], *beside)
    return by_rows(sum(part.astype(f32) for part in (line[0], *arrived))), *beside


def ring_sum(values):
    size = lax.axis_size("tensor")
    step = 1
    while step < size:
        pairs = [(i, i ^ step) for i in range(size)]
        values = values + lax.ppermute(values, "tensor", pairs)
        step *= 2
    return values


def together(*values):
    return lax.optimization_barrier(values)


def swap_cores(values):
    return lax.ppermute(values, "dp", [(0, 1), (1, 0)])


def contract(left, right, left_dim, right_dim):
    return lax.dot_general(
        left, right, (((left_dim,), (right_dim,)), ((), ())), preferred_element_type=f32
    )


def allowed(rows, first, wide, col_ref, row_ref):
    query = first + lax.broadcasted_iota(jnp.int32, (rows, wide), 0)
    key = lax.broadcasted_iota(jnp.int32, (rows, wide), 1)
    return (key <= query) & (col_ref[first : first + rows, :] == row_ref[:, :wide])


def probabilities(query, key, mask):
    scores = jnp.where(mask, contract(query, key, 1, 1), masked_score)
    weights = jnp.exp(scores - jnp.max(scores, axis=1, keepdims=True))
    return weights * (1.0 / jnp.sum(weights, axis=1, keepdims=True))


def turn(values, cosine, low, high):
    size = values.shape[1]
    return (
        values * cosine
        + pltpu.roll(values, size - HALF, 1) * low
        + pltpu.roll(values, HALF, 1) * high
    )


def attention_kernel(
    x_ref, w_ref, col_ref, row_ref, cos_ref, low_ref, high_ref, out_ref, turned_ref, qkv_ref
):
    seq_len = out_ref.shape[0]
    tokens = turned_ref.shape[2]
    heads = out_ref.shape[1] // HEAD_DIM
    last = (heads + 1) * HEAD_DIM
    step = QUERY_ROWS
    for first in range(0, seq_len, step):
        at = slice(first, first + step)
        wide = first + step
        blocks = range(first // tokens, wide // tokens)
        rows = jnp.concatenate([x_ref[block, :tokens, :] for block in blocks], axis=0)
        joined = jnp.dot(rows, w_ref[...], preferred_element_type=f32)
        turned_part = turn(joined[:, :last], cos_ref[at, :], low_ref[at, :], high_ref[at, :])
        qkv_ref[at, :last] = turned_part.astype(bf16)
        qkv_ref[at, last:] = joined[:, last:].astype(bf16)
        mask = allowed(step, first, wide, col_ref, row_ref)
        key = qkv_ref[:wide, heads * HEAD_DIM : last]
        value = qkv_ref[:wide, last:]
        for head in range(heads):
            place = slice(head * HEAD_DIM, (head + 1) * HEAD_DIM)
            query = qkv_ref[at, place] * SCALE
            probs = probabilities(query, key, mask).astype(bf16)
            context = jnp.dot(probs, value, preferred_element_type=f32)
            out_ref[at, place] = context.astype(bf16)
            for block in range(step // tokens):
                turned_ref[first // tokens + block, place, :] = context[
                    block * tokens : (block + 1) * tokens
                ].T.astype(bf16)


def attention_back_kernel(
    qkv_ref, grad_ref, col_ref, row_ref, cos_ref, low_ref, high_ref, out_ref, turned_ref, key_sum, value_sum
):
    seq_len = qkv_ref.shape[0]
    heads = grad_ref.shape[1] // HEAD_DIM
    tokens = grad_ref.shape[2]
    last = (heads + 1) * HEAD_DIM
    step = QUERY_ROWS
    for first in reversed(range(0, seq_len, step)):
        at = slice(first, first + step)
        wide = first + step
        mask = allowed(step, first, wide, col_ref, row_ref)
        key = qkv_ref[:wide, heads * HEAD_DIM : last]
        value = qkv_ref[:wide, last:]
        key_grad = jnp.zeros((wide, HEAD_DIM), f32)
        value_grad = jnp.zeros((wide, HEAD_DIM), f32)
        query_grads = []
        for head in range(heads):
            place = slice(head * HEAD_DIM, (head + 1) * HEAD_DIM)
            query = qkv_ref[at, place] * SCALE
            grad = [
                grad_ref[first // tokens + block, place, :].astype(f32).T.astype(bf16)
                for block in range(step // tokens)
            ]
            grad = jnp.concatenate(grad, axis=0)
            probs = probabilities(query, key, mask)
            probs_grad = contract(grad, value, 1, 1)
            row_dot = jnp.sum(probs * probs_grad, axis=1, keepdims=True)
            score_grad = (probs * (probs_grad - row_dot)).astype(bf16)
            query_grads.append(jnp.dot(score_grad, key, preferred_element_type=f32) * SCALE)
            key_grad += contract(score_grad, query, 0, 0)
            value_grad += contract(probs.astype(bf16), grad, 0, 0)
        if wide == seq_len:
            key_sum[...] = key_grad
            value_sum[...] = value_grad
        else:
            key_sum[:wide, :] += key_grad
            value_sum[:wide, :] += value_grad
        both = jnp.concatenate(query_grads + [key_sum[at, :]], axis=1)
        both = turn(both, cos_ref[at, :], -low_ref[at, :], -high_ref[at, :])
        out_ref[at, :last] = both.astype(bf16)
        out_ref[at, last:] = value_sum[at, :].astype(bf16)
        for block in range(step // tokens):
            part = slice(block * tokens, (block + 1) * tokens)
            to = first // tokens + block
            turned_ref[to, :last, :] = both[part].T.astype(bf16)
            turned_ref[to, last:, :] = value_sum[first : first + step, :][part].T.astype(bf16)


def run_attention(gathered, joined_weights, marks, tables):
    planes = gathered.shape[0]
    seq_len = marks[0].shape[0]
    joined_width = joined_weights.shape[1]
    query_width = joined_width - 2 * HEAD_DIM
    vmem = pl.BlockSpec(memory_space=pltpu.VMEM)
    return pl.pallas_call(
        attention_kernel,
        out_shape=(
            jax.ShapeDtypeStruct((seq_len, query_width), bf16),
            jax.ShapeDtypeStruct((planes, query_width, seq_len // planes), bf16),
            jax.ShapeDtypeStruct((seq_len, joined_width), bf16),
        ),
        in_specs=[vmem] * 7,
        out_specs=(vmem,) * 3,
        compiler_params=pltpu.CompilerParams(vmem_limit_bytes=48 * 1024 * 1024),
        cost_estimate=pl.CostEstimate(
            flops=4 << 30, bytes_accessed=8 << 20, transcendentals=0
        ),
    )(gathered, joined_weights, *marks, *tables)


def run_attention_back(qkv, context_grad, marks, tables):
    seq_len, joined_width = qkv.shape
    planes = context_grad.shape[0]
    vmem = pl.BlockSpec(memory_space=pltpu.VMEM)
    return pl.pallas_call(
        attention_back_kernel,
        out_shape=(
            jax.ShapeDtypeStruct((seq_len, joined_width), bf16),
            jax.ShapeDtypeStruct((planes, joined_width, seq_len // planes), bf16),
        ),
        in_specs=[vmem] * 7,
        out_specs=(vmem, vmem),
        scratch_shapes=[pltpu.VMEM((seq_len, HEAD_DIM), f32)] * 2,
        compiler_params=pltpu.CompilerParams(vmem_limit_bytes=48 * 1024 * 1024),
        cost_estimate=pl.CostEstimate(
            flops=8 << 30, bytes_accessed=4 << 20, transcendentals=0
        ),
    )(qkv, context_grad, *marks, *tables)


def rope_tables(seq_len, repeats):
    frequency = np.float32(rope_theta) ** (np.arange(HALF, dtype=np.float32) * np.float32(-2.0 / HEAD_DIM))
    angles = np.arange(seq_len, dtype=np.float32)[:, None] * frequency.astype(np.float32)[None, :]
    cosine, sine = np.cos(angles), np.sin(angles)
    nothing = np.zeros_like(sine)

    def heads(first, second):
        return jnp.asarray(np.tile(np.concatenate([first, second], axis=1), (1, repeats)))

    return heads(cosine, cosine), heads(-sine, nothing), heads(nothing, sine)


def segment_marks(key_seg):
    marks = jnp.where(key_seg == 0, -1 - jnp.arange(key_seg.shape[0], dtype=jnp.int32), key_seg)
    return marks[:, None], marks[None, :]


def expert_kernel(groups, first_ref, *refs):
    rows_refs, cots_refs = refs[:groups], refs[groups : 2 * groups]
    w_ref = refs[2 * groups]
    back_outs = refs[2 * groups + 1 : 3 * groups + 1]
    x_ref, c_ref, gate_ref, up_ref, hid_ref, pick_ref, down_ref = refs[3 * groups + 1 :]
    sources, tokens, _ = rows_refs[0].shape
    width = x_ref.shape[2]
    inner = w_ref.shape[2]
    e = pl.program_id(0)
    expert = first_ref[0] + e
    lane = lax.broadcasted_iota(jnp.int32, (CAP, LANES), 1)
    row_id = lax.broadcasted_iota(jnp.int32, (EXPERTS, tokens), 0)
    slot = lax.broadcasted_iota(jnp.int32, (CAP, tokens), 0).astype(f32)
    at = pl.ds(pl.multiple_of(e * CAP, CAP), CAP)
    every = [(group, source) for group in range(groups) for source in range(sources)]
    gates = []
    for order, (group, source) in enumerate(every):
        table = cots_refs[group][source, :EXPERTS, width:].astype(f32)
        rank = jnp.sum(jnp.where(row_id == expert, table, 0.0), axis=0, keepdims=True)
        pick = (rank == slot).astype(bf16)
        pick_ref[order, at] = pick
        rows = jnp.dot(pick, rows_refs[group][source], preferred_element_type=f32)
        cots = jnp.dot(pick, cots_refs[group][source, :, :width], preferred_element_type=f32)
        own = (lane == expert) | (lane == expert + EXPERTS)
        gates.append(jnp.sum(jnp.where(own, rows[:, width:], 0.0), axis=1, keepdims=True))
        x_ref[0, order * CAP : (order + 1) * CAP] = rows[:, :width].astype(bf16)
        c_ref[0, order * CAP : (order + 1) * CAP] = cots.astype(bf16)
    gate = jnp.concatenate(gates, axis=0)

    join_chunks(down_ref, w_ref.at[2], HOLDERS)
    x = x_ref[0]
    gate_pre = jnp.dot(x, w_ref[0], preferred_element_type=f32)
    up_pre = jnp.dot(x, w_ref[1], preferred_element_type=f32)
    back = contract(c_ref[0], down_ref[...], 1, 1)
    sig = 1.0 / (1.0 + jnp.exp(-gate_pre))
    silu = gate_pre * sig
    hidden = (silu * up_pre).astype(bf16)
    gate_grad = jnp.sum(back * hidden.astype(f32), axis=1, keepdims=True)
    grad = gate * back
    gate_pre_grad = (grad * up_pre * (sig + silu * (1.0 - sig))).astype(bf16)
    up_pre_grad = (grad * silu).astype(bf16)
    gate_ref[0] = gate_pre_grad
    up_ref[0] = up_pre_grad
    hid_ref[0] = (gate * hidden.astype(f32)).astype(bf16)
    row_grad = contract(gate_pre_grad, w_ref[0], 1, 1) + contract(up_pre_grad, w_ref[1], 1, 1)
    high = gate_grad.astype(bf16).astype(f32)
    lane = lax.broadcasted_iota(jnp.int32, (len(every) * CAP, LANES), 1)
    tail = jnp.where(lane == expert, high, 0.0)
    tail += jnp.where(lane == expert + EXPERTS, gate_grad - high, 0.0)
    for order, (group, source) in enumerate(every):
        place = slice(order * CAP, (order + 1) * CAP)
        back_outs[group][source, at, :width] = row_grad[place].astype(bf16)
        back_outs[group][source, at, width:] = tail[place].astype(bf16)

    @pl.when(e == 1)
    def _():
        for order, (group, source) in enumerate(every):
            back_outs[group][source] = contract(
                pick_ref[order], back_outs[group][source], 0, 0
            ).astype(bf16)


def join_chunks(to_ref, from_ref, holders):
    inner = from_ref.shape[1]
    rows = inner // HOLDERS
    chunks = to_ref.shape[1] // inner
    for holder in range(holders):
        for chunk in range(chunks):
            start = (holder * chunks + chunk) * rows
            to_ref[
                holder * rows : (holder + 1) * rows, chunk * inner : (chunk + 1) * inner
            ] = from_ref[start : start + rows, :]


def run_experts(first, rows, cots, weights):
    groups = len(rows)
    sources, tokens, padded = rows[0].shape
    width = padded - LANES
    inner = weights.shape[2]
    slots = groups * sources * CAP

    def once(columns):
        return pl.BlockSpec(
            (sources, tokens, columns), lambda e: (0, 0, 0), pipeline_mode=pl.Buffered(1)
        )

    def by_expert(*shape):
        return pl.BlockSpec(shape, lambda e: (e, 0, 0))

    acts = jax.ShapeDtypeStruct((2, slots, inner), bf16)
    wide = jax.ShapeDtypeStruct((2, slots, width), bf16)
    outs = pl.pallas_call(
        functools.partial(expert_kernel, groups),
        grid=(2,),
        out_shape=(
            *[jax.ShapeDtypeStruct((sources, tokens, padded), bf16)] * groups,
            wide,
            wide,
            acts,
            acts,
            acts,
            jax.ShapeDtypeStruct((groups * sources, 2 * CAP, tokens), bf16),
        ),
        in_specs=[pl.BlockSpec(memory_space=pltpu.SMEM)]
        + [once(padded)] * (2 * groups)
        + [by_expert(3, width, inner)],
        out_specs=(
            *[once(padded)] * groups,
            by_expert(1, slots, width),
            by_expert(1, slots, width),
            by_expert(1, slots, inner),
            by_expert(1, slots, inner),
            by_expert(1, slots, inner),
            pl.BlockSpec((groups * sources, 2 * CAP, tokens), lambda e: (0, 0, 0)),
        ),
        scratch_shapes=[pltpu.VMEM((inner, width), bf16)],
        compiler_params=pltpu.CompilerParams(vmem_limit_bytes=56 * 1024 * 1024),
        cost_estimate=pl.CostEstimate(
            flops=2 * 2 * 6 * slots * width * inner, bytes_accessed=24 << 20, transcendentals=0
        ),
    )(first, *rows, *cots, weights)
    return outs[:groups], outs[groups:-1], outs[-1]


def mixture_kernel(groups, *refs):
    pick_refs, hid_refs = refs[:groups], refs[groups : 2 * groups]
    w_ref = refs[2 * groups]
    outs, down_ref = refs[2 * groups + 1 : -1], refs[-1]
    e = pl.program_id(0)
    at = pl.ds(pl.multiple_of(e * CAP, CAP), CAP)
    join_chunks(down_ref, w_ref.at[0], HOLDERS)
    sources = [
        (pick_ref, hid_ref, source)
        for pick_ref, hid_ref in zip(pick_refs, hid_refs)
        for source in range(pick_ref.shape[0])
    ]
    to = {}
    for order, (pick_ref, hid_ref, source) in enumerate(sources):
        to[order] = (outs[order // SIDE], order % SIDE, pick_ref, source)
    order = 0
    for pick_ref, hid_ref in zip(pick_refs, hid_refs):
        mixed = jnp.dot(hid_ref[0], down_ref[...], preferred_element_type=f32).astype(bf16)
        for source in range(pick_ref.shape[0]):
            out, place, _, _ = to[order]
            out[place, at] = mixed[source * CAP : (source + 1) * CAP]
            order += 1

    @pl.when(e == 1)
    def _():
        for out, place, pick_ref, source in to.values():
            out[place] = contract(pick_ref[source], out[place], 0, 0).astype(bf16)


def run_mixture(picks, hidden, weights):
    width, inner = weights.shape[1:]
    groups = len(picks)

    def once(shape):
        return pl.BlockSpec(shape, lambda e: (0, 0, 0), pipeline_mode=pl.Buffered(1))

    shapes = [(SIDE, picks[0].shape[2], width)] * SIDE
    return pl.pallas_call(
        functools.partial(mixture_kernel, groups),
        grid=(2,),
        out_shape=[jax.ShapeDtypeStruct(shape, bf16) for shape in shapes],
        in_specs=[once(pick.shape) for pick in picks]
        + [pl.BlockSpec((1,) + hid.shape[1:], lambda e: (e, 0, 0)) for hid in hidden]
        + [pl.BlockSpec((1, width, inner), lambda e: (3 * e + 2, 0, 0))],
        out_specs=[once(shape) for shape in shapes],
        scratch_shapes=[pltpu.VMEM((inner, width), bf16)],
        compiler_params=pltpu.CompilerParams(vmem_limit_bytes=40 * 1024 * 1024),
        cost_estimate=pl.CostEstimate(flops=1 << 32, bytes_accessed=1 << 20, transcendentals=0),
    )(*picks, *hidden, weights)


def weight_grad_kernel(half_ref, *refs):
    groups = (len(refs) - 2) // 5
    x_refs, c_refs, gate_refs, up_refs, hid_refs = (
        refs[i * groups : (i + 1) * groups] for i in range(5)
    )
    outs = refs[5 * groups :]
    width = x_refs[0].shape[2]
    inner = gate_refs[0].shape[2]
    rows = width // 2
    down_rows = inner // HOLDERS
    chunks = width // inner
    for out_ref, half in zip(outs, (1 - half_ref[0], half_ref[0])):
        cols = pl.ds(pl.multiple_of(half * rows, LANES), rows)
        down_cols = pl.ds(pl.multiple_of(half * (inner // 2), LANES), inner // 2)
        gate = jnp.zeros((rows, inner), f32)
        up = jnp.zeros((rows, inner), f32)
        down = jnp.zeros((inner // 2, width), f32)
        for i in range(groups):
            x = x_refs[i][0, :, cols]
            gate += contract(x, gate_refs[i][0], 0, 0)
            up += contract(x, up_refs[i][0], 0, 0)
        out_ref[0] = gate.astype(bf16)
        out_ref[1] = up.astype(bf16)
        for i in range(groups):
            down += contract(hid_refs[i][0, :, down_cols], c_refs[i][0], 0, 0)
        for holder in range(HOLDERS // 2):
            for chunk in range(chunks):
                at = (holder * chunks + chunk) * down_rows
                out_ref[2, at : at + down_rows, :] = down[
                    holder * down_rows : (holder + 1) * down_rows,
                    chunk * inner : (chunk + 1) * inner,
                ].astype(bf16)


def run_weight_grads(core, saved):
    x, c, gate, up, hid = zip(*saved)
    width = x[0].shape[2]
    inner = gate[0].shape[2]
    operands = (*x, *c, *gate, *up, *hid)
    out = jax.ShapeDtypeStruct((6, width // 2, inner), bf16)
    out_spec = pl.BlockSpec((3, width // 2, inner), lambda e: (e, 0, 0))
    return pl.pallas_call(
        weight_grad_kernel,
        grid=(2,),
        out_shape=(out, out),
        in_specs=[pl.BlockSpec(memory_space=pltpu.SMEM)]
        + [pl.BlockSpec((1,) + v.shape[1:], lambda e: (e, 0, 0)) for v in operands],
        out_specs=(out_spec, out_spec),
        compiler_params=pltpu.CompilerParams(vmem_limit_bytes=52 * 1024 * 1024),
        cost_estimate=pl.CostEstimate(
            flops=1 << 28, bytes_accessed=1 << 20, transcendentals=0
        ),
    )(core, *operands)


def local(
    tokens,
    segments,
    routes,
    norm1_gain,
    w_query,
    w_key,
    w_value,
    w_out,
    norm2_gain,
    w_router,
    w_gate,
    w_up,
    w_down,
    cotangent,
):
    tok_rows, width = tokens.shape
    seq_len = segments.shape[1]
    query_width = w_query.shape[1]
    kv_width = w_key.shape[1]
    joined_width = query_width + 2 * kv_width
    local_experts = w_gate.shape[0]
    experts = w_router.shape[1]
    owners = lax.axis_size("expert")
    planes = lax.axis_size("tensor")
    owner = lax.axis_index("expert")
    first_expert = owner * local_experts
    key_seg = segments[0]
    hidden_width = w_gate.shape[2]

    token_f32 = tokens.astype(f32)
    inverse_one = rms_inverse(token_f32)
    normed_low = (token_f32 * inverse_one * norm1_gain).astype(bf16)
    joined_weights = jnp.concatenate([w_query, w_key, w_value], axis=1)
    core = lax.axis_index("dp")

    def half_of(rows):
        count = rows.shape[0] // 2
        return lax.dynamic_slice_in_dim(rows, core * count, count, 0)

    def both_halves(half):
        other = swap_cores(half)
        first, second = jnp.where(core == 0, half, other), jnp.where(core == 0, other, half)
        return jnp.concatenate([first, second], axis=1).reshape(-1, half.shape[2])

    gathered = lax.all_gather(
        by_rows(jnp.concatenate([normed_low, half_of(w_out)], axis=0)), "tensor", axis=0
    )

    expert_ids = jnp.arange(experts, dtype=jnp.int32)
    onehot = (routes[:, :, None] == expert_ids[None, None, :]).astype(f32)
    member = jnp.sum(onehot, axis=1)
    lower = (jnp.arange(tok_rows)[:, None] <= jnp.arange(tok_rows)[None, :]).astype(bf16)
    rank = jnp.einsum("te,tu->eu", member.astype(bf16), lower, preferred_element_type=f32)
    rank = jnp.where(member.T > 0, rank - 1.0, -1.0).astype(bf16)
    extra = jnp.pad(rank, ((0, tok_rows - experts), (0, LANES - tok_rows)))
    cot_payload = jnp.concatenate([cotangent, extra], axis=1)

    chunks = width // hidden_width
    down_rows = w_down.shape[1]
    part_rows = w_gate.shape[1]
    down_parts = w_down.reshape(local_experts, down_rows, chunks, hidden_width)
    down_parts = down_parts.transpose(0, 2, 1, 3).reshape(local_experts, part_rows, hidden_width)
    weights = jnp.stack([w_gate, w_up, down_parts], axis=1)
    weights = weights.reshape(3 * local_experts, part_rows, hidden_width)
    tables = rope_tables(seq_len, query_width // HEAD_DIM + 1)
    marks = segment_marks(key_seg)
    cot_parts = gather_second(gather_first(cot_payload))
    gathered, weights, joined_weights, col, row, *cot_parts = together(
        gathered, weights, joined_weights, *marks, *cot_parts
    )
    marks = col, row
    weights_all = lax.all_gather(weights, ("dp", "tensor"), axis=1, tiled=True)
    context, context_blocks, qkv = run_attention(gathered, joined_weights, marks, tables)
    context_blocks, joined_half = together(context_blocks, half_of(by_rows(joined_weights.T)))
    half_joined = lax.all_gather(joined_half, "tensor", axis=0)
    context_home = lax.all_to_all(context_blocks, "tensor", split_axis=0, concat_axis=0)
    w_out_all = both_halves(gathered[:, tok_rows:])
    context_home, w_out_all = together(context_home, w_out_all)
    context_home = context_home.reshape(planes * query_width, tok_rows)
    mid = token_f32 + contract(context_home, w_out_all, 0, 0)
    inverse_two = rms_inverse(mid)
    normed_two = (mid * inverse_two * norm2_gain).astype(bf16)
    logits = dot32(normed_two, w_router)
    logits = jnp.where(member > 0, logits, masked_score)
    chosen_exp = jnp.where(
        member > 0, jnp.exp(logits - jnp.max(logits, axis=1, keepdims=True)), 0.0
    )
    gates = chosen_exp / jnp.sum(chosen_exp, axis=1, keepdims=True)
    gate_high, gate_low = split_two(gates)
    payload = jnp.concatenate(
        [normed_two, gate_high, gate_low, jnp.zeros((tok_rows, LANES - 2 * experts), bf16)],
        axis=1,
    )
    line = gather_first(payload)
    before, behind = (cross(line, 1, step) for step in STEPS[1:3])

    first_expert = first_expert.astype(jnp.int32).reshape(1)
    def compute(rows, cots):
        return run_experts(first_expert, rows, cots, weights_all)

    own = compute([line], cot_parts[:1])
    line, before, behind, *own_saved = together(line, before, behind, *own[1])
    far = cross(line, 1, STEPS[3])
    near = compute([before, behind], cot_parts[1:3])
    far, *near_saved = together(far, *near[1])
    last = compute([far], cot_parts[3:])
    done = [(*own[0], *near[0], *last[0]), (own_saved, near_saved, last[1])]
    back_line = scatter_first(done[0])
    *back_line, given, kept, half_joined = together(
        *back_line, *run_weight_grads(core.astype(jnp.int32).reshape(1), done[1]), half_joined
    )
    kept = (kept.astype(f32) + swap_cores(given).astype(f32)).astype(bf16)
    back_home, kept = scatter_second(back_line, kept)

    cot_f32 = cotangent.astype(f32)
    grad_tail = back_home[:, width:]
    gate_grad = grad_tail[:, :experts] + grad_tail[:, experts : 2 * experts]
    chosen_grad = gates * (gate_grad - jnp.sum(gates * gate_grad, axis=1, keepdims=True))
    logit_grad = chosen_grad.astype(bf16)
    normed_two_grad = back_home[:, :width] + jnp.einsum(
        "te,de->td", logit_grad, w_router, preferred_element_type=f32
    )
    mid_part, norm2_part = rms_backward(mid, inverse_two, norm2_gain, normed_two_grad)
    mid_grad = cot_f32 + mid_part
    attention_low = by_rows(mid_grad.astype(bf16))
    context_grad = by_rows(contract(w_out_all, attention_low, 1, 1).astype(bf16))
    context_grad, logit_grad, kept, half_joined = together(
        context_grad, logit_grad, kept, half_joined
    )
    weight_sum = lax.psum_scatter(kept, "tensor", scatter_dimension=1, tiled=True)
    mix_parts = run_mixture(
        [own[2], near[2], last[2]], [own_saved[4], near_saved[4], last[1][4]], weights_all
    )
    mix_line = scatter_first(mix_parts)
    sharers = lax.axis_size("dp") * owners
    columns = joined_width + query_width

    def to_sharers(parts):
        arrived = lax.all_to_all(parts, ("dp", "expert"), split_axis=0, concat_axis=0)
        return jnp.sum(arrived.astype(f32), axis=0)

    router_part = contract(logit_grad, normed_two, 0, 0)
    shared = jnp.concatenate([router_part, norm2_part[None]]).astype(bf16)
    shared_size = shared.size
    extra = -(-shared_size // (columns * sharers))
    shared = jnp.pad(shared.reshape(-1), (0, extra * columns * sharers - shared_size))
    context_grad = lax.all_to_all(
        context_grad.reshape(planes, query_width, tok_rows), "tensor", split_axis=0, concat_axis=0
    )
    context_grad, shared = together(context_grad, shared)
    shared = to_sharers(shared.reshape(sharers, extra, columns))
    joined_grad, joined_blocks = run_attention_back(qkv, context_grad, marks, tables)
    joined_blocks, shared = together(joined_blocks, shared)
    joined_home = lax.all_to_all(joined_blocks, "tensor", split_axis=0, concat_axis=0)
    joined_all = both_halves(half_joined)
    attention_all = lax.all_gather(attention_low, "tensor", axis=0, tiled=True)
    normed_all = gathered[:, :tok_rows].reshape(seq_len, width)
    joined_part = contract(normed_all, joined_grad, 0, 0)
    out_part = contract(attention_all, context, 0, 0)
    norm1_part = jnp.sum(joined_part * joined_weights.astype(f32), axis=1) / norm1_gain
    ringed = ring_sum(jnp.concatenate([shared, norm1_part.reshape(-1, columns)], axis=0))

    block = width // sharers
    sides = jnp.concatenate([joined_part.astype(bf16), out_part.astype(bf16)], axis=1)
    sides, joined_home, *mix_line = together(sides, joined_home, *mix_line)
    output = (mid + scatter_second(mix_line)[0]).astype(bf16)
    total = to_sharers(sides.reshape(sharers, block, columns))
    total = jnp.concatenate([total, ringed], axis=0).astype(bf16)
    total = jnp.pad(total, ((0, -total.shape[0] % 8), (0, 0)))
    spread = lax.all_to_all(
        jnp.broadcast_to(total[None], (sharers,) + total.shape),
        ("dp", "expert"),
        split_axis=0,
        concat_axis=0,
    )
    normed_one_grad = contract(joined_home.reshape(-1, tok_rows), joined_all, 0, 0)
    spread, weight_sum = together(spread, weight_sum)
    sides = spread[:, :block].reshape(width, columns).astype(f32)
    shared = spread[:, block : block + extra].astype(f32).reshape(-1)
    shared = shared[:shared_size].reshape(experts + 1, width)
    norm1_rows = width // columns
    norm1_sum = spread[:, block + extra : block + extra + norm1_rows].astype(f32)
    norm1_sum = jnp.sum(norm1_sum, axis=0).reshape(width)
    joined_sum = sides[:, :joined_width]
    out_sum = sides[:, joined_width:].T
    weight_sum = weight_sum.reshape(local_experts, 3, part_rows, hidden_width)
    w_gate_grad = weight_sum[:, 0].astype(f32)
    w_up_grad = weight_sum[:, 1].astype(f32)
    w_down_grad = weight_sum[:, 2].reshape(local_experts, chunks, down_rows, hidden_width)
    w_down_grad = w_down_grad.transpose(0, 2, 1, 3).reshape(local_experts, down_rows, width)
    w_down_grad = w_down_grad.astype(f32)
    input_part, _ = rms_backward(token_f32, inverse_one, norm1_gain, normed_one_grad)
    input_grad = mid_grad + input_part
    return (
        output,
        input_grad,
        norm1_sum,
        joined_sum[:, :query_width],
        joined_sum[:, query_width : query_width + kv_width],
        joined_sum[:, query_width + kv_width :],
        out_sum,
        shared[experts],
        shared[:experts].T,
        w_gate_grad,
        w_up_grad,
        w_down_grad,
    )


def solution(mesh):
    rows = P(("dp", "expert", "tensor"), None)
    columns = P(None, "tensor")
    experts = P("expert", ("dp", "tensor"), None)
    return jax.shard_map(
        local,
        mesh=mesh,
        in_specs=(
            rows,
            P(("dp", "expert"), None),
            rows,
            P(),
            columns,
            columns,
            columns,
            P("tensor", None),
            P(),
            P(),
            experts,
            experts,
            experts,
            rows,
        ),
        out_specs=(
            rows,
            rows,
            P(),
            columns,
            columns,
            columns,
            P("tensor", None),
            P(),
            P(),
            experts,
            experts,
            experts,
        ),
        check_vma=False,
    )
```

```python
import functools

import jax
import jax.numpy as jnp
import numpy as np
from jax import lax
from jax.experimental import pallas as pl
from jax.experimental.layout import Layout, with_layout_constraint
from jax.experimental.pallas import tpu as pltpu
from jax.sharding import PartitionSpec as P

HEAD_DIM = 64
HALF = HEAD_DIM // 2
TOP = 8
CAP = 64
EXPERTS = 32
HOLDERS = 16
LANES = 128

epsilon_norm = 1e-06
rope_theta = 10000.0
masked_score = -1e30
QUERY_ROWS = 512
SCALE = HEAD_DIM ** (-0.5)
f32 = jnp.float32
bf16 = jnp.bfloat16


def rms_inverse(values):
    return lax.rsqrt(jnp.mean(values * values, axis=-1, keepdims=True) + epsilon_norm)


def rms_backward(values, inverse, norm_gain, grad_out):
    scaled = grad_out * norm_gain
    grad_in = inverse * scaled - values * (inverse * inverse * inverse) * jnp.mean(
        scaled * values, axis=-1, keepdims=True
    )
    return (grad_in, grad_out * values * inverse)


def dot32(left, right):
    return jnp.dot(left, right, preferred_element_type=f32)


def split_two(values):
    high = values.astype(bf16)
    return high, (values - high.astype(f32)).astype(bf16)


SIDE = 4
STEPS = (0, 1, -1, 2)


def by_rows(values):
    return with_layout_constraint(values, Layout(major_to_minor=tuple(range(values.ndim))))


def cross(values, stage, step):
    pairs = []
    plane = SIDE * SIDE
    for core in range(2):
        for x in range(SIDE):
            for y in range(SIDE):
                if core == stage:
                    to = x * SIDE + (y + step) % SIDE
                else:
                    to = (x + step) % SIDE * SIDE + y
                pairs.append((core * plane + x * SIDE + y, core * plane + to))
    return lax.ppermute(values, ("dp", "expert"), pairs)


def gather_first(values):
    values = by_rows(values)
    line = jnp.stack([values] + [cross(values, 0, step) for step in STEPS[1:]])
    return by_rows(line)


def gather_second(line):
    return [line] + [cross(line, 1, step) for step in STEPS[1:]]


def scatter_first(parts):
    arrived = [parts[0]] + [
        by_rows(cross(part, 1, -step)) for part, step in zip(parts[1:], STEPS[1:])
    ]
    return [
        by_rows(sum(part[place].astype(f32) for part in arrived).astype(bf16))
        for place in range(SIDE)
    ]


def scatter_second(line, *beside):
    arrived = [cross(part, 0, -step) for part, step in zip(line[1:], STEPS[1:])]
    arrived[0], *beside = together(arrived[0], *beside)
    return by_rows(sum(part.astype(f32) for part in (line[0], *arrived))), *beside


def ring_sum(values):
    size = lax.axis_size("tensor")
    step = 1
    while step < size:
        pairs = [(i, i ^ step) for i in range(size)]
        values = values + lax.ppermute(values, "tensor", pairs)
        step *= 2
    return values


def together(*values):
    return lax.optimization_barrier(values)


def swap_cores(values):
    return lax.ppermute(values, "dp", [(0, 1), (1, 0)])


def contract(left, right, left_dim, right_dim):
    return lax.dot_general(
        left, right, (((left_dim,), (right_dim,)), ((), ())), preferred_element_type=f32
    )


def allowed(rows, first, wide, col_ref, row_ref):
    query = first + lax.broadcasted_iota(jnp.int32, (rows, wide), 0)
    key = lax.broadcasted_iota(jnp.int32, (rows, wide), 1)
    return (key <= query) & (col_ref[first : first + rows, :] == row_ref[:, :wide])


def probabilities(query, key, mask):
    scores = jnp.where(mask, contract(query, key, 1, 1), masked_score)
    weights = jnp.exp(scores - jnp.max(scores, axis=1, keepdims=True))
    return weights * (1.0 / jnp.sum(weights, axis=1, keepdims=True))


def turn(values, cosine, low, high):
    size = values.shape[1]
    return (
        values * cosine
        + pltpu.roll(values, size - HALF, 1) * low
        + pltpu.roll(values, HALF, 1) * high
    )


def attention_kernel(
    x_ref, w_ref, col_ref, row_ref, cos_ref, low_ref, high_ref, out_ref, turned_ref, qkv_ref, rest_ref
):
    seq_len = out_ref.shape[0]
    tokens = turned_ref.shape[2]
    rest_ref[...] = x_ref[:, tokens:, :]
    heads = out_ref.shape[1] // HEAD_DIM
    last = (heads + 1) * HEAD_DIM
    step = QUERY_ROWS
    for first in range(0, seq_len, step):
        at = slice(first, first + step)
        wide = first + step
        blocks = range(first // tokens, wide // tokens)
        rows = jnp.concatenate([x_ref[block, :tokens, :] for block in blocks], axis=0)
        joined = contract(rows, w_ref[...], 1, 1)
        turned_part = turn(joined[:, :last], cos_ref[at, :], low_ref[at, :], high_ref[at, :])
        qkv_ref[at, :last] = turned_part.astype(bf16)
        qkv_ref[at, last:] = joined[:, last:].astype(bf16)
        mask = allowed(step, first, wide, col_ref, row_ref)
        key = qkv_ref[:wide, heads * HEAD_DIM : last]
        value = qkv_ref[:wide, last:]
        for head in range(heads):
            place = slice(head * HEAD_DIM, (head + 1) * HEAD_DIM)
            query = qkv_ref[at, place] * SCALE
            probs = probabilities(query, key, mask).astype(bf16)
            context = jnp.dot(probs, value, preferred_element_type=f32)
            out_ref[at, place] = context.astype(bf16)
            for block in range(step // tokens):
                turned_ref[first // tokens + block, place, :] = context[
                    block * tokens : (block + 1) * tokens
                ].T.astype(bf16)


def attention_back_kernel(
    qkv_ref, grad_ref, col_ref, row_ref, cos_ref, low_ref, high_ref, out_ref, turned_ref, key_sum, value_sum
):
    seq_len = qkv_ref.shape[0]
    heads = grad_ref.shape[1] // HEAD_DIM
    tokens = grad_ref.shape[2]
    last = (heads + 1) * HEAD_DIM
    step = QUERY_ROWS
    for first in reversed(range(0, seq_len, step)):
        at = slice(first, first + step)
        wide = first + step
        mask = allowed(step, first, wide, col_ref, row_ref)
        key = qkv_ref[:wide, heads * HEAD_DIM : last]
        value = qkv_ref[:wide, last:]
        key_grad = jnp.zeros((wide, HEAD_DIM), f32)
        value_grad = jnp.zeros((wide, HEAD_DIM), f32)
        query_grads = []
        for head in range(heads):
            place = slice(head * HEAD_DIM, (head + 1) * HEAD_DIM)
            query = qkv_ref[at, place] * SCALE
            grad = [
                grad_ref[first // tokens + block, place, :].astype(f32).T.astype(bf16)
                for block in range(step // tokens)
            ]
            grad = jnp.concatenate(grad, axis=0)
            probs = probabilities(query, key, mask)
            probs_grad = contract(grad, value, 1, 1)
            row_dot = jnp.sum(probs * probs_grad, axis=1, keepdims=True)
            score_grad = (probs * (probs_grad - row_dot)).astype(bf16)
            query_grads.append(jnp.dot(score_grad, key, preferred_element_type=f32) * SCALE)
            key_grad += contract(score_grad, query, 0, 0)
            value_grad += contract(probs.astype(bf16), grad, 0, 0)
        if wide == seq_len:
            key_sum[...] = key_grad
            value_sum[...] = value_grad
        else:
            key_sum[:wide, :] += key_grad
            value_sum[:wide, :] += value_grad
        both = jnp.concatenate(query_grads + [key_sum[at, :]], axis=1)
        both = turn(both, cos_ref[at, :], -low_ref[at, :], -high_ref[at, :])
        out_ref[at, :last] = both.astype(bf16)
        out_ref[at, last:] = value_sum[at, :].astype(bf16)
        for block in range(step // tokens):
            part = slice(block * tokens, (block + 1) * tokens)
            to = first // tokens + block
            turned_ref[to, :last, :] = both[part].T.astype(bf16)
            turned_ref[to, last:, :] = value_sum[first : first + step, :][part].T.astype(bf16)


def run_attention(gathered, joined_rows, marks, tables):
    planes = gathered.shape[0]
    seq_len = marks[0].shape[0]
    joined_width = joined_rows.shape[0]
    query_width = joined_width - 2 * HEAD_DIM
    vmem = pl.BlockSpec(memory_space=pltpu.VMEM)
    return pl.pallas_call(
        attention_kernel,
        out_shape=(
            jax.ShapeDtypeStruct((seq_len, query_width), bf16),
            jax.ShapeDtypeStruct((planes, query_width, seq_len // planes), bf16),
            jax.ShapeDtypeStruct((seq_len, joined_width), bf16),
            jax.ShapeDtypeStruct(
                (planes, gathered.shape[1] - seq_len // planes, gathered.shape[2]), bf16
            ),
        ),
        in_specs=[vmem] * 7,
        out_specs=(vmem,) * 4,
        compiler_params=pltpu.CompilerParams(vmem_limit_bytes=48 * 1024 * 1024),
        cost_estimate=pl.CostEstimate(
            flops=4 << 30, bytes_accessed=8 << 20, transcendentals=0
        ),
    )(gathered, joined_rows, *marks, *tables)


def run_attention_back(qkv, context_grad, marks, tables):
    seq_len, joined_width = qkv.shape
    planes = context_grad.shape[0]
    vmem = pl.BlockSpec(memory_space=pltpu.VMEM)
    return pl.pallas_call(
        attention_back_kernel,
        out_shape=(
            jax.ShapeDtypeStruct((seq_len, joined_width), bf16),
            jax.ShapeDtypeStruct((planes, joined_width, seq_len // planes), bf16),
        ),
        in_specs=[vmem] * 7,
        out_specs=(vmem, vmem),
        scratch_shapes=[pltpu.VMEM((seq_len, HEAD_DIM), f32)] * 2,
        compiler_params=pltpu.CompilerParams(vmem_limit_bytes=48 * 1024 * 1024),
        cost_estimate=pl.CostEstimate(
            flops=8 << 30, bytes_accessed=4 << 20, transcendentals=0
        ),
    )(qkv, context_grad, *marks, *tables)


def rope_tables(seq_len, repeats):
    frequency = np.float32(rope_theta) ** (np.arange(HALF, dtype=np.float32) * np.float32(-2.0 / HEAD_DIM))
    angles = np.arange(seq_len, dtype=np.float32)[:, None] * frequency.astype(np.float32)[None, :]
    cosine, sine = np.cos(angles), np.sin(angles)
    nothing = np.zeros_like(sine)

    def heads(first, second):
        return jnp.asarray(np.tile(np.concatenate([first, second], axis=1), (1, repeats)))

    return heads(cosine, cosine), heads(-sine, nothing), heads(nothing, sine)


def segment_marks(key_seg):
    marks = jnp.where(key_seg == 0, -1 - jnp.arange(key_seg.shape[0], dtype=jnp.int32), key_seg)
    return marks[:, None], marks[None, :]


def expert_kernel(groups, first_ref, *refs):
    rows_refs, cots_refs = refs[:groups], refs[groups : 2 * groups]
    w_ref = refs[2 * groups]
    back_outs = refs[2 * groups + 1 : 3 * groups + 1]
    x_ref, c_ref, gate_ref, up_ref, hid_ref, pick_ref = refs[3 * groups + 1 : 3 * groups + 7]
    down_ref, next_x, next_c, gates_ref = refs[3 * groups + 7 :]
    sources, tokens, _ = rows_refs[0].shape
    width = x_ref.shape[2]
    e = pl.program_id(0)
    expert = first_ref[0] + e
    at = pl.ds(pl.multiple_of(e * CAP, CAP), CAP)
    every = [(group, source) for group in range(groups) for source in range(sources)]

    @pl.when(e == 0)
    def _():
        pair = 2 * CAP
        lane = lax.broadcasted_iota(jnp.int32, (pair, LANES), 1)
        expert_of = expert + lax.broadcasted_iota(jnp.int32, (pair, LANES), 0) // CAP
        own = (lane == expert_of) | (lane == expert_of + EXPERTS)
        row_id = lax.broadcasted_iota(jnp.int32, (EXPERTS, tokens), 0)
        slot = lax.broadcasted_iota(jnp.int32, (pair, tokens), 0)
        place_of = jnp.where(slot < CAP, slot, slot - CAP).astype(f32)
        for order, (group, source) in enumerate(every):
            table = cots_refs[group][source, :EXPERTS, width:].astype(f32)
            ranks = [
                jnp.sum(jnp.where(row_id == expert + i, table, 0.0), axis=0, keepdims=True)
                for i in range(2)
            ]
            pick = (jnp.where(slot < CAP, ranks[0], ranks[1]) == place_of).astype(bf16)
            pick_ref[order] = pick
            rows = jnp.dot(pick, rows_refs[group][source], preferred_element_type=f32)
            cots = jnp.dot(pick, cots_refs[group][source, :, :width], preferred_element_type=f32)
            gate = jnp.sum(jnp.where(own, rows[:, width:], 0.0), axis=1, keepdims=True)
            gate = jnp.broadcast_to(gate, (pair, LANES))
            place = slice(order * CAP, (order + 1) * CAP)
            x_ref[0, place] = rows[:CAP, :width].astype(bf16)
            c_ref[0, place] = cots[:CAP].astype(bf16)
            gates_ref[0, place] = gate[:CAP]
            next_x[place] = rows[CAP:, :width].astype(bf16)
            next_c[place] = cots[CAP:].astype(bf16)
            gates_ref[1, place] = gate[CAP:]

    @pl.when(e == 1)
    def _():
        x_ref[0] = next_x[...]
        c_ref[0] = next_c[...]

    gate = gates_ref[e][:, :1]
    join_chunks(down_ref, w_ref.at[2], HOLDERS)
    x = x_ref[0]
    gate_pre = jnp.dot(x, w_ref[0], preferred_element_type=f32)
    up_pre = jnp.dot(x, w_ref[1], preferred_element_type=f32)
    back = contract(c_ref[0], down_ref[...], 1, 1)
    sig = 1.0 / (1.0 + jnp.exp(-gate_pre))
    silu = gate_pre * sig
    hidden = (silu * up_pre).astype(bf16)
    gate_grad = jnp.sum(back * hidden.astype(f32), axis=1, keepdims=True)
    grad = gate * back
    gate_pre_grad = (grad * up_pre * (sig + silu * (1.0 - sig))).astype(bf16)
    up_pre_grad = (grad * silu).astype(bf16)
    gate_ref[0] = gate_pre_grad
    up_ref[0] = up_pre_grad
    hid_ref[0] = (gate * hidden.astype(f32)).astype(bf16)
    row_grad = contract(gate_pre_grad, w_ref[0], 1, 1) + contract(up_pre_grad, w_ref[1], 1, 1)
    high = gate_grad.astype(bf16).astype(f32)
    lane = lax.broadcasted_iota(jnp.int32, (len(every) * CAP, LANES), 1)
    tail = jnp.where(lane == expert, high, 0.0)
    tail += jnp.where(lane == expert + EXPERTS, gate_grad - high, 0.0)
    for order, (group, source) in enumerate(every):
        place = slice(order * CAP, (order + 1) * CAP)
        back_outs[group][source, at, :width] = row_grad[place].astype(bf16)
        back_outs[group][source, at, width:] = tail[place].astype(bf16)

    @pl.when(e == 1)
    def _():
        for order, (group, source) in enumerate(every):
            back_outs[group][source] = contract(
                pick_ref[order], back_outs[group][source], 0, 0
            ).astype(bf16)


def join_chunks(to_ref, from_ref, holders):
    inner = from_ref.shape[1]
    rows = inner // HOLDERS
    chunks = to_ref.shape[1] // inner
    for holder in range(holders):
        for chunk in range(chunks):
            start = (holder * chunks + chunk) * rows
            to_ref[
                holder * rows : (holder + 1) * rows, chunk * inner : (chunk + 1) * inner
            ] = from_ref[start : start + rows, :]


def run_experts(first, rows, cots, weights):
    groups = len(rows)
    sources, tokens, padded = rows[0].shape
    width = padded - LANES
    inner = weights.shape[2]
    slots = groups * sources * CAP

    def once(columns):
        return pl.BlockSpec(
            (sources, tokens, columns), lambda e: (0, 0, 0), pipeline_mode=pl.Buffered(1)
        )

    def by_expert(*shape):
        return pl.BlockSpec(shape, lambda e: (e, 0, 0))

    acts = jax.ShapeDtypeStruct((2, slots, inner), bf16)
    wide = jax.ShapeDtypeStruct((2, slots, width), bf16)
    outs = pl.pallas_call(
        functools.partial(expert_kernel, groups),
        grid=(2,),
        out_shape=(
            *[jax.ShapeDtypeStruct((sources, tokens, padded), bf16)] * groups,
            wide,
            wide,
            acts,
            acts,
            acts,
            jax.ShapeDtypeStruct((groups * sources, 2 * CAP, tokens), bf16),
        ),
        in_specs=[pl.BlockSpec(memory_space=pltpu.SMEM)]
        + [once(padded)] * (2 * groups)
        + [by_expert(3, width, inner)],
        out_specs=(
            *[once(padded)] * groups,
            by_expert(1, slots, width),
            by_expert(1, slots, width),
            by_expert(1, slots, inner),
            by_expert(1, slots, inner),
            by_expert(1, slots, inner),
            pl.BlockSpec((groups * sources, 2 * CAP, tokens), lambda e: (0, 0, 0)),
        ),
        scratch_shapes=[
            pltpu.VMEM((inner, width), bf16),
            pltpu.VMEM((slots, width), bf16),
            pltpu.VMEM((slots, width), bf16),
            pltpu.VMEM((2, slots, LANES), f32),
        ],
        compiler_params=pltpu.CompilerParams(vmem_limit_bytes=56 * 1024 * 1024),
        cost_estimate=pl.CostEstimate(
            flops=2 * 2 * 6 * slots * width * inner, bytes_accessed=24 << 20, transcendentals=0
        ),
    )(first, *rows, *cots, weights)
    return outs[:groups], outs[groups:-1], outs[-1]


def mixture_kernel(groups, *refs):
    pick_refs, hid_refs = refs[:groups], refs[groups : 2 * groups]
    w_ref = refs[2 * groups]
    outs, down_ref = refs[2 * groups + 1 : -1], refs[-1]
    e = pl.program_id(0)
    at = pl.ds(pl.multiple_of(e * CAP, CAP), CAP)
    join_chunks(down_ref, w_ref.at[0], HOLDERS)
    sources = [
        (pick_ref, hid_ref, source)
        for pick_ref, hid_ref in zip(pick_refs, hid_refs)
        for source in range(pick_ref.shape[0])
    ]
    to = {}
    for order, (pick_ref, hid_ref, source) in enumerate(sources):
        to[order] = (outs[order // SIDE], order % SIDE, pick_ref, source)
    order = 0
    for pick_ref, hid_ref in zip(pick_refs, hid_refs):
        mixed = jnp.dot(hid_ref[0], down_ref[...], preferred_element_type=f32).astype(bf16)
        for source in range(pick_ref.shape[0]):
            out, place, _, _ = to[order]
            out[place, at] = mixed[source * CAP : (source + 1) * CAP]
            order += 1

    @pl.when(e == 1)
    def _():
        for out, place, pick_ref, source in to.values():
            out[place] = contract(pick_ref[source], out[place], 0, 0).astype(bf16)


def run_mixture(picks, hidden, weights):
    width, inner = weights.shape[1:]
    groups = len(picks)

    def once(shape):
        return pl.BlockSpec(shape, lambda e: (0, 0, 0), pipeline_mode=pl.Buffered(1))

    shapes = [(SIDE, picks[0].shape[2], width)] * SIDE
    return pl.pallas_call(
        functools.partial(mixture_kernel, groups),
        grid=(2,),
        out_shape=[jax.ShapeDtypeStruct(shape, bf16) for shape in shapes],
        in_specs=[once(pick.shape) for pick in picks]
        + [pl.BlockSpec((1,) + hid.shape[1:], lambda e: (e, 0, 0)) for hid in hidden]
        + [pl.BlockSpec((1, width, inner), lambda e: (3 * e + 2, 0, 0))],
        out_specs=[once(shape) for shape in shapes],
        scratch_shapes=[pltpu.VMEM((inner, width), bf16)],
        compiler_params=pltpu.CompilerParams(vmem_limit_bytes=40 * 1024 * 1024),
        cost_estimate=pl.CostEstimate(flops=1 << 32, bytes_accessed=1 << 20, transcendentals=0),
    )(*picks, *hidden, weights)


def weight_grad_kernel(groups, half_ref, *refs):
    x_refs, c_refs, gate_refs, up_refs, hid_refs = (
        refs[i * groups : (i + 1) * groups] for i in range(5)
    )
    *onto, out_ref = refs[5 * groups :]
    width = x_refs[0].shape[2]
    inner = gate_refs[0].shape[2]
    half = half_ref[0]
    rows = width // 2
    down_rows = inner // HOLDERS
    chunks = width // inner
    cols = pl.ds(pl.multiple_of(half * rows, LANES), rows)
    down_cols = pl.ds(pl.multiple_of(half * (inner // 2), LANES), inner // 2)
    gate = jnp.zeros((rows, inner), f32)
    up = jnp.zeros((rows, inner), f32)
    down = jnp.zeros((inner // 2, width), f32)
    for i in range(groups):
        x = x_refs[i][0, :, cols]
        gate += contract(x, gate_refs[i][0], 0, 0)
        up += contract(x, up_refs[i][0], 0, 0)

    def put(place, at, values):
        if onto:
            values = values + onto[0][place, at, :].astype(f32)
        out_ref[place, at, :] = values.astype(bf16)

    put(0, slice(0, rows), gate)
    put(1, slice(0, rows), up)
    for i in range(groups):
        down += contract(hid_refs[i][0, :, down_cols], c_refs[i][0], 0, 0)
    for holder in range(HOLDERS // 2):
        for chunk in range(chunks):
            start = (holder * chunks + chunk) * down_rows
            put(
                2,
                slice(start, start + down_rows),
                down[
                    holder * down_rows : (holder + 1) * down_rows,
                    chunk * inner : (chunk + 1) * inner,
                ],
            )


def run_weight_grads(half, saved, *onto):
    x, c, gate, up, hid = zip(*saved)
    width = x[0].shape[2]
    inner = gate[0].shape[2]
    operands = (*x, *c, *gate, *up, *hid)
    out_spec = pl.BlockSpec((3, width // 2, inner), lambda e: (e, 0, 0))
    return pl.pallas_call(
        functools.partial(weight_grad_kernel, len(saved)),
        grid=(2,),
        out_shape=jax.ShapeDtypeStruct((6, width // 2, inner), bf16),
        in_specs=[pl.BlockSpec(memory_space=pltpu.SMEM)]
        + [pl.BlockSpec((1,) + v.shape[1:], lambda e: (e, 0, 0)) for v in operands]
        + [out_spec] * len(onto),
        out_specs=out_spec,
        compiler_params=pltpu.CompilerParams(vmem_limit_bytes=52 * 1024 * 1024),
        cost_estimate=pl.CostEstimate(flops=1 << 28, bytes_accessed=1 << 20, transcendentals=0),
    )(half, *operands, *onto)


def sides_kernel(
    x_ref, grad_ref, w_ref, all_ref, context_ref, normed_ref, logit_ref, norm_ref, gain_ref, out_ref, shared_ref
):
    planes, tokens = x_ref.shape[0], normed_ref.shape[0]
    joined_width = grad_ref.shape[1]
    experts = logit_ref.shape[1]
    step = x_ref.shape[2] // 2
    for first in range(0, x_ref.shape[2], step):
        at = slice(first, first + step)
        rows = jnp.concatenate([x_ref[plane, :tokens, at] for plane in range(planes)], axis=0)
        joined = contract(grad_ref[...], rows, 0, 0)
        out_ref[:joined_width, at] = joined.astype(bf16)
        out_ref[joined_width:, at] = contract(context_ref[...], all_ref[:, at], 0, 0).astype(bf16)
        norm1 = jnp.sum(joined * w_ref[:, at].astype(f32), axis=0, keepdims=True) / gain_ref[:, at]
        norm2 = jnp.sum(norm_ref[:, at], axis=0, keepdims=True)
        shared_ref[:experts, at] = contract(logit_ref[...], normed_ref[:, at], 0, 0).astype(bf16)
        shared_ref[experts : experts + 1, at] = norm2.astype(bf16)
        shared_ref[experts + 1 : experts + 2, at] = norm1.astype(bf16)


def run_sides(gathered, joined_grad, joined_rows, attention_all, context, normed_two, logits, norm_terms, gain):
    vmem = pl.BlockSpec(memory_space=pltpu.VMEM)
    width = gathered.shape[2]
    rows = joined_grad.shape[1] + context.shape[1]
    return pl.pallas_call(
        sides_kernel,
        out_shape=(
            jax.ShapeDtypeStruct((rows, width), bf16),
            jax.ShapeDtypeStruct((logits.shape[1] + 2, width), bf16),
        ),
        in_specs=[vmem] * 9,
        out_specs=(vmem, vmem),
        compiler_params=pltpu.CompilerParams(vmem_limit_bytes=40 * 1024 * 1024),
        cost_estimate=pl.CostEstimate(flops=1 << 31, bytes_accessed=12 << 20, transcendentals=0),
    )(gathered, joined_grad, joined_rows, attention_all, context, normed_two, logits, norm_terms, gain)


def local(
    tokens,
    segments,
    routes,
    norm1_gain,
    w_query,
    w_key,
    w_value,
    w_out,
    norm2_gain,
    w_router,
    w_gate,
    w_up,
    w_down,
    cotangent,
):
    tok_rows, width = tokens.shape
    seq_len = segments.shape[1]
    query_width = w_query.shape[1]
    kv_width = w_key.shape[1]
    joined_width = query_width + 2 * kv_width
    local_experts = w_gate.shape[0]
    experts = w_router.shape[1]
    owners = lax.axis_size("expert")
    planes = lax.axis_size("tensor")
    owner = lax.axis_index("expert")
    first_expert = owner * local_experts
    key_seg = segments[0]
    hidden_width = w_gate.shape[2]

    token_f32 = tokens.astype(f32)
    inverse_one = rms_inverse(token_f32)
    normed_low = (token_f32 * inverse_one * norm1_gain).astype(bf16)
    joined_rows = by_rows(jnp.concatenate([w_query.T, w_key.T, w_value.T], axis=0))
    core = lax.axis_index("dp")

    def half_of(rows):
        count = rows.shape[0] // 2
        return lax.dynamic_slice_in_dim(rows, core * count, count, 0)

    def both_halves(half):
        other = swap_cores(half)
        first, second = jnp.where(core == 0, half, other), jnp.where(core == 0, other, half)
        return jnp.concatenate([first, second], axis=1).reshape(-1, half.shape[2])

    gathered = lax.all_gather(
        by_rows(jnp.concatenate([normed_low, half_of(w_out)], axis=0)), "tensor", axis=0
    )

    expert_ids = jnp.arange(experts, dtype=jnp.int32)
    onehot = (routes[:, :, None] == expert_ids[None, None, :]).astype(f32)
    member = jnp.sum(onehot, axis=1)
    lower = (jnp.arange(tok_rows)[:, None] <= jnp.arange(tok_rows)[None, :]).astype(bf16)
    rank = jnp.einsum("te,tu->eu", member.astype(bf16), lower, preferred_element_type=f32)
    rank = jnp.where(member.T > 0, rank - 1.0, -1.0).astype(bf16)
    extra = jnp.pad(rank, ((0, tok_rows - experts), (0, LANES - tok_rows)))
    cot_payload = jnp.concatenate([cotangent, extra], axis=1)

    chunks = width // hidden_width
    down_rows = w_down.shape[1]
    part_rows = w_gate.shape[1]
    down_parts = w_down.reshape(local_experts, down_rows, chunks, hidden_width)
    down_parts = down_parts.transpose(0, 2, 1, 3).reshape(local_experts, part_rows, hidden_width)
    weights = jnp.stack([w_gate, w_up, down_parts], axis=1)
    weights = weights.reshape(3 * local_experts, part_rows, hidden_width)
    tables = rope_tables(seq_len, query_width // HEAD_DIM + 1)
    marks = segment_marks(key_seg)
    cot_parts = gather_second(gather_first(cot_payload))
    joined_half = by_rows(half_of(joined_rows))
    gathered, weights, joined_rows, joined_half, col, row, *cot_parts = together(
        gathered, weights, joined_rows, joined_half, *marks, *cot_parts
    )
    marks = col, row
    weights_all = lax.all_gather(weights, ("dp", "tensor"), axis=1, tiled=True)
    context, context_blocks, qkv, half_out = run_attention(
        gathered, joined_rows, marks, tables
    )
    context_home = lax.all_to_all(context_blocks, "tensor", split_axis=0, concat_axis=0)
    w_out_all = both_halves(half_out)
    context_home, w_out_all, joined_half = together(context_home, w_out_all, joined_half)
    half_joined = lax.all_gather(joined_half, "tensor", axis=0)
    context_home = context_home.reshape(planes * query_width, tok_rows)
    mid = token_f32 + contract(context_home, w_out_all, 0, 0)
    inverse_two = rms_inverse(mid)
    normed_two = (mid * inverse_two * norm2_gain).astype(bf16)
    logits = dot32(normed_two, w_router)
    logits = jnp.where(member > 0, logits, masked_score)
    chosen_exp = jnp.where(
        member > 0, jnp.exp(logits - jnp.max(logits, axis=1, keepdims=True)), 0.0
    )
    gates = chosen_exp / jnp.sum(chosen_exp, axis=1, keepdims=True)
    gate_high, gate_low = split_two(gates)
    payload = jnp.concatenate(
        [normed_two, gate_high, gate_low, jnp.zeros((tok_rows, LANES - 2 * experts), bf16)],
        axis=1,
    )
    line = gather_first(payload)
    before, behind = (cross(line, 1, step) for step in STEPS[1:3])

    first_expert = first_expert.astype(jnp.int32).reshape(1)
    def compute(rows, cots):
        return run_experts(first_expert, rows, cots, weights_all)

    own = compute([line], cot_parts[:1])
    line, before, behind, *own_saved = together(line, before, behind, *own[1])
    far = cross(line, 1, STEPS[3])
    near = compute([before, behind], cot_parts[1:3])
    far, *near_saved = together(far, *near[1])
    last = compute([far], cot_parts[3:])
    done = [(*own[0], *near[0], *last[0]), (own_saved, near_saved, last[1])]
    back_line = scatter_first(done[0])
    mix_parts = run_mixture(
        [own[2], near[2], last[2]], [own_saved[4], near_saved[4], last[1][4]], weights_all
    )
    given = run_weight_grads((1 - core).astype(jnp.int32).reshape(1), done[1])
    n_line = len(back_line)
    *both, given, half_joined = together(*back_line, *mix_parts, given, half_joined)
    back_line, mix_parts = both[:n_line], both[n_line:]
    back_home, received = scatter_second(back_line, swap_cores(given))

    cot_f32 = cotangent.astype(f32)
    grad_tail = back_home[:, width:]
    gate_grad = grad_tail[:, :experts] + grad_tail[:, experts : 2 * experts]
    chosen_grad = gates * (gate_grad - jnp.sum(gates * gate_grad, axis=1, keepdims=True))
    logit_grad = chosen_grad.astype(bf16)
    normed_two_grad = back_home[:, :width] + jnp.einsum(
        "te,de->td", logit_grad, w_router, preferred_element_type=f32
    )
    mid_part, norm2_terms = rms_backward(mid, inverse_two, norm2_gain, normed_two_grad)
    mid_grad = cot_f32 + mid_part
    attention_low = by_rows(mid_grad.astype(bf16))
    norm2_terms = by_rows(norm2_terms)
    context_grad = by_rows(contract(w_out_all, attention_low, 1, 1).astype(bf16))
    received, *mix_parts, context_grad, logit_grad = together(
        received, *mix_parts, context_grad, logit_grad
    )
    mix_line = scatter_first(mix_parts)
    kept = run_weight_grads(core.astype(jnp.int32).reshape(1), done[1], received)
    context_grad = lax.all_to_all(
        context_grad.reshape(planes, query_width, tok_rows), "tensor", split_axis=0, concat_axis=0
    )
    context_grad, kept = together(context_grad, kept)
    weight_sum = lax.psum_scatter(kept, "tensor", scatter_dimension=1, tiled=True)
    joined_grad, joined_blocks = run_attention_back(qkv, context_grad, marks, tables)
    joined_home = lax.all_to_all(joined_blocks, "tensor", split_axis=0, concat_axis=0)
    attention_all = lax.all_gather(attention_low, "tensor", axis=0, tiled=True)
    sides, shared = run_sides(
        gathered,
        joined_grad,
        joined_rows,
        attention_all,
        context,
        normed_two,
        logit_grad,
        norm2_terms,
        norm1_gain[None],
    )

    sharers = lax.axis_size("dp") * owners
    share = sides.shape[0] // sharers
    shared_shape = shared.shape
    shared_rows = shared.size // LANES
    shared = jnp.pad(shared.reshape(shared_rows, LANES), ((0, sharers * share - shared_rows), (0, 0)))
    blocks = jnp.concatenate(
        [sides.reshape(sharers, share, width), shared.reshape(sharers, share, LANES)], axis=2
    )
    blocks, joined_home, *mix_line = together(blocks, joined_home, *mix_line)
    output = (mid + scatter_second(mix_line)[0]).astype(bf16)
    arrived = lax.all_to_all(blocks, ("dp", "expert"), split_axis=0, concat_axis=0)
    total = jnp.sum(arrived.astype(f32), axis=0).astype(bf16)
    spread = lax.all_to_all(
        jnp.broadcast_to(total[None], arrived.shape), ("dp", "expert"), split_axis=0, concat_axis=0
    )
    joined_all = both_halves(half_joined)
    normed_one_grad = contract(joined_home.reshape(-1, tok_rows), joined_all, 0, 0)
    spread, weight_sum = together(by_rows(spread), weight_sum)
    shared = ring_sum(by_rows(spread[:, :, width:].reshape(-1, LANES)[:shared_rows]))
    shared = shared.astype(f32).reshape(shared_shape)
    sides = spread[:, :, :width].reshape(-1, width).astype(f32)
    joined_sum = sides[:joined_width].T
    out_sum = sides[joined_width:]
    weight_sum = weight_sum.reshape(local_experts, 3, part_rows, hidden_width)
    w_gate_grad = weight_sum[:, 0].astype(f32)
    w_up_grad = weight_sum[:, 1].astype(f32)
    w_down_grad = weight_sum[:, 2].reshape(local_experts, chunks, down_rows, hidden_width)
    w_down_grad = w_down_grad.transpose(0, 2, 1, 3).reshape(local_experts, down_rows, width)
    w_down_grad = w_down_grad.astype(f32)
    input_part, _ = rms_backward(token_f32, inverse_one, norm1_gain, normed_one_grad)
    input_grad = mid_grad + input_part
    return (
        output,
        input_grad,
        shared[experts + 1],
        joined_sum[:, :query_width],
        joined_sum[:, query_width : query_width + kv_width],
        joined_sum[:, query_width + kv_width :],
        out_sum,
        shared[experts],
        shared[:experts].T,
        w_gate_grad,
        w_up_grad,
        w_down_grad,
    )


def solution(mesh):
    rows = P(("dp", "expert", "tensor"), None)
    columns = P(None, "tensor")
    experts = P("expert", ("dp", "tensor"), None)
    return jax.shard_map(
        local,
        mesh=mesh,
        in_specs=(
            rows,
            P(("dp", "expert"), None),
            rows,
            P(),
            columns,
            columns,
            columns,
            P("tensor", None),
            P(),
            P(),
            experts,
            experts,
            experts,
            rows,
        ),
        out_specs=(
            rows,
            rows,
            P(),
            columns,
            columns,
            columns,
            P("tensor", None),
            P(),
            P(),
            experts,
            experts,
            experts,
        ),
        check_vma=False,
    )
```

```python
import functools

import jax
import jax.numpy as jnp
import numpy as np
from jax import lax
from jax.experimental import pallas as pl
from jax.experimental.layout import Layout, with_layout_constraint
from jax.experimental.pallas import tpu as pltpu
from jax.sharding import PartitionSpec as P

HEAD_DIM = 64
HALF = HEAD_DIM // 2
TOP = 8
CAP = 64
EXPERTS = 32
HOLDERS = 16
LANES = 128

epsilon_norm = 1e-06
rope_theta = 10000.0
masked_score = -1e30
QUERY_ROWS = 512
SCALE = HEAD_DIM ** (-0.5)
f32 = jnp.float32
bf16 = jnp.bfloat16


def rms_inverse(values):
    return lax.rsqrt(jnp.mean(values * values, axis=-1, keepdims=True) + epsilon_norm)


def rms_backward(values, inverse, norm_gain, grad_out):
    scaled = grad_out * norm_gain
    grad_in = inverse * scaled - values * (inverse * inverse * inverse) * jnp.mean(
        scaled * values, axis=-1, keepdims=True
    )
    return (grad_in, grad_out * values * inverse)


def dot32(left, right):
    return jnp.dot(left, right, preferred_element_type=f32)


def split_two(values):
    high = values.astype(bf16)
    return high, (values - high.astype(f32)).astype(bf16)


SIDE = 4
STEPS = (0, 1, -1, 2)


def by_rows(values):
    return with_layout_constraint(values, Layout(major_to_minor=tuple(range(values.ndim))))


def cross(values, stage, step):
    pairs = []
    plane = SIDE * SIDE
    for core in range(2):
        for x in range(SIDE):
            for y in range(SIDE):
                if core == stage:
                    to = x * SIDE + (y + step) % SIDE
                else:
                    to = (x + step) % SIDE * SIDE + y
                pairs.append((core * plane + x * SIDE + y, core * plane + to))
    return lax.ppermute(values, ("dp", "expert"), pairs)


def gather_first(values):
    values = by_rows(values)
    line = jnp.stack([values] + [cross(values, 0, step) for step in STEPS[1:]])
    return by_rows(line)


def gather_second(line):
    return [line] + [cross(line, 1, step) for step in STEPS[1:]]


def scatter_first(parts):
    return [parts[0]] + [
        by_rows(cross(part, 1, -step)) for part, step in zip(parts[1:], STEPS[1:])
    ]


def sum_first(arrived):
    return [
        by_rows(sum(part[place].astype(f32) for part in arrived).astype(bf16))
        for place in range(SIDE)
    ]


def scatter_second(line, *beside):
    arrived = [cross(part, 0, -step) for part, step in zip(line[1:], STEPS[1:])]
    arrived[0], *beside = together(arrived[0], *beside)
    return by_rows(sum(part.astype(f32) for part in (line[0], *arrived))), *beside


def ring_sum(values):
    size = lax.axis_size("tensor")
    step = 1
    while step < size:
        pairs = [(i, i ^ step) for i in range(size)]
        values = values + lax.ppermute(values, "tensor", pairs)
        step *= 2
    return values


def together(*values):
    return lax.optimization_barrier(values)


def swap_cores(values):
    return lax.ppermute(values, "dp", [(0, 1), (1, 0)])


def contract(left, right, left_dim, right_dim):
    return lax.dot_general(
        left, right, (((left_dim,), (right_dim,)), ((), ())), preferred_element_type=f32
    )


def allowed(rows, first, wide, col_ref, row_ref):
    query = first + lax.broadcasted_iota(jnp.int32, (rows, wide), 0)
    key = lax.broadcasted_iota(jnp.int32, (rows, wide), 1)
    return (key <= query) & (col_ref[first : first + rows, :] == row_ref[:, :wide])


def probabilities(query, key, mask):
    scores = jnp.where(mask, contract(query, key, 1, 1), masked_score)
    weights = jnp.exp(scores - jnp.max(scores, axis=1, keepdims=True))
    return weights * (1.0 / jnp.sum(weights, axis=1, keepdims=True))


def turn(values, cosine, low, high):
    size = values.shape[1]
    return (
        values * cosine
        + pltpu.roll(values, size - HALF, 1) * low
        + pltpu.roll(values, HALF, 1) * high
    )


def attention_kernel(
    x_ref, w_ref, col_ref, row_ref, cos_ref, low_ref, high_ref, out_ref, turned_ref, qkv_ref, rest_ref
):
    seq_len = out_ref.shape[0]
    tokens = turned_ref.shape[2]
    rest_ref[...] = x_ref[:, tokens:, :]
    heads = out_ref.shape[1] // HEAD_DIM
    last = (heads + 1) * HEAD_DIM
    step = QUERY_ROWS
    for first in range(0, seq_len, step):
        at = slice(first, first + step)
        wide = first + step
        blocks = range(first // tokens, wide // tokens)
        rows = jnp.concatenate([x_ref[block, :tokens, :] for block in blocks], axis=0)
        joined = contract(rows, w_ref[...], 1, 1)
        turned_part = turn(joined[:, :last], cos_ref[at, :], low_ref[at, :], high_ref[at, :])
        qkv_ref[at, :last] = turned_part.astype(bf16)
        qkv_ref[at, last:] = joined[:, last:].astype(bf16)
        mask = allowed(step, first, wide, col_ref, row_ref)
        key = qkv_ref[:wide, heads * HEAD_DIM : last]
        value = qkv_ref[:wide, last:]
        for head in range(heads):
            place = slice(head * HEAD_DIM, (head + 1) * HEAD_DIM)
            query = qkv_ref[at, place] * SCALE
            probs = probabilities(query, key, mask).astype(bf16)
            context = jnp.dot(probs, value, preferred_element_type=f32)
            out_ref[at, place] = context.astype(bf16)
            for block in range(step // tokens):
                turned_ref[first // tokens + block, place, :] = context[
                    block * tokens : (block + 1) * tokens
                ].T.astype(bf16)


def attention_back_kernel(
    qkv_ref, grad_ref, col_ref, row_ref, cos_ref, low_ref, high_ref, out_ref, turned_ref, key_sum, value_sum
):
    seq_len = qkv_ref.shape[0]
    heads = grad_ref.shape[1] // HEAD_DIM
    tokens = grad_ref.shape[2]
    last = (heads + 1) * HEAD_DIM
    step = QUERY_ROWS
    for first in reversed(range(0, seq_len, step)):
        at = slice(first, first + step)
        wide = first + step
        mask = allowed(step, first, wide, col_ref, row_ref)
        key = qkv_ref[:wide, heads * HEAD_DIM : last]
        value = qkv_ref[:wide, last:]
        key_grad = jnp.zeros((wide, HEAD_DIM), f32)
        value_grad = jnp.zeros((wide, HEAD_DIM), f32)
        query_grads = []
        for head in range(heads):
            place = slice(head * HEAD_DIM, (head + 1) * HEAD_DIM)
            query = qkv_ref[at, place] * SCALE
            grad = [
                grad_ref[first // tokens + block, place, :].astype(f32).T.astype(bf16)
                for block in range(step // tokens)
            ]
            grad = jnp.concatenate(grad, axis=0)
            probs = probabilities(query, key, mask)
            probs_grad = contract(grad, value, 1, 1)
            row_dot = jnp.sum(probs * probs_grad, axis=1, keepdims=True)
            score_grad = (probs * (probs_grad - row_dot)).astype(bf16)
            query_grads.append(jnp.dot(score_grad, key, preferred_element_type=f32) * SCALE)
            key_grad += contract(score_grad, query, 0, 0)
            value_grad += contract(probs.astype(bf16), grad, 0, 0)
        if wide == seq_len:
            key_sum[...] = key_grad
            value_sum[...] = value_grad
        else:
            key_sum[:wide, :] += key_grad
            value_sum[:wide, :] += value_grad
        both = jnp.concatenate(query_grads + [key_sum[at, :]], axis=1)
        both = turn(both, cos_ref[at, :], -low_ref[at, :], -high_ref[at, :])
        out_ref[at, :last] = both.astype(bf16)
        out_ref[at, last:] = value_sum[at, :].astype(bf16)
        for block in range(step // tokens):
            part = slice(block * tokens, (block + 1) * tokens)
            to = first // tokens + block
            turned_ref[to, :last, :] = both[part].T.astype(bf16)
            turned_ref[to, last:, :] = value_sum[first : first + step, :][part].T.astype(bf16)


def run_attention(gathered, joined_rows, marks, tables):
    planes = gathered.shape[0]
    seq_len = marks[0].shape[0]
    joined_width = joined_rows.shape[0]
    query_width = joined_width - 2 * HEAD_DIM
    vmem = pl.BlockSpec(memory_space=pltpu.VMEM)
    return pl.pallas_call(
        attention_kernel,
        out_shape=(
            jax.ShapeDtypeStruct((seq_len, query_width), bf16),
            jax.ShapeDtypeStruct((planes, query_width, seq_len // planes), bf16),
            jax.ShapeDtypeStruct((seq_len, joined_width), bf16),
            jax.ShapeDtypeStruct(
                (planes, gathered.shape[1] - seq_len // planes, gathered.shape[2]), bf16
            ),
        ),
        in_specs=[vmem] * 7,
        out_specs=(vmem,) * 4,
        compiler_params=pltpu.CompilerParams(vmem_limit_bytes=48 * 1024 * 1024),
        cost_estimate=pl.CostEstimate(
            flops=4 << 30, bytes_accessed=8 << 20, transcendentals=0
        ),
    )(gathered, joined_rows, *marks, *tables)


def run_attention_back(qkv, context_grad, marks, tables):
    seq_len, joined_width = qkv.shape
    planes = context_grad.shape[0]
    vmem = pl.BlockSpec(memory_space=pltpu.VMEM)
    return pl.pallas_call(
        attention_back_kernel,
        out_shape=(
            jax.ShapeDtypeStruct((seq_len, joined_width), bf16),
            jax.ShapeDtypeStruct((planes, joined_width, seq_len // planes), bf16),
        ),
        in_specs=[vmem] * 7,
        out_specs=(vmem, vmem),
        scratch_shapes=[pltpu.VMEM((seq_len, HEAD_DIM), f32)] * 2,
        compiler_params=pltpu.CompilerParams(vmem_limit_bytes=48 * 1024 * 1024),
        cost_estimate=pl.CostEstimate(
            flops=1 << 28, bytes_accessed=1 << 20, transcendentals=0
        ),
    )(qkv, context_grad, *marks, *tables)


def rope_tables(seq_len, repeats):
    frequency = np.float32(rope_theta) ** (np.arange(HALF, dtype=np.float32) * np.float32(-2.0 / HEAD_DIM))
    angles = np.arange(seq_len, dtype=np.float32)[:, None] * frequency.astype(np.float32)[None, :]
    cosine, sine = np.cos(angles), np.sin(angles)
    nothing = np.zeros_like(sine)

    def heads(first, second):
        return jnp.asarray(np.tile(np.concatenate([first, second], axis=1), (1, repeats)))

    return heads(cosine, cosine), heads(-sine, nothing), heads(nothing, sine)


def segment_marks(key_seg):
    marks = jnp.where(key_seg == 0, -1 - jnp.arange(key_seg.shape[0], dtype=jnp.int32), key_seg)
    return marks[:, None], marks[None, :]


def expert_kernel(groups, first_ref, *refs):
    rows_refs, cots_refs = refs[:groups], refs[groups : 2 * groups]
    w_ref = refs[2 * groups]
    back_outs = refs[2 * groups + 1 : 3 * groups + 1]
    x_ref, c_ref, gate_ref, up_ref, hid_ref, pick_ref = refs[3 * groups + 1 : 3 * groups + 7]
    down_ref, next_x, next_c, gates_ref = refs[3 * groups + 7 :]
    sources, tokens, _ = rows_refs[0].shape
    width = x_ref.shape[2]
    e = pl.program_id(0)
    expert = first_ref[0] + e
    at = pl.ds(pl.multiple_of(e * CAP, CAP), CAP)
    every = [(group, source) for group in range(groups) for source in range(sources)]

    @pl.when(e == 0)
    def _():
        pair = 2 * CAP
        lane = lax.broadcasted_iota(jnp.int32, (pair, LANES), 1)
        expert_of = expert + lax.broadcasted_iota(jnp.int32, (pair, LANES), 0) // CAP
        own = (lane == expert_of) | (lane == expert_of + EXPERTS)
        row_id = lax.broadcasted_iota(jnp.int32, (EXPERTS, tokens), 0)
        slot = lax.broadcasted_iota(jnp.int32, (pair, tokens), 0)
        place_of = jnp.where(slot < CAP, slot, slot - CAP).astype(f32)
        for order, (group, source) in enumerate(every):
            table = cots_refs[group][source, :EXPERTS, width:].astype(f32)
            ranks = [
                jnp.sum(jnp.where(row_id == expert + i, table, 0.0), axis=0, keepdims=True)
                for i in range(2)
            ]
            pick = (jnp.where(slot < CAP, ranks[0], ranks[1]) == place_of).astype(bf16)
            pick_ref[order] = pick
            rows = jnp.dot(pick, rows_refs[group][source], preferred_element_type=f32)
            cots = jnp.dot(pick, cots_refs[group][source, :, :width], preferred_element_type=f32)
            gate = jnp.sum(jnp.where(own, rows[:, width:], 0.0), axis=1, keepdims=True)
            gate = jnp.broadcast_to(gate, (pair, LANES))
            place = slice(order * CAP, (order + 1) * CAP)
            x_ref[0, place] = rows[:CAP, :width].astype(bf16)
            c_ref[0, place] = cots[:CAP].astype(bf16)
            gates_ref[0, place] = gate[:CAP]
            next_x[place] = rows[CAP:, :width].astype(bf16)
            next_c[place] = cots[CAP:].astype(bf16)
            gates_ref[1, place] = gate[CAP:]

    @pl.when(e == 1)
    def _():
        x_ref[0] = next_x[...]
        c_ref[0] = next_c[...]

    gate = gates_ref[e][:, :1]
    join_chunks(down_ref, w_ref.at[2], HOLDERS)
    x = x_ref[0]
    gate_pre = jnp.dot(x, w_ref[0], preferred_element_type=f32)
    up_pre = jnp.dot(x, w_ref[1], preferred_element_type=f32)
    back = contract(c_ref[0], down_ref[...], 1, 1)
    sig = 1.0 / (1.0 + jnp.exp(-gate_pre))
    silu = gate_pre * sig
    hidden = (silu * up_pre).astype(bf16)
    gate_grad = jnp.sum(back * hidden.astype(f32), axis=1, keepdims=True)
    grad = gate * back
    gate_pre_grad = (grad * up_pre * (sig + silu * (1.0 - sig))).astype(bf16)
    up_pre_grad = (grad * silu).astype(bf16)
    gate_ref[0] = gate_pre_grad
    up_ref[0] = up_pre_grad
    hid_ref[0] = (gate * hidden.astype(f32)).astype(bf16)
    row_grad = contract(gate_pre_grad, w_ref[0], 1, 1) + contract(up_pre_grad, w_ref[1], 1, 1)
    high = gate_grad.astype(bf16).astype(f32)
    lane = lax.broadcasted_iota(jnp.int32, (len(every) * CAP, LANES), 1)
    tail = jnp.where(lane == expert, high, 0.0)
    tail += jnp.where(lane == expert + EXPERTS, gate_grad - high, 0.0)
    for order, (group, source) in enumerate(every):
        place = slice(order * CAP, (order + 1) * CAP)
        back_outs[group][source, at, :width] = row_grad[place].astype(bf16)
        back_outs[group][source, at, width:] = tail[place].astype(bf16)

    @pl.when(e == 1)
    def _():
        for order, (group, source) in enumerate(every):
            back_outs[group][source] = contract(
                pick_ref[order], back_outs[group][source], 0, 0
            ).astype(bf16)


def join_chunks(to_ref, from_ref, holders):
    inner = from_ref.shape[1]
    rows = inner // HOLDERS
    chunks = to_ref.shape[1] // inner
    for holder in range(holders):
        for chunk in range(chunks):
            start = (holder * chunks + chunk) * rows
            to_ref[
                holder * rows : (holder + 1) * rows, chunk * inner : (chunk + 1) * inner
            ] = from_ref[start : start + rows, :]


def run_experts(first, rows, cots, weights):
    groups = len(rows)
    sources, tokens, padded = rows[0].shape
    width = padded - LANES
    inner = weights.shape[2]
    slots = groups * sources * CAP

    def once(columns):
        return pl.BlockSpec(
            (sources, tokens, columns), lambda e: (0, 0, 0), pipeline_mode=pl.Buffered(1)
        )

    def by_expert(*shape):
        return pl.BlockSpec(shape, lambda e: (e, 0, 0))

    acts = jax.ShapeDtypeStruct((2, slots, inner), bf16)
    wide = jax.ShapeDtypeStruct((2, slots, width), bf16)
    outs = pl.pallas_call(
        functools.partial(expert_kernel, groups),
        grid=(2,),
        out_shape=(
            *[jax.ShapeDtypeStruct((sources, tokens, padded), bf16)] * groups,
            wide,
            wide,
            acts,
            acts,
            acts,
            jax.ShapeDtypeStruct((groups * sources, 2 * CAP, tokens), bf16),
        ),
        in_specs=[pl.BlockSpec(memory_space=pltpu.SMEM)]
        + [once(padded)] * (2 * groups)
        + [by_expert(3, width, inner)],
        out_specs=(
            *[once(padded)] * groups,
            by_expert(1, slots, width),
            by_expert(1, slots, width),
            by_expert(1, slots, inner),
            by_expert(1, slots, inner),
            by_expert(1, slots, inner),
            pl.BlockSpec((groups * sources, 2 * CAP, tokens), lambda e: (0, 0, 0)),
        ),
        scratch_shapes=[
            pltpu.VMEM((inner, width), bf16),
            pltpu.VMEM((slots, width), bf16),
            pltpu.VMEM((slots, width), bf16),
            pltpu.VMEM((2, slots, LANES), f32),
        ],
        compiler_params=pltpu.CompilerParams(vmem_limit_bytes=56 * 1024 * 1024),
        cost_estimate=pl.CostEstimate(
            flops=2 * 2 * 6 * slots * width * inner, bytes_accessed=24 << 20, transcendentals=0
        ),
    )(first, *rows, *cots, weights)
    return outs[:groups], outs[groups:-1], outs[-1]


def mixture_kernel(groups, *refs):
    pick_refs, hid_refs = refs[:groups], refs[groups : 2 * groups]
    w_ref = refs[2 * groups]
    outs, down_ref = refs[2 * groups + 1 : -1], refs[-1]
    e = pl.program_id(0)
    at = pl.ds(pl.multiple_of(e * CAP, CAP), CAP)
    join_chunks(down_ref, w_ref.at[0], HOLDERS)
    sources = [
        (pick_ref, hid_ref, source)
        for pick_ref, hid_ref in zip(pick_refs, hid_refs)
        for source in range(pick_ref.shape[0])
    ]
    to = {}
    for order, (pick_ref, hid_ref, source) in enumerate(sources):
        to[order] = (outs[order // SIDE], order % SIDE, pick_ref, source)
    order = 0
    for pick_ref, hid_ref in zip(pick_refs, hid_refs):
        mixed = jnp.dot(hid_ref[0], down_ref[...], preferred_element_type=f32).astype(bf16)
        for source in range(pick_ref.shape[0]):
            out, place, _, _ = to[order]
            out[place, at] = mixed[source * CAP : (source + 1) * CAP]
            order += 1

    @pl.when(e == 1)
    def _():
        for out, place, pick_ref, source in to.values():
            out[place] = contract(pick_ref[source], out[place], 0, 0).astype(bf16)


def run_mixture(picks, hidden, weights):
    width, inner = weights.shape[1:]
    groups = len(picks)

    def once(shape):
        return pl.BlockSpec(shape, lambda e: (0, 0, 0), pipeline_mode=pl.Buffered(1))

    shapes = [(SIDE, picks[0].shape[2], width)] * SIDE
    return pl.pallas_call(
        functools.partial(mixture_kernel, groups),
        grid=(2,),
        out_shape=[jax.ShapeDtypeStruct(shape, bf16) for shape in shapes],
        in_specs=[once(pick.shape) for pick in picks]
        + [pl.BlockSpec((1,) + hid.shape[1:], lambda e: (e, 0, 0)) for hid in hidden]
        + [pl.BlockSpec((1, width, inner), lambda e: (3 * e + 2, 0, 0))],
        out_specs=[once(shape) for shape in shapes],
        scratch_shapes=[pltpu.VMEM((inner, width), bf16)],
        compiler_params=pltpu.CompilerParams(vmem_limit_bytes=40 * 1024 * 1024),
        cost_estimate=pl.CostEstimate(flops=1 << 32, bytes_accessed=1 << 20, transcendentals=0),
    )(*picks, *hidden, weights)


def weight_grad_kernel(groups, half_ref, *refs):
    x_refs, c_refs, gate_refs, up_refs, hid_refs = (
        refs[i * groups : (i + 1) * groups] for i in range(5)
    )
    *onto, out_ref = refs[5 * groups :]
    width = x_refs[0].shape[2]
    inner = gate_refs[0].shape[2]
    half = half_ref[0]
    rows = width // 2
    down_rows = inner // HOLDERS
    chunks = width // inner
    cols = pl.ds(pl.multiple_of(half * rows, LANES), rows)
    down_cols = pl.ds(pl.multiple_of(half * (inner // 2), LANES), inner // 2)
    gate = jnp.zeros((rows, inner), f32)
    up = jnp.zeros((rows, inner), f32)
    down = jnp.zeros((inner // 2, width), f32)
    for i in range(groups):
        x = x_refs[i][0, :, cols]
        gate += contract(x, gate_refs[i][0], 0, 0)
        up += contract(x, up_refs[i][0], 0, 0)

    def put(place, at, values):
        if onto:
            values = values + onto[0][place, at, :].astype(f32)
        out_ref[place, at, :] = values.astype(bf16)

    put(0, slice(0, rows), gate)
    put(1, slice(0, rows), up)
    for i in range(groups):
        down += contract(hid_refs[i][0, :, down_cols], c_refs[i][0], 0, 0)
    for holder in range(HOLDERS // 2):
        for chunk in range(chunks):
            start = (holder * chunks + chunk) * down_rows
            put(
                2,
                slice(start, start + down_rows),
                down[
                    holder * down_rows : (holder + 1) * down_rows,
                    chunk * inner : (chunk + 1) * inner,
                ],
            )


def run_weight_grads(half, saved, *onto):
    x, c, gate, up, hid = zip(*saved)
    width = x[0].shape[2]
    inner = gate[0].shape[2]
    operands = (*x, *c, *gate, *up, *hid)
    out_spec = pl.BlockSpec((3, width // 2, inner), lambda e: (e, 0, 0))
    return pl.pallas_call(
        functools.partial(weight_grad_kernel, len(saved)),
        grid=(2,),
        out_shape=jax.ShapeDtypeStruct((6, width // 2, inner), bf16),
        in_specs=[pl.BlockSpec(memory_space=pltpu.SMEM)]
        + [pl.BlockSpec((1,) + v.shape[1:], lambda e: (e, 0, 0)) for v in operands]
        + [out_spec] * len(onto),
        out_specs=out_spec,
        compiler_params=pltpu.CompilerParams(vmem_limit_bytes=52 * 1024 * 1024),
        cost_estimate=pl.CostEstimate(flops=1 << 28, bytes_accessed=1 << 20, transcendentals=0),
    )(half, *operands, *onto)


def sides_kernel(
    x_ref, grad_ref, w_ref, all_ref, context_ref, normed_ref, logit_ref, norm_ref, gain_ref, out_ref, shared_ref
):
    planes, tokens = x_ref.shape[0], normed_ref.shape[0]
    joined_width = grad_ref.shape[1]
    experts = logit_ref.shape[1]
    step = x_ref.shape[2] // 2
    for first in range(0, x_ref.shape[2], step):
        at = slice(first, first + step)
        rows = jnp.concatenate([x_ref[plane, :tokens, at] for plane in range(planes)], axis=0)
        joined = contract(grad_ref[...], rows, 0, 0)
        out_ref[:joined_width, at] = joined.astype(bf16)
        out_ref[joined_width:, at] = contract(context_ref[...], all_ref[:, at], 0, 0).astype(bf16)
        norm1 = jnp.sum(joined * w_ref[:, at].astype(f32), axis=0, keepdims=True) / gain_ref[:, at]
        norm2 = jnp.sum(norm_ref[:, at], axis=0, keepdims=True)
        shared_ref[:experts, at] = contract(logit_ref[...], normed_ref[:, at], 0, 0).astype(bf16)
        shared_ref[experts : experts + 1, at] = norm2.astype(bf16)
        shared_ref[experts + 1 : experts + 2, at] = norm1.astype(bf16)


def run_sides(gathered, joined_grad, joined_rows, attention_all, context, normed_two, logits, norm_terms, gain):
    vmem = pl.BlockSpec(memory_space=pltpu.VMEM)
    width = gathered.shape[2]
    rows = joined_grad.shape[1] + context.shape[1]
    return pl.pallas_call(
        sides_kernel,
        out_shape=(
            jax.ShapeDtypeStruct((rows, width), bf16),
            jax.ShapeDtypeStruct((logits.shape[1] + 2, width), bf16),
        ),
        in_specs=[vmem] * 9,
        out_specs=(vmem, vmem),
        compiler_params=pltpu.CompilerParams(vmem_limit_bytes=40 * 1024 * 1024),
        cost_estimate=pl.CostEstimate(flops=1 << 31, bytes_accessed=12 << 20, transcendentals=0),
    )(gathered, joined_grad, joined_rows, attention_all, context, normed_two, logits, norm_terms, gain)


def local(
    tokens,
    segments,
    routes,
    norm1_gain,
    w_query,
    w_key,
    w_value,
    w_out,
    norm2_gain,
    w_router,
    w_gate,
    w_up,
    w_down,
    cotangent,
):
    tok_rows, width = tokens.shape
    seq_len = segments.shape[1]
    query_width = w_query.shape[1]
    kv_width = w_key.shape[1]
    joined_width = query_width + 2 * kv_width
    local_experts = w_gate.shape[0]
    experts = w_router.shape[1]
    owners = lax.axis_size("expert")
    planes = lax.axis_size("tensor")
    owner = lax.axis_index("expert")
    first_expert = owner * local_experts
    key_seg = segments[0]
    hidden_width = w_gate.shape[2]

    token_f32 = tokens.astype(f32)
    inverse_one = rms_inverse(token_f32)
    normed_low = (token_f32 * inverse_one * norm1_gain).astype(bf16)
    joined_rows = by_rows(jnp.concatenate([w_query.T, w_key.T, w_value.T], axis=0))
    core = lax.axis_index("dp")

    def half_of(rows):
        count = rows.shape[0] // 2
        return lax.dynamic_slice_in_dim(rows, core * count, count, 0)

    def both_halves(half):
        other = swap_cores(half)
        first, second = jnp.where(core == 0, half, other), jnp.where(core == 0, other, half)
        return jnp.concatenate([first, second], axis=1).reshape(-1, half.shape[2])

    gathered = lax.all_gather(
        by_rows(jnp.concatenate([normed_low, half_of(w_out)], axis=0)), "tensor", axis=0
    )

    expert_ids = jnp.arange(experts, dtype=jnp.int32)
    onehot = (routes[:, :, None] == expert_ids[None, None, :]).astype(f32)
    member = jnp.sum(onehot, axis=1)
    lower = (jnp.arange(tok_rows)[:, None] <= jnp.arange(tok_rows)[None, :]).astype(bf16)
    rank = jnp.einsum("te,tu->eu", member.astype(bf16), lower, preferred_element_type=f32)
    rank = jnp.where(member.T > 0, rank - 1.0, -1.0).astype(bf16)
    extra = jnp.pad(rank, ((0, tok_rows - experts), (0, LANES - tok_rows)))
    cot_payload = jnp.concatenate([cotangent, extra], axis=1)

    chunks = width // hidden_width
    down_rows = w_down.shape[1]
    part_rows = w_gate.shape[1]
    down_parts = w_down.reshape(local_experts, down_rows, chunks, hidden_width)
    down_parts = down_parts.transpose(0, 2, 1, 3).reshape(local_experts, part_rows, hidden_width)
    weights = jnp.stack([w_gate, w_up, down_parts], axis=1)
    weights = weights.reshape(3 * local_experts, part_rows, hidden_width)
    tables = rope_tables(seq_len, query_width // HEAD_DIM + 1)
    marks = segment_marks(key_seg)
    cot_parts = gather_second(gather_first(cot_payload))
    joined_half = by_rows(half_of(joined_rows))
    gathered, weights, joined_rows, joined_half, col, row, *cot_parts = together(
        gathered, weights, joined_rows, joined_half, *marks, *cot_parts
    )
    marks = col, row
    weights_all = lax.all_gather(weights, ("dp", "tensor"), axis=1, tiled=True)
    context, context_blocks, qkv, half_out = run_attention(
        gathered, joined_rows, marks, tables
    )
    context_home = lax.all_to_all(context_blocks, "tensor", split_axis=0, concat_axis=0)
    w_out_all = both_halves(half_out)
    context_home, w_out_all, joined_half = together(context_home, w_out_all, joined_half)
    half_joined = lax.all_gather(joined_half, "tensor", axis=0)
    context_home = context_home.reshape(planes * query_width, tok_rows)
    mid = token_f32 + contract(context_home, w_out_all, 0, 0)
    inverse_two = rms_inverse(mid)
    normed_two = (mid * inverse_two * norm2_gain).astype(bf16)
    logits = dot32(normed_two, w_router)
    logits = jnp.where(member > 0, logits, masked_score)
    chosen_exp = jnp.where(
        member > 0, jnp.exp(logits - jnp.max(logits, axis=1, keepdims=True)), 0.0
    )
    gates = chosen_exp / jnp.sum(chosen_exp, axis=1, keepdims=True)
    gate_high, gate_low = split_two(gates)
    payload = jnp.concatenate(
        [normed_two, gate_high, gate_low, jnp.zeros((tok_rows, LANES - 2 * experts), bf16)],
        axis=1,
    )
    line = gather_first(payload)
    before, behind = (cross(line, 1, step) for step in STEPS[1:3])

    first_expert = first_expert.astype(jnp.int32).reshape(1)
    def compute(rows, cots):
        return run_experts(first_expert, rows, cots, weights_all)

    own = compute([line], cot_parts[:1])
    line, before, behind, *own_saved = together(line, before, behind, *own[1])
    far = cross(line, 1, STEPS[3])
    near = compute([before, behind], cot_parts[1:3])
    far, *near_saved = together(far, *near[1])
    last = compute([far], cot_parts[3:])
    done = [(*own[0], *near[0], *last[0]), (own_saved, near_saved, last[1])]
    back_line = scatter_first(done[0])
    mix_parts = run_mixture(
        [own[2], near[2], last[2]], [own_saved[4], near_saved[4], last[1][4]], weights_all
    )
    given = run_weight_grads((1 - core).astype(jnp.int32).reshape(1), done[1])
    n_line = len(back_line)
    *both, given, half_joined = together(*back_line, *mix_parts, given, half_joined)
    back_line, mix_parts = sum_first(both[:n_line]), both[n_line:]
    back_home, received = scatter_second(back_line, swap_cores(given))

    cot_f32 = cotangent.astype(f32)
    grad_tail = back_home[:, width:]
    gate_grad = grad_tail[:, :experts] + grad_tail[:, experts : 2 * experts]
    chosen_grad = gates * (gate_grad - jnp.sum(gates * gate_grad, axis=1, keepdims=True))
    logit_grad = chosen_grad.astype(bf16)
    normed_two_grad = back_home[:, :width] + jnp.einsum(
        "te,de->td", logit_grad, w_router, preferred_element_type=f32
    )
    mid_part, norm2_terms = rms_backward(mid, inverse_two, norm2_gain, normed_two_grad)
    mid_grad = cot_f32 + mid_part
    attention_low = by_rows(mid_grad.astype(bf16))
    norm2_terms = by_rows(norm2_terms)
    context_grad = by_rows(contract(w_out_all, attention_low, 1, 1).astype(bf16))
    received, *mix_parts, context_grad, logit_grad = together(
        received, *mix_parts, context_grad, logit_grad
    )
    mix_arrived = scatter_first(mix_parts)
    kept = run_weight_grads(core.astype(jnp.int32).reshape(1), done[1], received)
    context_grad = lax.all_to_all(
        context_grad.reshape(planes, query_width, tok_rows), "tensor", split_axis=0, concat_axis=0
    )
    context_grad, kept = together(context_grad, kept)
    weight_sum = lax.psum_scatter(kept, "tensor", scatter_dimension=1, tiled=True)
    joined_grad, joined_blocks = run_attention_back(qkv, context_grad, marks, tables)
    joined_home = lax.all_to_all(joined_blocks, "tensor", split_axis=0, concat_axis=0)
    attention_all = lax.all_gather(attention_low, "tensor", axis=0, tiled=True)
    sides, shared = run_sides(
        gathered,
        joined_grad,
        joined_rows,
        attention_all,
        context,
        normed_two,
        logit_grad,
        norm2_terms,
        norm1_gain[None],
    )

    share = sides.shape[0] // (2 * owners)
    shared_shape = shared.shape
    shared_rows = shared.size // LANES
    shared = shared.reshape(shared_rows, LANES)
    shared = jnp.pad(shared, ((0, 2 * owners * share - shared_rows), (0, 0)))
    blocks = jnp.concatenate(
        [sides.reshape(2, owners, share, width), shared.reshape(2, owners, share, LANES)], axis=3
    )
    blocks, joined_home, *mix_arrived = together(blocks, joined_home, *mix_arrived)
    def of_core(which):
        return lax.dynamic_index_in_dim(blocks, which, 0, keepdims=False)

    part = of_core(core).astype(f32) + swap_cores(of_core(1 - core)).astype(f32)
    arrived = lax.all_to_all(part.astype(bf16), "expert", split_axis=0, concat_axis=0)
    arrived, joined_all, *mix_line = together(
        arrived, both_halves(half_joined), *sum_first(mix_arrived)
    )
    total = jnp.sum(arrived.astype(f32), axis=0)

    def to_owners(values):
        values = jnp.broadcast_to(values.astype(bf16)[None], (owners,) + values.shape)
        return lax.all_to_all(values, "expert", split_axis=0, concat_axis=0)

    def both_cores(own):
        other = swap_cores(own)
        first, second = jnp.where(core == 0, own, other), jnp.where(core == 0, other, own)
        return jnp.concatenate([first, second], axis=0).reshape(-1, own.shape[2])

    normed_one_grad = contract(joined_home.reshape(-1, tok_rows), joined_all, 0, 0)
    sides, shared, normed_one_grad, mixture = together(
        to_owners(total[:, :width]),
        ring_sum(total[:, width:]),
        normed_one_grad,
        scatter_second(mix_line)[0],
    )
    output = (mid + mixture).astype(bf16)
    shared = both_cores(to_owners(shared))[:shared_rows]
    shared = shared.astype(f32).reshape(shared_shape)
    sides, weight_sum = together(both_cores(sides), weight_sum)
    sides = sides.astype(f32)
    joined_sum = sides[:joined_width].T
    out_sum = sides[joined_width:]
    weight_sum = weight_sum.reshape(local_experts, 3, part_rows, hidden_width)
    w_gate_grad = weight_sum[:, 0].astype(f32)
    w_up_grad = weight_sum[:, 1].astype(f32)
    w_down_grad = weight_sum[:, 2].reshape(local_experts, chunks, down_rows, hidden_width)
    w_down_grad = w_down_grad.transpose(0, 2, 1, 3).reshape(local_experts, down_rows, width)
    w_down_grad = w_down_grad.astype(f32)
    input_part, _ = rms_backward(token_f32, inverse_one, norm1_gain, normed_one_grad)
    input_grad = mid_grad + input_part
    return (
        output,
        input_grad,
        shared[experts + 1],
        joined_sum[:, :query_width],
        joined_sum[:, query_width : query_width + kv_width],
        joined_sum[:, query_width + kv_width :],
        out_sum,
        shared[experts],
        shared[:experts].T,
        w_gate_grad,
        w_up_grad,
        w_down_grad,
    )


def solution(mesh):
    rows = P(("dp", "expert", "tensor"), None)
    columns = P(None, "tensor")
    experts = P("expert", ("dp", "tensor"), None)
    return jax.shard_map(
        local,
        mesh=mesh,
        in_specs=(
            rows,
            P(("dp", "expert"), None),
            rows,
            P(),
            columns,
            columns,
            columns,
            P("tensor", None),
            P(),
            P(),
            experts,
            experts,
            experts,
            rows,
        ),
        out_specs=(
            rows,
            rows,
            P(),
            columns,
            columns,
            columns,
            P("tensor", None),
            P(),
            P(),
            experts,
            experts,
            experts,
        ),
        check_vma=False,
    )
```

```python
import functools

import jax
import jax.numpy as jnp
import numpy as np
from jax import lax
from jax.experimental import pallas as pl
from jax.experimental.layout import Layout, with_layout_constraint
from jax.experimental.pallas import tpu as pltpu
from jax.sharding import PartitionSpec as P

HEAD_DIM = 64
HALF = HEAD_DIM // 2
TOP = 8
CAP = 64
EXPERTS = 32
HOLDERS = 16
LANES = 128

epsilon_norm = 1e-06
rope_theta = 10000.0
masked_score = -1e30
QUERY_ROWS = 512
SCALE = HEAD_DIM ** (-0.5)
f32 = jnp.float32
bf16 = jnp.bfloat16


def rms_inverse(values):
    return lax.rsqrt(jnp.mean(values * values, axis=-1, keepdims=True) + epsilon_norm)


def rms_backward(values, inverse, norm_gain, grad_out):
    scaled = grad_out * norm_gain
    grad_in = inverse * scaled - values * (inverse * inverse * inverse) * jnp.mean(
        scaled * values, axis=-1, keepdims=True
    )
    return (grad_in, grad_out * values * inverse)


def dot32(left, right):
    return jnp.dot(left, right, preferred_element_type=f32)


def split_two(values):
    high = values.astype(bf16)
    return high, (values - high.astype(f32)).astype(bf16)


SIDE = 4
STEPS = (0, 1, -1, 2)


def by_rows(values):
    return with_layout_constraint(values, Layout(major_to_minor=tuple(range(values.ndim))))


def cross(values, stage, step):
    pairs = []
    plane = SIDE * SIDE
    for core in range(2):
        for x in range(SIDE):
            for y in range(SIDE):
                if core == stage:
                    to = x * SIDE + (y + step) % SIDE
                else:
                    to = (x + step) % SIDE * SIDE + y
                pairs.append((core * plane + x * SIDE + y, core * plane + to))
    return lax.ppermute(values, ("dp", "expert"), pairs)


def gather_first(values):
    values = by_rows(values)
    line = jnp.stack([values] + [cross(values, 0, step) for step in STEPS[1:]])
    return by_rows(line)


def gather_second(line):
    return [line] + [cross(line, 1, step) for step in STEPS[1:]]


def owner_of(place, me):
    return jnp.asarray([0, 2, 3, 1])[(place - me) % SIDE]


def scatter_first(parts):
    return [parts[0]] + [
        by_rows(cross(part, 1, -step)) for part, step in zip(parts[1:], STEPS[1:])
    ]


def sum_first(arrived):
    return [
        by_rows(sum(part[place].astype(f32) for part in arrived).astype(bf16))
        for place in range(SIDE)
    ]


def scatter_second(line, *beside):
    arrived = [cross(part, 0, -step) for part, step in zip(line[1:], STEPS[1:])]
    arrived[0], *beside = together(arrived[0], *beside)
    return by_rows(sum(part.astype(f32) for part in (line[0], *arrived))), *beside


def ring_sum(values):
    size = lax.axis_size("tensor")
    step = 1
    while step < size:
        pairs = [(i, i ^ step) for i in range(size)]
        values = values + lax.ppermute(values, "tensor", pairs)
        step *= 2
    return values


def together(*values):
    return lax.optimization_barrier(values)


def swap_cores(values):
    return lax.ppermute(values, "dp", [(0, 1), (1, 0)])


def contract(left, right, left_dim, right_dim):
    return lax.dot_general(
        left, right, (((left_dim,), (right_dim,)), ((), ())), preferred_element_type=f32
    )


def allowed(rows, first, wide, col_ref, row_ref):
    query = first + lax.broadcasted_iota(jnp.int32, (rows, wide), 0)
    key = lax.broadcasted_iota(jnp.int32, (rows, wide), 1)
    return (key <= query) & (col_ref[first : first + rows, :] == row_ref[:, :wide])


def probabilities(query, key, mask):
    scores = jnp.where(mask, contract(query, key, 1, 1), masked_score)
    weights = jnp.exp(scores - jnp.max(scores, axis=1, keepdims=True))
    return weights * (1.0 / jnp.sum(weights, axis=1, keepdims=True))


def turn(values, cosine, sine):
    size = values.shape[1]
    first = lax.broadcasted_iota(jnp.int32, values.shape, 1) % HEAD_DIM < HALF
    other = jnp.where(
        first, -pltpu.roll(values, size - HALF, 1), pltpu.roll(values, HALF, 1)
    )
    tables = [jnp.concatenate([table] * (size // LANES), axis=1) for table in (cosine, sine)]
    return values * tables[0] + other * tables[1]


def attention_kernel(
    x_ref, w_ref, col_ref, row_ref, cos_ref, sin_ref, out_ref, turned_ref, qkv_ref, rest_ref
):
    seq_len = out_ref.shape[0]
    tokens = turned_ref.shape[2]
    rest_ref[...] = x_ref[:, tokens:, :]
    heads = out_ref.shape[1] // HEAD_DIM
    last = (heads + 1) * HEAD_DIM
    step = QUERY_ROWS
    for first in range(0, seq_len, step):
        at = slice(first, first + step)
        wide = first + step
        blocks = range(first // tokens, wide // tokens)
        rows = jnp.concatenate([x_ref[block, :tokens, :] for block in blocks], axis=0)
        joined = contract(rows, w_ref[...], 1, 1)
        turned_part = turn(joined[:, :last], cos_ref[at, :], sin_ref[at, :])
        qkv_ref[at, :last] = turned_part.astype(bf16)
        qkv_ref[at, last:] = joined[:, last:].astype(bf16)
        mask = allowed(step, first, wide, col_ref, row_ref)
        key = qkv_ref[:wide, heads * HEAD_DIM : last]
        value = qkv_ref[:wide, last:]
        for head in range(heads):
            place = slice(head * HEAD_DIM, (head + 1) * HEAD_DIM)
            query = qkv_ref[at, place] * SCALE
            probs = probabilities(query, key, mask).astype(bf16)
            context = jnp.dot(probs, value, preferred_element_type=f32)
            out_ref[at, place] = context.astype(bf16)
            for block in range(step // tokens):
                turned_ref[first // tokens + block, place, :] = context[
                    block * tokens : (block + 1) * tokens
                ].T.astype(bf16)


def attention_back_kernel(
    qkv_ref, grad_ref, col_ref, row_ref, cos_ref, sin_ref, out_ref, turned_ref, key_sum, value_sum
):
    seq_len = qkv_ref.shape[0]
    heads = grad_ref.shape[1] // HEAD_DIM
    tokens = grad_ref.shape[2]
    last = (heads + 1) * HEAD_DIM
    step = QUERY_ROWS
    for first in reversed(range(0, seq_len, step)):
        at = slice(first, first + step)
        wide = first + step
        mask = allowed(step, first, wide, col_ref, row_ref)
        key = qkv_ref[:wide, heads * HEAD_DIM : last]
        value = qkv_ref[:wide, last:]
        key_grad = jnp.zeros((wide, HEAD_DIM), f32)
        value_grad = jnp.zeros((wide, HEAD_DIM), f32)
        query_grads = []
        for head in range(heads):
            place = slice(head * HEAD_DIM, (head + 1) * HEAD_DIM)
            query = qkv_ref[at, place] * SCALE
            grad = [
                grad_ref[first // tokens + block, place, :].astype(f32).T.astype(bf16)
                for block in range(step // tokens)
            ]
            grad = jnp.concatenate(grad, axis=0)
            probs = probabilities(query, key, mask)
            probs_grad = contract(grad, value, 1, 1)
            row_dot = jnp.sum(probs * probs_grad, axis=1, keepdims=True)
            score_grad = (probs * (probs_grad - row_dot)).astype(bf16)
            query_grads.append(jnp.dot(score_grad, key, preferred_element_type=f32) * SCALE)
            key_grad += contract(score_grad, query, 0, 0)
            value_grad += contract(probs.astype(bf16), grad, 0, 0)
        if wide == seq_len:
            key_sum[...] = key_grad
            value_sum[...] = value_grad
        else:
            key_sum[:wide, :] += key_grad
            value_sum[:wide, :] += value_grad
        both = jnp.concatenate(query_grads + [key_sum[at, :]], axis=1)
        both = turn(both, cos_ref[at, :], -sin_ref[at, :])
        out_ref[at, :last] = both.astype(bf16)
        out_ref[at, last:] = value_sum[at, :].astype(bf16)
        for block in range(step // tokens):
            part = slice(block * tokens, (block + 1) * tokens)
            to = first // tokens + block
            turned_ref[to, :last, :] = both[part].T.astype(bf16)
            turned_ref[to, last:, :] = value_sum[first : first + step, :][part].T.astype(bf16)


def run_attention(gathered, joined_rows, marks, tables):
    planes = gathered.shape[0]
    seq_len = marks[0].shape[0]
    joined_width = joined_rows.shape[0]
    query_width = joined_width - 2 * HEAD_DIM
    vmem = pl.BlockSpec(memory_space=pltpu.VMEM)
    return pl.pallas_call(
        attention_kernel,
        out_shape=(
            jax.ShapeDtypeStruct((seq_len, query_width), bf16),
            jax.ShapeDtypeStruct((planes, query_width, seq_len // planes), bf16),
            jax.ShapeDtypeStruct((seq_len, joined_width), bf16),
            jax.ShapeDtypeStruct(
                (planes, gathered.shape[1] - seq_len // planes, gathered.shape[2]), bf16
            ),
        ),
        in_specs=[vmem] * 6,
        out_specs=(vmem,) * 4,
        compiler_params=pltpu.CompilerParams(vmem_limit_bytes=48 * 1024 * 1024),
        cost_estimate=pl.CostEstimate(
            flops=4 << 30, bytes_accessed=8 << 20, transcendentals=0
        ),
    )(gathered, joined_rows, *marks, *tables)


def run_attention_back(qkv, context_grad, marks, tables):
    seq_len, joined_width = qkv.shape
    planes = context_grad.shape[0]
    vmem = pl.BlockSpec(memory_space=pltpu.VMEM)
    return pl.pallas_call(
        attention_back_kernel,
        out_shape=(
            jax.ShapeDtypeStruct((seq_len, joined_width), bf16),
            jax.ShapeDtypeStruct((planes, joined_width, seq_len // planes), bf16),
        ),
        in_specs=[vmem] * 6,
        out_specs=(vmem, vmem),
        scratch_shapes=[pltpu.VMEM((seq_len, HEAD_DIM), f32)] * 2,
        compiler_params=pltpu.CompilerParams(vmem_limit_bytes=48 * 1024 * 1024),
        cost_estimate=pl.CostEstimate(
            flops=1 << 28, bytes_accessed=1 << 20, transcendentals=0
        ),
    )(qkv, context_grad, *marks, *tables)


def rope_tables(seq_len):
    frequency = np.float32(rope_theta) ** (np.arange(HALF, dtype=np.float32) * np.float32(-2.0 / HEAD_DIM))
    angles = np.arange(seq_len, dtype=np.float32)[:, None] * frequency.astype(np.float32)[None, :]
    angles = np.tile(angles, (1, LANES // HALF))
    return jnp.asarray(np.cos(angles)), jnp.asarray(np.sin(angles))


def segment_marks(key_seg):
    marks = jnp.where(key_seg == 0, -1 - jnp.arange(key_seg.shape[0], dtype=jnp.int32), key_seg)
    return marks[:, None], marks[None, :]


def expert_kernel(groups, first_ref, *refs):
    rows_refs, cots_refs = refs[:groups], refs[groups : 2 * groups]
    w_ref = refs[2 * groups]
    back_outs = refs[2 * groups + 1 : 3 * groups + 1]
    x_ref, c_ref, gate_ref, up_ref, hid_ref, pick_ref = refs[3 * groups + 1 : 3 * groups + 7]
    down_ref, next_x, next_c, gates_ref = refs[3 * groups + 7 :]
    sources, tokens, _ = rows_refs[0].shape
    width = x_ref.shape[2]
    e = pl.program_id(0)
    expert = first_ref[0] + e
    at = pl.ds(pl.multiple_of(e * CAP, CAP), CAP)
    every = [(group, source) for group in range(groups) for source in range(sources)]

    @pl.when(e == 0)
    def _():
        pair = 2 * CAP
        lane = lax.broadcasted_iota(jnp.int32, (pair, LANES), 1)
        expert_of = expert + lax.broadcasted_iota(jnp.int32, (pair, LANES), 0) // CAP
        own = (lane == expert_of) | (lane == expert_of + EXPERTS)
        row_id = lax.broadcasted_iota(jnp.int32, (EXPERTS, tokens), 0)
        slot = lax.broadcasted_iota(jnp.int32, (pair, tokens), 0)
        place_of = jnp.where(slot < CAP, slot, slot - CAP).astype(f32)
        for order, (group, source) in enumerate(every):
            table = cots_refs[group][source, :EXPERTS, width:].astype(f32)
            ranks = [
                jnp.sum(jnp.where(row_id == expert + i, table, 0.0), axis=0, keepdims=True)
                for i in range(2)
            ]
            pick = (jnp.where(slot < CAP, ranks[0], ranks[1]) == place_of).astype(bf16)
            pick_ref[order] = pick
            rows = jnp.dot(pick, rows_refs[group][source], preferred_element_type=f32)
            cots = jnp.dot(pick, cots_refs[group][source, :, :width], preferred_element_type=f32)
            gate = jnp.sum(jnp.where(own, rows[:, width:], 0.0), axis=1, keepdims=True)
            gate = jnp.broadcast_to(gate, (pair, LANES))
            place = slice(order * CAP, (order + 1) * CAP)
            x_ref[0, place] = rows[:CAP, :width].astype(bf16)
            c_ref[0, place] = cots[:CAP].astype(bf16)
            gates_ref[0, place] = gate[:CAP]
            next_x[place] = rows[CAP:, :width].astype(bf16)
            next_c[place] = cots[CAP:].astype(bf16)
            gates_ref[1, place] = gate[CAP:]

    @pl.when(e == 1)
    def _():
        x_ref[0] = next_x[...]
        c_ref[0] = next_c[...]

    gate = gates_ref[e][:, :1]
    join_chunks(down_ref, w_ref.at[2], HOLDERS)
    x = x_ref[0]
    gate_pre = jnp.dot(x, w_ref[0], preferred_element_type=f32)
    up_pre = jnp.dot(x, w_ref[1], preferred_element_type=f32)
    back = contract(c_ref[0], down_ref[...], 1, 1)
    sig = 1.0 / (1.0 + jnp.exp(-gate_pre))
    silu = gate_pre * sig
    hidden = (silu * up_pre).astype(bf16)
    gate_grad = jnp.sum(back * hidden.astype(f32), axis=1, keepdims=True)
    grad = gate * back
    gate_pre_grad = (grad * up_pre * (sig + silu * (1.0 - sig))).astype(bf16)
    up_pre_grad = (grad * silu).astype(bf16)
    gate_ref[0] = gate_pre_grad
    up_ref[0] = up_pre_grad
    hid_ref[0] = (gate * hidden.astype(f32)).astype(bf16)
    row_grad = contract(gate_pre_grad, w_ref[0], 1, 1) + contract(up_pre_grad, w_ref[1], 1, 1)
    high = gate_grad.astype(bf16).astype(f32)
    lane = lax.broadcasted_iota(jnp.int32, (len(every) * CAP, LANES), 1)
    tail = jnp.where(lane == expert, high, 0.0)
    tail += jnp.where(lane == expert + EXPERTS, gate_grad - high, 0.0)
    for order, (group, source) in enumerate(every):
        place = slice(order * CAP, (order + 1) * CAP)
        back_outs[group][source, at, :width] = row_grad[place].astype(bf16)
        back_outs[group][source, at, width:] = tail[place].astype(bf16)

    @pl.when(e == 1)
    def _():
        for order, (group, source) in enumerate(every):
            back_outs[group][source] = contract(
                pick_ref[order], back_outs[group][source], 0, 0
            ).astype(bf16)


def join_chunks(to_ref, from_ref, holders):
    inner = from_ref.shape[1]
    rows = inner // HOLDERS
    chunks = to_ref.shape[1] // inner
    for holder in range(holders):
        for chunk in range(chunks):
            start = (holder * chunks + chunk) * rows
            to_ref[
                holder * rows : (holder + 1) * rows, chunk * inner : (chunk + 1) * inner
            ] = from_ref[start : start + rows, :]


def run_experts(first, rows, cots, weights):
    groups = len(rows)
    sources, tokens, padded = rows[0].shape
    width = padded - LANES
    inner = weights.shape[2]
    slots = groups * sources * CAP

    def once(columns):
        return pl.BlockSpec(
            (sources, tokens, columns), lambda e: (0, 0, 0), pipeline_mode=pl.Buffered(1)
        )

    def by_expert(*shape):
        return pl.BlockSpec(shape, lambda e: (e, 0, 0))

    acts = jax.ShapeDtypeStruct((2, slots, inner), bf16)
    wide = jax.ShapeDtypeStruct((2, slots, width), bf16)
    outs = pl.pallas_call(
        functools.partial(expert_kernel, groups),
        grid=(2,),
        out_shape=(
            *[jax.ShapeDtypeStruct((sources, tokens, padded), bf16)] * groups,
            wide,
            wide,
            acts,
            acts,
            acts,
            jax.ShapeDtypeStruct((groups * sources, 2 * CAP, tokens), bf16),
        ),
        in_specs=[pl.BlockSpec(memory_space=pltpu.SMEM)]
        + [once(padded)] * (2 * groups)
        + [by_expert(3, width, inner)],
        out_specs=(
            *[once(padded)] * groups,
            by_expert(1, slots, width),
            by_expert(1, slots, width),
            by_expert(1, slots, inner),
            by_expert(1, slots, inner),
            by_expert(1, slots, inner),
            pl.BlockSpec((groups * sources, 2 * CAP, tokens), lambda e: (0, 0, 0)),
        ),
        scratch_shapes=[
            pltpu.VMEM((inner, width), bf16),
            pltpu.VMEM((slots, width), bf16),
            pltpu.VMEM((slots, width), bf16),
            pltpu.VMEM((2, slots, LANES), f32),
        ],
        compiler_params=pltpu.CompilerParams(vmem_limit_bytes=56 * 1024 * 1024),
        cost_estimate=pl.CostEstimate(
            flops=2 * 2 * 6 * slots * width * inner, bytes_accessed=24 << 20, transcendentals=0
        ),
    )(first, *rows, *cots, weights)
    return outs[:groups], outs[groups:-1], outs[-1]


def mixture_kernel(groups, *refs):
    pick_refs, hid_refs = refs[:groups], refs[groups : 2 * groups]
    w_ref = refs[2 * groups]
    outs, down_ref = refs[2 * groups + 1 : -1], refs[-1]
    e = pl.program_id(0)
    at = pl.ds(pl.multiple_of(e * CAP, CAP), CAP)
    join_chunks(down_ref, w_ref.at[0], HOLDERS)
    sources = [
        (pick_ref, hid_ref, source)
        for pick_ref, hid_ref in zip(pick_refs, hid_refs)
        for source in range(pick_ref.shape[0])
    ]
    to = {}
    for order, (pick_ref, hid_ref, source) in enumerate(sources):
        to[order] = (outs[order // SIDE], order % SIDE, pick_ref, source)
    order = 0
    for pick_ref, hid_ref in zip(pick_refs, hid_refs):
        mixed = jnp.dot(hid_ref[0], down_ref[...], preferred_element_type=f32).astype(bf16)
        for source in range(pick_ref.shape[0]):
            out, place, _, _ = to[order]
            out[place, at] = mixed[source * CAP : (source + 1) * CAP]
            order += 1

    @pl.when(e == 1)
    def _():
        for out, place, pick_ref, source in to.values():
            out[place] = contract(pick_ref[source], out[place], 0, 0).astype(bf16)


def run_mixture(picks, hidden, weights):
    width, inner = weights.shape[1:]
    groups = len(picks)

    def once(shape):
        return pl.BlockSpec(shape, lambda e: (0, 0, 0), pipeline_mode=pl.Buffered(1))

    shapes = [(SIDE, picks[0].shape[2], width)] * SIDE
    return pl.pallas_call(
        functools.partial(mixture_kernel, groups),
        grid=(2,),
        out_shape=[jax.ShapeDtypeStruct(shape, bf16) for shape in shapes],
        in_specs=[once(pick.shape) for pick in picks]
        + [pl.BlockSpec((1,) + hid.shape[1:], lambda e: (e, 0, 0)) for hid in hidden]
        + [pl.BlockSpec((1, width, inner), lambda e: (3 * e + 2, 0, 0))],
        out_specs=[once(shape) for shape in shapes],
        scratch_shapes=[pltpu.VMEM((inner, width), bf16)],
        compiler_params=pltpu.CompilerParams(vmem_limit_bytes=40 * 1024 * 1024),
        cost_estimate=pl.CostEstimate(flops=1 << 32, bytes_accessed=1 << 20, transcendentals=0),
    )(*picks, *hidden, weights)


def weight_grad_kernel(groups, half_ref, *refs):
    x_refs, c_refs, gate_refs, up_refs, hid_refs = (
        refs[i * groups : (i + 1) * groups] for i in range(5)
    )
    *onto, out_ref = refs[5 * groups :]
    width = x_refs[0].shape[2]
    inner = gate_refs[0].shape[2]
    half = half_ref[0]
    rows = width // 2
    down_rows = inner // HOLDERS
    chunks = width // inner
    cols = pl.ds(pl.multiple_of(half * rows, LANES), rows)
    down_cols = pl.ds(pl.multiple_of(half * (inner // 2), LANES), inner // 2)
    gate = jnp.zeros((rows, inner), f32)
    up = jnp.zeros((rows, inner), f32)
    down = jnp.zeros((inner // 2, width), f32)
    for i in range(groups):
        x = x_refs[i][0, :, cols]
        gate += contract(x, gate_refs[i][0], 0, 0)
        up += contract(x, up_refs[i][0], 0, 0)

    def put(place, at, values):
        if onto:
            values = values + onto[0][place, at, :].astype(f32)
        out_ref[place, at, :] = values.astype(bf16)

    put(0, slice(0, rows), gate)
    put(1, slice(0, rows), up)
    for i in range(groups):
        down += contract(hid_refs[i][0, :, down_cols], c_refs[i][0], 0, 0)
    for holder in range(HOLDERS // 2):
        for chunk in range(chunks):
            start = (holder * chunks + chunk) * down_rows
            put(
                2,
                slice(start, start + down_rows),
                down[
                    holder * down_rows : (holder + 1) * down_rows,
                    chunk * inner : (chunk + 1) * inner,
                ],
            )


def run_weight_grads(half, saved, *onto):
    x, c, gate, up, hid = zip(*saved)
    width = x[0].shape[2]
    inner = gate[0].shape[2]
    operands = (*x, *c, *gate, *up, *hid)
    out_spec = pl.BlockSpec((3, width // 2, inner), lambda e: (e, 0, 0))
    return pl.pallas_call(
        functools.partial(weight_grad_kernel, len(saved)),
        grid=(2,),
        out_shape=jax.ShapeDtypeStruct((6, width // 2, inner), bf16),
        in_specs=[pl.BlockSpec(memory_space=pltpu.SMEM)]
        + [pl.BlockSpec((1,) + v.shape[1:], lambda e: (e, 0, 0)) for v in operands]
        + [out_spec] * len(onto),
        out_specs=out_spec,
        compiler_params=pltpu.CompilerParams(vmem_limit_bytes=52 * 1024 * 1024),
        cost_estimate=pl.CostEstimate(flops=1 << 28, bytes_accessed=1 << 20, transcendentals=0),
    )(half, *operands, *onto)


def sides_kernel(
    x_ref, grad_ref, w_ref, all_ref, context_ref, normed_ref, logit_ref, norm_ref, gain_ref, out_ref, shared_ref
):
    planes, tokens = x_ref.shape[0], normed_ref.shape[0]
    joined_width = grad_ref.shape[1]
    experts = logit_ref.shape[1]
    step = x_ref.shape[2] // 2
    for first in range(0, x_ref.shape[2], step):
        at = slice(first, first + step)
        rows = jnp.concatenate([x_ref[plane, :tokens, at] for plane in range(planes)], axis=0)
        joined = contract(grad_ref[...], rows, 0, 0)
        out_ref[:joined_width, at] = joined.astype(bf16)
        out_ref[joined_width:, at] = contract(context_ref[...], all_ref[:, at], 0, 0).astype(bf16)
        norm1 = jnp.sum(joined * w_ref[:, at].astype(f32), axis=0, keepdims=True) / gain_ref[:, at]
        norm2 = jnp.sum(norm_ref[:, at], axis=0, keepdims=True)
        shared_ref[:experts, at] = contract(logit_ref[...], normed_ref[:, at], 0, 0).astype(bf16)
        shared_ref[experts : experts + 1, at] = norm2.astype(bf16)
        shared_ref[experts + 1 : experts + 2, at] = norm1.astype(bf16)


def run_sides(gathered, joined_grad, joined_rows, attention_all, context, normed_two, logits, norm_terms, gain):
    vmem = pl.BlockSpec(memory_space=pltpu.VMEM)
    width = gathered.shape[2]
    rows = joined_grad.shape[1] + context.shape[1]
    return pl.pallas_call(
        sides_kernel,
        out_shape=(
            jax.ShapeDtypeStruct((rows, width), bf16),
            jax.ShapeDtypeStruct((logits.shape[1] + 2, width), bf16),
        ),
        in_specs=[vmem] * 9,
        out_specs=(vmem, vmem),
        compiler_params=pltpu.CompilerParams(vmem_limit_bytes=40 * 1024 * 1024),
        cost_estimate=pl.CostEstimate(flops=1 << 31, bytes_accessed=12 << 20, transcendentals=0),
    )(gathered, joined_grad, joined_rows, attention_all, context, normed_two, logits, norm_terms, gain)


def local(
    tokens,
    segments,
    routes,
    norm1_gain,
    w_query,
    w_key,
    w_value,
    w_out,
    norm2_gain,
    w_router,
    w_gate,
    w_up,
    w_down,
    cotangent,
):
    tok_rows, width = tokens.shape
    seq_len = segments.shape[1]
    query_width = w_query.shape[1]
    kv_width = w_key.shape[1]
    joined_width = query_width + 2 * kv_width
    local_experts = w_gate.shape[0]
    experts = w_router.shape[1]
    owners = lax.axis_size("expert")
    planes = lax.axis_size("tensor")
    owner = lax.axis_index("expert")
    first_expert = owner * local_experts
    key_seg = segments[0]
    hidden_width = w_gate.shape[2]

    token_f32 = tokens.astype(f32)
    inverse_one = rms_inverse(token_f32)
    normed_low = (token_f32 * inverse_one * norm1_gain).astype(bf16)
    joined_rows = by_rows(jnp.concatenate([w_query.T, w_key.T, w_value.T], axis=0))
    core = lax.axis_index("dp")

    def half_of(rows):
        count = rows.shape[0] // 2
        return lax.dynamic_slice_in_dim(rows, core * count, count, 0)

    def both_halves(half):
        other = swap_cores(half)
        first, second = jnp.where(core == 0, half, other), jnp.where(core == 0, other, half)
        return jnp.concatenate([first, second], axis=1).reshape(-1, half.shape[2])

    gathered = lax.all_gather(
        by_rows(jnp.concatenate([normed_low, half_of(w_out)], axis=0)), "tensor", axis=0
    )

    expert_ids = jnp.arange(experts, dtype=jnp.int32)
    onehot = (routes[:, :, None] == expert_ids[None, None, :]).astype(f32)
    member = jnp.sum(onehot, axis=1)
    lower = (jnp.arange(tok_rows)[:, None] <= jnp.arange(tok_rows)[None, :]).astype(bf16)
    rank = jnp.einsum("te,tu->eu", member.astype(bf16), lower, preferred_element_type=f32)
    rank = jnp.where(member.T > 0, rank - 1.0, -1.0).astype(bf16)
    extra = jnp.pad(rank, ((0, tok_rows - experts), (0, LANES - tok_rows)))
    cot_payload = jnp.concatenate([cotangent, extra], axis=1)

    chunks = width // hidden_width
    down_rows = w_down.shape[1]
    part_rows = w_gate.shape[1]
    down_parts = w_down.reshape(local_experts, down_rows, chunks, hidden_width)
    down_parts = down_parts.transpose(0, 2, 1, 3).reshape(local_experts, part_rows, hidden_width)
    weights = jnp.stack([w_gate, w_up, down_parts], axis=1)
    weights = weights.reshape(3 * local_experts, part_rows, hidden_width)
    tables = rope_tables(seq_len)
    marks = segment_marks(key_seg)
    cot_parts = gather_second(gather_first(cot_payload))
    joined_half = by_rows(half_of(joined_rows))
    gathered, weights, joined_rows, joined_half, col, row, *cot_parts = together(
        gathered, weights, joined_rows, joined_half, *marks, *cot_parts
    )
    marks = col, row
    weights_all = lax.all_gather(weights, ("dp", "tensor"), axis=1, tiled=True)
    context, context_blocks, qkv, half_out = run_attention(
        gathered, joined_rows, marks, tables
    )
    context_home = lax.all_to_all(context_blocks, "tensor", split_axis=0, concat_axis=0)
    w_out_all = both_halves(half_out)
    context_home, w_out_all, joined_half = together(context_home, w_out_all, joined_half)
    half_joined = lax.all_gather(joined_half, "tensor", axis=0)
    context_home = context_home.reshape(planes * query_width, tok_rows)
    mid = token_f32 + contract(context_home, w_out_all, 0, 0)
    inverse_two = rms_inverse(mid)
    normed_two = (mid * inverse_two * norm2_gain).astype(bf16)
    logits = dot32(normed_two, w_router)
    logits = jnp.where(member > 0, logits, masked_score)
    chosen_exp = jnp.where(
        member > 0, jnp.exp(logits - jnp.max(logits, axis=1, keepdims=True)), 0.0
    )
    gates = chosen_exp / jnp.sum(chosen_exp, axis=1, keepdims=True)
    gate_high, gate_low = split_two(gates)
    payload = jnp.concatenate(
        [normed_two, gate_high, gate_low, jnp.zeros((tok_rows, LANES - 2 * experts), bf16)],
        axis=1,
    )
    line = gather_first(payload)
    before, behind = (cross(line, 1, step) for step in STEPS[1:3])

    first_expert = first_expert.astype(jnp.int32).reshape(1)
    def compute(rows, cots):
        return run_experts(first_expert, rows, cots, weights_all)

    own = compute([line], cot_parts[:1])
    line, before, behind, *own_saved = together(line, before, behind, *own[1])
    far = cross(line, 1, STEPS[3])
    near = compute([before, behind], cot_parts[1:3])
    far, *near_saved = together(far, *near[1])
    last = compute([far], cot_parts[3:])
    done = [(*own[0], *near[0], *last[0]), (own_saved, near_saved, last[1])]
    back_line = scatter_first(done[0])
    mix_parts = run_mixture(
        [own[2], near[2], last[2]], [own_saved[4], near_saved[4], last[1][4]], weights_all
    )
    given = run_weight_grads((1 - core).astype(jnp.int32).reshape(1), done[1])
    n_line = len(back_line)
    *both, given, half_joined = together(*back_line, *mix_parts, given, half_joined)
    back_line, mix_parts = sum_first(both[:n_line]), both[n_line:]
    back_home, received = scatter_second(back_line, swap_cores(given))

    cot_f32 = cotangent.astype(f32)
    grad_tail = back_home[:, width:]
    gate_grad = grad_tail[:, :experts] + grad_tail[:, experts : 2 * experts]
    chosen_grad = gates * (gate_grad - jnp.sum(gates * gate_grad, axis=1, keepdims=True))
    logit_grad = chosen_grad.astype(bf16)
    normed_two_grad = back_home[:, :width] + jnp.einsum(
        "te,de->td", logit_grad, w_router, preferred_element_type=f32
    )
    mid_part, norm2_terms = rms_backward(mid, inverse_two, norm2_gain, normed_two_grad)
    mid_grad = cot_f32 + mid_part
    attention_low = by_rows(mid_grad.astype(bf16))
    norm2_terms = by_rows(norm2_terms)
    context_grad = by_rows(contract(w_out_all, attention_low, 1, 1).astype(bf16))
    received, *mix_parts, context_grad, logit_grad = together(
        received, *mix_parts, context_grad, logit_grad
    )
    mix_arrived = scatter_first(mix_parts)
    kept = run_weight_grads(core.astype(jnp.int32).reshape(1), done[1], received)
    context_grad = lax.all_to_all(
        context_grad.reshape(planes, query_width, tok_rows), "tensor", split_axis=0, concat_axis=0
    )
    context_grad, kept = together(context_grad, kept)
    joined_grad, joined_blocks = run_attention_back(qkv, context_grad, marks, tables)
    joined_home = lax.all_to_all(joined_blocks, "tensor", split_axis=0, concat_axis=0)
    attention_all = lax.all_gather(attention_low, "tensor", axis=0, tiled=True)
    sides, shared = run_sides(
        gathered,
        joined_grad,
        joined_rows,
        attention_all,
        context,
        normed_two,
        logit_grad,
        norm2_terms,
        norm1_gain[None],
    )

    share = sides.shape[0] // (2 * owners)
    shared_shape = shared.shape
    shared_rows = shared.size // LANES
    shared = shared.reshape(shared_rows, LANES)
    shared = jnp.pad(shared, ((0, 2 * owners * share - shared_rows), (0, 0)))
    blocks = jnp.concatenate(
        [sides.reshape(2, owners, share, width), shared.reshape(2, owners, share, LANES)], axis=3
    )
    blocks, joined_home, kept, *mix_arrived = together(blocks, joined_home, kept, *mix_arrived)
    weight_sum = lax.psum_scatter(kept, "tensor", scatter_dimension=1, tiled=True)

    def of_core(which):
        return lax.dynamic_index_in_dim(blocks, which, 0, keepdims=False)

    part = of_core(core).astype(f32) + swap_cores(of_core(1 - core)).astype(f32)
    arrived = lax.all_to_all(part.astype(bf16), "expert", split_axis=0, concat_axis=0)

    def rows_of(which):
        count = joined_width // 2
        rows = lax.dynamic_slice_in_dim(joined_home, which * count, count, 1)
        return rows.reshape(-1, tok_rows)

    normed_one_grad = contract(rows_of(core), half_joined.reshape(-1, width), 0, 0)
    normed_one_grad += contract(
        rows_of(1 - core), swap_cores(half_joined).reshape(-1, width), 0, 0
    )
    arrived, normed_one_grad, *mix_line = together(
        arrived, normed_one_grad, *sum_first(mix_arrived)
    )
    total = jnp.sum(arrived.astype(f32), axis=0)
    sides = total[:, :width].astype(bf16)
    sides = lax.all_to_all(
        jnp.broadcast_to(sides[None], (owners,) + sides.shape), "expert", split_axis=0, concat_axis=0
    )

    def both_cores(own):
        other = swap_cores(own)
        first, second = jnp.where(core == 0, own, other), jnp.where(core == 0, other, own)
        return jnp.concatenate([first, second], axis=0).reshape(-1, own.shape[2])

    ringed = by_rows(ring_sum(total[:, width:]))
    every = jnp.concatenate(gather_second(gather_first(ringed))).reshape((-1,) + ringed.shape)
    row, column = jnp.arange(owners) // SIDE, jnp.arange(owners) % SIDE
    row, column = owner_of(row, owner // SIDE), owner_of(column, owner % SIDE)
    order = jnp.where(core == 0, row * SIDE + column, column * SIDE + row)
    shared = both_cores(every[order])[:shared_rows].reshape(shared_shape)
    mixture = scatter_second(mix_line)[0]
    sides, mixture = together(sides, mixture)
    output = (mid + mixture).astype(bf16)
    sides, weight_sum = together(both_cores(sides), weight_sum)
    sides = sides.astype(f32)
    joined_sum = sides[:joined_width].T
    out_sum = sides[joined_width:]
    weight_sum = weight_sum.reshape(local_experts, 3, part_rows, hidden_width)
    w_gate_grad = weight_sum[:, 0].astype(f32)
    w_up_grad = weight_sum[:, 1].astype(f32)
    w_down_grad = weight_sum[:, 2].reshape(local_experts, chunks, down_rows, hidden_width)
    w_down_grad = w_down_grad.transpose(0, 2, 1, 3).reshape(local_experts, down_rows, width)
    w_down_grad = w_down_grad.astype(f32)
    input_part, _ = rms_backward(token_f32, inverse_one, norm1_gain, normed_one_grad)
    input_grad = mid_grad + input_part
    return (
        output,
        input_grad,
        shared[experts + 1],
        joined_sum[:, :query_width],
        joined_sum[:, query_width : query_width + kv_width],
        joined_sum[:, query_width + kv_width :],
        out_sum,
        shared[experts],
        shared[:experts].T,
        w_gate_grad,
        w_up_grad,
        w_down_grad,
    )


def solution(mesh):
    rows = P(("dp", "expert", "tensor"), None)
    columns = P(None, "tensor")
    experts = P("expert", ("dp", "tensor"), None)
    return jax.shard_map(
        local,
        mesh=mesh,
        in_specs=(
            rows,
            P(("dp", "expert"), None),
            rows,
            P(),
            columns,
            columns,
            columns,
            P("tensor", None),
            P(),
            P(),
            experts,
            experts,
            experts,
            rows,
        ),
        out_specs=(
            rows,
            rows,
            P(),
            columns,
            columns,
            columns,
            P("tensor", None),
            P(),
            P(),
            experts,
            experts,
            experts,
        ),
        check_vma=False,
    )
```

```python
import functools

import jax
import jax.numpy as jnp
import numpy as np
from jax import lax
from jax.experimental import pallas as pl
from jax.experimental.layout import Layout, with_layout_constraint
from jax.experimental.pallas import tpu as pltpu
from jax.sharding import PartitionSpec as P

HEAD_DIM = 64
HALF = HEAD_DIM // 2
TOP = 8
CAP = 64
EXPERTS = 32
HOLDERS = 16
LANES = 128

epsilon_norm = 1e-06
rope_theta = 10000.0
masked_score = -1e30
QUERY_ROWS = 512
SCALE = HEAD_DIM ** (-0.5)
f32 = jnp.float32
bf16 = jnp.bfloat16


def rms_inverse(values):
    return lax.rsqrt(jnp.mean(values * values, axis=-1, keepdims=True) + epsilon_norm)


def rms_backward(values, inverse, norm_gain, grad_out):
    scaled = grad_out * norm_gain
    grad_in = inverse * scaled - values * (inverse * inverse * inverse) * jnp.mean(
        scaled * values, axis=-1, keepdims=True
    )
    return (grad_in, grad_out * values * inverse)


def dot32(left, right):
    return jnp.dot(left, right, preferred_element_type=f32)


SIDE = 4
STEPS = (0, 1, -1, 2)


def by_rows(values):
    return with_layout_constraint(values, Layout(major_to_minor=tuple(range(values.ndim))))


def cross(values, stage, step):
    pairs = []
    plane = SIDE * SIDE
    for core in range(2):
        for x in range(SIDE):
            for y in range(SIDE):
                if core == stage:
                    to = x * SIDE + (y + step) % SIDE
                else:
                    to = (x + step) % SIDE * SIDE + y
                pairs.append((core * plane + x * SIDE + y, core * plane + to))
    return lax.ppermute(values, ("dp", "expert"), pairs)


def gather_first(values):
    values = by_rows(values)
    line = jnp.stack([values] + [cross(values, 0, step) for step in STEPS[1:]])
    return by_rows(line)


def gather_second(line):
    return [line] + [cross(line, 1, step) for step in STEPS[1:]]


def scatter_first(parts):
    return [parts[0]] + [
        by_rows(cross(part, 1, -step)) for part, step in zip(parts[1:], STEPS[1:])
    ]


def sum_kernel(*refs):
    arrived, outs = refs[:SIDE], refs[SIDE:]
    total = sum(ref[0].astype(f32) for ref in arrived).astype(bf16)
    for place, out in enumerate(outs):

        @pl.when(pl.program_id(0) == place)
        def _():
            out[...] = total


def sum_first(arrived):
    rows, columns = arrived[0].shape[1:]
    return pl.pallas_call(
        sum_kernel,
        grid=(SIDE,),
        out_shape=[jax.ShapeDtypeStruct((rows, columns), bf16)] * SIDE,
        in_specs=[pl.BlockSpec((1, rows, columns), lambda place: (place, 0, 0))] * SIDE,
        out_specs=[pl.BlockSpec((rows, columns), lambda place: (0, 0))] * SIDE,
        compiler_params=pltpu.CompilerParams(vmem_limit_bytes=24 * 1024 * 1024),
        cost_estimate=pl.CostEstimate(flops=1 << 22, bytes_accessed=8 << 20, transcendentals=0),
    )(*arrived)


def scatter_second(line):
    return [line[0]] + [
        by_rows(cross(part, 0, -step)) for part, step in zip(line[1:], STEPS[1:])
    ]


def ring_sum(values):
    size = lax.axis_size("tensor")
    step = 1
    while step < size:
        pairs = [(i, i ^ step) for i in range(size)]
        values = values + lax.ppermute(values, "tensor", pairs)
        step *= 2
    return values


def together(*values):
    return lax.optimization_barrier(values)


def swap_cores(values):
    return lax.ppermute(values, "dp", [(0, 1), (1, 0)])


def contract(left, right, left_dim, right_dim):
    return lax.dot_general(
        left, right, (((left_dim,), (right_dim,)), ((), ())), preferred_element_type=f32
    )


def allowed(rows, first, wide, col_ref, row_ref):
    query = first + lax.broadcasted_iota(jnp.int32, (rows, wide), 0)
    key = lax.broadcasted_iota(jnp.int32, (rows, wide), 1)
    return (key <= query) & (col_ref[first : first + rows, :] == row_ref[:, :wide])


def probabilities(query, key, mask):
    scores = jnp.where(mask, contract(query, key, 1, 1), masked_score)
    weights = jnp.exp(scores - jnp.max(scores, axis=1, keepdims=True))
    return weights * (1.0 / jnp.sum(weights, axis=1, keepdims=True))


def turn(values, cosine, sine):
    size = values.shape[1]
    first = lax.broadcasted_iota(jnp.int32, values.shape, 1) % HEAD_DIM < HALF
    other = jnp.where(
        first, -pltpu.roll(values, size - HALF, 1), pltpu.roll(values, HALF, 1)
    )
    tables = [jnp.concatenate([table] * (size // LANES), axis=1) for table in (cosine, sine)]
    return values * tables[0] + other * tables[1]


def attention_kernel(
    x_ref, w_ref, col_ref, row_ref, cos_ref, sin_ref, out_ref, turned_ref, qkv_ref, rest_ref
):
    seq_len = out_ref.shape[0]
    tokens = turned_ref.shape[2]
    rest_ref[...] = x_ref[:, tokens:, :]
    heads = out_ref.shape[1] // HEAD_DIM
    last = (heads + 1) * HEAD_DIM
    step = QUERY_ROWS
    for first in range(0, seq_len, step):
        at = slice(first, first + step)
        wide = first + step
        blocks = range(first // tokens, wide // tokens)
        rows = jnp.concatenate([x_ref[block, :tokens, :] for block in blocks], axis=0)
        joined = contract(rows, w_ref[...], 1, 1)
        turned_part = turn(joined[:, :last], cos_ref[at, :], sin_ref[at, :])
        qkv_ref[at, :last] = turned_part.astype(bf16)
        qkv_ref[at, last:] = joined[:, last:].astype(bf16)
        mask = allowed(step, first, wide, col_ref, row_ref)
        key = qkv_ref[:wide, heads * HEAD_DIM : last]
        value = qkv_ref[:wide, last:]
        for head in range(heads):
            place = slice(head * HEAD_DIM, (head + 1) * HEAD_DIM)
            query = qkv_ref[at, place] * SCALE
            probs = probabilities(query, key, mask).astype(bf16)
            context = jnp.dot(probs, value, preferred_element_type=f32)
            out_ref[at, place] = context.astype(bf16)
            for block in range(step // tokens):
                turned_ref[first // tokens + block, place, :] = context[
                    block * tokens : (block + 1) * tokens
                ].T.astype(bf16)


def attention_back_kernel(
    qkv_ref, grad_ref, col_ref, row_ref, cos_ref, sin_ref, out_ref, turned_ref, key_sum, value_sum
):
    seq_len = qkv_ref.shape[0]
    heads = grad_ref.shape[1] // HEAD_DIM
    tokens = grad_ref.shape[2]
    last = (heads + 1) * HEAD_DIM
    step = QUERY_ROWS
    for first in reversed(range(0, seq_len, step)):
        at = slice(first, first + step)
        wide = first + step
        mask = allowed(step, first, wide, col_ref, row_ref)
        key = qkv_ref[:wide, heads * HEAD_DIM : last]
        value = qkv_ref[:wide, last:]
        key_grad = jnp.zeros((wide, HEAD_DIM), f32)
        value_grad = jnp.zeros((wide, HEAD_DIM), f32)
        query_grads = []
        for head in range(heads):
            place = slice(head * HEAD_DIM, (head + 1) * HEAD_DIM)
            query = qkv_ref[at, place] * SCALE
            grad = [
                grad_ref[first // tokens + block, place, :].astype(f32).T.astype(bf16)
                for block in range(step // tokens)
            ]
            grad = jnp.concatenate(grad, axis=0)
            probs = probabilities(query, key, mask)
            probs_grad = contract(grad, value, 1, 1)
            row_dot = jnp.sum(probs * probs_grad, axis=1, keepdims=True)
            score_grad = (probs * (probs_grad - row_dot)).astype(bf16)
            query_grads.append(jnp.dot(score_grad, key, preferred_element_type=f32) * SCALE)
            key_grad += contract(score_grad, query, 0, 0)
            value_grad += contract(probs.astype(bf16), grad, 0, 0)
        if wide == seq_len:
            key_sum[...] = key_grad
            value_sum[...] = value_grad
        else:
            key_sum[:wide, :] += key_grad
            value_sum[:wide, :] += value_grad
        both = jnp.concatenate(query_grads + [key_sum[at, :]], axis=1)
        both = turn(both, cos_ref[at, :], -sin_ref[at, :])
        out_ref[at, :last] = both.astype(bf16)
        out_ref[at, last:] = value_sum[at, :].astype(bf16)
        for block in range(step // tokens):
            part = slice(block * tokens, (block + 1) * tokens)
            to = first // tokens + block
            turned_ref[to, :last, :] = both[part].T.astype(bf16)
            turned_ref[to, last:, :] = value_sum[first : first + step, :][part].T.astype(bf16)


def run_attention(gathered, joined_rows, marks, tables):
    planes = gathered.shape[0]
    seq_len = marks[0].shape[0]
    joined_width = joined_rows.shape[0]
    query_width = joined_width - 2 * HEAD_DIM
    vmem = pl.BlockSpec(memory_space=pltpu.VMEM)
    return pl.pallas_call(
        attention_kernel,
        out_shape=(
            jax.ShapeDtypeStruct((seq_len, query_width), bf16),
            jax.ShapeDtypeStruct((planes, query_width, seq_len // planes), bf16),
            jax.ShapeDtypeStruct((seq_len, joined_width), bf16),
            jax.ShapeDtypeStruct(
                (planes, gathered.shape[1] - seq_len // planes, gathered.shape[2]), bf16
            ),
        ),
        in_specs=[vmem] * 6,
        out_specs=(vmem,) * 4,
        compiler_params=pltpu.CompilerParams(vmem_limit_bytes=48 * 1024 * 1024),
        cost_estimate=pl.CostEstimate(
            flops=4 << 30, bytes_accessed=8 << 20, transcendentals=0
        ),
    )(gathered, joined_rows, *marks, *tables)


def run_attention_back(qkv, context_grad, marks, tables):
    seq_len, joined_width = qkv.shape
    planes = context_grad.shape[0]
    vmem = pl.BlockSpec(memory_space=pltpu.VMEM)
    return pl.pallas_call(
        attention_back_kernel,
        out_shape=(
            jax.ShapeDtypeStruct((seq_len, joined_width), bf16),
            jax.ShapeDtypeStruct((planes, joined_width, seq_len // planes), bf16),
        ),
        in_specs=[vmem] * 6,
        out_specs=(vmem, vmem),
        scratch_shapes=[pltpu.VMEM((seq_len, HEAD_DIM), f32)] * 2,
        compiler_params=pltpu.CompilerParams(vmem_limit_bytes=48 * 1024 * 1024),
        cost_estimate=pl.CostEstimate(
            flops=1 << 28, bytes_accessed=1 << 20, transcendentals=0
        ),
    )(qkv, context_grad, *marks, *tables)


def rope_tables(seq_len):
    frequency = np.float32(rope_theta) ** (np.arange(HALF, dtype=np.float32) * np.float32(-2.0 / HEAD_DIM))
    angles = np.arange(seq_len, dtype=np.float32)[:, None] * frequency.astype(np.float32)[None, :]
    angles = np.tile(angles, (1, LANES // HALF))
    return jnp.asarray(np.cos(angles)), jnp.asarray(np.sin(angles))


def segment_marks(key_seg):
    marks = jnp.where(key_seg == 0, -1 - jnp.arange(key_seg.shape[0], dtype=jnp.int32), key_seg)
    return marks[:, None], marks[None, :]


def expert_kernel(groups, first_ref, *refs):
    rows_refs, cots_refs = refs[:groups], refs[groups : 2 * groups]
    w_ref = refs[2 * groups]
    back_outs = refs[2 * groups + 1 : 3 * groups + 1]
    x_ref, c_ref, gate_ref, up_ref, hid_ref, pick_ref = refs[3 * groups + 1 : 3 * groups + 7]
    down_ref, next_x, next_c, gates_ref = refs[3 * groups + 7 :]
    sources, tokens, _ = rows_refs[0].shape
    width = x_ref.shape[2]
    e = pl.program_id(0)
    expert = first_ref[0] + e
    at = pl.ds(pl.multiple_of(e * CAP, CAP), CAP)
    every = [(group, source) for group in range(groups) for source in range(sources)]

    @pl.when(e == 0)
    def _():
        pair = 2 * CAP
        lane = lax.broadcasted_iota(jnp.int32, (pair, LANES), 1)
        expert_of = expert + lax.broadcasted_iota(jnp.int32, (pair, LANES), 0) // CAP
        own = (lane == expert_of) | (lane == expert_of + EXPERTS)
        row_id = lax.broadcasted_iota(jnp.int32, (EXPERTS, tokens), 0)
        slot = lax.broadcasted_iota(jnp.int32, (pair, tokens), 0)
        place_of = jnp.where(slot < CAP, slot, slot - CAP).astype(f32)
        for order, (group, source) in enumerate(every):
            table = cots_refs[group][source, :EXPERTS, width:].astype(f32)
            ranks = [
                jnp.sum(jnp.where(row_id == expert + i, table, 0.0), axis=0, keepdims=True)
                for i in range(2)
            ]
            pick = (jnp.where(slot < CAP, ranks[0], ranks[1]) == place_of).astype(bf16)
            pick_ref[order] = pick
            rows = jnp.dot(pick, rows_refs[group][source], preferred_element_type=f32)
            cots = jnp.dot(pick, cots_refs[group][source, :, :width], preferred_element_type=f32)
            gate = jnp.sum(jnp.where(own, rows[:, width:], 0.0), axis=1, keepdims=True)
            gate = jnp.broadcast_to(gate, (pair, LANES))
            place = slice(order * CAP, (order + 1) * CAP)
            x_ref[0, place] = rows[:CAP, :width].astype(bf16)
            c_ref[0, place] = cots[:CAP].astype(bf16)
            gates_ref[0, place] = gate[:CAP]
            next_x[place] = rows[CAP:, :width].astype(bf16)
            next_c[place] = cots[CAP:].astype(bf16)
            gates_ref[1, place] = gate[CAP:]

    @pl.when(e == 1)
    def _():
        x_ref[0] = next_x[...]
        c_ref[0] = next_c[...]

    gate = gates_ref[e][:, :1]
    join_chunks(down_ref, w_ref.at[2], HOLDERS)
    x = x_ref[0]
    gate_pre = jnp.dot(x, w_ref[0], preferred_element_type=f32)
    up_pre = jnp.dot(x, w_ref[1], preferred_element_type=f32)
    back = contract(c_ref[0], down_ref[...], 1, 1)
    sig = 1.0 / (1.0 + jnp.exp(-gate_pre))
    silu = gate_pre * sig
    hidden = (silu * up_pre).astype(bf16)
    gate_grad = jnp.sum(back * hidden.astype(f32), axis=1, keepdims=True)
    grad = gate * back
    gate_pre_grad = (grad * up_pre * (sig + silu * (1.0 - sig))).astype(bf16)
    up_pre_grad = (grad * silu).astype(bf16)
    gate_ref[0] = gate_pre_grad
    up_ref[0] = up_pre_grad
    hid_ref[0] = (gate * hidden.astype(f32)).astype(bf16)
    row_grad = contract(gate_pre_grad, w_ref[0], 1, 1) + contract(up_pre_grad, w_ref[1], 1, 1)
    high = gate_grad.astype(bf16).astype(f32)
    lane = lax.broadcasted_iota(jnp.int32, (len(every) * CAP, LANES), 1)
    tail = jnp.where(lane == expert, high, 0.0)
    tail += jnp.where(lane == expert + EXPERTS, gate_grad - high, 0.0)
    for order, (group, source) in enumerate(every):
        place = slice(order * CAP, (order + 1) * CAP)
        back_outs[group][source, at, :width] = row_grad[place].astype(bf16)
        back_outs[group][source, at, width:] = tail[place].astype(bf16)

    @pl.when(e == 1)
    def _():
        for order, (group, source) in enumerate(every):
            back_outs[group][source] = contract(
                pick_ref[order], back_outs[group][source], 0, 0
            ).astype(bf16)


def home_kernel(
    context_ref, w_out_ref, tokens_ref, gain_ref, router_ref, member_ref, mid_ref, inverse_ref, payload_ref, gates_ref
):
    width = tokens_ref.shape[1]
    mid = tokens_ref[...].astype(f32) + contract(context_ref[...], w_out_ref[...], 0, 0)
    inverse = rms_inverse(mid)
    normed = (mid * inverse * gain_ref[...]).astype(bf16)
    mid_ref[...] = mid
    inverse_ref[...] = inverse
    payload_ref[:, :width] = normed
    member = member_ref[...] > 0
    logits = jnp.where(member, contract(normed, router_ref[...], 1, 1), masked_score)
    chosen = jnp.where(member, jnp.exp(logits - jnp.max(logits, axis=1, keepdims=True)), 0.0)
    gates = chosen / jnp.sum(chosen, axis=1, keepdims=True)
    gates_ref[...] = gates
    high = gates.astype(bf16).astype(f32)
    rest = jnp.zeros((gates.shape[0], LANES - 2 * gates.shape[1]), f32)
    payload_ref[:, width:] = jnp.concatenate([high, gates - high, rest], axis=1).astype(bf16)


def run_home(context, w_out, tokens, gain, router, member):
    rows, width = tokens.shape
    vmem = pl.BlockSpec(memory_space=pltpu.VMEM)
    return pl.pallas_call(
        home_kernel,
        out_shape=(
            jax.ShapeDtypeStruct((rows, width), f32),
            jax.ShapeDtypeStruct((rows, 1), f32),
            jax.ShapeDtypeStruct((rows, width + LANES), bf16),
            jax.ShapeDtypeStruct(member.shape, f32),
        ),
        in_specs=[vmem] * 6,
        out_specs=(vmem,) * 4,
        compiler_params=pltpu.CompilerParams(vmem_limit_bytes=24 * 1024 * 1024),
        cost_estimate=pl.CostEstimate(flops=1 << 30, bytes_accessed=8 << 20, transcendentals=0),
    )(context, w_out, tokens, gain, router, member)


def home_back_kernel(*refs):
    parts, refs = refs[:SIDE], refs[SIDE:]
    gates_ref, router_ref, mid_ref, inverse_ref, gain_ref, cot_ref, w_out_ref = refs[:7]
    grad_ref, low_ref, context_ref, logit_ref, norm_ref = refs[7:]
    width = mid_ref.shape[1]
    gates = gates_ref[...]
    experts = gates.shape[1]
    total = sum(ref[...].astype(f32) for ref in parts)
    tail = total[:, width:]
    gate_grad = tail[:, :experts] + tail[:, experts : 2 * experts]
    chosen = gates * (gate_grad - jnp.sum(gates * gate_grad, axis=1, keepdims=True))
    logit_grad = chosen.astype(bf16)
    logit_ref[...] = logit_grad
    normed_grad = total[:, :width] + jnp.dot(
        logit_grad, router_ref[...], preferred_element_type=f32
    )
    mid, inverse = mid_ref[...], inverse_ref[...]
    scaled = normed_grad * gain_ref[...]
    norm_ref[...] = jnp.sum(normed_grad * mid * inverse, axis=0, keepdims=True)
    mean = jnp.mean(scaled * mid, axis=1, keepdims=True)
    grad = cot_ref[...].astype(f32) + inverse * scaled - mid * (inverse * inverse * inverse) * mean
    grad_ref[...] = grad
    low = grad.astype(bf16)
    low_ref[...] = low
    context_ref[...] = contract(w_out_ref[...], low, 1, 1).astype(bf16)


def run_home_back(parts, gates, router, mid, inverse, gain, cotangent, w_out):
    rows, width = mid.shape
    vmem = pl.BlockSpec(memory_space=pltpu.VMEM)
    return pl.pallas_call(
        home_back_kernel,
        out_shape=(
            jax.ShapeDtypeStruct((rows, width), f32),
            jax.ShapeDtypeStruct((rows, width), bf16),
            jax.ShapeDtypeStruct((w_out.shape[0], rows), bf16),
            jax.ShapeDtypeStruct(gates.shape, bf16),
            jax.ShapeDtypeStruct((1, width), f32),
        ),
        in_specs=[vmem] * (SIDE + 7),
        out_specs=(vmem,) * 5,
        compiler_params=pltpu.CompilerParams(vmem_limit_bytes=24 * 1024 * 1024),
        cost_estimate=pl.CostEstimate(flops=1 << 30, bytes_accessed=8 << 20, transcendentals=0),
    )(*parts, gates, router, mid, inverse, gain, cotangent, w_out)


def join_chunks(to_ref, from_ref, holders):
    inner = from_ref.shape[1]
    rows = inner // HOLDERS
    chunks = to_ref.shape[1] // inner
    for holder in range(holders):
        for chunk in range(chunks):
            start = (holder * chunks + chunk) * rows
            to_ref[
                holder * rows : (holder + 1) * rows, chunk * inner : (chunk + 1) * inner
            ] = from_ref[start : start + rows, :]


def run_experts(first, rows, cots, weights):
    groups = len(rows)
    sources, tokens, padded = rows[0].shape
    width = padded - LANES
    inner = weights.shape[2]
    slots = groups * sources * CAP

    def once(columns):
        return pl.BlockSpec(
            (sources, tokens, columns), lambda e: (0, 0, 0), pipeline_mode=pl.Buffered(1)
        )

    def by_expert(*shape):
        return pl.BlockSpec(shape, lambda e: (e, 0, 0))

    acts = jax.ShapeDtypeStruct((2, slots, inner), bf16)
    wide = jax.ShapeDtypeStruct((2, slots, width), bf16)
    outs = pl.pallas_call(
        functools.partial(expert_kernel, groups),
        grid=(2,),
        out_shape=(
            *[jax.ShapeDtypeStruct((sources, tokens, padded), bf16)] * groups,
            wide,
            wide,
            acts,
            acts,
            acts,
            jax.ShapeDtypeStruct((groups * sources, 2 * CAP, tokens), bf16),
        ),
        in_specs=[pl.BlockSpec(memory_space=pltpu.SMEM)]
        + [once(padded)] * (2 * groups)
        + [by_expert(3, width, inner)],
        out_specs=(
            *[once(padded)] * groups,
            by_expert(1, slots, width),
            by_expert(1, slots, width),
            by_expert(1, slots, inner),
            by_expert(1, slots, inner),
            by_expert(1, slots, inner),
            pl.BlockSpec((groups * sources, 2 * CAP, tokens), lambda e: (0, 0, 0)),
        ),
        scratch_shapes=[
            pltpu.VMEM((inner, width), bf16),
            pltpu.VMEM((slots, width), bf16),
            pltpu.VMEM((slots, width), bf16),
            pltpu.VMEM((2, slots, LANES), f32),
        ],
        compiler_params=pltpu.CompilerParams(vmem_limit_bytes=56 * 1024 * 1024),
        cost_estimate=pl.CostEstimate(
            flops=2 * 2 * 6 * slots * width * inner, bytes_accessed=24 << 20, transcendentals=0
        ),
    )(first, *rows, *cots, weights)
    return outs[:groups], outs[groups:-1], outs[-1]


def mixture_kernel(groups, *refs):
    pick_refs, hid_refs = refs[:groups], refs[groups : 2 * groups]
    w_ref = refs[2 * groups]
    outs, down_ref = refs[2 * groups + 1 : -1], refs[-1]
    e = pl.program_id(0)
    at = pl.ds(pl.multiple_of(e * CAP, CAP), CAP)
    join_chunks(down_ref, w_ref.at[0], HOLDERS)
    sources = [
        (pick_ref, hid_ref, source)
        for pick_ref, hid_ref in zip(pick_refs, hid_refs)
        for source in range(pick_ref.shape[0])
    ]
    to = {}
    for order, (pick_ref, hid_ref, source) in enumerate(sources):
        to[order] = (outs[order // SIDE], order % SIDE, pick_ref, source)
    order = 0
    for pick_ref, hid_ref in zip(pick_refs, hid_refs):
        mixed = jnp.dot(hid_ref[0], down_ref[...], preferred_element_type=f32).astype(bf16)
        for source in range(pick_ref.shape[0]):
            out, place, _, _ = to[order]
            out[place, at] = mixed[source * CAP : (source + 1) * CAP]
            order += 1

    @pl.when(e == 1)
    def _():
        for out, place, pick_ref, source in to.values():
            out[place] = contract(pick_ref[source], out[place], 0, 0).astype(bf16)


def run_mixture(picks, hidden, weights):
    width, inner = weights.shape[1:]
    groups = len(picks)

    def once(shape):
        return pl.BlockSpec(shape, lambda e: (0, 0, 0), pipeline_mode=pl.Buffered(1))

    shapes = [(SIDE, picks[0].shape[2], width)] * SIDE
    return pl.pallas_call(
        functools.partial(mixture_kernel, groups),
        grid=(2,),
        out_shape=[jax.ShapeDtypeStruct(shape, bf16) for shape in shapes],
        in_specs=[once(pick.shape) for pick in picks]
        + [pl.BlockSpec((1,) + hid.shape[1:], lambda e: (e, 0, 0)) for hid in hidden]
        + [pl.BlockSpec((1, width, inner), lambda e: (3 * e + 2, 0, 0))],
        out_specs=[once(shape) for shape in shapes],
        scratch_shapes=[pltpu.VMEM((inner, width), bf16)],
        compiler_params=pltpu.CompilerParams(vmem_limit_bytes=40 * 1024 * 1024),
        cost_estimate=pl.CostEstimate(flops=1 << 32, bytes_accessed=1 << 20, transcendentals=0),
    )(*picks, *hidden, weights)


def weight_grad_kernel(groups, half_ref, *refs):
    x_refs, c_refs, gate_refs, up_refs, hid_refs = (
        refs[i * groups : (i + 1) * groups] for i in range(5)
    )
    *onto, out_ref = refs[5 * groups :]
    width = x_refs[0].shape[2]
    inner = gate_refs[0].shape[2]
    half = half_ref[0]
    rows = width // 2
    down_rows = inner // HOLDERS
    chunks = width // inner
    cols = pl.ds(pl.multiple_of(half * rows, LANES), rows)
    down_cols = pl.ds(pl.multiple_of(half * (inner // 2), LANES), inner // 2)
    gate = jnp.zeros((rows, inner), f32)
    up = jnp.zeros((rows, inner), f32)
    down = jnp.zeros((inner // 2, width), f32)
    for i in range(groups):
        x = x_refs[i][0, :, cols]
        gate += contract(x, gate_refs[i][0], 0, 0)
        up += contract(x, up_refs[i][0], 0, 0)

    def put(place, at, values):
        if onto:
            values = values + onto[0][place, at, :].astype(f32)
        out_ref[place, at, :] = values.astype(bf16)

    put(0, slice(0, rows), gate)
    put(1, slice(0, rows), up)
    for i in range(groups):
        down += contract(hid_refs[i][0, :, down_cols], c_refs[i][0], 0, 0)
    for holder in range(HOLDERS // 2):
        for chunk in range(chunks):
            start = (holder * chunks + chunk) * down_rows
            put(
                2,
                slice(start, start + down_rows),
                down[
                    holder * down_rows : (holder + 1) * down_rows,
                    chunk * inner : (chunk + 1) * inner,
                ],
            )


def run_weight_grads(half, saved, *onto):
    x, c, gate, up, hid = zip(*saved)
    width = x[0].shape[2]
    inner = gate[0].shape[2]
    operands = (*x, *c, *gate, *up, *hid)
    out_spec = pl.BlockSpec((3, width // 2, inner), lambda e: (e, 0, 0))
    return pl.pallas_call(
        functools.partial(weight_grad_kernel, len(saved)),
        grid=(2,),
        out_shape=jax.ShapeDtypeStruct((6, width // 2, inner), bf16),
        in_specs=[pl.BlockSpec(memory_space=pltpu.SMEM)]
        + [pl.BlockSpec((1,) + v.shape[1:], lambda e: (e, 0, 0)) for v in operands]
        + [out_spec] * len(onto),
        out_specs=out_spec,
        compiler_params=pltpu.CompilerParams(vmem_limit_bytes=52 * 1024 * 1024),
        cost_estimate=pl.CostEstimate(flops=1 << 28, bytes_accessed=1 << 20, transcendentals=0),
    )(half, *operands, *onto)


def sides_kernel(
    x_ref, grad_ref, w_ref, all_ref, context_ref, normed_ref, logit_ref, norm_ref, gain_ref, out_ref, shared_ref
):
    planes, tokens = x_ref.shape[0], normed_ref.shape[0]
    joined_width = grad_ref.shape[1]
    experts = logit_ref.shape[1]
    step = x_ref.shape[2] // 2
    for first in range(0, x_ref.shape[2], step):
        at = slice(first, first + step)
        rows = jnp.concatenate([x_ref[plane, :tokens, at] for plane in range(planes)], axis=0)
        joined = contract(grad_ref[...], rows, 0, 0)
        out_ref[:joined_width, at] = joined.astype(bf16)
        out_ref[joined_width:, at] = contract(context_ref[...], all_ref[:, at], 0, 0).astype(bf16)
        norm1 = jnp.sum(joined * w_ref[:, at].astype(f32), axis=0, keepdims=True) / gain_ref[:, at]
        norm2 = norm_ref[:, at]
        shared_ref[:experts, at] = contract(logit_ref[...], normed_ref[:, at], 0, 0).astype(bf16)
        shared_ref[experts : experts + 1, at] = norm2.astype(bf16)
        shared_ref[experts + 1 : experts + 2, at] = norm1.astype(bf16)


def run_sides(gathered, joined_grad, joined_rows, attention_all, context, normed_two, logits, norm_terms, gain):
    vmem = pl.BlockSpec(memory_space=pltpu.VMEM)
    width = gathered.shape[2]
    rows = joined_grad.shape[1] + context.shape[1]
    return pl.pallas_call(
        sides_kernel,
        out_shape=(
            jax.ShapeDtypeStruct((rows, width), bf16),
            jax.ShapeDtypeStruct((logits.shape[1] + 2, width), bf16),
        ),
        in_specs=[vmem] * 9,
        out_specs=(vmem, vmem),
        compiler_params=pltpu.CompilerParams(vmem_limit_bytes=40 * 1024 * 1024),
        cost_estimate=pl.CostEstimate(flops=1 << 31, bytes_accessed=12 << 20, transcendentals=0),
    )(gathered, joined_grad, joined_rows, attention_all, context, normed_two, logits, norm_terms, gain)


def local(
    tokens,
    segments,
    routes,
    norm1_gain,
    w_query,
    w_key,
    w_value,
    w_out,
    norm2_gain,
    w_router,
    w_gate,
    w_up,
    w_down,
    cotangent,
):
    tok_rows, width = tokens.shape
    seq_len = segments.shape[1]
    query_width = w_query.shape[1]
    kv_width = w_key.shape[1]
    joined_width = query_width + 2 * kv_width
    local_experts = w_gate.shape[0]
    experts = w_router.shape[1]
    owners = lax.axis_size("expert")
    planes = lax.axis_size("tensor")
    owner = lax.axis_index("expert")
    first_expert = owner * local_experts
    key_seg = segments[0]
    hidden_width = w_gate.shape[2]

    token_f32 = tokens.astype(f32)
    inverse_one = rms_inverse(token_f32)
    normed_low = (token_f32 * inverse_one * norm1_gain).astype(bf16)
    joined_rows = by_rows(jnp.concatenate([w_query.T, w_key.T, w_value.T], axis=0))
    core = lax.axis_index("dp")

    def half_of(rows):
        count = rows.shape[0] // 2
        return lax.dynamic_slice_in_dim(rows, core * count, count, 0)

    def both_halves(half):
        other = swap_cores(half)
        first, second = jnp.where(core == 0, half, other), jnp.where(core == 0, other, half)
        return jnp.concatenate([first, second], axis=1).reshape(-1, half.shape[2])

    gathered = lax.all_gather(
        by_rows(jnp.concatenate([normed_low, half_of(w_out)], axis=0)), "tensor", axis=0
    )

    expert_ids = jnp.arange(experts, dtype=jnp.int32)
    onehot = (routes[:, :, None] == expert_ids[None, None, :]).astype(f32)
    member = jnp.sum(onehot, axis=1)
    lower = (jnp.arange(tok_rows)[:, None] <= jnp.arange(tok_rows)[None, :]).astype(bf16)
    rank = jnp.einsum("te,tu->eu", member.astype(bf16), lower, preferred_element_type=f32)
    rank = jnp.where(member.T > 0, rank - 1.0, -1.0).astype(bf16)
    extra = jnp.pad(rank, ((0, tok_rows - experts), (0, LANES - tok_rows)))
    cot_payload = jnp.concatenate([cotangent, extra], axis=1)

    chunks = width // hidden_width
    down_rows = w_down.shape[1]
    part_rows = w_gate.shape[1]
    down_parts = w_down.reshape(local_experts, down_rows, chunks, hidden_width)
    down_parts = down_parts.transpose(0, 2, 1, 3).reshape(local_experts, part_rows, hidden_width)
    weights = jnp.stack([w_gate, w_up, down_parts], axis=1)
    weights = weights.reshape(3 * local_experts, part_rows, hidden_width)
    tables = rope_tables(seq_len)
    marks = segment_marks(key_seg)
    cot_parts = gather_second(gather_first(cot_payload))
    joined_half = by_rows(half_of(joined_rows))
    gathered, weights, joined_rows, joined_half, member, col, row, *cot_parts = together(
        gathered, weights, joined_rows, joined_half, by_rows(member), *marks, *cot_parts
    )
    marks = col, row
    weights_all = lax.all_gather(weights, ("dp", "tensor"), axis=1, tiled=True)
    context, context_blocks, qkv, half_out = run_attention(
        gathered, joined_rows, marks, tables
    )
    context_home = lax.all_to_all(context_blocks, "tensor", split_axis=0, concat_axis=0)
    w_out_all = both_halves(half_out)
    context_home, w_out_all, joined_half = together(context_home, w_out_all, joined_half)
    half_joined = lax.all_gather(joined_half, "tensor", axis=0)
    router = by_rows(w_router.T)
    mid, inverse_two, payload, gates = run_home(
        context_home.reshape(planes * query_width, tok_rows),
        w_out_all,
        tokens,
        norm2_gain[None],
        router,
        member,
    )
    line = gather_first(payload)
    before, behind = (cross(line, 1, step) for step in STEPS[1:3])

    first_expert = first_expert.astype(jnp.int32).reshape(1)
    def compute(rows, cots):
        return run_experts(first_expert, rows, cots, weights_all)

    own = compute([line], cot_parts[:1])
    line, before, behind, *own_saved = together(line, before, behind, *own[1])
    far = cross(line, 1, STEPS[3])
    near = compute([before, behind], cot_parts[1:3])
    far, *near_saved = together(far, *near[1])
    last = compute([far], cot_parts[3:])
    done = [(*own[0], *near[0], *last[0]), (own_saved, near_saved, last[1])]
    back_line = scatter_first(done[0])
    mix_parts = run_mixture(
        [own[2], near[2], last[2]], [own_saved[4], near_saved[4], last[1][4]], weights_all
    )
    given = run_weight_grads((1 - core).astype(jnp.int32).reshape(1), done[1])
    n_line = len(back_line)
    *both, given, half_joined = together(*back_line, *mix_parts, given, half_joined)
    back_line, mix_parts = sum_first(both[:n_line]), both[n_line:]
    back_home = scatter_second(back_line)
    back_home[1], received = together(back_home[1], swap_cores(given))

    mid_grad, attention_low, context_grad, logit_grad, norm2_part = run_home_back(
        back_home, gates, router, mid, inverse_two, norm2_gain[None], cotangent, w_out_all
    )
    received, *mix_parts, context_grad, logit_grad = together(
        received, *mix_parts, context_grad, logit_grad
    )
    mix_arrived = scatter_first(mix_parts)
    kept = run_weight_grads(core.astype(jnp.int32).reshape(1), done[1], received)
    context_grad = lax.all_to_all(
        context_grad.reshape(planes, query_width, tok_rows), "tensor", split_axis=0, concat_axis=0
    )
    context_grad, kept = together(context_grad, kept)
    joined_grad, joined_blocks = run_attention_back(qkv, context_grad, marks, tables)
    joined_home = lax.all_to_all(joined_blocks, "tensor", split_axis=0, concat_axis=0)
    attention_all = lax.all_gather(attention_low, "tensor", axis=0, tiled=True)
    sides, shared = run_sides(
        gathered,
        joined_grad,
        joined_rows,
        attention_all,
        context,
        payload,
        logit_grad,
        norm2_part,
        norm1_gain[None],
    )

    share = sides.shape[0] // (2 * owners)
    shared_shape = shared.shape
    shared_rows = shared.size // LANES
    shared = shared.reshape(shared_rows, LANES)
    shared = jnp.pad(shared, ((0, 2 * owners * share - shared_rows), (0, 0)))
    blocks = jnp.concatenate(
        [sides.reshape(2, owners, share, width), shared.reshape(2, owners, share, LANES)], axis=3
    )
    blocks, joined_home, kept, *mix_arrived = together(blocks, joined_home, kept, *mix_arrived)
    weight_sum = lax.psum_scatter(kept, "tensor", scatter_dimension=1, tiled=True)

    def of_core(which):
        return lax.dynamic_index_in_dim(blocks, which, 0, keepdims=False)

    part = of_core(core).astype(f32) + swap_cores(of_core(1 - core)).astype(f32)
    arrived = lax.all_to_all(part.astype(bf16), "expert", split_axis=0, concat_axis=0)

    def rows_of(which):
        count = joined_width // 2
        rows = lax.dynamic_slice_in_dim(joined_home, which * count, count, 1)
        return rows.reshape(-1, tok_rows)

    normed_one_grad = contract(rows_of(core), half_joined.reshape(-1, width), 0, 0)
    normed_one_grad += contract(
        rows_of(1 - core), swap_cores(half_joined).reshape(-1, width), 0, 0
    )
    arrived, normed_one_grad, *mix_line = together(
        arrived, normed_one_grad, *sum_first(mix_arrived)
    )
    total = jnp.sum(arrived.astype(f32), axis=0)
    total = jnp.concatenate([total[:, :width], ring_sum(total[:, width:])], axis=1).astype(bf16)
    spread = lax.all_to_all(
        jnp.broadcast_to(total[None], arrived.shape), "expert", split_axis=0, concat_axis=0
    )
    mixture = sum(part.astype(f32) for part in scatter_second(mix_line))
    spread, mixture = together(by_rows(spread), mixture)
    output = (mid + mixture).astype(bf16)
    spread, weight_sum = together(spread, weight_sum)
    other = swap_cores(spread)
    first, second = jnp.where(core == 0, spread, other), jnp.where(core == 0, other, spread)
    shared = jnp.concatenate([first, second], axis=0)[:, :, width:].reshape(-1, LANES)
    shared = shared[:shared_rows].astype(f32).reshape(shared_shape)
    first = first[:, :, :width].reshape(-1, width)
    second = second[:, :, :width].reshape(-1, width)
    query_sum = first[:query_width].astype(f32).T
    key_sum = first[query_width:].astype(f32).T
    value_sum = second[:kv_width].astype(f32).T
    out_sum = second[kv_width:].astype(f32)
    weight_sum = weight_sum.reshape(local_experts, 3, part_rows, hidden_width)
    w_gate_grad = weight_sum[:, 0].astype(f32)
    w_up_grad = weight_sum[:, 1].astype(f32)
    w_down_grad = weight_sum[:, 2].reshape(local_experts, chunks, down_rows, hidden_width)
    w_down_grad = w_down_grad.transpose(0, 2, 1, 3).reshape(local_experts, down_rows, width)
    w_down_grad = w_down_grad.astype(f32)
    input_part, _ = rms_backward(token_f32, inverse_one, norm1_gain, normed_one_grad)
    input_grad = mid_grad + input_part
    return (
        output,
        input_grad,
        shared[experts + 1],
        query_sum,
        key_sum,
        value_sum,
        out_sum,
        shared[experts],
        shared[:experts].T,
        w_gate_grad,
        w_up_grad,
        w_down_grad,
    )


def solution(mesh):
    rows = P(("dp", "expert", "tensor"), None)
    columns = P(None, "tensor")
    experts = P("expert", ("dp", "tensor"), None)
    return jax.shard_map(
        local,
        mesh=mesh,
        in_specs=(
            rows,
            P(("dp", "expert"), None),
            rows,
            P(),
            columns,
            columns,
            columns,
            P("tensor", None),
            P(),
            P(),
            experts,
            experts,
            experts,
            rows,
        ),
        out_specs=(
            rows,
            rows,
            P(),
            columns,
            columns,
            columns,
            P("tensor", None),
            P(),
            P(),
            experts,
            experts,
            experts,
        ),
        check_vma=False,
    )
```

```python
import functools

import jax
import jax.numpy as jnp
import numpy as np
from jax import lax
from jax.experimental import pallas as pl
from jax.experimental.layout import Layout, with_layout_constraint
from jax.experimental.pallas import tpu as pltpu
from jax.sharding import PartitionSpec as P

HEAD_DIM = 64
HALF = HEAD_DIM // 2
TOP = 8
CAP = 64
EXPERTS = 32
HOLDERS = 16
VMEM_BYTES = 57 * 1024 * 1024
LANES = 128

epsilon_norm = 1e-06
rope_theta = 10000.0
masked_score = -1e30
QUERY_ROWS = 512
SCALE = HEAD_DIM ** (-0.5)
f32 = jnp.float32
bf16 = jnp.bfloat16


def rms_inverse(values):
    return lax.rsqrt(jnp.mean(values * values, axis=-1, keepdims=True) + epsilon_norm)


def rms_backward(values, inverse, norm_gain, grad_out):
    scaled = grad_out * norm_gain
    grad_in = inverse * scaled - values * (inverse * inverse * inverse) * jnp.mean(
        scaled * values, axis=-1, keepdims=True
    )
    return (grad_in, grad_out * values * inverse)


def dot32(left, right):
    return jnp.dot(left, right, preferred_element_type=f32)


SIDE = 4
STEPS = (0, 1, -1, 2)


def by_rows(values):
    return with_layout_constraint(values, Layout(major_to_minor=tuple(range(values.ndim))))


def cross(values, stage, step):
    pairs = []
    plane = SIDE * SIDE
    for core in range(2):
        for x in range(SIDE):
            for y in range(SIDE):
                if core == stage:
                    to = x * SIDE + (y + step) % SIDE
                else:
                    to = (x + step) % SIDE * SIDE + y
                pairs.append((core * plane + x * SIDE + y, core * plane + to))
    return lax.ppermute(values, ("dp", "expert"), pairs)


def gather_first(values):
    values = by_rows(values)
    line = jnp.stack([values] + [cross(values, 0, step) for step in STEPS[1:]])
    return by_rows(line)


def gather_second(line):
    return [line] + [cross(line, 1, step) for step in STEPS[1:]]


def scatter_first(parts):
    return [parts[0]] + [
        by_rows(cross(part, 1, -step)) for part, step in zip(parts[1:], STEPS[1:])
    ]


def sum_kernel(*refs):
    arrived, outs = refs[:SIDE], refs[SIDE:]
    total = sum(ref[0].astype(f32) for ref in arrived).astype(bf16)
    for place, out in enumerate(outs):

        @pl.when(pl.program_id(0) == place)
        def _():
            out[...] = total


def sum_first(arrived):
    rows, columns = arrived[0].shape[1:]
    return pl.pallas_call(
        sum_kernel,
        grid=(SIDE,),
        out_shape=[jax.ShapeDtypeStruct((rows, columns), bf16)] * SIDE,
        in_specs=[pl.BlockSpec((1, rows, columns), lambda place: (place, 0, 0))] * SIDE,
        out_specs=[pl.BlockSpec((rows, columns), lambda place: (0, 0))] * SIDE,
        compiler_params=pltpu.CompilerParams(vmem_limit_bytes=24 * 1024 * 1024),
        cost_estimate=pl.CostEstimate(flops=1 << 22, bytes_accessed=8 << 20, transcendentals=0),
    )(*arrived)


def scatter_second(line):
    return [line[0]] + [
        by_rows(cross(part, 0, -step)) for part, step in zip(line[1:], STEPS[1:])
    ]


def ring_sum(values):
    size = lax.axis_size("tensor")
    arrived = [
        lax.ppermute(values, "tensor", [(i, (i + step) % size) for i in range(size)])
        for step in range(1, size)
    ]
    return sum(arrived, values)


def together(*values):
    return lax.optimization_barrier(values)


def swap_cores(values):
    return lax.ppermute(values, "dp", [(0, 1), (1, 0)])


def contract(left, right, left_dim, right_dim):
    return lax.dot_general(
        left, right, (((left_dim,), (right_dim,)), ((), ())), preferred_element_type=f32
    )


def allowed(rows, first, wide, col_ref, row_ref):
    query = first + lax.broadcasted_iota(jnp.int32, (rows, wide), 0)
    key = lax.broadcasted_iota(jnp.int32, (rows, wide), 1)
    return (key <= query) & (col_ref[first : first + rows, :] == row_ref[:, :wide])


def probabilities(query, key, mask):
    scores = jnp.where(mask, contract(query, key, 1, 1), masked_score)
    weights = jnp.exp(scores - jnp.max(scores, axis=1, keepdims=True))
    return weights * (1.0 / jnp.sum(weights, axis=1, keepdims=True))


def turn(values, cosine, sine):
    size = values.shape[1]
    first = lax.broadcasted_iota(jnp.int32, values.shape, 1) % HEAD_DIM < HALF
    other = jnp.where(
        first, -pltpu.roll(values, size - HALF, 1), pltpu.roll(values, HALF, 1)
    )
    tables = [jnp.concatenate([table] * (size // LANES), axis=1) for table in (cosine, sine)]
    return values * tables[0] + other * tables[1]


def attention_kernel(
    x_ref, w_ref, col_ref, row_ref, cos_ref, sin_ref, out_ref, turned_ref, qkv_ref, rest_ref
):
    seq_len = out_ref.shape[0]
    tokens = turned_ref.shape[2]
    rest_ref[...] = x_ref[:, tokens:, :]
    heads = out_ref.shape[1] // HEAD_DIM
    last = (heads + 1) * HEAD_DIM
    step = QUERY_ROWS
    for first in range(0, seq_len, step):
        at = slice(first, first + step)
        wide = first + step
        blocks = range(first // tokens, wide // tokens)
        rows = jnp.concatenate([x_ref[block, :tokens, :] for block in blocks], axis=0)
        joined = contract(rows, w_ref[...], 1, 1)
        turned_part = turn(joined[:, :last], cos_ref[at, :], sin_ref[at, :])
        qkv_ref[at, :last] = turned_part.astype(bf16)
        qkv_ref[at, last:] = joined[:, last:].astype(bf16)
        mask = allowed(step, first, wide, col_ref, row_ref)
        key = qkv_ref[:wide, heads * HEAD_DIM : last]
        value = qkv_ref[:wide, last:]
        for head in range(heads):
            place = slice(head * HEAD_DIM, (head + 1) * HEAD_DIM)
            query = qkv_ref[at, place] * SCALE
            probs = probabilities(query, key, mask).astype(bf16)
            context = jnp.dot(probs, value, preferred_element_type=f32)
            out_ref[at, place] = context.astype(bf16)
            for block in range(step // tokens):
                turned_ref[first // tokens + block, place, :] = context[
                    block * tokens : (block + 1) * tokens
                ].T.astype(bf16)


def attention_back_kernel(
    qkv_ref, grad_ref, col_ref, row_ref, cos_ref, sin_ref, out_ref, turned_ref, key_sum, value_sum
):
    seq_len = qkv_ref.shape[0]
    heads = grad_ref.shape[1] // HEAD_DIM
    tokens = grad_ref.shape[2]
    last = (heads + 1) * HEAD_DIM
    step = QUERY_ROWS
    for first in reversed(range(0, seq_len, step)):
        at = slice(first, first + step)
        wide = first + step
        mask = allowed(step, first, wide, col_ref, row_ref)
        key = qkv_ref[:wide, heads * HEAD_DIM : last]
        value = qkv_ref[:wide, last:]
        key_grad = jnp.zeros((wide, HEAD_DIM), f32)
        value_grad = jnp.zeros((wide, HEAD_DIM), f32)
        query_grads = []
        for head in range(heads):
            place = slice(head * HEAD_DIM, (head + 1) * HEAD_DIM)
            query = qkv_ref[at, place] * SCALE
            grad = [
                grad_ref[first // tokens + block, place, :].astype(f32).T.astype(bf16)
                for block in range(step // tokens)
            ]
            grad = jnp.concatenate(grad, axis=0)
            probs = probabilities(query, key, mask)
            probs_grad = contract(grad, value, 1, 1)
            row_dot = jnp.sum(probs * probs_grad, axis=1, keepdims=True)
            score_grad = (probs * (probs_grad - row_dot)).astype(bf16)
            query_grads.append(jnp.dot(score_grad, key, preferred_element_type=f32) * SCALE)
            key_grad += contract(score_grad, query, 0, 0)
            value_grad += contract(probs.astype(bf16), grad, 0, 0)
        if wide == seq_len:
            key_sum[...] = key_grad
            value_sum[...] = value_grad
        else:
            key_sum[:wide, :] += key_grad
            value_sum[:wide, :] += value_grad
        both = jnp.concatenate(query_grads + [key_sum[at, :]], axis=1)
        both = turn(both, cos_ref[at, :], -sin_ref[at, :])
        out_ref[at, :last] = both.astype(bf16)
        out_ref[at, last:] = value_sum[at, :].astype(bf16)
        for block in range(step // tokens):
            part = slice(block * tokens, (block + 1) * tokens)
            to = first // tokens + block
            turned_ref[to, :last, :] = both[part].T.astype(bf16)
            turned_ref[to, last:, :] = value_sum[first : first + step, :][part].T.astype(bf16)


def run_attention(gathered, joined_rows, marks, tables):
    planes = gathered.shape[0]
    seq_len = marks[0].shape[0]
    joined_width = joined_rows.shape[0]
    query_width = joined_width - 2 * HEAD_DIM
    vmem = pl.BlockSpec(memory_space=pltpu.VMEM)
    return pl.pallas_call(
        attention_kernel,
        out_shape=(
            jax.ShapeDtypeStruct((seq_len, query_width), bf16),
            jax.ShapeDtypeStruct((planes, query_width, seq_len // planes), bf16),
            jax.ShapeDtypeStruct((seq_len, joined_width), bf16),
            jax.ShapeDtypeStruct(
                (planes, gathered.shape[1] - seq_len // planes, gathered.shape[2]), bf16
            ),
        ),
        in_specs=[vmem] * 6,
        out_specs=(vmem,) * 4,
        compiler_params=pltpu.CompilerParams(vmem_limit_bytes=VMEM_BYTES),
        cost_estimate=pl.CostEstimate(
            flops=4 << 30, bytes_accessed=8 << 20, transcendentals=0
        ),
    )(gathered, joined_rows, *marks, *tables)


def run_attention_back(qkv, context_grad, marks, tables):
    seq_len, joined_width = qkv.shape
    planes = context_grad.shape[0]
    vmem = pl.BlockSpec(memory_space=pltpu.VMEM)
    return pl.pallas_call(
        attention_back_kernel,
        out_shape=(
            jax.ShapeDtypeStruct((seq_len, joined_width), bf16),
            jax.ShapeDtypeStruct((planes, joined_width, seq_len // planes), bf16),
        ),
        in_specs=[vmem] * 6,
        out_specs=(vmem, vmem),
        scratch_shapes=[pltpu.VMEM((seq_len, HEAD_DIM), f32)] * 2,
        compiler_params=pltpu.CompilerParams(vmem_limit_bytes=VMEM_BYTES),
        cost_estimate=pl.CostEstimate(
            flops=1 << 28, bytes_accessed=1 << 20, transcendentals=0
        ),
    )(qkv, context_grad, *marks, *tables)


def rope_tables(seq_len):
    frequency = np.float32(rope_theta) ** (np.arange(HALF, dtype=np.float32) * np.float32(-2.0 / HEAD_DIM))
    angles = np.arange(seq_len, dtype=np.float32)[:, None] * frequency.astype(np.float32)[None, :]
    angles = np.tile(angles, (1, LANES // HALF))
    return jnp.asarray(np.cos(angles)), jnp.asarray(np.sin(angles))


def segment_marks(key_seg):
    marks = jnp.where(key_seg == 0, -1 - jnp.arange(key_seg.shape[0], dtype=jnp.int32), key_seg)
    return marks[:, None], marks[None, :]


def expert_kernel(groups, first_ref, *refs):
    rows_refs, cots_refs = refs[:groups], refs[groups : 2 * groups]
    w_ref = refs[2 * groups]
    back_outs = refs[2 * groups + 1 : 3 * groups + 1]
    x_ref, c_ref, gate_ref, up_ref, hid_ref, pick_ref = refs[3 * groups + 1 : 3 * groups + 7]
    down_ref, next_x, next_c, gates_ref = refs[3 * groups + 7 :]
    sources, tokens, _ = rows_refs[0].shape
    width = x_ref.shape[2]
    e = pl.program_id(0)
    expert = first_ref[0] + e
    at = pl.ds(pl.multiple_of(e * CAP, CAP), CAP)
    every = [(group, source) for group in range(groups) for source in range(sources)]

    @pl.when(e == 0)
    def _():
        pair = 2 * CAP
        lane = lax.broadcasted_iota(jnp.int32, (pair, LANES), 1)
        expert_of = expert + lax.broadcasted_iota(jnp.int32, (pair, LANES), 0) // CAP
        own = (lane == expert_of) | (lane == expert_of + EXPERTS)
        row_id = lax.broadcasted_iota(jnp.int32, (EXPERTS, tokens), 0)
        slot = lax.broadcasted_iota(jnp.int32, (pair, tokens), 0)
        place_of = jnp.where(slot < CAP, slot, slot - CAP).astype(f32)
        for order, (group, source) in enumerate(every):
            table = cots_refs[group][source, :EXPERTS, width:].astype(f32)
            ranks = [
                jnp.sum(jnp.where(row_id == expert + i, table, 0.0), axis=0, keepdims=True)
                for i in range(2)
            ]
            pick = (jnp.where(slot < CAP, ranks[0], ranks[1]) == place_of).astype(bf16)
            pick_ref[order] = pick
            rows = jnp.dot(pick, rows_refs[group][source], preferred_element_type=f32)
            cots = jnp.dot(pick, cots_refs[group][source, :, :width], preferred_element_type=f32)
            gate = jnp.sum(jnp.where(own, rows[:, width:], 0.0), axis=1, keepdims=True)
            gate = jnp.broadcast_to(gate, (pair, LANES))
            place = slice(order * CAP, (order + 1) * CAP)
            x_ref[0, place] = rows[:CAP, :width].astype(bf16)
            c_ref[0, place] = cots[:CAP].astype(bf16)
            gates_ref[0, place] = gate[:CAP]
            next_x[place] = rows[CAP:, :width].astype(bf16)
            next_c[place] = cots[CAP:].astype(bf16)
            gates_ref[1, place] = gate[CAP:]

    @pl.when(e == 1)
    def _():
        x_ref[0] = next_x[...]
        c_ref[0] = next_c[...]

    gate = gates_ref[e][:, :1]
    join_chunks(down_ref, w_ref.at[2], HOLDERS)
    x = x_ref[0]
    gate_pre = jnp.dot(x, w_ref[0], preferred_element_type=f32)
    up_pre = jnp.dot(x, w_ref[1], preferred_element_type=f32)
    back = contract(c_ref[0], down_ref[...], 1, 1)
    sig = 1.0 / (1.0 + jnp.exp(-gate_pre))
    silu = gate_pre * sig
    hidden = (silu * up_pre).astype(bf16)
    gate_grad = jnp.sum(back * hidden.astype(f32), axis=1, keepdims=True)
    grad = gate * back
    gate_pre_grad = (grad * up_pre * (sig + silu * (1.0 - sig))).astype(bf16)
    up_pre_grad = (grad * silu).astype(bf16)
    gate_ref[0] = gate_pre_grad
    up_ref[0] = up_pre_grad
    hid_ref[0] = (gate * hidden.astype(f32)).astype(bf16)
    row_grad = contract(gate_pre_grad, w_ref[0], 1, 1) + contract(up_pre_grad, w_ref[1], 1, 1)
    high = gate_grad.astype(bf16).astype(f32)
    lane = lax.broadcasted_iota(jnp.int32, (len(every) * CAP, LANES), 1)
    tail = jnp.where(lane == expert, high, 0.0)
    tail += jnp.where(lane == expert + EXPERTS, gate_grad - high, 0.0)
    for order, (group, source) in enumerate(every):
        place = slice(order * CAP, (order + 1) * CAP)
        back_outs[group][source, at, :width] = row_grad[place].astype(bf16)
        back_outs[group][source, at, width:] = tail[place].astype(bf16)

    @pl.when(e == 1)
    def _():
        for order, (group, source) in enumerate(every):
            back_outs[group][source] = contract(
                pick_ref[order], back_outs[group][source], 0, 0
            ).astype(bf16)


def home_kernel(
    context_ref, w_out_ref, tokens_ref, gain_ref, router_ref, member_ref, mid_ref, inverse_ref, payload_ref, gates_ref
):
    width = tokens_ref.shape[1]
    mid = tokens_ref[...].astype(f32) + contract(context_ref[...], w_out_ref[...], 0, 0)
    inverse = rms_inverse(mid)
    normed = (mid * inverse * gain_ref[...]).astype(bf16)
    mid_ref[...] = mid
    inverse_ref[...] = inverse
    payload_ref[:, :width] = normed
    member = member_ref[...] > 0
    logits = jnp.where(member, contract(normed, router_ref[...], 1, 1), masked_score)
    chosen = jnp.where(member, jnp.exp(logits - jnp.max(logits, axis=1, keepdims=True)), 0.0)
    gates = chosen / jnp.sum(chosen, axis=1, keepdims=True)
    gates_ref[...] = gates
    high = gates.astype(bf16).astype(f32)
    rest = jnp.zeros((gates.shape[0], LANES - 2 * gates.shape[1]), f32)
    payload_ref[:, width:] = jnp.concatenate([high, gates - high, rest], axis=1).astype(bf16)


def run_home(context, w_out, tokens, gain, router, member):
    rows, width = tokens.shape
    vmem = pl.BlockSpec(memory_space=pltpu.VMEM)
    return pl.pallas_call(
        home_kernel,
        out_shape=(
            jax.ShapeDtypeStruct((rows, width), f32),
            jax.ShapeDtypeStruct((rows, 1), f32),
            jax.ShapeDtypeStruct((rows, width + LANES), bf16),
            jax.ShapeDtypeStruct(member.shape, f32),
        ),
        in_specs=[vmem] * 6,
        out_specs=(vmem,) * 4,
        compiler_params=pltpu.CompilerParams(vmem_limit_bytes=24 * 1024 * 1024),
        cost_estimate=pl.CostEstimate(flops=1 << 30, bytes_accessed=8 << 20, transcendentals=0),
    )(context, w_out, tokens, gain, router, member)


def home_back_kernel(*refs):
    parts, refs = refs[:SIDE], refs[SIDE:]
    gates_ref, router_ref, mid_ref, inverse_ref, gain_ref, cot_ref, w_out_ref = refs[:7]
    grad_ref, low_ref, context_ref, logit_ref, norm_ref = refs[7:]
    width = mid_ref.shape[1]
    gates = gates_ref[...]
    experts = gates.shape[1]
    total = sum(ref[...].astype(f32) for ref in parts)
    tail = total[:, width:]
    gate_grad = tail[:, :experts] + tail[:, experts : 2 * experts]
    chosen = gates * (gate_grad - jnp.sum(gates * gate_grad, axis=1, keepdims=True))
    logit_grad = chosen.astype(bf16)
    logit_ref[...] = logit_grad
    normed_grad = total[:, :width] + jnp.dot(
        logit_grad, router_ref[...], preferred_element_type=f32
    )
    mid, inverse = mid_ref[...], inverse_ref[...]
    scaled = normed_grad * gain_ref[...]
    norm_ref[...] = jnp.sum(normed_grad * mid * inverse, axis=0, keepdims=True)
    mean = jnp.mean(scaled * mid, axis=1, keepdims=True)
    grad = cot_ref[...].astype(f32) + inverse * scaled - mid * (inverse * inverse * inverse) * mean
    grad_ref[...] = grad
    low = grad.astype(bf16)
    low_ref[...] = low
    context_ref[...] = contract(w_out_ref[...], low, 1, 1).astype(bf16)


def run_home_back(parts, gates, router, mid, inverse, gain, cotangent, w_out):
    rows, width = mid.shape
    vmem = pl.BlockSpec(memory_space=pltpu.VMEM)
    return pl.pallas_call(
        home_back_kernel,
        out_shape=(
            jax.ShapeDtypeStruct((rows, width), f32),
            jax.ShapeDtypeStruct((rows, width), bf16),
            jax.ShapeDtypeStruct((w_out.shape[0], rows), bf16),
            jax.ShapeDtypeStruct(gates.shape, bf16),
            jax.ShapeDtypeStruct((1, width), f32),
        ),
        in_specs=[vmem] * (SIDE + 7),
        out_specs=(vmem,) * 5,
        compiler_params=pltpu.CompilerParams(vmem_limit_bytes=24 * 1024 * 1024),
        cost_estimate=pl.CostEstimate(flops=1 << 30, bytes_accessed=8 << 20, transcendentals=0),
    )(*parts, gates, router, mid, inverse, gain, cotangent, w_out)


def join_chunks(to_ref, from_ref, holders):
    inner = from_ref.shape[1]
    rows = inner // HOLDERS
    chunks = to_ref.shape[1] // inner
    for holder in range(holders):
        for chunk in range(chunks):
            start = (holder * chunks + chunk) * rows
            to_ref[
                holder * rows : (holder + 1) * rows, chunk * inner : (chunk + 1) * inner
            ] = from_ref[start : start + rows, :]


def run_experts(first, rows, cots, weights):
    groups = len(rows)
    sources, tokens, padded = rows[0].shape
    width = padded - LANES
    inner = weights.shape[2]
    slots = groups * sources * CAP

    def once(columns):
        return pl.BlockSpec(
            (sources, tokens, columns), lambda e: (0, 0, 0), pipeline_mode=pl.Buffered(1)
        )

    def by_expert(*shape):
        return pl.BlockSpec(shape, lambda e: (e, 0, 0))

    acts = jax.ShapeDtypeStruct((2, slots, inner), bf16)
    wide = jax.ShapeDtypeStruct((2, slots, width), bf16)
    outs = pl.pallas_call(
        functools.partial(expert_kernel, groups),
        grid=(2,),
        out_shape=(
            *[jax.ShapeDtypeStruct((sources, tokens, padded), bf16)] * groups,
            wide,
            wide,
            acts,
            acts,
            acts,
            jax.ShapeDtypeStruct((groups * sources, 2 * CAP, tokens), bf16),
        ),
        in_specs=[pl.BlockSpec(memory_space=pltpu.SMEM)]
        + [once(padded)] * (2 * groups)
        + [by_expert(3, width, inner)],
        out_specs=(
            *[once(padded)] * groups,
            by_expert(1, slots, width),
            by_expert(1, slots, width),
            by_expert(1, slots, inner),
            by_expert(1, slots, inner),
            by_expert(1, slots, inner),
            pl.BlockSpec((groups * sources, 2 * CAP, tokens), lambda e: (0, 0, 0)),
        ),
        scratch_shapes=[
            pltpu.VMEM((inner, width), bf16),
            pltpu.VMEM((slots, width), bf16),
            pltpu.VMEM((slots, width), bf16),
            pltpu.VMEM((2, slots, LANES), f32),
        ],
        compiler_params=pltpu.CompilerParams(vmem_limit_bytes=VMEM_BYTES),
        cost_estimate=pl.CostEstimate(
            flops=2 * 2 * 6 * slots * width * inner, bytes_accessed=24 << 20, transcendentals=0
        ),
    )(first, *rows, *cots, weights)
    return outs[:groups], outs[groups:-1], outs[-1]


def mixture_kernel(groups, *refs):
    pick_refs, hid_refs = refs[:groups], refs[groups : 2 * groups]
    w_ref = refs[2 * groups]
    outs, down_ref = refs[2 * groups + 1 : -1], refs[-1]
    e = pl.program_id(0)
    at = pl.ds(pl.multiple_of(e * CAP, CAP), CAP)
    join_chunks(down_ref, w_ref.at[0], HOLDERS)
    sources = [
        (pick_ref, hid_ref, source)
        for pick_ref, hid_ref in zip(pick_refs, hid_refs)
        for source in range(pick_ref.shape[0])
    ]
    to = {}
    for order, (pick_ref, hid_ref, source) in enumerate(sources):
        to[order] = (outs[order // SIDE], order % SIDE, pick_ref, source)
    order = 0
    for pick_ref, hid_ref in zip(pick_refs, hid_refs):
        mixed = jnp.dot(hid_ref[0], down_ref[...], preferred_element_type=f32).astype(bf16)
        for source in range(pick_ref.shape[0]):
            out, place, _, _ = to[order]
            out[place, at] = mixed[source * CAP : (source + 1) * CAP]
            order += 1

    @pl.when(e == 1)
    def _():
        for out, place, pick_ref, source in to.values():
            out[place] = contract(pick_ref[source], out[place], 0, 0).astype(bf16)


def run_mixture(picks, hidden, weights):
    width, inner = weights.shape[1:]
    groups = len(picks)

    def once(shape):
        return pl.BlockSpec(shape, lambda e: (0, 0, 0), pipeline_mode=pl.Buffered(1))

    shapes = [(SIDE, picks[0].shape[2], width)] * SIDE
    return pl.pallas_call(
        functools.partial(mixture_kernel, groups),
        grid=(2,),
        out_shape=[jax.ShapeDtypeStruct(shape, bf16) for shape in shapes],
        in_specs=[once(pick.shape) for pick in picks]
        + [pl.BlockSpec((1,) + hid.shape[1:], lambda e: (e, 0, 0)) for hid in hidden]
        + [pl.BlockSpec((1, width, inner), lambda e: (3 * e + 2, 0, 0))],
        out_specs=[once(shape) for shape in shapes],
        scratch_shapes=[pltpu.VMEM((inner, width), bf16)],
        compiler_params=pltpu.CompilerParams(vmem_limit_bytes=VMEM_BYTES),
        cost_estimate=pl.CostEstimate(flops=1 << 32, bytes_accessed=1 << 20, transcendentals=0),
    )(*picks, *hidden, weights)


def weight_grad_kernel(groups, half_ref, *refs):
    x_refs, c_refs, gate_refs, up_refs, hid_refs = (
        refs[i * groups : (i + 1) * groups] for i in range(5)
    )
    *onto, out_ref = refs[5 * groups :]
    width = x_refs[0].shape[2]
    inner = gate_refs[0].shape[2]
    half = half_ref[0]
    rows = width // 2
    down_rows = inner // HOLDERS
    chunks = width // inner
    cols = pl.ds(pl.multiple_of(half * rows, LANES), rows)
    down_cols = pl.ds(pl.multiple_of(half * (inner // 2), LANES), inner // 2)
    gate = jnp.zeros((rows, inner), f32)
    up = jnp.zeros((rows, inner), f32)
    down = jnp.zeros((inner // 2, width), f32)
    for i in range(groups):
        x = x_refs[i][0, :, cols]
        gate += contract(x, gate_refs[i][0], 0, 0)
        up += contract(x, up_refs[i][0], 0, 0)

    def put(place, at, values):
        if onto:
            values = values + onto[0][place, at, :].astype(f32)
        out_ref[place, at, :] = values.astype(bf16)

    put(0, slice(0, rows), gate)
    put(1, slice(0, rows), up)
    for i in range(groups):
        down += contract(hid_refs[i][0, :, down_cols], c_refs[i][0], 0, 0)
    for holder in range(HOLDERS // 2):
        for chunk in range(chunks):
            start = (holder * chunks + chunk) * down_rows
            put(
                2,
                slice(start, start + down_rows),
                down[
                    holder * down_rows : (holder + 1) * down_rows,
                    chunk * inner : (chunk + 1) * inner,
                ],
            )


def run_weight_grads(half, saved, *onto):
    x, c, gate, up, hid = zip(*saved)
    width = x[0].shape[2]
    inner = gate[0].shape[2]
    operands = (*x, *c, *gate, *up, *hid)
    out_spec = pl.BlockSpec((3, width // 2, inner), lambda e: (e, 0, 0))
    return pl.pallas_call(
        functools.partial(weight_grad_kernel, len(saved)),
        grid=(2,),
        out_shape=jax.ShapeDtypeStruct((6, width // 2, inner), bf16),
        in_specs=[pl.BlockSpec(memory_space=pltpu.SMEM)]
        + [pl.BlockSpec((1,) + v.shape[1:], lambda e: (e, 0, 0)) for v in operands]
        + [out_spec] * len(onto),
        out_specs=out_spec,
        compiler_params=pltpu.CompilerParams(vmem_limit_bytes=VMEM_BYTES),
        cost_estimate=pl.CostEstimate(flops=1 << 28, bytes_accessed=1 << 20, transcendentals=0),
    )(half, *operands, *onto)


def sides_kernel(
    x_ref, grad_ref, w_ref, all_ref, context_ref, normed_ref, logit_ref, norm_ref, gain_ref, out_ref, shared_ref
):
    planes, tokens = x_ref.shape[0], normed_ref.shape[0]
    joined_width = grad_ref.shape[1]
    experts = logit_ref.shape[1]
    step = x_ref.shape[2] // 2
    for first in range(0, x_ref.shape[2], step):
        at = slice(first, first + step)
        rows = jnp.concatenate([x_ref[plane, :tokens, at] for plane in range(planes)], axis=0)
        joined = contract(grad_ref[...], rows, 0, 0)
        out_ref[:joined_width, at] = joined.astype(bf16)
        out_ref[joined_width:, at] = contract(context_ref[...], all_ref[:, at], 0, 0).astype(bf16)
        norm1 = jnp.sum(joined * w_ref[:, at].astype(f32), axis=0, keepdims=True) / gain_ref[:, at]
        norm2 = norm_ref[:, at]
        shared_ref[:experts, at] = contract(logit_ref[...], normed_ref[:, at], 0, 0).astype(bf16)
        shared_ref[experts : experts + 1, at] = norm2.astype(bf16)
        shared_ref[experts + 1 : experts + 2, at] = norm1.astype(bf16)


def run_sides(gathered, joined_grad, joined_rows, attention_all, context, normed_two, logits, norm_terms, gain):
    vmem = pl.BlockSpec(memory_space=pltpu.VMEM)
    width = gathered.shape[2]
    rows = joined_grad.shape[1] + context.shape[1]
    return pl.pallas_call(
        sides_kernel,
        out_shape=(
            jax.ShapeDtypeStruct((rows, width), bf16),
            jax.ShapeDtypeStruct((logits.shape[1] + 2, width), bf16),
        ),
        in_specs=[vmem] * 9,
        out_specs=(vmem, vmem),
        compiler_params=pltpu.CompilerParams(vmem_limit_bytes=VMEM_BYTES),
        cost_estimate=pl.CostEstimate(flops=1 << 20, bytes_accessed=1 << 16, transcendentals=0),
    )(gathered, joined_grad, joined_rows, attention_all, context, normed_two, logits, norm_terms, gain)


def local(
    tokens,
    segments,
    routes,
    norm1_gain,
    w_query,
    w_key,
    w_value,
    w_out,
    norm2_gain,
    w_router,
    w_gate,
    w_up,
    w_down,
    cotangent,
):
    tok_rows, width = tokens.shape
    seq_len = segments.shape[1]
    query_width = w_query.shape[1]
    kv_width = w_key.shape[1]
    joined_width = query_width + 2 * kv_width
    local_experts = w_gate.shape[0]
    experts = w_router.shape[1]
    owners = lax.axis_size("expert")
    planes = lax.axis_size("tensor")
    owner = lax.axis_index("expert")
    first_expert = owner * local_experts
    key_seg = segments[0]
    hidden_width = w_gate.shape[2]

    token_f32 = tokens.astype(f32)
    inverse_one = rms_inverse(token_f32)
    normed_low = (token_f32 * inverse_one * norm1_gain).astype(bf16)
    joined_rows = by_rows(jnp.concatenate([w_query.T, w_key.T, w_value.T], axis=0))
    core = lax.axis_index("dp")

    def half_of(rows):
        count = rows.shape[0] // 2
        return lax.dynamic_slice_in_dim(rows, core * count, count, 0)

    def both_halves(half):
        other = swap_cores(half)
        first, second = jnp.where(core == 0, half, other), jnp.where(core == 0, other, half)
        return jnp.concatenate([first, second], axis=1).reshape(-1, half.shape[2])

    gathered = lax.all_gather(
        by_rows(jnp.concatenate([normed_low, half_of(w_out)], axis=0)), "tensor", axis=0
    )

    expert_ids = jnp.arange(experts, dtype=jnp.int32)
    onehot = (routes[:, :, None] == expert_ids[None, None, :]).astype(f32)
    member = jnp.sum(onehot, axis=1)
    lower = (jnp.arange(tok_rows)[:, None] <= jnp.arange(tok_rows)[None, :]).astype(bf16)
    rank = jnp.einsum("te,tu->eu", member.astype(bf16), lower, preferred_element_type=f32)
    rank = jnp.where(member.T > 0, rank - 1.0, -1.0).astype(bf16)
    extra = jnp.pad(rank, ((0, tok_rows - experts), (0, LANES - tok_rows)))
    cot_payload = jnp.concatenate([cotangent, extra], axis=1)

    chunks = width // hidden_width
    down_rows = w_down.shape[1]
    part_rows = w_gate.shape[1]
    down_parts = w_down.reshape(local_experts, down_rows, chunks, hidden_width)
    down_parts = down_parts.transpose(0, 2, 1, 3).reshape(local_experts, part_rows, hidden_width)
    weights = jnp.stack([w_gate, w_up, down_parts], axis=1)
    weights = weights.reshape(3 * local_experts, part_rows, hidden_width)
    tables = rope_tables(seq_len)
    marks = segment_marks(key_seg)
    cot_parts = gather_second(gather_first(cot_payload))
    joined_half = by_rows(half_of(joined_rows))
    gathered, weights, joined_rows, joined_half, member, col, row, *cot_parts = together(
        gathered, weights, joined_rows, joined_half, by_rows(member), *marks, *cot_parts
    )
    marks = col, row
    weights_all = lax.all_gather(weights, ("dp", "tensor"), axis=1, tiled=True)
    context, context_blocks, qkv, half_out = run_attention(
        gathered, joined_rows, marks, tables
    )
    context_home = lax.all_to_all(context_blocks, "tensor", split_axis=0, concat_axis=0)
    w_out_all = both_halves(half_out)
    context_home, w_out_all, joined_half = together(context_home, w_out_all, joined_half)
    half_joined = lax.all_gather(joined_half, "tensor", axis=0)
    router = by_rows(w_router.T)
    mid, inverse_two, payload, gates = run_home(
        context_home.reshape(planes * query_width, tok_rows),
        w_out_all,
        tokens,
        norm2_gain[None],
        router,
        member,
    )
    line = gather_first(payload)
    before, behind = (cross(line, 1, step) for step in STEPS[1:3])

    first_expert = first_expert.astype(jnp.int32).reshape(1)
    def compute(rows, cots):
        return run_experts(first_expert, rows, cots, weights_all)

    own = compute([line], cot_parts[:1])
    line, before, behind, *own_saved = together(line, before, behind, *own[1])
    far = cross(line, 1, STEPS[3])
    near = compute([before, behind], cot_parts[1:3])
    far, *near_saved = together(far, *near[1])
    last = compute([far], cot_parts[3:])
    done = [(*own[0], *near[0], *last[0]), (own_saved, near_saved, last[1])]
    back_line = scatter_first(done[0])
    mix_parts = run_mixture(
        [own[2], near[2], last[2]], [own_saved[4], near_saved[4], last[1][4]], weights_all
    )
    given = run_weight_grads((1 - core).astype(jnp.int32).reshape(1), done[1])
    n_line = len(back_line)
    *both, given, half_joined = together(*back_line, *mix_parts, given, half_joined)
    back_line, mix_parts = sum_first(both[:n_line]), both[n_line:]
    back_home = scatter_second(back_line)
    back_home[1], received = together(back_home[1], swap_cores(given))

    mid_grad, attention_low, context_grad, logit_grad, norm2_part = run_home_back(
        back_home, gates, router, mid, inverse_two, norm2_gain[None], cotangent, w_out_all
    )
    received, *mix_parts, context_grad, logit_grad = together(
        received, *mix_parts, context_grad, logit_grad
    )
    mix_arrived = scatter_first(mix_parts)
    kept = run_weight_grads(core.astype(jnp.int32).reshape(1), done[1], received)
    context_grad = lax.all_to_all(
        context_grad.reshape(planes, query_width, tok_rows), "tensor", split_axis=0, concat_axis=0
    )
    context_grad, kept = together(context_grad, kept)
    joined_grad, joined_blocks = run_attention_back(qkv, context_grad, marks, tables)
    joined_home = lax.all_to_all(joined_blocks, "tensor", split_axis=0, concat_axis=0)
    attention_all = lax.all_gather(attention_low, "tensor", axis=0, tiled=True)
    sides, shared = run_sides(
        gathered,
        joined_grad,
        joined_rows,
        attention_all,
        context,
        payload,
        logit_grad,
        norm2_part,
        norm1_gain[None],
    )

    share = sides.shape[0] // (2 * owners)
    shared_shape = shared.shape
    shared_rows = shared.size // LANES
    shared = shared.reshape(shared_rows, LANES)
    shared = jnp.pad(shared, ((0, 2 * owners * share - shared_rows), (0, 0)))
    blocks = jnp.concatenate(
        [sides.reshape(2, owners, share, width), shared.reshape(2, owners, share, LANES)], axis=3
    )
    def of_core(which):
        return lax.dynamic_index_in_dim(blocks, which, 0, keepdims=False)

    blocks, theirs, joined_home, kept, *mix_arrived = together(
        blocks, swap_cores(of_core(1 - core)), joined_home, kept, *mix_arrived
    )
    weight_sum = lax.psum_scatter(kept, "tensor", scatter_dimension=1, tiled=True)

    part = of_core(core).astype(f32) + theirs.astype(f32)
    arrived = lax.all_to_all(part.astype(bf16), "expert", split_axis=0, concat_axis=0)

    def rows_of(which):
        count = joined_width // 2
        rows = lax.dynamic_slice_in_dim(joined_home, which * count, count, 1)
        return rows.reshape(-1, tok_rows)

    normed_one_grad = contract(rows_of(core), half_joined.reshape(-1, width), 0, 0)
    normed_one_grad += contract(
        rows_of(1 - core), swap_cores(half_joined).reshape(-1, width), 0, 0
    )
    arrived, normed_one_grad, *mix_line = together(
        arrived, normed_one_grad, *sum_first(mix_arrived)
    )
    total = jnp.sum(arrived.astype(f32), axis=0)
    total = jnp.concatenate([total[:, :width], ring_sum(total[:, width:])], axis=1).astype(bf16)
    spread = lax.all_to_all(
        jnp.broadcast_to(total[None], arrived.shape), "expert", split_axis=0, concat_axis=0
    )
    mixture = sum(part.astype(f32) for part in scatter_second(mix_line))
    spread, mixture = together(by_rows(spread), mixture)
    output = (mid + mixture).astype(bf16)
    spread, weight_sum = together(spread, weight_sum)
    other = swap_cores(spread)
    first, second = jnp.where(core == 0, spread, other), jnp.where(core == 0, other, spread)
    shared = jnp.concatenate([first, second], axis=0)[:, :, width:].reshape(-1, LANES)
    shared = shared[:shared_rows].astype(f32).reshape(shared_shape)
    first = first[:, :, :width].reshape(-1, width)
    second = second[:, :, :width].reshape(-1, width)
    query_sum = first[:query_width].astype(f32).T
    key_sum = first[query_width:].astype(f32).T
    value_sum = second[:kv_width].astype(f32).T
    out_sum = second[kv_width:].astype(f32)
    weight_sum = weight_sum.reshape(local_experts, 3, part_rows, hidden_width)
    w_gate_grad = weight_sum[:, 0].astype(f32)
    w_up_grad = weight_sum[:, 1].astype(f32)
    w_down_grad = weight_sum[:, 2].reshape(local_experts, chunks, down_rows, hidden_width)
    w_down_grad = w_down_grad.transpose(0, 2, 1, 3).reshape(local_experts, down_rows, width)
    w_down_grad = w_down_grad.astype(f32)
    input_part, _ = rms_backward(token_f32, inverse_one, norm1_gain, normed_one_grad)
    input_grad = mid_grad + input_part
    return (
        output,
        input_grad,
        shared[experts + 1],
        query_sum,
        key_sum,
        value_sum,
        out_sum,
        shared[experts],
        shared[:experts].T,
        w_gate_grad,
        w_up_grad,
        w_down_grad,
    )


def solution(mesh):
    rows = P(("dp", "expert", "tensor"), None)
    columns = P(None, "tensor")
    experts = P("expert", ("dp", "tensor"), None)
    return jax.shard_map(
        local,
        mesh=mesh,
        in_specs=(
            rows,
            P(("dp", "expert"), None),
            rows,
            P(),
            columns,
            columns,
            columns,
            P("tensor", None),
            P(),
            P(),
            experts,
            experts,
            experts,
            rows,
        ),
        out_specs=(
            rows,
            rows,
            P(),
            columns,
            columns,
            columns,
            P("tensor", None),
            P(),
            P(),
            experts,
            experts,
            experts,
        ),
        check_vma=False,
    )
```

```python
import functools

import jax
import jax.numpy as jnp
import numpy as np
from jax import lax
from jax.experimental import pallas as pl
from jax.experimental.layout import Layout, with_layout_constraint
from jax.experimental.pallas import tpu as pltpu
from jax.sharding import PartitionSpec as P

HEAD_DIM = 64
HALF = HEAD_DIM // 2
TOP = 8
CAP = 64
EXPERTS = 32
HOLDERS = 16
VMEM_BYTES = 57 * 1024 * 1024
LANES = 128

epsilon_norm = 1e-06
rope_theta = 10000.0
masked_score = -1e30
QUERY_ROWS = 512
SCALE = HEAD_DIM ** (-0.5)
f32 = jnp.float32
bf16 = jnp.bfloat16


def rms_inverse(values):
    return lax.rsqrt(jnp.mean(values * values, axis=-1, keepdims=True) + epsilon_norm)


def rms_backward(values, inverse, norm_gain, grad_out):
    scaled = grad_out * norm_gain
    grad_in = inverse * scaled - values * (inverse * inverse * inverse) * jnp.mean(
        scaled * values, axis=-1, keepdims=True
    )
    return (grad_in, grad_out * values * inverse)


def dot32(left, right):
    return jnp.dot(left, right, preferred_element_type=f32)


SIDE = 4
STEPS = (0, 1, -1, 2)


def by_rows(values):
    return with_layout_constraint(values, Layout(major_to_minor=tuple(range(values.ndim))))


def cross(values, stage, step):
    pairs = []
    plane = SIDE * SIDE
    for core in range(2):
        for x in range(SIDE):
            for y in range(SIDE):
                if core == stage:
                    to = x * SIDE + (y + step) % SIDE
                else:
                    to = (x + step) % SIDE * SIDE + y
                pairs.append((core * plane + x * SIDE + y, core * plane + to))
    return lax.ppermute(values, ("dp", "expert"), pairs)


def gather_first(values):
    values = by_rows(values)
    line = jnp.stack([values] + [cross(values, 0, step) for step in STEPS[1:]])
    return by_rows(line)


def gather_second(line):
    return [line] + [cross(line, 1, step) for step in STEPS[1:]]


def scatter_first(parts):
    return [parts[0]] + [
        by_rows(cross(part, 1, -step)) for part, step in zip(parts[1:], STEPS[1:])
    ]


def sum_kernel(*refs):
    arrived, outs = refs[:SIDE], refs[SIDE:]
    total = sum(ref[0].astype(f32) for ref in arrived).astype(bf16)
    for place, out in enumerate(outs):

        @pl.when(pl.program_id(0) == place)
        def _():
            out[...] = total


def sum_first(arrived):
    rows, columns = arrived[0].shape[1:]
    return pl.pallas_call(
        sum_kernel,
        grid=(SIDE,),
        out_shape=[jax.ShapeDtypeStruct((rows, columns), bf16)] * SIDE,
        in_specs=[pl.BlockSpec((1, rows, columns), lambda place: (place, 0, 0))] * SIDE,
        out_specs=[pl.BlockSpec((rows, columns), lambda place: (0, 0))] * SIDE,
        compiler_params=pltpu.CompilerParams(vmem_limit_bytes=24 * 1024 * 1024),
        cost_estimate=pl.CostEstimate(flops=1 << 22, bytes_accessed=8 << 20, transcendentals=0),
    )(*arrived)


def scatter_second(line):
    return [line[0]] + [
        by_rows(cross(part, 0, -step)) for part, step in zip(line[1:], STEPS[1:])
    ]


def ring_sum(values):
    size = lax.axis_size("tensor")
    step = 1
    while step < size:
        pairs = [(i, i ^ step) for i in range(size)]
        values = values + lax.ppermute(values, "tensor", pairs)
        step *= 2
    return values


def together(*values):
    return lax.optimization_barrier(values)


def swap_cores(values):
    return lax.ppermute(values, "dp", [(0, 1), (1, 0)])


def contract(left, right, left_dim, right_dim):
    return lax.dot_general(
        left, right, (((left_dim,), (right_dim,)), ((), ())), preferred_element_type=f32
    )


def allowed(rows, first, wide, col_ref, row_ref):
    query = first + lax.broadcasted_iota(jnp.int32, (rows, wide), 0)
    key = lax.broadcasted_iota(jnp.int32, (rows, wide), 1)
    return (key <= query) & (col_ref[first : first + rows, :] == row_ref[:, :wide])


def probabilities(query, key, mask):
    scores = jnp.where(mask, contract(query, key, 1, 1), masked_score)
    weights = jnp.exp(scores - jnp.max(scores, axis=1, keepdims=True))
    return weights * (1.0 / jnp.sum(weights, axis=1, keepdims=True))


def turn(values, cosine, sine):
    size = values.shape[1]
    first = lax.broadcasted_iota(jnp.int32, values.shape, 1) % HEAD_DIM < HALF
    other = jnp.where(
        first, -pltpu.roll(values, size - HALF, 1), pltpu.roll(values, HALF, 1)
    )
    tables = [jnp.concatenate([table] * (size // LANES), axis=1) for table in (cosine, sine)]
    return values * tables[0] + other * tables[1]


def attention_kernel(
    x_ref, w_ref, col_ref, row_ref, cos_ref, sin_ref, out_ref, turned_ref, qkv_ref
):
    seq_len = out_ref.shape[0]
    tokens = turned_ref.shape[2]
    heads = out_ref.shape[1] // HEAD_DIM
    last = (heads + 1) * HEAD_DIM
    step = QUERY_ROWS
    for first in range(0, seq_len, step):
        at = slice(first, first + step)
        wide = first + step
        blocks = range(first // tokens, wide // tokens)
        rows = jnp.concatenate([x_ref[block, :tokens, :] for block in blocks], axis=0)
        joined = contract(rows, w_ref[...], 1, 1)
        turned_part = turn(joined[:, :last], cos_ref[at, :], sin_ref[at, :])
        qkv_ref[at, :last] = turned_part.astype(bf16)
        qkv_ref[at, last:] = joined[:, last:].astype(bf16)
        mask = allowed(step, first, wide, col_ref, row_ref)
        key = qkv_ref[:wide, heads * HEAD_DIM : last]
        value = qkv_ref[:wide, last:]
        for head in range(heads):
            place = slice(head * HEAD_DIM, (head + 1) * HEAD_DIM)
            query = qkv_ref[at, place] * SCALE
            probs = probabilities(query, key, mask).astype(bf16)
            context = jnp.dot(probs, value, preferred_element_type=f32)
            out_ref[at, place] = context.astype(bf16)
            for block in range(step // tokens):
                turned_ref[first // tokens + block, place, :] = context[
                    block * tokens : (block + 1) * tokens
                ].T.astype(bf16)


def attention_back_kernel(
    qkv_ref, grad_ref, col_ref, row_ref, cos_ref, sin_ref, out_ref, turned_ref, key_sum, value_sum
):
    seq_len = qkv_ref.shape[0]
    heads = grad_ref.shape[1] // HEAD_DIM
    tokens = grad_ref.shape[2]
    last = (heads + 1) * HEAD_DIM
    step = QUERY_ROWS
    for first in reversed(range(0, seq_len, step)):
        at = slice(first, first + step)
        wide = first + step
        mask = allowed(step, first, wide, col_ref, row_ref)
        key = qkv_ref[:wide, heads * HEAD_DIM : last]
        value = qkv_ref[:wide, last:]
        key_grad = jnp.zeros((wide, HEAD_DIM), f32)
        value_grad = jnp.zeros((wide, HEAD_DIM), f32)
        query_grads = []
        for head in range(heads):
            place = slice(head * HEAD_DIM, (head + 1) * HEAD_DIM)
            query = qkv_ref[at, place] * SCALE
            grad = [
                grad_ref[first // tokens + block, place, :].astype(f32).T.astype(bf16)
                for block in range(step // tokens)
            ]
            grad = jnp.concatenate(grad, axis=0)
            probs = probabilities(query, key, mask)
            probs_grad = contract(grad, value, 1, 1)
            row_dot = jnp.sum(probs * probs_grad, axis=1, keepdims=True)
            score_grad = (probs * (probs_grad - row_dot)).astype(bf16)
            query_grads.append(jnp.dot(score_grad, key, preferred_element_type=f32) * SCALE)
            key_grad += contract(score_grad, query, 0, 0)
            value_grad += contract(probs.astype(bf16), grad, 0, 0)
        if wide == seq_len:
            key_sum[...] = key_grad
            value_sum[...] = value_grad
        else:
            key_sum[:wide, :] += key_grad
            value_sum[:wide, :] += value_grad
        both = jnp.concatenate(query_grads + [key_sum[at, :]], axis=1)
        both = turn(both, cos_ref[at, :], -sin_ref[at, :])
        out_ref[at, :last] = both.astype(bf16)
        out_ref[at, last:] = value_sum[at, :].astype(bf16)
        for block in range(step // tokens):
            part = slice(block * tokens, (block + 1) * tokens)
            to = first // tokens + block
            turned_ref[to, :last, :] = both[part].T.astype(bf16)
            turned_ref[to, last:, :] = value_sum[first : first + step, :][part].T.astype(bf16)


def run_attention(gathered, joined_rows, marks, tables):
    planes = gathered.shape[0]
    seq_len = marks[0].shape[0]
    joined_width = joined_rows.shape[0]
    query_width = joined_width - 2 * HEAD_DIM
    vmem = pl.BlockSpec(memory_space=pltpu.VMEM)
    return pl.pallas_call(
        attention_kernel,
        out_shape=(
            jax.ShapeDtypeStruct((seq_len, query_width), bf16),
            jax.ShapeDtypeStruct((planes, query_width, seq_len // planes), bf16),
            jax.ShapeDtypeStruct((seq_len, joined_width), bf16),
        ),
        in_specs=[vmem] * 6,
        out_specs=(vmem,) * 3,
        compiler_params=pltpu.CompilerParams(vmem_limit_bytes=VMEM_BYTES),
        cost_estimate=pl.CostEstimate(
            flops=1 << 28, bytes_accessed=1 << 20, transcendentals=0
        ),
    )(gathered, joined_rows, *marks, *tables)


def run_attention_back(qkv, context_grad, marks, tables):
    seq_len, joined_width = qkv.shape
    planes = context_grad.shape[0]
    vmem = pl.BlockSpec(memory_space=pltpu.VMEM)
    return pl.pallas_call(
        attention_back_kernel,
        out_shape=(
            jax.ShapeDtypeStruct((seq_len, joined_width), bf16),
            jax.ShapeDtypeStruct((planes, joined_width, seq_len // planes), bf16),
        ),
        in_specs=[vmem] * 6,
        out_specs=(vmem, vmem),
        scratch_shapes=[pltpu.VMEM((seq_len, HEAD_DIM), f32)] * 2,
        compiler_params=pltpu.CompilerParams(vmem_limit_bytes=VMEM_BYTES),
        cost_estimate=pl.CostEstimate(
            flops=1 << 28, bytes_accessed=1 << 20, transcendentals=0
        ),
    )(qkv, context_grad, *marks, *tables)


def rope_tables(seq_len):
    frequency = np.float32(rope_theta) ** (np.arange(HALF, dtype=np.float32) * np.float32(-2.0 / HEAD_DIM))
    angles = np.arange(seq_len, dtype=np.float32)[:, None] * frequency.astype(np.float32)[None, :]
    angles = np.tile(angles, (1, LANES // HALF))
    return jnp.asarray(np.cos(angles)), jnp.asarray(np.sin(angles))


def segment_marks(key_seg):
    marks = jnp.where(key_seg == 0, -1 - jnp.arange(key_seg.shape[0], dtype=jnp.int32), key_seg)
    return marks[:, None], marks[None, :]


def expert_kernel(groups, first_ref, *refs):
    rows_refs, cots_refs = refs[:groups], refs[groups : 2 * groups]
    w_ref = refs[2 * groups]
    back_outs = refs[2 * groups + 1 : 3 * groups + 1]
    x_ref, c_ref, gate_ref, up_ref, hid_ref, pick_ref = refs[3 * groups + 1 : 3 * groups + 7]
    down_ref, next_x, next_c, gates_ref = refs[3 * groups + 7 :]
    sources, tokens, _ = rows_refs[0].shape
    width = x_ref.shape[2]
    e = pl.program_id(0)
    expert = first_ref[0] + e
    at = pl.ds(pl.multiple_of(e * CAP, CAP), CAP)
    every = [(group, source) for group in range(groups) for source in range(sources)]

    @pl.when(e == 0)
    def _():
        pair = 2 * CAP
        lane = lax.broadcasted_iota(jnp.int32, (pair, LANES), 1)
        expert_of = expert + lax.broadcasted_iota(jnp.int32, (pair, LANES), 0) // CAP
        own = (lane == expert_of) | (lane == expert_of + EXPERTS)
        row_id = lax.broadcasted_iota(jnp.int32, (EXPERTS, tokens), 0)
        slot = lax.broadcasted_iota(jnp.int32, (pair, tokens), 0)
        place_of = jnp.where(slot < CAP, slot, slot - CAP).astype(f32)
        for order, (group, source) in enumerate(every):
            table = cots_refs[group][source, :EXPERTS, width:].astype(f32)
            ranks = [
                jnp.sum(jnp.where(row_id == expert + i, table, 0.0), axis=0, keepdims=True)
                for i in range(2)
            ]
            pick = (jnp.where(slot < CAP, ranks[0], ranks[1]) == place_of).astype(bf16)
            pick_ref[order] = pick
            rows = jnp.dot(pick, rows_refs[group][source], preferred_element_type=f32)
            cots = jnp.dot(pick, cots_refs[group][source, :, :width], preferred_element_type=f32)
            gate = jnp.sum(jnp.where(own, rows[:, width:], 0.0), axis=1, keepdims=True)
            gate = jnp.broadcast_to(gate, (pair, LANES))
            place = slice(order * CAP, (order + 1) * CAP)
            x_ref[0, place] = rows[:CAP, :width].astype(bf16)
            c_ref[0, place] = cots[:CAP].astype(bf16)
            gates_ref[0, place] = gate[:CAP]
            next_x[place] = rows[CAP:, :width].astype(bf16)
            next_c[place] = cots[CAP:].astype(bf16)
            gates_ref[1, place] = gate[CAP:]

    @pl.when(e == 1)
    def _():
        x_ref[0] = next_x[...]
        c_ref[0] = next_c[...]

    gate = gates_ref[e][:, :1]
    join_chunks(down_ref, w_ref.at[2], HOLDERS)
    x = x_ref[0]
    gate_pre = jnp.dot(x, w_ref[0], preferred_element_type=f32)
    up_pre = jnp.dot(x, w_ref[1], preferred_element_type=f32)
    back = contract(c_ref[0], down_ref[...], 1, 1)
    sig = 1.0 / (1.0 + jnp.exp(-gate_pre))
    silu = gate_pre * sig
    hidden = (silu * up_pre).astype(bf16)
    gate_grad = jnp.sum(back * hidden.astype(f32), axis=1, keepdims=True)
    grad = gate * back
    gate_pre_grad = (grad * up_pre * (sig + silu * (1.0 - sig))).astype(bf16)
    up_pre_grad = (grad * silu).astype(bf16)
    gate_ref[0] = gate_pre_grad
    up_ref[0] = up_pre_grad
    hid_ref[0] = (gate * hidden.astype(f32)).astype(bf16)
    row_grad = contract(gate_pre_grad, w_ref[0], 1, 1) + contract(up_pre_grad, w_ref[1], 1, 1)
    high = gate_grad.astype(bf16).astype(f32)
    lane = lax.broadcasted_iota(jnp.int32, (len(every) * CAP, LANES), 1)
    tail = jnp.where(lane == expert, high, 0.0)
    tail += jnp.where(lane == expert + EXPERTS, gate_grad - high, 0.0)
    for order, (group, source) in enumerate(every):
        place = slice(order * CAP, (order + 1) * CAP)
        back_outs[group][source, at, :width] = row_grad[place].astype(bf16)
        back_outs[group][source, at, width:] = tail[place].astype(bf16)

    @pl.when(e == 1)
    def _():
        for order, (group, source) in enumerate(every):
            back_outs[group][source] = contract(
                pick_ref[order], back_outs[group][source], 0, 0
            ).astype(bf16)


def home_kernel(
    context_ref, w_out_ref, tokens_ref, gain_ref, router_ref, member_ref, mid_ref, inverse_ref, payload_ref, gates_ref
):
    width = tokens_ref.shape[1]
    mid = tokens_ref[...].astype(f32) + contract(context_ref[...], w_out_ref[...], 0, 0)
    inverse = rms_inverse(mid)
    normed = (mid * inverse * gain_ref[...]).astype(bf16)
    mid_ref[...] = mid
    inverse_ref[...] = inverse
    payload_ref[:, :width] = normed
    member = member_ref[...] > 0
    logits = jnp.where(member, contract(normed, router_ref[...], 1, 1), masked_score)
    chosen = jnp.where(member, jnp.exp(logits - jnp.max(logits, axis=1, keepdims=True)), 0.0)
    gates = chosen / jnp.sum(chosen, axis=1, keepdims=True)
    gates_ref[...] = gates
    high = gates.astype(bf16).astype(f32)
    rest = jnp.zeros((gates.shape[0], LANES - 2 * gates.shape[1]), f32)
    payload_ref[:, width:] = jnp.concatenate([high, gates - high, rest], axis=1).astype(bf16)


def run_home(context, w_out, tokens, gain, router, member):
    rows, width = tokens.shape
    vmem = pl.BlockSpec(memory_space=pltpu.VMEM)
    return pl.pallas_call(
        home_kernel,
        out_shape=(
            jax.ShapeDtypeStruct((rows, width), f32),
            jax.ShapeDtypeStruct((rows, 1), f32),
            jax.ShapeDtypeStruct((rows, width + LANES), bf16),
            jax.ShapeDtypeStruct(member.shape, f32),
        ),
        in_specs=[vmem] * 6,
        out_specs=(vmem,) * 4,
        compiler_params=pltpu.CompilerParams(vmem_limit_bytes=24 * 1024 * 1024),
        cost_estimate=pl.CostEstimate(flops=1 << 30, bytes_accessed=8 << 20, transcendentals=0),
    )(context, w_out, tokens, gain, router, member)


def home_back_kernel(*refs):
    parts, refs = refs[:SIDE], refs[SIDE:]
    gates_ref, router_ref, mid_ref, inverse_ref, gain_ref, cot_ref, w_out_ref = refs[:7]
    grad_ref, low_ref, context_ref, logit_ref, norm_ref = refs[7:]
    width = mid_ref.shape[1]
    gates = gates_ref[...]
    experts = gates.shape[1]
    total = sum(ref[...].astype(f32) for ref in parts)
    tail = total[:, width:]
    gate_grad = tail[:, :experts] + tail[:, experts : 2 * experts]
    chosen = gates * (gate_grad - jnp.sum(gates * gate_grad, axis=1, keepdims=True))
    logit_grad = chosen.astype(bf16)
    logit_ref[...] = logit_grad
    normed_grad = total[:, :width] + jnp.dot(
        logit_grad, router_ref[...], preferred_element_type=f32
    )
    mid, inverse = mid_ref[...], inverse_ref[...]
    scaled = normed_grad * gain_ref[...]
    norm_ref[...] = jnp.sum(normed_grad * mid * inverse, axis=0, keepdims=True)
    mean = jnp.mean(scaled * mid, axis=1, keepdims=True)
    grad = cot_ref[...].astype(f32) + inverse * scaled - mid * (inverse * inverse * inverse) * mean
    grad_ref[...] = grad
    low = grad.astype(bf16)
    low_ref[...] = low
    context_ref[...] = contract(w_out_ref[...], low, 1, 1).astype(bf16)


def run_home_back(parts, gates, router, mid, inverse, gain, cotangent, w_out):
    rows, width = mid.shape
    vmem = pl.BlockSpec(memory_space=pltpu.VMEM)
    return pl.pallas_call(
        home_back_kernel,
        out_shape=(
            jax.ShapeDtypeStruct((rows, width), f32),
            jax.ShapeDtypeStruct((rows, width), bf16),
            jax.ShapeDtypeStruct((w_out.shape[0], rows), bf16),
            jax.ShapeDtypeStruct(gates.shape, bf16),
            jax.ShapeDtypeStruct((1, width), f32),
        ),
        in_specs=[vmem] * (SIDE + 7),
        out_specs=(vmem,) * 5,
        compiler_params=pltpu.CompilerParams(vmem_limit_bytes=24 * 1024 * 1024),
        cost_estimate=pl.CostEstimate(flops=1 << 30, bytes_accessed=8 << 20, transcendentals=0),
    )(*parts, gates, router, mid, inverse, gain, cotangent, w_out)


def join_chunks(to_ref, from_ref, holders):
    inner = from_ref.shape[1]
    rows = inner // HOLDERS
    chunks = to_ref.shape[1] // inner
    for holder in range(holders):
        for chunk in range(chunks):
            start = (holder * chunks + chunk) * rows
            to_ref[
                holder * rows : (holder + 1) * rows, chunk * inner : (chunk + 1) * inner
            ] = from_ref[start : start + rows, :]


def run_experts(first, rows, cots, weights):
    groups = len(rows)
    sources, tokens, padded = rows[0].shape
    width = padded - LANES
    inner = weights.shape[2]
    slots = groups * sources * CAP

    def once(columns):
        return pl.BlockSpec(
            (sources, tokens, columns), lambda e: (0, 0, 0), pipeline_mode=pl.Buffered(1)
        )

    def by_expert(*shape):
        return pl.BlockSpec(shape, lambda e: (e, 0, 0))

    acts = jax.ShapeDtypeStruct((2, slots, inner), bf16)
    wide = jax.ShapeDtypeStruct((2, slots, width), bf16)
    outs = pl.pallas_call(
        functools.partial(expert_kernel, groups),
        grid=(2,),
        out_shape=(
            *[jax.ShapeDtypeStruct((sources, tokens, padded), bf16)] * groups,
            wide,
            wide,
            acts,
            acts,
            acts,
            jax.ShapeDtypeStruct((groups * sources, 2 * CAP, tokens), bf16),
        ),
        in_specs=[pl.BlockSpec(memory_space=pltpu.SMEM)]
        + [once(padded)] * (2 * groups)
        + [by_expert(3, width, inner)],
        out_specs=(
            *[once(padded)] * groups,
            by_expert(1, slots, width),
            by_expert(1, slots, width),
            by_expert(1, slots, inner),
            by_expert(1, slots, inner),
            by_expert(1, slots, inner),
            pl.BlockSpec((groups * sources, 2 * CAP, tokens), lambda e: (0, 0, 0)),
        ),
        scratch_shapes=[
            pltpu.VMEM((inner, width), bf16),
            pltpu.VMEM((slots, width), bf16),
            pltpu.VMEM((slots, width), bf16),
            pltpu.VMEM((2, slots, LANES), f32),
        ],
        compiler_params=pltpu.CompilerParams(vmem_limit_bytes=VMEM_BYTES),
        cost_estimate=pl.CostEstimate(
            flops=2 * 2 * 6 * slots * width * inner, bytes_accessed=24 << 20, transcendentals=0
        ),
    )(first, *rows, *cots, weights)
    return outs[:groups], outs[groups:-1], outs[-1]


def mixture_kernel(groups, *refs):
    pick_refs, hid_refs = refs[:groups], refs[groups : 2 * groups]
    w_ref = refs[2 * groups]
    outs, down_ref = refs[2 * groups + 1 : -1], refs[-1]
    e = pl.program_id(0)
    at = pl.ds(pl.multiple_of(e * CAP, CAP), CAP)
    join_chunks(down_ref, w_ref.at[0], HOLDERS)
    sources = [
        (pick_ref, hid_ref, source)
        for pick_ref, hid_ref in zip(pick_refs, hid_refs)
        for source in range(pick_ref.shape[0])
    ]
    to = {}
    for order, (pick_ref, hid_ref, source) in enumerate(sources):
        to[order] = (outs[order // SIDE], order % SIDE, pick_ref, source)
    order = 0
    for pick_ref, hid_ref in zip(pick_refs, hid_refs):
        mixed = jnp.dot(hid_ref[0], down_ref[...], preferred_element_type=f32).astype(bf16)
        for source in range(pick_ref.shape[0]):
            out, place, _, _ = to[order]
            out[place, at] = mixed[source * CAP : (source + 1) * CAP]
            order += 1

    @pl.when(e == 1)
    def _():
        for out, place, pick_ref, source in to.values():
            out[place] = contract(pick_ref[source], out[place], 0, 0).astype(bf16)


def run_mixture(picks, hidden, weights):
    width, inner = weights.shape[1:]
    groups = len(picks)

    def once(shape):
        return pl.BlockSpec(shape, lambda e: (0, 0, 0), pipeline_mode=pl.Buffered(1))

    shapes = [(SIDE, picks[0].shape[2], width)] * SIDE
    return pl.pallas_call(
        functools.partial(mixture_kernel, groups),
        grid=(2,),
        out_shape=[jax.ShapeDtypeStruct(shape, bf16) for shape in shapes],
        in_specs=[once(pick.shape) for pick in picks]
        + [pl.BlockSpec((1,) + hid.shape[1:], lambda e: (e, 0, 0)) for hid in hidden]
        + [pl.BlockSpec((1, width, inner), lambda e: (3 * e + 2, 0, 0))],
        out_specs=[once(shape) for shape in shapes],
        scratch_shapes=[pltpu.VMEM((inner, width), bf16)],
        compiler_params=pltpu.CompilerParams(vmem_limit_bytes=VMEM_BYTES),
        cost_estimate=pl.CostEstimate(flops=1 << 32, bytes_accessed=1 << 20, transcendentals=0),
    )(*picks, *hidden, weights)


def weight_grad_kernel(groups, half_ref, *refs):
    x_refs, c_refs, gate_refs, up_refs, hid_refs = (
        refs[i * groups : (i + 1) * groups] for i in range(5)
    )
    *onto, out_ref = refs[5 * groups :]
    width = x_refs[0].shape[2]
    inner = gate_refs[0].shape[2]
    half = half_ref[0]
    rows = width // 2
    down_rows = inner // HOLDERS
    chunks = width // inner
    cols = pl.ds(pl.multiple_of(half * rows, LANES), rows)
    down_cols = pl.ds(pl.multiple_of(half * (inner // 2), LANES), inner // 2)
    gate = jnp.zeros((rows, inner), f32)
    up = jnp.zeros((rows, inner), f32)
    down = jnp.zeros((inner // 2, width), f32)
    for i in range(groups):
        x = x_refs[i][0, :, cols]
        gate += contract(x, gate_refs[i][0], 0, 0)
        up += contract(x, up_refs[i][0], 0, 0)

    def put(place, at, values):
        if onto:
            values = values + onto[0][place, at, :].astype(f32)
        out_ref[place, at, :] = values.astype(bf16)

    put(0, slice(0, rows), gate)
    put(1, slice(0, rows), up)
    for i in range(groups):
        down += contract(hid_refs[i][0, :, down_cols], c_refs[i][0], 0, 0)
    for holder in range(HOLDERS // 2):
        for chunk in range(chunks):
            start = (holder * chunks + chunk) * down_rows
            put(
                2,
                slice(start, start + down_rows),
                down[
                    holder * down_rows : (holder + 1) * down_rows,
                    chunk * inner : (chunk + 1) * inner,
                ],
            )


def run_weight_grads(half, saved, *onto):
    x, c, gate, up, hid = zip(*saved)
    width = x[0].shape[2]
    inner = gate[0].shape[2]
    operands = (*x, *c, *gate, *up, *hid)
    out_spec = pl.BlockSpec((3, width // 2, inner), lambda e: (e, 0, 0))
    return pl.pallas_call(
        functools.partial(weight_grad_kernel, len(saved)),
        grid=(2,),
        out_shape=jax.ShapeDtypeStruct((6, width // 2, inner), bf16),
        in_specs=[pl.BlockSpec(memory_space=pltpu.SMEM)]
        + [pl.BlockSpec((1,) + v.shape[1:], lambda e: (e, 0, 0)) for v in operands]
        + [out_spec] * len(onto),
        out_specs=out_spec,
        compiler_params=pltpu.CompilerParams(vmem_limit_bytes=VMEM_BYTES),
        cost_estimate=pl.CostEstimate(flops=1 << 28, bytes_accessed=1 << 20, transcendentals=0),
    )(half, *operands, *onto)


def joined_kernel(
    x_ref, grad_ref, w_ref, normed_ref, logit_ref, norm_ref, gain_ref, out_ref, shared_ref
):
    planes = x_ref.shape[0]
    tokens = grad_ref.shape[0] // planes
    experts = logit_ref.shape[1]
    step = x_ref.shape[2] // 2
    for first in range(0, x_ref.shape[2], step):
        at = slice(first, first + step)
        rows = jnp.concatenate([x_ref[plane, :tokens, at] for plane in range(planes)], axis=0)
        joined = contract(grad_ref[...], rows, 0, 0)
        out_ref[:, at] = joined.astype(bf16)
        norm1 = jnp.sum(joined * w_ref[:, at].astype(f32), axis=0, keepdims=True) / gain_ref[:, at]
        shared_ref[:experts, at] = contract(logit_ref[...], normed_ref[:, at], 0, 0).astype(bf16)
        shared_ref[experts : experts + 1, at] = norm_ref[:, at].astype(bf16)
        shared_ref[experts + 1 : experts + 2, at] = norm1.astype(bf16)


def run_joined(gathered, joined_grad, joined_rows, normed_two, logits, norm_terms, gain):
    vmem = pl.BlockSpec(memory_space=pltpu.VMEM)
    width = gathered.shape[2]
    return pl.pallas_call(
        joined_kernel,
        out_shape=(
            jax.ShapeDtypeStruct((joined_grad.shape[1], width), bf16),
            jax.ShapeDtypeStruct((logits.shape[1] + 2, width), bf16),
        ),
        in_specs=[vmem] * 7,
        out_specs=(vmem, vmem),
        compiler_params=pltpu.CompilerParams(vmem_limit_bytes=VMEM_BYTES),
        cost_estimate=pl.CostEstimate(flops=1 << 20, bytes_accessed=1 << 16, transcendentals=0),
    )(gathered, joined_grad, joined_rows, normed_two, logits, norm_terms, gain)


def out_kernel(all_ref, context_ref, out_ref):
    out_ref[...] = contract(context_ref[...], all_ref[...], 0, 0).astype(bf16)


def run_out(attention_all, context):
    width = attention_all.shape[1]
    rows, columns = context.shape
    step = width // 4
    return pl.pallas_call(
        out_kernel,
        grid=(4,),
        out_shape=jax.ShapeDtypeStruct((columns, width), bf16),
        in_specs=[
            pl.BlockSpec((rows, step), lambda i: (0, i)),
            pl.BlockSpec((rows, columns), lambda i: (0, 0)),
        ],
        out_specs=pl.BlockSpec((columns, step), lambda i: (0, i)),
        compiler_params=pltpu.CompilerParams(vmem_limit_bytes=VMEM_BYTES),
        cost_estimate=pl.CostEstimate(flops=1 << 20, bytes_accessed=1 << 16, transcendentals=0),
    )(attention_all, context)


def local(
    tokens,
    segments,
    routes,
    norm1_gain,
    w_query,
    w_key,
    w_value,
    w_out,
    norm2_gain,
    w_router,
    w_gate,
    w_up,
    w_down,
    cotangent,
):
    tok_rows, width = tokens.shape
    seq_len = segments.shape[1]
    query_width = w_query.shape[1]
    kv_width = w_key.shape[1]
    joined_width = query_width + 2 * kv_width
    local_experts = w_gate.shape[0]
    experts = w_router.shape[1]
    owners = lax.axis_size("expert")
    planes = lax.axis_size("tensor")
    owner = lax.axis_index("expert")
    first_expert = owner * local_experts
    key_seg = segments[0]
    hidden_width = w_gate.shape[2]

    token_f32 = tokens.astype(f32)
    inverse_one = rms_inverse(token_f32)
    normed_low = (token_f32 * inverse_one * norm1_gain).astype(bf16)
    joined_rows = by_rows(jnp.concatenate([w_query.T, w_key.T, w_value.T], axis=0))
    core = lax.axis_index("dp")

    def half_of(rows):
        count = rows.shape[0] // 2
        return lax.dynamic_slice_in_dim(rows, core * count, count, 0)

    place = jnp.where(core == 0, owner % SIDE, owner // SIDE)
    quarter = w_out.shape[0] // SIDE
    w_out_part = lax.dynamic_slice_in_dim(w_out, place * quarter, quarter, 0)
    gathered = lax.all_gather(
        by_rows(jnp.concatenate([normed_low, w_out_part], axis=0)), "tensor", axis=0
    )

    expert_ids = jnp.arange(experts, dtype=jnp.int32)
    onehot = (routes[:, :, None] == expert_ids[None, None, :]).astype(f32)
    member = jnp.sum(onehot, axis=1)
    lower = (jnp.arange(tok_rows)[:, None] <= jnp.arange(tok_rows)[None, :]).astype(bf16)
    rank = jnp.einsum("te,tu->eu", member.astype(bf16), lower, preferred_element_type=f32)
    rank = jnp.where(member.T > 0, rank - 1.0, -1.0).astype(bf16)
    extra = jnp.pad(rank, ((0, tok_rows - experts), (0, LANES - tok_rows)))
    cot_payload = jnp.concatenate([cotangent, extra], axis=1)

    chunks = width // hidden_width
    down_rows = w_down.shape[1]
    part_rows = w_gate.shape[1]
    down_parts = w_down.reshape(local_experts, down_rows, chunks, hidden_width)
    down_parts = down_parts.transpose(0, 2, 1, 3).reshape(local_experts, part_rows, hidden_width)
    weights = jnp.stack([w_gate, w_up, down_parts], axis=1)
    weights = weights.reshape(3 * local_experts, part_rows, hidden_width)
    tables = rope_tables(seq_len)
    marks = segment_marks(key_seg)
    cot_parts = gather_second(gather_first(cot_payload))
    joined_half = by_rows(half_of(joined_rows))
    gathered, weights, joined_rows, joined_half, member, col, row, *cot_parts = together(
        gathered, weights, joined_rows, joined_half, by_rows(member), *marks, *cot_parts
    )
    marks = col, row
    weights_all = lax.all_gather(weights, ("dp", "tensor"), axis=1, tiled=True)
    quarters = by_rows(gathered[:, tok_rows:])
    quarters = [quarters] + [by_rows(cross(quarters, 0, step)) for step in STEPS[1:]]
    context, context_blocks, qkv = run_attention(gathered, joined_rows, marks, tables)
    context_home = lax.all_to_all(context_blocks, "tensor", split_axis=0, concat_axis=0)
    w_out_all = jnp.zeros((planes, SIDE * quarter, width), bf16)
    for step, part in zip(STEPS, quarters):
        start = (place - step) % SIDE * quarter
        w_out_all = lax.dynamic_update_slice(w_out_all, part, (0, start, 0))
    w_out_all = by_rows(w_out_all.reshape(-1, width))
    context_home, w_out_all, joined_half = together(context_home, w_out_all, joined_half)
    half_joined = lax.all_gather(joined_half, "tensor", axis=0)
    router = by_rows(w_router.T)
    mid, inverse_two, payload, gates = run_home(
        context_home.reshape(planes * query_width, tok_rows),
        w_out_all,
        tokens,
        norm2_gain[None],
        router,
        member,
    )
    line = gather_first(payload)
    before, behind = (cross(line, 1, step) for step in STEPS[1:3])

    first_expert = first_expert.astype(jnp.int32).reshape(1)
    def compute(rows, cots):
        return run_experts(first_expert, rows, cots, weights_all)

    own = compute([line], cot_parts[:1])
    line, before, behind, *own_saved = together(line, before, behind, *own[1])
    far = cross(line, 1, STEPS[3])
    near = compute([before, behind], cot_parts[1:3])
    far, *near_saved = together(far, *near[1])
    last = compute([far], cot_parts[3:])
    done = [(*own[0], *near[0], *last[0]), (own_saved, near_saved, last[1])]
    back_line = scatter_first(done[0])
    mix_parts = run_mixture(
        [own[2], near[2], last[2]], [own_saved[4], near_saved[4], last[1][4]], weights_all
    )
    given = run_weight_grads((1 - core).astype(jnp.int32).reshape(1), done[1])
    n_line = len(back_line)
    *both, given, half_joined = together(*back_line, *mix_parts, given, half_joined)
    back_line, mix_parts = sum_first(both[:n_line]), both[n_line:]
    back_home = scatter_second(back_line)
    back_home[1], received = together(back_home[1], swap_cores(given))

    mid_grad, attention_low, context_grad, logit_grad, norm2_part = run_home_back(
        back_home, gates, router, mid, inverse_two, norm2_gain[None], cotangent, w_out_all
    )
    received, *mix_parts, context_grad, logit_grad = together(
        received, *mix_parts, context_grad, logit_grad
    )
    mix_arrived = scatter_first(mix_parts)
    kept = run_weight_grads(core.astype(jnp.int32).reshape(1), done[1], received)
    context_grad = lax.all_to_all(
        context_grad.reshape(planes, query_width, tok_rows), "tensor", split_axis=0, concat_axis=0
    )
    context_grad, kept = together(context_grad, kept)
    joined_grad, joined_blocks = run_attention_back(qkv, context_grad, marks, tables)
    joined_home = lax.all_to_all(joined_blocks, "tensor", split_axis=0, concat_axis=0)
    attention_all = lax.all_gather(attention_low, "tensor", axis=0, tiled=True)
    joined_part, shared = run_joined(
        gathered, joined_grad, joined_rows, payload, logit_grad, norm2_part, norm1_gain[None]
    )
    sides = jnp.concatenate([joined_part, run_out(attention_all, context)], axis=0)

    share = sides.shape[0] // (2 * owners)
    shared_shape = shared.shape
    shared_rows = shared.size // LANES
    shared = shared.reshape(shared_rows, LANES)
    shared = jnp.pad(shared, ((0, 2 * owners * share - shared_rows), (0, 0)))
    blocks = jnp.concatenate(
        [sides.reshape(2, owners, share, width), shared.reshape(2, owners, share, LANES)], axis=3
    )
    def of_core(which):
        return lax.dynamic_index_in_dim(blocks, which, 0, keepdims=False)

    blocks, theirs, joined_home, kept, *mix_arrived = together(
        blocks, swap_cores(of_core(1 - core)), joined_home, kept, *mix_arrived
    )
    weight_sum = lax.psum_scatter(kept, "tensor", scatter_dimension=1, tiled=True)

    part = of_core(core).astype(f32) + theirs.astype(f32)
    arrived = lax.all_to_all(part.astype(bf16), "expert", split_axis=0, concat_axis=0)

    def rows_of(which):
        count = joined_width // 2
        rows = lax.dynamic_slice_in_dim(joined_home, which * count, count, 1)
        return rows.reshape(-1, tok_rows)

    normed_one_grad = contract(rows_of(core), half_joined.reshape(-1, width), 0, 0)
    normed_one_grad += contract(
        rows_of(1 - core), swap_cores(half_joined).reshape(-1, width), 0, 0
    )
    arrived, normed_one_grad, *mix_line = together(
        arrived, normed_one_grad, *sum_first(mix_arrived)
    )
    total = jnp.sum(arrived.astype(f32), axis=0)
    total = jnp.concatenate([total[:, :width], ring_sum(total[:, width:])], axis=1).astype(bf16)
    spread = lax.all_to_all(
        jnp.broadcast_to(total[None], arrived.shape), "expert", split_axis=0, concat_axis=0
    )
    mixture = sum(part.astype(f32) for part in scatter_second(mix_line))
    spread, mixture = together(by_rows(spread), mixture)
    output = (mid + mixture).astype(bf16)
    spread, weight_sum = together(spread, weight_sum)
    other = swap_cores(spread)
    first, second = jnp.where(core == 0, spread, other), jnp.where(core == 0, other, spread)
    shared = jnp.concatenate([first, second], axis=0)[:, :, width:].reshape(-1, LANES)
    shared = shared[:shared_rows].astype(f32).reshape(shared_shape)
    first = first[:, :, :width].reshape(-1, width)
    second = second[:, :, :width].reshape(-1, width)
    query_sum = first[:query_width].astype(f32).T
    key_sum = first[query_width:].astype(f32).T
    value_sum = second[:kv_width].astype(f32).T
    out_sum = second[kv_width:].astype(f32)
    weight_sum = weight_sum.reshape(local_experts, 3, part_rows, hidden_width)
    w_gate_grad = weight_sum[:, 0].astype(f32)
    w_up_grad = weight_sum[:, 1].astype(f32)
    w_down_grad = weight_sum[:, 2].reshape(local_experts, chunks, down_rows, hidden_width)
    w_down_grad = w_down_grad.transpose(0, 2, 1, 3).reshape(local_experts, down_rows, width)
    w_down_grad = w_down_grad.astype(f32)
    input_part, _ = rms_backward(token_f32, inverse_one, norm1_gain, normed_one_grad)
    input_grad = mid_grad + input_part
    return (
        output,
        input_grad,
        shared[experts + 1],
        query_sum,
        key_sum,
        value_sum,
        out_sum,
        shared[experts],
        shared[:experts].T,
        w_gate_grad,
        w_up_grad,
        w_down_grad,
    )


def solution(mesh):
    rows = P(("dp", "expert", "tensor"), None)
    columns = P(None, "tensor")
    experts = P("expert", ("dp", "tensor"), None)
    return jax.shard_map(
        local,
        mesh=mesh,
        in_specs=(
            rows,
            P(("dp", "expert"), None),
            rows,
            P(),
            columns,
            columns,
            columns,
            P("tensor", None),
            P(),
            P(),
            experts,
            experts,
            experts,
            rows,
        ),
        out_specs=(
            rows,
            rows,
            P(),
            columns,
            columns,
            columns,
            P("tensor", None),
            P(),
            P(),
            experts,
            experts,
            experts,
        ),
        check_vma=False,
    )
```

```python
import functools

import jax
import jax.numpy as jnp
import numpy as np
from jax import lax
from jax.experimental import pallas as pl
from jax.experimental.layout import Layout, with_layout_constraint
from jax.experimental.pallas import tpu as pltpu
from jax.sharding import PartitionSpec as P

HEAD_DIM = 64
HALF = HEAD_DIM // 2
TOP = 8
CAP = 64
EXPERTS = 32
HOLDERS = 16
VMEM_BYTES = 57 * 1024 * 1024
LANES = 128

epsilon_norm = 1e-06
rope_theta = 10000.0
masked_score = -1e30
QUERY_ROWS = 512
SCALE = HEAD_DIM ** (-0.5)
f32 = jnp.float32
bf16 = jnp.bfloat16


def rms_inverse(values):
    return lax.rsqrt(jnp.mean(values * values, axis=-1, keepdims=True) + epsilon_norm)


def rms_backward(values, inverse, norm_gain, grad_out):
    scaled = grad_out * norm_gain
    grad_in = inverse * scaled - values * (inverse * inverse * inverse) * jnp.mean(
        scaled * values, axis=-1, keepdims=True
    )
    return (grad_in, grad_out * values * inverse)


def dot32(left, right):
    return jnp.dot(left, right, preferred_element_type=f32)


SIDE = 4
STEPS = (0, 1, -1, 2)


def by_rows(values):
    return with_layout_constraint(values, Layout(major_to_minor=tuple(range(values.ndim))))


def cross(values, stage, step):
    pairs = []
    plane = SIDE * SIDE
    for core in range(2):
        for x in range(SIDE):
            for y in range(SIDE):
                if core == stage:
                    to = x * SIDE + (y + step) % SIDE
                else:
                    to = (x + step) % SIDE * SIDE + y
                pairs.append((core * plane + x * SIDE + y, core * plane + to))
    return lax.ppermute(values, ("dp", "expert"), pairs)


def gather_first(values):
    values = by_rows(values)
    line = jnp.stack([values] + [cross(values, 0, step) for step in STEPS[1:]])
    return by_rows(line)


def gather_second(line):
    return [line] + [cross(line, 1, step) for step in STEPS[1:]]


def scatter_first(parts):
    return [parts[0]] + [
        by_rows(cross(part, 1, -step)) for part, step in zip(parts[1:], STEPS[1:])
    ]


def sum_kernel(*refs):
    arrived, outs = refs[:SIDE], refs[SIDE:]
    total = sum(ref[0].astype(f32) for ref in arrived).astype(bf16)
    for place, out in enumerate(outs):

        @pl.when(pl.program_id(0) == place)
        def _():
            out[...] = total


def sum_first(arrived):
    rows, columns = arrived[0].shape[1:]
    return pl.pallas_call(
        sum_kernel,
        grid=(SIDE,),
        out_shape=[jax.ShapeDtypeStruct((rows, columns), bf16)] * SIDE,
        in_specs=[pl.BlockSpec((1, rows, columns), lambda place: (place, 0, 0))] * SIDE,
        out_specs=[pl.BlockSpec((rows, columns), lambda place: (0, 0))] * SIDE,
        compiler_params=pltpu.CompilerParams(vmem_limit_bytes=24 * 1024 * 1024),
        cost_estimate=pl.CostEstimate(flops=1 << 22, bytes_accessed=8 << 20, transcendentals=0),
    )(*arrived)


def scatter_second(line):
    return [line[0]] + [
        by_rows(cross(part, 0, -step)) for part, step in zip(line[1:], STEPS[1:])
    ]


def ring_sum(values):
    size = lax.axis_size("tensor")
    step = 1
    while step < size:
        pairs = [(i, i ^ step) for i in range(size)]
        values = values + lax.ppermute(values, "tensor", pairs)
        step *= 2
    return values


def together(*values):
    return lax.optimization_barrier(values)


def swap_cores(values):
    return lax.ppermute(values, "dp", [(0, 1), (1, 0)])


def contract(left, right, left_dim, right_dim):
    return lax.dot_general(
        left, right, (((left_dim,), (right_dim,)), ((), ())), preferred_element_type=f32
    )


def allowed(rows, first, wide, col_ref, row_ref):
    query = first + lax.broadcasted_iota(jnp.int32, (rows, wide), 0)
    key = lax.broadcasted_iota(jnp.int32, (rows, wide), 1)
    return (key <= query) & (col_ref[first : first + rows, :] == row_ref[:, :wide])


def probabilities(query, key, mask):
    scores = jnp.where(mask, contract(query, key, 1, 1), masked_score)
    weights = jnp.exp(scores - jnp.max(scores, axis=1, keepdims=True))
    return weights * (1.0 / jnp.sum(weights, axis=1, keepdims=True))


def turn(values, cosine, sine):
    size = values.shape[1]
    first = lax.broadcasted_iota(jnp.int32, values.shape, 1) % HEAD_DIM < HALF
    other = jnp.where(
        first, -pltpu.roll(values, size - HALF, 1), pltpu.roll(values, HALF, 1)
    )
    tables = [jnp.concatenate([table] * (size // LANES), axis=1) for table in (cosine, sine)]
    return values * tables[0] + other * tables[1]


def attention_kernel(
    x_ref, w_ref, col_ref, row_ref, cos_ref, sin_ref, out_ref, turned_ref, qkv_ref
):
    seq_len = out_ref.shape[0]
    tokens = turned_ref.shape[2]
    heads = out_ref.shape[1] // HEAD_DIM
    last = (heads + 1) * HEAD_DIM
    step = QUERY_ROWS
    for first in range(0, seq_len, step):
        at = slice(first, first + step)
        wide = first + step
        blocks = range(first // tokens, wide // tokens)
        rows = jnp.concatenate([x_ref[block, :tokens, :] for block in blocks], axis=0)
        joined = contract(rows, w_ref[...], 1, 1)
        turned_part = turn(joined[:, :last], cos_ref[at, :], sin_ref[at, :])
        qkv_ref[at, :last] = turned_part.astype(bf16)
        qkv_ref[at, last:] = joined[:, last:].astype(bf16)
        mask = allowed(step, first, wide, col_ref, row_ref)
        key = qkv_ref[:wide, heads * HEAD_DIM : last]
        value = qkv_ref[:wide, last:]
        for head in range(heads):
            place = slice(head * HEAD_DIM, (head + 1) * HEAD_DIM)
            query = qkv_ref[at, place] * SCALE
            probs = probabilities(query, key, mask).astype(bf16)
            context = jnp.dot(probs, value, preferred_element_type=f32)
            out_ref[at, place] = context.astype(bf16)
            for block in range(step // tokens):
                turned_ref[first // tokens + block, place, :] = context[
                    block * tokens : (block + 1) * tokens
                ].T.astype(bf16)


def attention_back_kernel(
    qkv_ref, grad_ref, col_ref, row_ref, cos_ref, sin_ref, out_ref, turned_ref, key_sum, value_sum
):
    seq_len = qkv_ref.shape[0]
    heads = grad_ref.shape[1] // HEAD_DIM
    tokens = grad_ref.shape[2]
    last = (heads + 1) * HEAD_DIM
    step = QUERY_ROWS
    for first in reversed(range(0, seq_len, step)):
        at = slice(first, first + step)
        wide = first + step
        mask = allowed(step, first, wide, col_ref, row_ref)
        key = qkv_ref[:wide, heads * HEAD_DIM : last]
        value = qkv_ref[:wide, last:]
        key_grad = jnp.zeros((wide, HEAD_DIM), f32)
        value_grad = jnp.zeros((wide, HEAD_DIM), f32)
        query_grads = []
        for head in range(heads):
            place = slice(head * HEAD_DIM, (head + 1) * HEAD_DIM)
            query = qkv_ref[at, place] * SCALE
            grad = [
                grad_ref[first // tokens + block, place, :].astype(f32).T.astype(bf16)
                for block in range(step // tokens)
            ]
            grad = jnp.concatenate(grad, axis=0)
            probs = probabilities(query, key, mask)
            probs_grad = contract(grad, value, 1, 1)
            row_dot = jnp.sum(probs * probs_grad, axis=1, keepdims=True)
            score_grad = (probs * (probs_grad - row_dot)).astype(bf16)
            query_grads.append(jnp.dot(score_grad, key, preferred_element_type=f32) * SCALE)
            key_grad += contract(score_grad, query, 0, 0)
            value_grad += contract(probs.astype(bf16), grad, 0, 0)
        if wide == seq_len:
            key_sum[...] = key_grad
            value_sum[...] = value_grad
        else:
            key_sum[:wide, :] += key_grad
            value_sum[:wide, :] += value_grad
        both = jnp.concatenate(query_grads + [key_sum[at, :]], axis=1)
        both = turn(both, cos_ref[at, :], -sin_ref[at, :])
        out_ref[at, :last] = both.astype(bf16)
        out_ref[at, last:] = value_sum[at, :].astype(bf16)
        for block in range(step // tokens):
            part = slice(block * tokens, (block + 1) * tokens)
            to = first // tokens + block
            turned_ref[to, :last, :] = both[part].T.astype(bf16)
            turned_ref[to, last:, :] = value_sum[first : first + step, :][part].T.astype(bf16)


def run_attention(gathered, joined_rows, marks, tables):
    planes = gathered.shape[0]
    seq_len = marks[0].shape[0]
    joined_width = joined_rows.shape[0]
    query_width = joined_width - 2 * HEAD_DIM
    vmem = pl.BlockSpec(memory_space=pltpu.VMEM)
    return pl.pallas_call(
        attention_kernel,
        out_shape=(
            jax.ShapeDtypeStruct((seq_len, query_width), bf16),
            jax.ShapeDtypeStruct((planes, query_width, seq_len // planes), bf16),
            jax.ShapeDtypeStruct((seq_len, joined_width), bf16),
        ),
        in_specs=[vmem] * 6,
        out_specs=(vmem,) * 3,
        compiler_params=pltpu.CompilerParams(vmem_limit_bytes=VMEM_BYTES),
        cost_estimate=pl.CostEstimate(
            flops=1 << 28, bytes_accessed=1 << 20, transcendentals=0
        ),
    )(gathered, joined_rows, *marks, *tables)


def run_attention_back(qkv, context_grad, marks, tables):
    seq_len, joined_width = qkv.shape
    planes = context_grad.shape[0]
    vmem = pl.BlockSpec(memory_space=pltpu.VMEM)
    return pl.pallas_call(
        attention_back_kernel,
        out_shape=(
            jax.ShapeDtypeStruct((seq_len, joined_width), bf16),
            jax.ShapeDtypeStruct((planes, joined_width, seq_len // planes), bf16),
        ),
        in_specs=[vmem] * 6,
        out_specs=(vmem, vmem),
        scratch_shapes=[pltpu.VMEM((seq_len, HEAD_DIM), f32)] * 2,
        compiler_params=pltpu.CompilerParams(vmem_limit_bytes=VMEM_BYTES),
        cost_estimate=pl.CostEstimate(
            flops=1 << 28, bytes_accessed=1 << 20, transcendentals=0
        ),
    )(qkv, context_grad, *marks, *tables)


def rope_tables(seq_len):
    frequency = np.float32(rope_theta) ** (np.arange(HALF, dtype=np.float32) * np.float32(-2.0 / HEAD_DIM))
    angles = np.arange(seq_len, dtype=np.float32)[:, None] * frequency.astype(np.float32)[None, :]
    angles = np.tile(angles, (1, LANES // HALF))
    return jnp.asarray(np.cos(angles)), jnp.asarray(np.sin(angles))


def segment_marks(key_seg):
    marks = jnp.where(key_seg == 0, -1 - jnp.arange(key_seg.shape[0], dtype=jnp.int32), key_seg)
    return marks[:, None], marks[None, :]


def expert_kernel(groups, first_ref, *refs):
    rows_refs, cots_refs = refs[:groups], refs[groups : 2 * groups]
    w_ref = refs[2 * groups]
    back_outs = refs[2 * groups + 1 : 3 * groups + 1]
    x_ref, c_ref, gate_ref, up_ref, hid_ref, pick_ref = refs[3 * groups + 1 : 3 * groups + 7]
    down_ref, next_x, next_c, gates_ref = refs[3 * groups + 7 :]
    sources, tokens, _ = rows_refs[0].shape
    width = x_ref.shape[2]
    e = pl.program_id(0)
    expert = first_ref[0] + e
    at = pl.ds(pl.multiple_of(e * CAP, CAP), CAP)
    every = [(group, source) for group in range(groups) for source in range(sources)]

    @pl.when(e == 0)
    def _():
        pair = 2 * CAP
        lane = lax.broadcasted_iota(jnp.int32, (pair, LANES), 1)
        expert_of = expert + lax.broadcasted_iota(jnp.int32, (pair, LANES), 0) // CAP
        own = (lane == expert_of) | (lane == expert_of + EXPERTS)
        row_id = lax.broadcasted_iota(jnp.int32, (EXPERTS, tokens), 0)
        slot = lax.broadcasted_iota(jnp.int32, (pair, tokens), 0)
        place_of = jnp.where(slot < CAP, slot, slot - CAP).astype(f32)
        for order, (group, source) in enumerate(every):
            table = cots_refs[group][source, :EXPERTS, width:].astype(f32)
            ranks = [
                jnp.sum(jnp.where(row_id == expert + i, table, 0.0), axis=0, keepdims=True)
                for i in range(2)
            ]
            pick = (jnp.where(slot < CAP, ranks[0], ranks[1]) == place_of).astype(bf16)
            pick_ref[order] = pick
            rows = jnp.dot(pick, rows_refs[group][source], preferred_element_type=f32)
            cots = jnp.dot(pick, cots_refs[group][source, :, :width], preferred_element_type=f32)
            gate = jnp.sum(jnp.where(own, rows[:, width:], 0.0), axis=1, keepdims=True)
            gate = jnp.broadcast_to(gate, (pair, LANES))
            place = slice(order * CAP, (order + 1) * CAP)
            x_ref[0, place] = rows[:CAP, :width].astype(bf16)
            c_ref[0, place] = cots[:CAP].astype(bf16)
            gates_ref[0, place] = gate[:CAP]
            next_x[place] = rows[CAP:, :width].astype(bf16)
            next_c[place] = cots[CAP:].astype(bf16)
            gates_ref[1, place] = gate[CAP:]

    @pl.when(e == 1)
    def _():
        x_ref[0] = next_x[...]
        c_ref[0] = next_c[...]

    gate = gates_ref[e][:, :1]
    join_chunks(down_ref, w_ref.at[2], HOLDERS)
    x = x_ref[0]
    gate_pre = jnp.dot(x, w_ref[0], preferred_element_type=f32)
    up_pre = jnp.dot(x, w_ref[1], preferred_element_type=f32)
    back = contract(c_ref[0], down_ref[...], 1, 1)
    sig = 1.0 / (1.0 + jnp.exp(-gate_pre))
    silu = gate_pre * sig
    hidden = (silu * up_pre).astype(bf16)
    gate_grad = jnp.sum(back * hidden.astype(f32), axis=1, keepdims=True)
    grad = gate * back
    gate_pre_grad = (grad * up_pre * (sig + silu * (1.0 - sig))).astype(bf16)
    up_pre_grad = (grad * silu).astype(bf16)
    gate_ref[0] = gate_pre_grad
    up_ref[0] = up_pre_grad
    hid_ref[0] = (gate * hidden.astype(f32)).astype(bf16)
    row_grad = contract(gate_pre_grad, w_ref[0], 1, 1) + contract(up_pre_grad, w_ref[1], 1, 1)
    high = gate_grad.astype(bf16).astype(f32)
    lane = lax.broadcasted_iota(jnp.int32, (len(every) * CAP, LANES), 1)
    tail = jnp.where(lane == expert, high, 0.0)
    tail += jnp.where(lane == expert + EXPERTS, gate_grad - high, 0.0)
    for order, (group, source) in enumerate(every):
        place = slice(order * CAP, (order + 1) * CAP)
        back_outs[group][source, at, :width] = row_grad[place].astype(bf16)
        back_outs[group][source, at, width:] = tail[place].astype(bf16)

    @pl.when(e == 1)
    def _():
        for order, (group, source) in enumerate(every):
            back_outs[group][source] = contract(
                pick_ref[order], back_outs[group][source], 0, 0
            ).astype(bf16)


def home_kernel(
    context_ref, w_out_ref, tokens_ref, gain_ref, router_ref, member_ref, mid_ref, inverse_ref, payload_ref, gates_ref
):
    width = tokens_ref.shape[1]
    mid = tokens_ref[...].astype(f32) + contract(context_ref[...], w_out_ref[...], 0, 0)
    inverse = rms_inverse(mid)
    normed = (mid * inverse * gain_ref[...]).astype(bf16)
    mid_ref[...] = mid
    inverse_ref[...] = inverse
    payload_ref[:, :width] = normed
    member = member_ref[...] > 0
    logits = jnp.where(member, contract(normed, router_ref[...], 1, 1), masked_score)
    chosen = jnp.where(member, jnp.exp(logits - jnp.max(logits, axis=1, keepdims=True)), 0.0)
    gates = chosen / jnp.sum(chosen, axis=1, keepdims=True)
    gates_ref[...] = gates
    high = gates.astype(bf16).astype(f32)
    rest = jnp.zeros((gates.shape[0], LANES - 2 * gates.shape[1]), f32)
    payload_ref[:, width:] = jnp.concatenate([high, gates - high, rest], axis=1).astype(bf16)


def run_home(context, w_out, tokens, gain, router, member):
    rows, width = tokens.shape
    vmem = pl.BlockSpec(memory_space=pltpu.VMEM)
    return pl.pallas_call(
        home_kernel,
        out_shape=(
            jax.ShapeDtypeStruct((rows, width), f32),
            jax.ShapeDtypeStruct((rows, 1), f32),
            jax.ShapeDtypeStruct((rows, width + LANES), bf16),
            jax.ShapeDtypeStruct(member.shape, f32),
        ),
        in_specs=[vmem] * 6,
        out_specs=(vmem,) * 4,
        compiler_params=pltpu.CompilerParams(vmem_limit_bytes=24 * 1024 * 1024),
        cost_estimate=pl.CostEstimate(flops=1 << 30, bytes_accessed=8 << 20, transcendentals=0),
    )(context, w_out, tokens, gain, router, member)


def home_back_kernel(*refs):
    parts, refs = refs[:SIDE], refs[SIDE:]
    gates_ref, router_ref, mid_ref, inverse_ref, gain_ref, cot_ref, w_out_ref = refs[:7]
    grad_ref, low_ref, context_ref, logit_ref, norm_ref = refs[7:]
    width = mid_ref.shape[1]
    gates = gates_ref[...]
    experts = gates.shape[1]
    total = sum(ref[...].astype(f32) for ref in parts)
    tail = total[:, width:]
    gate_grad = tail[:, :experts] + tail[:, experts : 2 * experts]
    chosen = gates * (gate_grad - jnp.sum(gates * gate_grad, axis=1, keepdims=True))
    logit_grad = chosen.astype(bf16)
    logit_ref[...] = logit_grad
    normed_grad = total[:, :width] + jnp.dot(
        logit_grad, router_ref[...], preferred_element_type=f32
    )
    mid, inverse = mid_ref[...], inverse_ref[...]
    scaled = normed_grad * gain_ref[...]
    norm_ref[...] = jnp.sum(normed_grad * mid * inverse, axis=0, keepdims=True)
    mean = jnp.mean(scaled * mid, axis=1, keepdims=True)
    grad = cot_ref[...].astype(f32) + inverse * scaled - mid * (inverse * inverse * inverse) * mean
    grad_ref[...] = grad
    low = grad.astype(bf16)
    low_ref[...] = low
    context_ref[...] = contract(w_out_ref[...], low, 1, 1).astype(bf16)


def run_home_back(parts, gates, router, mid, inverse, gain, cotangent, w_out):
    rows, width = mid.shape
    vmem = pl.BlockSpec(memory_space=pltpu.VMEM)
    return pl.pallas_call(
        home_back_kernel,
        out_shape=(
            jax.ShapeDtypeStruct((rows, width), f32),
            jax.ShapeDtypeStruct((rows, width), bf16),
            jax.ShapeDtypeStruct((w_out.shape[0], rows), bf16),
            jax.ShapeDtypeStruct(gates.shape, bf16),
            jax.ShapeDtypeStruct((1, width), f32),
        ),
        in_specs=[vmem] * (SIDE + 7),
        out_specs=(vmem,) * 5,
        compiler_params=pltpu.CompilerParams(vmem_limit_bytes=24 * 1024 * 1024),
        cost_estimate=pl.CostEstimate(flops=1 << 30, bytes_accessed=8 << 20, transcendentals=0),
    )(*parts, gates, router, mid, inverse, gain, cotangent, w_out)


def join_chunks(to_ref, from_ref, holders):
    inner = from_ref.shape[1]
    rows = inner // HOLDERS
    chunks = to_ref.shape[1] // inner
    for holder in range(holders):
        for chunk in range(chunks):
            start = (holder * chunks + chunk) * rows
            to_ref[
                holder * rows : (holder + 1) * rows, chunk * inner : (chunk + 1) * inner
            ] = from_ref[start : start + rows, :]


def run_experts(first, rows, cots, weights):
    groups = len(rows)
    sources, tokens, padded = rows[0].shape
    width = padded - LANES
    inner = weights.shape[2]
    slots = groups * sources * CAP

    def once(columns):
        return pl.BlockSpec(
            (sources, tokens, columns), lambda e: (0, 0, 0), pipeline_mode=pl.Buffered(1)
        )

    def by_expert(*shape):
        return pl.BlockSpec(shape, lambda e: (e, 0, 0))

    acts = jax.ShapeDtypeStruct((2, slots, inner), bf16)
    wide = jax.ShapeDtypeStruct((2, slots, width), bf16)
    outs = pl.pallas_call(
        functools.partial(expert_kernel, groups),
        grid=(2,),
        out_shape=(
            *[jax.ShapeDtypeStruct((sources, tokens, padded), bf16)] * groups,
            wide,
            wide,
            acts,
            acts,
            acts,
            jax.ShapeDtypeStruct((groups * sources, 2 * CAP, tokens), bf16),
        ),
        in_specs=[pl.BlockSpec(memory_space=pltpu.SMEM)]
        + [once(padded)] * (2 * groups)
        + [by_expert(3, width, inner)],
        out_specs=(
            *[once(padded)] * groups,
            by_expert(1, slots, width),
            by_expert(1, slots, width),
            by_expert(1, slots, inner),
            by_expert(1, slots, inner),
            by_expert(1, slots, inner),
            pl.BlockSpec((groups * sources, 2 * CAP, tokens), lambda e: (0, 0, 0)),
        ),
        scratch_shapes=[
            pltpu.VMEM((inner, width), bf16),
            pltpu.VMEM((slots, width), bf16),
            pltpu.VMEM((slots, width), bf16),
            pltpu.VMEM((2, slots, LANES), f32),
        ],
        compiler_params=pltpu.CompilerParams(vmem_limit_bytes=VMEM_BYTES),
        cost_estimate=pl.CostEstimate(
            flops=2 * 2 * 6 * slots * width * inner, bytes_accessed=24 << 20, transcendentals=0
        ),
    )(first, *rows, *cots, weights)
    return outs[:groups], outs[groups:-1], outs[-1]


def mixture_kernel(groups, *refs):
    pick_refs, hid_refs = refs[:groups], refs[groups : 2 * groups]
    w_ref = refs[2 * groups]
    outs, down_ref = refs[2 * groups + 1 : -1], refs[-1]
    e = pl.program_id(0)
    at = pl.ds(pl.multiple_of(e * CAP, CAP), CAP)
    join_chunks(down_ref, w_ref.at[0], HOLDERS)
    sources = [
        (pick_ref, hid_ref, source)
        for pick_ref, hid_ref in zip(pick_refs, hid_refs)
        for source in range(pick_ref.shape[0])
    ]
    to = {}
    for order, (pick_ref, hid_ref, source) in enumerate(sources):
        to[order] = (outs[order // SIDE], order % SIDE, pick_ref, source)
    order = 0
    for pick_ref, hid_ref in zip(pick_refs, hid_refs):
        mixed = jnp.dot(hid_ref[0], down_ref[...], preferred_element_type=f32).astype(bf16)
        for source in range(pick_ref.shape[0]):
            out, place, _, _ = to[order]
            out[place, at] = mixed[source * CAP : (source + 1) * CAP]
            order += 1

    @pl.when(e == 1)
    def _():
        for out, place, pick_ref, source in to.values():
            out[place] = contract(pick_ref[source], out[place], 0, 0).astype(bf16)


def run_mixture(picks, hidden, weights):
    width, inner = weights.shape[1:]
    groups = len(picks)

    def once(shape):
        return pl.BlockSpec(shape, lambda e: (0, 0, 0), pipeline_mode=pl.Buffered(1))

    shapes = [(SIDE, picks[0].shape[2], width)] * SIDE
    return pl.pallas_call(
        functools.partial(mixture_kernel, groups),
        grid=(2,),
        out_shape=[jax.ShapeDtypeStruct(shape, bf16) for shape in shapes],
        in_specs=[once(pick.shape) for pick in picks]
        + [pl.BlockSpec((1,) + hid.shape[1:], lambda e: (e, 0, 0)) for hid in hidden]
        + [pl.BlockSpec((1, width, inner), lambda e: (3 * e + 2, 0, 0))],
        out_specs=[once(shape) for shape in shapes],
        scratch_shapes=[pltpu.VMEM((inner, width), bf16)],
        compiler_params=pltpu.CompilerParams(vmem_limit_bytes=VMEM_BYTES),
        cost_estimate=pl.CostEstimate(flops=1 << 32, bytes_accessed=1 << 20, transcendentals=0),
    )(*picks, *hidden, weights)


def weight_grad_kernel(groups, half_ref, *refs):
    x_refs, c_refs, gate_refs, up_refs, hid_refs = (
        refs[i * groups : (i + 1) * groups] for i in range(5)
    )
    *onto, out_ref = refs[5 * groups :]
    width = x_refs[0].shape[2]
    inner = gate_refs[0].shape[2]
    half = half_ref[0]
    rows = width // 2
    down_rows = inner // HOLDERS
    chunks = width // inner
    cols = pl.ds(pl.multiple_of(half * rows, LANES), rows)
    down_cols = pl.ds(pl.multiple_of(half * (inner // 2), LANES), inner // 2)
    gate = jnp.zeros((rows, inner), f32)
    up = jnp.zeros((rows, inner), f32)
    down = jnp.zeros((inner // 2, width), f32)
    for i in range(groups):
        x = x_refs[i][0, :, cols]
        gate += contract(x, gate_refs[i][0], 0, 0)
        up += contract(x, up_refs[i][0], 0, 0)

    def put(place, at, values):
        if onto:
            values = values + onto[0][place, at, :].astype(f32)
        out_ref[place, at, :] = values.astype(bf16)

    put(0, slice(0, rows), gate)
    put(1, slice(0, rows), up)
    for i in range(groups):
        down += contract(hid_refs[i][0, :, down_cols], c_refs[i][0], 0, 0)
    for holder in range(HOLDERS // 2):
        for chunk in range(chunks):
            start = (holder * chunks + chunk) * down_rows
            put(
                2,
                slice(start, start + down_rows),
                down[
                    holder * down_rows : (holder + 1) * down_rows,
                    chunk * inner : (chunk + 1) * inner,
                ],
            )


def run_weight_grads(half, saved, *onto):
    x, c, gate, up, hid = zip(*saved)
    width = x[0].shape[2]
    inner = gate[0].shape[2]
    operands = (*x, *c, *gate, *up, *hid)
    out_spec = pl.BlockSpec((3, width // 2, inner), lambda e: (e, 0, 0))
    return pl.pallas_call(
        functools.partial(weight_grad_kernel, len(saved)),
        grid=(2,),
        out_shape=jax.ShapeDtypeStruct((6, width // 2, inner), bf16),
        in_specs=[pl.BlockSpec(memory_space=pltpu.SMEM)]
        + [pl.BlockSpec((1,) + v.shape[1:], lambda e: (e, 0, 0)) for v in operands]
        + [out_spec] * len(onto),
        out_specs=out_spec,
        compiler_params=pltpu.CompilerParams(vmem_limit_bytes=VMEM_BYTES),
        cost_estimate=pl.CostEstimate(flops=1 << 28, bytes_accessed=1 << 20, transcendentals=0),
    )(half, *operands, *onto)


def joined_kernel(
    x_ref, grad_ref, w_ref, normed_ref, logit_ref, norm_ref, gain_ref, out_ref, shared_ref
):
    planes = x_ref.shape[0]
    tokens = grad_ref.shape[0] // planes
    experts = logit_ref.shape[1]
    step = x_ref.shape[2] // 2
    for first in range(0, x_ref.shape[2], step):
        at = slice(first, first + step)
        rows = jnp.concatenate([x_ref[plane, :tokens, at] for plane in range(planes)], axis=0)
        joined = contract(grad_ref[...], rows, 0, 0)
        out_ref[:, at] = joined.astype(bf16)
        norm1 = jnp.sum(joined * w_ref[:, at].astype(f32), axis=0, keepdims=True) / gain_ref[:, at]
        shared_ref[:experts, at] = contract(logit_ref[...], normed_ref[:, at], 0, 0).astype(bf16)
        shared_ref[experts : experts + 1, at] = norm_ref[:, at].astype(bf16)
        shared_ref[experts + 1 : experts + 2, at] = norm1.astype(bf16)


def run_joined(gathered, joined_grad, joined_rows, normed_two, logits, norm_terms, gain):
    vmem = pl.BlockSpec(memory_space=pltpu.VMEM)
    width = gathered.shape[2]
    return pl.pallas_call(
        joined_kernel,
        out_shape=(
            jax.ShapeDtypeStruct((joined_grad.shape[1], width), bf16),
            jax.ShapeDtypeStruct((logits.shape[1] + 2, width), bf16),
        ),
        in_specs=[vmem] * 7,
        out_specs=(vmem, vmem),
        compiler_params=pltpu.CompilerParams(vmem_limit_bytes=VMEM_BYTES),
        cost_estimate=pl.CostEstimate(flops=1 << 20, bytes_accessed=1 << 16, transcendentals=0),
    )(gathered, joined_grad, joined_rows, normed_two, logits, norm_terms, gain)


def out_kernel(all_ref, context_ref, out_ref):
    out_ref[...] = contract(context_ref[...], all_ref[...], 0, 0).astype(bf16)


def run_out(attention_all, context):
    width = attention_all.shape[1]
    rows, columns = context.shape
    step = width // 4
    return pl.pallas_call(
        out_kernel,
        grid=(4,),
        out_shape=jax.ShapeDtypeStruct((columns, width), bf16),
        in_specs=[
            pl.BlockSpec((rows, step), lambda i: (0, i)),
            pl.BlockSpec((rows, columns), lambda i: (0, 0)),
        ],
        out_specs=pl.BlockSpec((columns, step), lambda i: (0, i)),
        compiler_params=pltpu.CompilerParams(vmem_limit_bytes=VMEM_BYTES),
        cost_estimate=pl.CostEstimate(flops=1 << 20, bytes_accessed=1 << 16, transcendentals=0),
    )(attention_all, context)


def local(
    tokens,
    segments,
    routes,
    norm1_gain,
    w_query,
    w_key,
    w_value,
    w_out,
    norm2_gain,
    w_router,
    w_gate,
    w_up,
    w_down,
    cotangent,
):
    tok_rows, width = tokens.shape
    seq_len = segments.shape[1]
    query_width = w_query.shape[1]
    kv_width = w_key.shape[1]
    joined_width = query_width + 2 * kv_width
    local_experts = w_gate.shape[0]
    experts = w_router.shape[1]
    owners = lax.axis_size("expert")
    planes = lax.axis_size("tensor")
    owner = lax.axis_index("expert")
    first_expert = owner * local_experts
    key_seg = segments[0]
    hidden_width = w_gate.shape[2]

    token_f32 = tokens.astype(f32)
    inverse_one = rms_inverse(token_f32)
    normed_low = (token_f32 * inverse_one * norm1_gain).astype(bf16)
    joined_rows = by_rows(jnp.concatenate([w_query.T, w_key.T, w_value.T], axis=0))
    core = lax.axis_index("dp")

    def half_of(rows):
        count = rows.shape[0] // 2
        return lax.dynamic_slice_in_dim(rows, core * count, count, 0)

    place = jnp.where(core == 0, owner % SIDE, owner // SIDE)
    quarter = w_out.shape[0] // SIDE
    w_out_part = lax.dynamic_slice_in_dim(w_out, place * quarter, quarter, 0)
    gathered = lax.all_gather(
        by_rows(jnp.concatenate([normed_low, w_out_part], axis=0)), "tensor", axis=0
    )

    expert_ids = jnp.arange(experts, dtype=jnp.int32)
    onehot = (routes[:, :, None] == expert_ids[None, None, :]).astype(f32)
    member = jnp.sum(onehot, axis=1)
    lower = (jnp.arange(tok_rows)[:, None] <= jnp.arange(tok_rows)[None, :]).astype(bf16)
    rank = jnp.einsum("te,tu->eu", member.astype(bf16), lower, preferred_element_type=f32)
    rank = jnp.where(member.T > 0, rank - 1.0, -1.0).astype(bf16)
    extra = jnp.pad(rank, ((0, tok_rows - experts), (0, LANES - tok_rows)))
    cot_payload = jnp.concatenate([cotangent, extra], axis=1)

    chunks = width // hidden_width
    down_rows = w_down.shape[1]
    part_rows = w_gate.shape[1]
    down_parts = w_down.reshape(local_experts, down_rows, chunks, hidden_width)
    down_parts = down_parts.transpose(0, 2, 1, 3).reshape(local_experts, part_rows, hidden_width)
    weights = jnp.stack([w_gate, w_up, down_parts], axis=1)
    weights = weights.reshape(3 * local_experts, part_rows, hidden_width)
    tables = rope_tables(seq_len)
    marks = segment_marks(key_seg)
    cot_parts = gather_second(gather_first(cot_payload))
    joined_half = by_rows(half_of(joined_rows))
    gathered, weights, joined_rows, joined_half, member, col, row, *cot_parts = together(
        gathered, weights, joined_rows, joined_half, by_rows(member), *marks, *cot_parts
    )
    marks = col, row
    weights_all = lax.all_gather(weights, ("dp", "tensor"), axis=1, tiled=True)
    quarters = by_rows(gathered[:, tok_rows:])
    quarters = [quarters] + [by_rows(cross(quarters, 0, step)) for step in STEPS[1:]]
    context, context_blocks, qkv = run_attention(gathered, joined_rows, marks, tables)
    context_home = lax.all_to_all(context_blocks, "tensor", split_axis=0, concat_axis=0)
    w_out_all = jnp.zeros((planes, SIDE * quarter, width), bf16)
    for step, part in zip(STEPS, quarters):
        start = (place - step) % SIDE * quarter
        w_out_all = lax.dynamic_update_slice(w_out_all, part, (0, start, 0))
    w_out_all = by_rows(w_out_all.reshape(-1, width))
    context_home, w_out_all, joined_half = together(context_home, w_out_all, joined_half)
    half_joined = lax.all_gather(joined_half, "tensor", axis=0)
    router = by_rows(w_router.T)
    mid, inverse_two, payload, gates = run_home(
        context_home.reshape(planes * query_width, tok_rows),
        w_out_all,
        tokens,
        norm2_gain[None],
        router,
        member,
    )
    line = gather_first(payload)
    before, behind = (cross(line, 1, step) for step in STEPS[1:3])

    first_expert = first_expert.astype(jnp.int32).reshape(1)
    def compute(rows, cots):
        return run_experts(first_expert, rows, cots, weights_all)

    own = compute([line], cot_parts[:1])
    line, before, behind, *own_saved = together(line, before, behind, *own[1])
    far = cross(line, 1, STEPS[3])
    near = compute([before, behind], cot_parts[1:3])
    far, *near_saved = together(far, *near[1])
    last = compute([far], cot_parts[3:])
    done = [(*own[0], *near[0], *last[0]), (own_saved, near_saved, last[1])]
    back_line = scatter_first(done[0])
    mix_parts = run_mixture(
        [own[2], near[2], last[2]], [own_saved[4], near_saved[4], last[1][4]], weights_all
    )
    given = run_weight_grads((1 - core).astype(jnp.int32).reshape(1), done[1])
    n_line = len(back_line)
    *both, given, half_joined = together(*back_line, *mix_parts, given, half_joined)
    back_line, mix_parts = sum_first(both[:n_line]), both[n_line:]
    back_home = scatter_second(back_line)
    back_home[1], received = together(back_home[1], swap_cores(given))

    mid_grad, attention_low, context_grad, logit_grad, norm2_part = run_home_back(
        back_home, gates, router, mid, inverse_two, norm2_gain[None], cotangent, w_out_all
    )
    received, *mix_parts, context_grad, logit_grad = together(
        received, *mix_parts, context_grad, logit_grad
    )
    mix_arrived = scatter_first(mix_parts)
    kept = run_weight_grads(core.astype(jnp.int32).reshape(1), done[1], received)
    context_grad = lax.all_to_all(
        context_grad.reshape(planes, query_width, tok_rows), "tensor", split_axis=0, concat_axis=0
    )
    context_grad, kept = together(context_grad, kept)
    weight_sum = lax.psum_scatter(kept, "tensor", scatter_dimension=1, tiled=True)
    joined_grad, joined_blocks = run_attention_back(qkv, context_grad, marks, tables)
    joined_home = lax.all_to_all(joined_blocks, "tensor", split_axis=0, concat_axis=0)
    attention_all = lax.all_gather(attention_low, "tensor", axis=0, tiled=True)
    joined_part, shared = run_joined(
        gathered, joined_grad, joined_rows, payload, logit_grad, norm2_part, norm1_gain[None]
    )
    sides = jnp.concatenate([joined_part, run_out(attention_all, context)], axis=0)

    share = sides.shape[0] // (2 * owners)
    shared_shape = shared.shape
    shared_rows = shared.size // LANES
    shared = shared.reshape(shared_rows, LANES)
    shared = jnp.pad(shared, ((0, 2 * owners * share - shared_rows), (0, 0)))
    blocks = jnp.concatenate(
        [sides.reshape(2, owners, share, width), shared.reshape(2, owners, share, LANES)], axis=3
    )
    def of_core(which):
        return lax.dynamic_index_in_dim(blocks, which, 0, keepdims=False)

    blocks, theirs, joined_home, *mix_arrived = together(
        blocks, swap_cores(of_core(1 - core)), joined_home, *mix_arrived
    )

    part = of_core(core).astype(f32) + theirs.astype(f32)
    arrived = lax.all_to_all(part.astype(bf16), "expert", split_axis=0, concat_axis=0)

    def rows_of(which):
        count = joined_width // 2
        rows = lax.dynamic_slice_in_dim(joined_home, which * count, count, 1)
        return rows.reshape(-1, tok_rows)

    normed_one_grad = contract(rows_of(core), half_joined.reshape(-1, width), 0, 0)
    normed_one_grad += contract(
        rows_of(1 - core), swap_cores(half_joined).reshape(-1, width), 0, 0
    )
    arrived, normed_one_grad, *mix_line = together(
        arrived, normed_one_grad, *sum_first(mix_arrived)
    )
    total = jnp.sum(arrived.astype(f32), axis=0)
    total = jnp.concatenate([total[:, :width], ring_sum(total[:, width:])], axis=1).astype(bf16)
    spread = lax.all_to_all(
        jnp.broadcast_to(total[None], arrived.shape), "expert", split_axis=0, concat_axis=0
    )
    mixture = sum(part.astype(f32) for part in scatter_second(mix_line))
    spread, mixture = together(by_rows(spread), mixture)
    output = (mid + mixture).astype(bf16)
    spread, weight_sum = together(spread, weight_sum)
    other = swap_cores(spread)
    first, second = jnp.where(core == 0, spread, other), jnp.where(core == 0, other, spread)
    shared = jnp.concatenate([first, second], axis=0)[:, :, width:].reshape(-1, LANES)
    shared = shared[:shared_rows].astype(f32).reshape(shared_shape)
    first = first[:, :, :width].reshape(-1, width)
    second = second[:, :, :width].reshape(-1, width)
    query_sum = first[:query_width].astype(f32).T
    key_sum = first[query_width:].astype(f32).T
    value_sum = second[:kv_width].astype(f32).T
    out_sum = second[kv_width:].astype(f32)
    weight_sum = weight_sum.reshape(local_experts, 3, part_rows, hidden_width)
    w_gate_grad = weight_sum[:, 0].astype(f32)
    w_up_grad = weight_sum[:, 1].astype(f32)
    w_down_grad = weight_sum[:, 2].reshape(local_experts, chunks, down_rows, hidden_width)
    w_down_grad = w_down_grad.transpose(0, 2, 1, 3).reshape(local_experts, down_rows, width)
    w_down_grad = w_down_grad.astype(f32)
    input_part, _ = rms_backward(token_f32, inverse_one, norm1_gain, normed_one_grad)
    input_grad = mid_grad + input_part
    return (
        output,
        input_grad,
        shared[experts + 1],
        query_sum,
        key_sum,
        value_sum,
        out_sum,
        shared[experts],
        shared[:experts].T,
        w_gate_grad,
        w_up_grad,
        w_down_grad,
    )


def solution(mesh):
    rows = P(("dp", "expert", "tensor"), None)
    columns = P(None, "tensor")
    experts = P("expert", ("dp", "tensor"), None)
    return jax.shard_map(
        local,
        mesh=mesh,
        in_specs=(
            rows,
            P(("dp", "expert"), None),
            rows,
            P(),
            columns,
            columns,
            columns,
            P("tensor", None),
            P(),
            P(),
            experts,
            experts,
            experts,
            rows,
        ),
        out_specs=(
            rows,
            rows,
            P(),
            columns,
            columns,
            columns,
            P("tensor", None),
            P(),
            P(),
            experts,
            experts,
            experts,
        ),
        check_vma=False,
    )
```
